32 devices in a mesh: dp: 4 (over z), row: 4 (over x, core), col: 2 (over y).
Axes of the slice: x: 2, y: 2, z: 4, core: 2. Of those that a mesh axis runs over, the one named last changes fastest.
Arguments:
- latent: bfloat16 [8, 64, 64, 16], P('dp', 'row', 'col'), may hold values from -6 to 6
- skip_input: bfloat16 [8, 64, 64, 1408], P('dp', 'row', 'col'), may hold values from -6 to 6
- text_states: bfloat16 [8, 333, 1024], P('dp'), may hold values from -6 to 6
- timesteps: int32 [8], P('dp'), may hold values from 0 to 999
- image_sides: int32 [8], P('dp'), may hold values from 32 to 64, as said below
- cotangent: bfloat16 [8, 64, 64, 32], P('dp', 'row', 'col'), may hold values from -6 to 6
- w_patch: bfloat16 [1408, 16], P(('row', 'col'), 'dp'), may hold values from -1.5 to 1.5
- w_skip: bfloat16 [2816, 1408], P(('row', 'col'), 'dp'), may hold values from -0.109375 to 0.109375
- w_time: bfloat16 [256, 1408], P(('row', 'col'), 'dp'), may hold values from -0.375 to 0.375
- w_shift: bfloat16 [1408, 1408], P(('row', 'col'), 'dp'), may hold values from -0.15625 to 0.15625
- w_qkv: bfloat16 [1408, 4224], P(('row', 'col'), 'dp'), may hold values from -0.15625 to 0.15625
- w_out: bfloat16 [1408, 1408], P(('row', 'col'), 'dp'), may hold values from -2.5 to 2.5
- w_query: bfloat16 [1408, 1408], P(('row', 'col'), 'dp'), may hold values from -0.15625 to 0.15625
- w_text: bfloat16 [1024, 2816], P(('row', 'col'), 'dp'), may hold values from -0.1875 to 0.1875
- w_cross: bfloat16 [1408, 1408], P(('row', 'col'), 'dp'), may hold values from -0.625 to 0.625
- w_up: bfloat16 [1408, 6144], P(('row', 'col'), 'dp'), may hold values from -0.15625 to 0.15625
- w_down: bfloat16 [6144, 1408], P(('row', 'col'), 'dp'), may hold values from -0.078125 to 0.078125
- w_final: bfloat16 [1408, 32], P(('row', 'col'), 'dp'), may hold values from -0.15625 to 0.15625
- norm_params: bfloat16 [1408, 12], P(('row', 'col'), 'dp'), as said below
Outputs:
- prediction: bfloat16 [8, 64, 64, 32], P('dp', 'row', 'col')
- latent_grad: float32 [8, 64, 64, 16], P('dp', 'row', 'col')
- skip_grad: float32 [8, 64, 64, 1408], P('dp', 'row', 'col')
- text_grad: float32 [8, 333, 1024], P('dp', None, ('row', 'col'))
- w_patch_grad: float32 [1408, 16], P(('row', 'col'), 'dp')
- w_skip_grad: float32 [2816, 1408], P(('row', 'col'), 'dp')
- w_time_grad: float32 [256, 1408], P(('row', 'col'), 'dp')
- w_shift_grad: float32 [1408, 1408], P(('row', 'col'), 'dp')
- w_qkv_grad: float32 [1408, 4224], P(('row', 'col'), 'dp')
- w_out_grad: float32 [1408, 1408], P(('row', 'col'), 'dp')
- w_query_grad: float32 [1408, 1408], P(('row', 'col'), 'dp')
- w_text_grad: float32 [1024, 2816], P(('row', 'col'), 'dp')
- w_cross_grad: float32 [1408, 1408], P(('row', 'col'), 'dp')
- w_up_grad: float32 [1408, 6144], P(('row', 'col'), 'dp')
- w_down_grad: float32 [6144, 1408], P(('row', 'col'), 'dp')
- w_final_grad: float32 [1408, 32], P(('row', 'col'), 'dp')
- norm_params_grad: float32 [1408, 12], P(('row', 'col'), 'dp')
The draws below stay inside these ranges and needn't reach their ends.
Inputs may be any that keep to these rules, and one draw needn't show every extreme that they name: `image_sides`: in each aligned run of 2 images, one image drawn from the seed has side 64; an image of side s has its first s grid rows and first s grid columns valid. `norm_params`: even columns are gains near 1, odd columns biases.
All inputs are finite; a program needn't handle non-finite values.
Results may differ from the reference program's by a relative error of at most 0.02.
Values may be sent and summed in bfloat16 or wider, within the bound.
No kernel may reach another device: no remote copies, remote signals or barrier semaphores. Data moves between devices by JAX's collectives and lax.ppermute only.
A program may use at most 896 MiB of HBM per device.

```python
import math
import jax
import jax.numpy as jnp
from jax import lax

D = 1408
HEADS = 16
HEAD_DIM = 88
FF = 6144
TEXT = 333
TEXT_DIM = 1024
FREQ = 256
PATCH_IN = 16
OUT_CH = 32
GRID = 64
IMG_DEV = 2
IMAGES = 8


def draw_image_sides(key, part):
    key = jax.random.fold_in(key, 11)
    key_one, key_two = jax.random.split(key)
    groups = IMAGES // IMG_DEV
    drawn = jax.random.randint(key_one, (groups, IMG_DEV), GRID // 2, GRID + 1)
    chosen = jax.random.randint(key_two, (groups, 1), 0, IMG_DEV)
    drawn = jnp.where(jnp.arange(IMG_DEV)[None, :] == chosen, GRID, drawn)
    return drawn.reshape(IMAGES).astype(jnp.int32)


def draw_norm_params(key, part):
    key = jax.random.fold_in(key, 7)
    key_one, key_two = jax.random.split(key)
    gains = 1.0 + 0.3 * jax.random.uniform(key_one, (D, 12), jnp.float32, -1.0, 1.0)
    biases = 0.3 * jax.random.normal(key_two, (D, 12), jnp.float32)
    bias_columns = (jnp.arange(12) % 2 == 1)[None, :]
    return jnp.where(bias_columns, biases, gains).astype(jnp.bfloat16)


def place_ends(values, own_key, smallest, high):
    longest = values.shape.index(max(values.shape))
    spots = []
    for shift in (0, 1):
        where = [jax.random.randint(jax.random.fold_in(own_key, axis), (), 0, length) for axis, length in enumerate(values.shape)]
        where[longest] = (where[longest] + shift) % values.shape[longest]
        spots.append(tuple(where))
    return values.at[spots[0]].set(smallest).at[spots[1]].set(high)


def block_levels(rng, shape, shards, smallest, largest):
    level, own = 1.0, jax.random.fold_in(rng, 6)
    for position, shards_of in shards:
        steps = jnp.exp(jax.random.uniform(jax.random.fold_in(own, position), (shards_of,), jnp.float32, smallest / len(shards), largest / len(shards)))
        level = level * jnp.repeat(steps, shape[position] // shards_of).reshape([-1 if axis == position else 1 for axis in range(len(shape))])
    return level


def normal_values(key, shape, deviation, reach, cuts=(), held_as=jnp.bfloat16):
    gain = block_levels(key, shape, cuts, -0.22, 0.18) if cuts else 1.0
    result = jax.random.normal(key, shape, jnp.float32) * deviation * gain
    return jnp.minimum(jnp.maximum(result, -reach), reach).astype(held_as)


def setup_inputs(seed: int = 0) -> dict:
    key_of = jax.random.split(jax.random.key(seed), 20)
    return {
        "latent": normal_values(key_of[0], (IMAGES, GRID, GRID, PATCH_IN), 1.0, 6.0, ((0, 4), (1, 4), (2, 2))),
        "skip_input": normal_values(key_of[1], (IMAGES, GRID, GRID, D), 1.0, 6.0, ((0, 4), (1, 4), (2, 2))),
        "text_states": normal_values(key_of[2], (IMAGES, TEXT, TEXT_DIM), 1.0, 6.0, ((0, 4),)),
        "timesteps": place_ends(jax.random.randint(key_of[3], (IMAGES,), 0, 1000), jax.random.fold_in(key_of[3], 1), 0, 999).astype(jnp.int32),
        "image_sides": draw_image_sides(jax.random.fold_in(key_of[19], 71), 0),
        "cotangent": normal_values(key_of[5], (IMAGES, GRID, GRID, OUT_CH), 1.0, 6.0, ((0, 4), (1, 4), (2, 2))),
        "w_patch": normal_values(key_of[6], (D, PATCH_IN), PATCH_IN ** -0.5, 1.5, ((0, 8), (1, 4))),
        "w_skip": normal_values(key_of[7], (2 * D, D), (2 * D) ** -0.5, 0.109375, ((0, 8), (1, 4))),
        "w_time": normal_values(key_of[8], (FREQ, D), FREQ ** -0.5, 0.375, ((0, 8), (1, 4))),
        "w_shift": normal_values(key_of[9], (D, D), D ** -0.5, 0.15625, ((0, 8), (1, 4))),
        "w_qkv": normal_values(key_of[10], (D, 3 * D), D ** -0.5, 0.15625, ((0, 8), (1, 4))),
        "w_out": normal_values(key_of[11], (D, D), (max(1, D * 16 // (GRID * GRID))) ** -0.5, 2.5, ((0, 8), (1, 4))),
        "w_query": normal_values(key_of[12], (D, D), D ** -0.5, 0.15625, ((0, 8), (1, 4))),
        "w_text": normal_values(key_of[13], (TEXT_DIM, 2 * D), TEXT_DIM ** -0.5, 0.1875, ((0, 8), (1, 4))),
        "w_cross": normal_values(key_of[14], (D, D), (D // 16) ** -0.5, 0.625, ((0, 8), (1, 4))),
        "w_up": normal_values(key_of[15], (D, FF), D ** -0.5, 0.15625, ((0, 8), (1, 4))),
        "w_down": normal_values(key_of[16], (FF, D), FF ** -0.5, 0.078125, ((0, 8), (1, 4))),
        "w_final": normal_values(key_of[17], (D, OUT_CH), D ** -0.5, 0.15625, ((0, 8), (1, 4))),
        "norm_params": draw_norm_params(jax.random.fold_in(key_of[19], 71), 0),
    }


EPSILON = 1e-06
PRECISE = lax.Precision.HIGHEST

@jax.custom_vjp
def low(v):
    return lax.optimization_barrier(v.astype(jnp.bfloat16)).astype(jnp.float32)

@jax.custom_vjp
def low_back(v):
    return v

def low_keep(v):
    return (low(v), None)

def low_pass(kept, grad):
    return (grad,)

def back_keep(v):
    return (v, None)

def back_low(kept, grad):
    return (low(grad),)
low.defvjp(low_keep, low_pass)
low_back.defvjp(back_keep, back_low)

def layer_norm(values_in):
    centred = values_in - lax.optimization_barrier(jnp.mean(values_in, axis=-1, keepdims=True))
    return centred * lax.rsqrt(lax.optimization_barrier(jnp.mean(centred * centred, axis=-1, keepdims=True)) + EPSILON)

def matmul(left_mat, right_mat):
    return jnp.dot(left_mat, right_mat, precision=PRECISE)

def turn_half(piece_half, cosine, sine_tab):
    quarter = cosine.shape[-1]
    lower = piece_half[..., :quarter]
    higher = piece_half[..., quarter:]
    return jnp.concatenate([lower * cosine - higher * sine_tab, higher * cosine + lower * sine_tab], axis=-1)

def rotate(values_in, tables, signum):
    cos_row, sin_row, cos_col, sin_col = tables
    half_dim = values_in.shape[-1] // 2
    return jnp.concatenate([turn_half(values_in[..., :half_dim], cos_row, signum * sin_row), turn_half(values_in[..., half_dim:], cos_col, signum * sin_col)], axis=-1)

def rope_tables(row_pos, col_pos, head_size):
    quarter = head_size // 4
    frequency = jnp.exp(jnp.arange(quarter, dtype=jnp.float32) * (-math.log(10000.0) / quarter))
    row_ang = row_pos.astype(jnp.float32)[:, None, None] * frequency
    col_ang = col_pos.astype(jnp.float32)[:, None, None] * frequency
    return (jnp.cos(row_ang), jnp.sin(row_ang), jnp.cos(col_ang), jnp.sin(col_ang))

def time_embed(step_values, freq_count):
    half_dim = freq_count // 2
    rate_list = jnp.exp(jnp.arange(half_dim, dtype=jnp.float32) * (-math.log(10000.0) / half_dim))
    angles = step_values.astype(jnp.float32)[..., None] * rate_list
    return jnp.concatenate([jnp.cos(angles), jnp.sin(angles)], axis=-1)

def image_forward(patch_rows, skip_rows, text_rows, image_side, embedding, weights):
    w_patch, w_skip, w_time, w_shift, w_qkv, w_out, w_query, w_text, w_cross, w_up, w_down, w_final, norms = weights
    tokens = patch_rows.shape[0]
    positions = jnp.arange(tokens, dtype=jnp.int32)
    row_pos = positions // GRID
    col_pos = positions % GRID
    valid = (row_pos < image_side) & (col_pos < image_side)
    score_scale = HEAD_DIM ** (-0.5)
    patch_feat = low_back(matmul(patch_rows, w_patch.T))
    joined = layer_norm(jnp.concatenate([patch_feat, skip_rows], axis=-1))
    gain_skip = jnp.concatenate([norms[:, 8], norms[:, 10]])
    bias_skip = jnp.concatenate([norms[:, 9], norms[:, 11]])
    residual = low_back(matmul(low(joined * gain_skip + bias_skip), w_skip))
    time_pre = low_back(matmul(low(embedding), w_time))
    time_shift = low_back(matmul(low(jax.nn.silu(time_pre)), w_shift))
    first_in = low(layer_norm(residual) * norms[:, 0] + norms[:, 1] + time_shift)
    qkv = low_back(matmul(first_in, w_qkv))
    query_pre = qkv[:, :D].reshape(tokens, HEADS, HEAD_DIM)
    key_pre = qkv[:, D:2 * D].reshape(tokens, HEADS, HEAD_DIM)
    value_pre = qkv[:, 2 * D:].reshape(tokens, HEADS, HEAD_DIM)
    tables = rope_tables(row_pos, col_pos, HEAD_DIM)
    queries = low(rotate(layer_norm(query_pre), tables, 1.0))
    keys = low(rotate(layer_norm(key_pre), tables, 1.0))
    values = low(value_pre)
    block = math.gcd(tokens, 512)

    def attend(query_block):
        scores = low_back(jnp.einsum('qhe,khe->hqk', query_block, keys, precision=PRECISE) * score_scale)
        scores = jnp.where(valid[None, None, :], scores, -jnp.inf)
        attn_probs = low(jax.nn.softmax(scores, axis=-1))
        return low_back(jnp.einsum('hqk,khe->qhe', attn_probs, values, precision=PRECISE))
    attended = lax.map(jax.checkpoint(attend), queries.reshape(tokens // block, block, HEADS, HEAD_DIM))
    attended = low(attended.reshape(tokens, D))
    residual = residual + low_back(matmul(attended, w_out))
    third_in = low(layer_norm(residual) * norms[:, 2] + norms[:, 3])
    cross_q = low_back(matmul(third_in, w_query)).reshape(tokens, HEADS, HEAD_DIM)
    text_kv = low_back(matmul(text_rows, w_text))
    text_len = text_rows.shape[0]
    cross_queries = low(layer_norm(cross_q))
    cross_keys = low(layer_norm(text_kv[:, :D].reshape(text_len, HEADS, HEAD_DIM)))
    cross_values = low(text_kv[:, D:].reshape(text_len, HEADS, HEAD_DIM))

    def cross_attend(query_block):
        scores = low_back(jnp.einsum('qhe,khe->hqk', query_block, cross_keys, precision=PRECISE) * score_scale)
        attn_probs = low(jax.nn.softmax(scores, axis=-1))
        return low_back(jnp.einsum('hqk,khe->qhe', attn_probs, cross_values, precision=PRECISE))
    crossed = lax.map(jax.checkpoint(cross_attend), cross_queries.reshape(tokens // block, block, HEADS, HEAD_DIM))
    residual = residual + low_back(matmul(low(crossed.reshape(tokens, D)), w_cross))
    second_in = low(layer_norm(residual) * norms[:, 4] + norms[:, 5])
    up_pre = low_back(matmul(second_in, w_up))
    residual = residual + low_back(matmul(low(jax.nn.gelu(up_pre, approximate=True)), w_down))
    last_in = low(layer_norm(residual) * norms[:, 6] + norms[:, 7])
    produced = low_back(matmul(last_in, w_final))
    return produced * valid[:, None].astype(jnp.float32)

def reference(latent, skip_input, text_states, timesteps, image_sides, cotangent, w_patch, w_skip, w_time, w_shift, w_qkv, w_out, w_query, w_text, w_cross, w_up, w_down, w_final, norm_params):
    weights = tuple((item.astype(jnp.float32) for item in (w_patch, w_skip, w_time, w_shift, w_qkv, w_out, w_query, w_text, w_cross, w_up, w_down, w_final, norm_params)))
    tokens = GRID * GRID
    patch_all = latent.astype(jnp.float32).reshape(IMAGES, tokens, PATCH_IN)
    skip_all = skip_input.astype(jnp.float32).reshape(IMAGES, tokens, D)
    text_all = text_states.astype(jnp.float32)
    cot_all = cotangent.astype(jnp.float32).reshape(IMAGES, tokens, OUT_CH)
    embeds = time_embed(timesteps, FREQ)

    def per_image(grad_total, sliced_in):
        patch_rows, skip_rows, text_rows, image_side, embedding, cot_rows = sliced_in

        def forward_fn(patch_arg, skip_arg, text_arg, weight_arg):
            return image_forward(patch_arg, skip_arg, text_arg, image_side, embedding, weight_arg)
        produced, pullback = jax.vjp(forward_fn, patch_rows, skip_rows, text_rows, weights)
        grad_patch, grad_skip, grad_text, grad_weights = pullback(cot_rows)
        grad_total = jax.tree.map(jnp.add, grad_total, grad_weights)
        return (grad_total, (produced.astype(jnp.bfloat16), grad_patch, grad_skip, grad_text))
    zero_grads = tuple((jnp.zeros_like(item) for item in weights))
    grad_total, (outputs, grad_patch, grad_skip, grad_text) = lax.scan(per_image, zero_grads, (patch_all, skip_all, text_all, image_sides, embeds, cot_all))
    return (outputs.reshape(IMAGES, GRID, GRID, OUT_CH), grad_patch.reshape(IMAGES, GRID, GRID, PATCH_IN), grad_skip.reshape(IMAGES, GRID, GRID, D), grad_text, grad_total[0], grad_total[1], grad_total[2], grad_total[3], grad_total[4], grad_total[5], grad_total[6], grad_total[7], grad_total[8], grad_total[9], grad_total[10], grad_total[11], grad_total[12])
```

```python
import functools
import math

import jax
import jax.numpy as jnp
from jax import lax
from jax.experimental import pallas as pl
from jax.experimental.pallas import tpu as pltpu
from jax.sharding import PartitionSpec as P

HEADS = 16
FREQ = 256


EPSILON = 1e-06


def layer_norm(values_in):
    centred = values_in - jnp.mean(values_in, axis=-1, keepdims=True)
    inverse = lax.rsqrt(jnp.mean(centred * centred, axis=-1, keepdims=True) + EPSILON)
    return (centred * inverse, inverse)


def norm_back(grad_normed, normed, inverse):
    mean_grad = jnp.mean(grad_normed, axis=-1, keepdims=True)
    mean_cross = jnp.mean(grad_normed * normed, axis=-1, keepdims=True)
    return inverse * (grad_normed - mean_grad - normed * mean_cross)


def turn_half(piece_half, cosine, sine_tab):
    quarter = cosine.shape[-1]
    lower = piece_half[..., :quarter]
    higher = piece_half[..., quarter:]
    return jnp.concatenate(
        [lower * cosine - higher * sine_tab, higher * cosine + lower * sine_tab], axis=-1
    )


def rotate(values_in, tables, signum):
    cos_row, sin_row, cos_col, sin_col = tables
    half_dim = values_in.shape[-1] // 2
    return jnp.concatenate(
        [
            turn_half(values_in[..., :half_dim], cos_row, signum * sin_row),
            turn_half(values_in[..., half_dim:], cos_col, signum * sin_col),
        ],
        axis=-1,
    )


def rope_tables(row_pos, col_pos, head_size):
    quarter = head_size // 4
    frequency = jnp.exp(jnp.arange(quarter, dtype=jnp.float32) * (-math.log(10000.0) / quarter))
    row_ang = row_pos.astype(jnp.float32)[:, None, None] * frequency
    col_ang = col_pos.astype(jnp.float32)[:, None, None] * frequency
    return (jnp.cos(row_ang), jnp.sin(row_ang), jnp.cos(col_ang), jnp.sin(col_ang))


def time_embed(step_values, freq_count):
    half_dim = freq_count // 2
    rate_list = jnp.exp(jnp.arange(half_dim, dtype=jnp.float32) * (-math.log(10000.0) / half_dim))
    angles = step_values.astype(jnp.float32)[..., None] * rate_list
    return jnp.concatenate([jnp.cos(angles), jnp.sin(angles)], axis=-1)


def gelu_tanh(inputs):
    return jax.nn.gelu(inputs, approximate=True)


def plain_dot(left_mat, right_mat):
    return jnp.dot(left_mat, right_mat, preferred_element_type=jnp.float32)


def left_dot(left_mat, right_mat):
    return lax.dot_general(
        left_mat, right_mat, (((0,), (0,)), ((), ())), preferred_element_type=jnp.float32
    )


def right_dot(left_mat, right_mat):
    return lax.dot_general(
        left_mat, right_mat, (((1,), (1,)), ((), ())), preferred_element_type=jnp.float32
    )


def block_size(key_count):
    block_len = key_count
    while block_len > 1024 and block_len % 2 == 0:
        block_len = block_len // 2
    return block_len


def local_gathered(
    latent,
    skip_input,
    text_states,
    timesteps,
    image_sides,
    cotangent,
    w_patch,
    w_skip,
    w_time,
    w_shift,
    w_qkv,
    w_out,
    w_query,
    w_text,
    w_cross,
    w_up,
    w_down,
    w_final,
    norm_params,
):
    widened = (
        lax.all_gather(w_patch, "dp", axis=1, tiled=True),
        lax.all_gather(w_skip, "dp", axis=1, tiled=True),
        lax.all_gather(w_time, "dp", axis=1, tiled=True),
        lax.all_gather(w_shift, "dp", axis=1, tiled=True),
        lax.all_gather(w_qkv, "dp", axis=1, tiled=True),
        lax.all_gather(w_out, "dp", axis=1, tiled=True),
        lax.all_gather(w_query, "dp", axis=1, tiled=True),
        lax.all_gather(w_text, "dp", axis=1, tiled=True),
        lax.all_gather(w_cross, "dp", axis=1, tiled=True),
        lax.all_gather(w_up, "dp", axis=1, tiled=True),
        lax.all_gather(w_down, "dp", axis=1, tiled=True),
        lax.all_gather(w_final, "dp", axis=1, tiled=True),
        lax.all_gather(norm_params, "dp", axis=1, tiled=True),
    )
    gathered = (
        lax.all_gather(widened[0], ("row", "col"), axis=0, tiled=True),
        lax.all_gather(widened[1], ("row", "col"), axis=0, tiled=True),
        lax.all_gather(widened[2], ("row", "col"), axis=0, tiled=True),
        lax.all_gather(widened[3], ("row", "col"), axis=0, tiled=True),
        lax.all_gather(widened[4], ("row", "col"), axis=0, tiled=True),
        lax.all_gather(widened[5], ("row", "col"), axis=0, tiled=True),
        lax.all_gather(widened[6], ("row", "col"), axis=0, tiled=True),
        lax.all_gather(widened[7], ("row", "col"), axis=0, tiled=True),
        lax.all_gather(widened[8], ("row", "col"), axis=0, tiled=True),
        lax.all_gather(widened[9], ("row", "col"), axis=0, tiled=True),
        lax.all_gather(widened[10], ("row", "col"), axis=0, tiled=True),
        lax.all_gather(widened[11], ("row", "col"), axis=0, tiled=True),
        lax.all_gather(widened[12], ("row", "col"), axis=0, tiled=True),
    )
    (
        f_patch,
        f_skip,
        f_time,
        f_shift,
        f_qkv,
        f_out,
        f_query,
        f_text,
        f_cross,
        f_up,
        f_down,
        f_final,
        f_norms,
    ) = gathered
    part_text = widened[7]
    images, rows_tile, cols_tile, patch_width = latent.shape
    tile_len = rows_tile * cols_tile
    row_count = images * tile_len
    model_width = f_qkv.shape[0]
    head_count = HEADS
    head_dim = model_width // head_count
    text_len = text_states.shape[1]
    grid_devices = lax.axis_size(("row", "col"))
    col_devices = lax.axis_size("col")
    grid_at = lax.axis_index(("row", "col"))
    row_at = lax.axis_index("row")
    col_at = lax.axis_index("col")
    score_scale = head_dim ** (-0.5)
    positions = jnp.arange(tile_len, dtype=jnp.int32)
    row_pos = row_at * rows_tile + positions // cols_tile
    col_pos = col_at * cols_tile + positions % cols_tile
    query_ok = (row_pos[None, :] < image_sides[:, None]) & (col_pos[None, :] < image_sides[:, None])
    keep_rows = query_ok.astype(jnp.float32).reshape(row_count, 1)
    tables = rope_tables(row_pos, col_pos, head_dim)
    norm_f = f_norms.astype(jnp.float32)

    def valid_keys(offset, block_len):
        index_list = offset + jnp.arange(block_len, dtype=jnp.int32)
        source = index_list // tile_len
        within = index_list % tile_len
        key_row = source // col_devices * rows_tile + within // cols_tile
        key_col = source % col_devices * cols_tile + within % cols_tile
        return (key_row[None, :] < image_sides[:, None]) & (key_col[None, :] < image_sides[:, None])

    patch_rows = latent.reshape(row_count, patch_width)
    patch_feat = right_dot(patch_rows, f_patch)
    skip_rows = skip_input.reshape(row_count, model_width).astype(jnp.float32)
    gain_skip = jnp.concatenate([norm_f[:, 8], norm_f[:, 10]])
    bias_skip = jnp.concatenate([norm_f[:, 9], norm_f[:, 11]])
    joined, joined_inv = layer_norm(jnp.concatenate([patch_feat, skip_rows], axis=-1))
    skip_in = (joined * gain_skip + bias_skip).astype(jnp.bfloat16)
    residual = plain_dot(skip_in, f_skip)
    embedding = time_embed(timesteps, FREQ).astype(jnp.bfloat16)
    time_pre = plain_dot(embedding, f_time)
    time_float, silu_pull = jax.vjp(jax.nn.silu, time_pre)
    time_act = time_float.astype(jnp.bfloat16)
    time_shift = plain_dot(time_act, f_shift)
    first_z, first_inv = layer_norm(residual)
    first_pre = (first_z * norm_f[:, 0] + norm_f[:, 1]).reshape(
        images, tile_len, model_width
    ) + time_shift[:, None, :]
    first_in = first_pre.reshape(row_count, model_width).astype(jnp.bfloat16)
    qkv = plain_dot(first_in, f_qkv)
    query_z, query_inv = layer_norm(
        qkv[:, :model_width].reshape(images, tile_len, head_count, head_dim)
    )
    key_z, key_inv = layer_norm(
        qkv[:, model_width : 2 * model_width].reshape(images, tile_len, head_count, head_dim)
    )
    queries = rotate(query_z, tables, 1.0).astype(jnp.bfloat16)
    queries_h = jnp.transpose(queries, (0, 2, 1, 3))
    keys = rotate(key_z, tables, 1.0).astype(jnp.bfloat16).reshape(images, tile_len, model_width)
    values = qkv[:, 2 * model_width :].astype(jnp.bfloat16).reshape(images, tile_len, model_width)
    start_carry = (
        jnp.full((images, head_count, tile_len), -1e30, jnp.float32),
        jnp.zeros((images, head_count, tile_len), jnp.float32),
        jnp.zeros((images, head_count, tile_len, head_dim), jnp.float32),
    )
    key_rows = lax.all_gather(keys, ("row", "col"), axis=1, tiled=True)
    value_rows = lax.all_gather(values, ("row", "col"), axis=1, tiled=True)
    key_count = key_rows.shape[1]
    block_len = block_size(key_count)

    def forward_block_step(block_index, running):
        running_max, weight_sum, accum_sum = running
        offset = block_index * block_len
        key_blk = lax.dynamic_slice_in_dim(key_rows, offset, block_len, 1).reshape(
            images, block_len, head_count, head_dim
        )
        value_blk = lax.dynamic_slice_in_dim(value_rows, offset, block_len, 1).reshape(
            images, block_len, head_count, head_dim
        )
        key_ok = valid_keys(offset, block_len)
        scores = (
            jnp.einsum("ihqe,ikhe->ihqk", queries_h, key_blk, preferred_element_type=jnp.float32)
            * score_scale
        )
        scores = jnp.where(key_ok[:, None, None, :], scores, -jnp.inf)
        new_max = jnp.maximum(running_max, jnp.max(scores, axis=-1))
        weight = jnp.exp(scores - new_max[..., None])
        rescale = jnp.exp(running_max - new_max)
        weight_sum = weight_sum * rescale + jnp.sum(weight, axis=-1)
        accum_sum = accum_sum * rescale[..., None] + jnp.einsum(
            "ihqk,ikhe->ihqe",
            weight.astype(jnp.bfloat16),
            value_blk,
            preferred_element_type=jnp.float32,
        )
        return (new_max, weight_sum, accum_sum)

    running_max, weight_sum, accum_sum = lax.fori_loop(
        0, key_count // block_len, forward_block_step, start_carry
    )
    attended = accum_sum / weight_sum[..., None]
    log_sum = running_max + jnp.log(weight_sum)
    att_low = (
        jnp.transpose(attended, (0, 2, 1, 3)).reshape(row_count, model_width).astype(jnp.bfloat16)
    )
    residual_two = residual + plain_dot(att_low, f_out)
    third_z, third_inv = layer_norm(residual_two)
    third_in = (third_z * norm_f[:, 2] + norm_f[:, 3]).astype(jnp.bfloat16)
    cross_pre = plain_dot(third_in, f_query)
    cq_z, cq_inv = layer_norm(cross_pre.reshape(images, tile_len, head_count, head_dim))
    cross_queries = cq_z.astype(jnp.bfloat16)
    text_kv = jnp.einsum("itc,cd->itd", text_states, f_text, preferred_element_type=jnp.float32)
    ck_z, ck_inv = layer_norm(
        text_kv[..., :model_width].reshape(images, text_len, head_count, head_dim)
    )
    cross_keys = ck_z.astype(jnp.bfloat16)
    cross_values = (
        text_kv[..., model_width:]
        .astype(jnp.bfloat16)
        .reshape(images, text_len, head_count, head_dim)
    )

    def cross_softmax():
        scores = (
            jnp.einsum(
                "iqhe,ikhe->ihqk", cross_queries, cross_keys, preferred_element_type=jnp.float32
            )
            * score_scale
        )
        return jax.nn.softmax(scores, axis=-1)

    crossed = jnp.einsum(
        "ihqk,ikhe->iqhe",
        cross_softmax().astype(jnp.bfloat16),
        cross_values,
        preferred_element_type=jnp.float32,
    )
    cross_low = crossed.reshape(row_count, model_width).astype(jnp.bfloat16)
    residual_three = residual_two + plain_dot(cross_low, f_cross)
    second_z, second_inv = layer_norm(residual_three)
    second_in = (second_z * norm_f[:, 4] + norm_f[:, 5]).astype(jnp.bfloat16)
    up_pre = plain_dot(second_in, f_up)
    hidden_float, gelu_pull = jax.vjp(gelu_tanh, up_pre)
    hidden_act = hidden_float.astype(jnp.bfloat16)
    residual_four = residual_three + plain_dot(hidden_act, f_down)
    last_z, last_inv = layer_norm(residual_four)
    last_in = (last_z * norm_f[:, 6] + norm_f[:, 7]).astype(jnp.bfloat16)
    produced = plain_dot(last_in, f_final)
    prediction = (
        (produced * keep_rows)
        .astype(jnp.bfloat16)
        .reshape(images, rows_tile, cols_tile, produced.shape[1])
    )
    grad_out = (
        cotangent.reshape(row_count, produced.shape[1]).astype(jnp.float32) * keep_rows
    ).astype(jnp.bfloat16)
    d_final = left_dot(last_in, grad_out)
    grad_last = right_dot(grad_out, f_final)
    gain_final = jnp.sum(grad_last * last_z, axis=0)
    bias_final = jnp.sum(grad_last, axis=0)
    grad_four = norm_back(grad_last * norm_f[:, 6], last_z, last_inv)
    low_four = grad_four.astype(jnp.bfloat16)
    d_down = left_dot(hidden_act, low_four)
    grad_hidden = right_dot(low_four, f_down)
    grad_up = gelu_pull(grad_hidden)[0].astype(jnp.bfloat16)
    d_up = left_dot(second_in, grad_up)
    grad_second = right_dot(grad_up, f_up)
    gain_second = jnp.sum(grad_second * second_z, axis=0)
    bias_second = jnp.sum(grad_second, axis=0)
    grad_three = grad_four + norm_back(grad_second * norm_f[:, 4], second_z, second_inv)
    low_three = grad_three.astype(jnp.bfloat16)
    d_cross = left_dot(cross_low, low_three)
    grad_crossed = (
        right_dot(low_three, f_cross)
        .astype(jnp.bfloat16)
        .reshape(images, tile_len, head_count, head_dim)
    )
    cross_probs = cross_softmax()
    cross_delta = jnp.transpose(
        jnp.sum(grad_crossed.astype(jnp.float32) * crossed, axis=-1), (0, 2, 1)
    )
    grad_probs = jnp.einsum(
        "iqhe,ikhe->ihqk", grad_crossed, cross_values, preferred_element_type=jnp.float32
    )
    grad_cscore = (cross_probs * (grad_probs - cross_delta[..., None])).astype(jnp.bfloat16)
    grad_cq = score_scale * jnp.einsum(
        "ihqk,ikhe->iqhe", grad_cscore, cross_keys, preferred_element_type=jnp.float32
    )
    part_ckey = score_scale * jnp.einsum(
        "ihqk,iqhe->ikhe", grad_cscore, cross_queries, preferred_element_type=jnp.float32
    )
    part_cvalue = jnp.einsum(
        "ihqk,iqhe->ikhe",
        cross_probs.astype(jnp.bfloat16),
        grad_crossed,
        preferred_element_type=jnp.float32,
    )
    grad_cross_q = (
        norm_back(grad_cq, cq_z, cq_inv).reshape(row_count, model_width).astype(jnp.bfloat16)
    )
    d_query = left_dot(third_in, grad_cross_q)
    grad_third = right_dot(grad_cross_q, f_query)
    gain_third = jnp.sum(grad_third * third_z, axis=0)
    bias_third = jnp.sum(grad_third, axis=0)
    grad_two = grad_three + norm_back(grad_third * norm_f[:, 2], third_z, third_inv)
    sum_ckey, sum_cvalue = lax.psum((part_ckey, part_cvalue), ("row", "col"))
    low_two = grad_two.astype(jnp.bfloat16)
    d_out = left_dot(att_low, low_two)
    grad_att = (
        right_dot(low_two, f_out)
        .astype(jnp.bfloat16)
        .reshape(images, tile_len, head_count, head_dim)
    )
    grad_att_h = jnp.transpose(grad_att, (0, 2, 1, 3))
    delta_rows = jnp.sum(grad_att_h.astype(jnp.float32) * attended, axis=-1)
    back_carry = (
        jnp.zeros((images, head_count, tile_len, head_dim), jnp.float32),
        jnp.zeros((images, tile_len * grid_devices, model_width), jnp.float32),
        jnp.zeros((images, tile_len * grid_devices, model_width), jnp.float32),
    )
    backward_key_rows = lax.all_gather(keys, ("row", "col"), axis=1, tiled=True)
    backward_value_rows = lax.all_gather(values, ("row", "col"), axis=1, tiled=True)
    key_count = backward_key_rows.shape[1]
    backward_block_len = block_size(key_count)

    def backward_block_step(block_index, running):
        grad_query, grad_key_all, grad_value_all = running
        offset = block_index * backward_block_len
        key_blk = lax.dynamic_slice_in_dim(
            backward_key_rows, offset, backward_block_len, 1
        ).reshape(images, backward_block_len, head_count, head_dim)
        value_blk = lax.dynamic_slice_in_dim(
            backward_value_rows, offset, backward_block_len, 1
        ).reshape(images, backward_block_len, head_count, head_dim)
        key_ok = valid_keys(offset, backward_block_len)
        scores = (
            jnp.einsum("ihqe,ikhe->ihqk", queries_h, key_blk, preferred_element_type=jnp.float32)
            * score_scale
        )
        scores = jnp.where(key_ok[:, None, None, :], scores, -jnp.inf)
        attn_probs = jnp.exp(scores - log_sum[..., None])
        grad_prob = jnp.einsum(
            "ihqe,ikhe->ihqk", grad_att_h, value_blk, preferred_element_type=jnp.float32
        )
        grad_score = (attn_probs * (grad_prob - delta_rows[..., None])).astype(jnp.bfloat16)
        grad_query = grad_query + score_scale * jnp.einsum(
            "ihqk,ikhe->ihqe", grad_score, key_blk, preferred_element_type=jnp.float32
        )
        key_part = score_scale * jnp.einsum(
            "ihqk,ihqe->ikhe", grad_score, queries_h, preferred_element_type=jnp.float32
        )
        value_part = jnp.einsum(
            "ihqk,ihqe->ikhe",
            attn_probs.astype(jnp.bfloat16),
            grad_att_h,
            preferred_element_type=jnp.float32,
        )
        grad_key_all = lax.dynamic_update_slice_in_dim(
            grad_key_all, key_part.reshape(images, backward_block_len, model_width), offset, 1
        )
        grad_value_all = lax.dynamic_update_slice_in_dim(
            grad_value_all, value_part.reshape(images, backward_block_len, model_width), offset, 1
        )
        return (grad_query, grad_key_all, grad_value_all)

    grad_query, grad_key_all, grad_value_all = lax.fori_loop(
        0, key_count // backward_block_len, backward_block_step, back_carry
    )
    grad_key_own, grad_value_own = (
        lax.psum_scatter(grad_key_all, ("row", "col"), scatter_dimension=1, tiled=True),
        lax.psum_scatter(grad_value_all, ("row", "col"), scatter_dimension=1, tiled=True),
    )
    grad_qn = rotate(jnp.transpose(grad_query, (0, 2, 1, 3)), tables, -1.0)
    grad_kn = rotate(grad_key_own.reshape(images, tile_len, head_count, head_dim), tables, -1.0)
    grad_qkv = jnp.concatenate(
        [
            norm_back(grad_qn, query_z, query_inv).reshape(row_count, model_width),
            norm_back(grad_kn, key_z, key_inv).reshape(row_count, model_width),
            grad_value_own.reshape(row_count, model_width),
        ],
        axis=-1,
    ).astype(jnp.bfloat16)
    d_qkv = left_dot(first_in, grad_qkv)
    grad_first = right_dot(grad_qkv, f_qkv)
    gain_first = jnp.sum(grad_first * first_z, axis=0)
    bias_first = jnp.sum(grad_first, axis=0)
    part_shift = jnp.sum(grad_first.reshape(images, tile_len, model_width), axis=1)
    grad_one = grad_two + norm_back(grad_first * norm_f[:, 0], first_z, first_inv)
    shift_grad = lax.psum(part_shift, ("row", "col"))
    grad_ckey = norm_back(sum_ckey, ck_z, ck_inv).reshape(images, text_len, model_width)
    grad_kv = jnp.concatenate(
        [grad_ckey, sum_cvalue.reshape(images, text_len, model_width)], axis=-1
    ).astype(jnp.bfloat16)
    text_slice = text_states.shape[2] // grid_devices
    text_cols = lax.dynamic_slice_in_dim(text_states, grid_at * text_slice, text_slice, 2)
    d_text_w = jnp.einsum("itc,itd->cd", text_cols, grad_kv, preferred_element_type=jnp.float32)
    text_grad = jnp.einsum("itd,cd->itc", grad_kv, part_text, preferred_element_type=jnp.float32)
    shift_low = shift_grad.astype(jnp.bfloat16)
    shift_slice = model_width // grid_devices
    act_cols = lax.dynamic_slice_in_dim(time_act, grid_at * shift_slice, shift_slice, 1)
    d_shift_w = jnp.einsum("ic,id->cd", act_cols, shift_low, preferred_element_type=jnp.float32)
    grad_time_act = right_dot(shift_low, f_shift)
    grad_time_pre = silu_pull(grad_time_act)[0].astype(jnp.bfloat16)
    freq_slice = embedding.shape[1] // grid_devices
    embed_cols = lax.dynamic_slice_in_dim(embedding, grid_at * freq_slice, freq_slice, 1)
    d_time_w = jnp.einsum(
        "ic,id->cd", embed_cols, grad_time_pre, preferred_element_type=jnp.float32
    )
    low_one = grad_one.astype(jnp.bfloat16)
    d_skip_w = left_dot(skip_in, low_one)
    grad_skip_in = right_dot(low_one, f_skip)
    gain_skips = jnp.sum(grad_skip_in * joined, axis=0)
    bias_skips = jnp.sum(grad_skip_in, axis=0)
    grad_joined = norm_back(grad_skip_in * gain_skip, joined, joined_inv)
    skip_grad = grad_joined[:, model_width:].reshape(images, rows_tile, cols_tile, model_width)
    grad_patch = grad_joined[:, :model_width].astype(jnp.bfloat16)
    d_patch = left_dot(grad_patch, patch_rows)
    latent_grad = plain_dot(grad_patch, f_patch).reshape(images, rows_tile, cols_tile, patch_width)
    d_norms = jnp.stack(
        [
            gain_first,
            bias_first,
            gain_third,
            bias_third,
            gain_second,
            bias_second,
            gain_final,
            bias_final,
            gain_skips[:model_width],
            bias_skips[:model_width],
            gain_skips[model_width:],
            bias_skips[model_width:],
        ],
        axis=1,
    )
    tile_done = (
        lax.psum_scatter(d_patch, ("row", "col"), scatter_dimension=0, tiled=True),
        lax.psum_scatter(d_skip_w, ("row", "col"), scatter_dimension=0, tiled=True),
        lax.psum_scatter(d_qkv, ("row", "col"), scatter_dimension=0, tiled=True),
        lax.psum_scatter(d_out, ("row", "col"), scatter_dimension=0, tiled=True),
        lax.psum_scatter(d_query, ("row", "col"), scatter_dimension=0, tiled=True),
        lax.psum_scatter(d_cross, ("row", "col"), scatter_dimension=0, tiled=True),
        lax.psum_scatter(d_up, ("row", "col"), scatter_dimension=0, tiled=True),
        lax.psum_scatter(d_down, ("row", "col"), scatter_dimension=0, tiled=True),
        lax.psum_scatter(d_final, ("row", "col"), scatter_dimension=0, tiled=True),
        lax.psum_scatter(d_norms, ("row", "col"), scatter_dimension=0, tiled=True),
    )
    reduced = (
        lax.psum_scatter(
            tile_done[0].astype(jnp.bfloat16), "dp", scatter_dimension=1, tiled=True
        ).astype(jnp.float32),
        lax.psum_scatter(
            tile_done[1].astype(jnp.bfloat16), "dp", scatter_dimension=1, tiled=True
        ).astype(jnp.float32),
        lax.psum_scatter(
            tile_done[2].astype(jnp.bfloat16), "dp", scatter_dimension=1, tiled=True
        ).astype(jnp.float32),
        lax.psum_scatter(
            tile_done[3].astype(jnp.bfloat16), "dp", scatter_dimension=1, tiled=True
        ).astype(jnp.float32),
        lax.psum_scatter(
            tile_done[4].astype(jnp.bfloat16), "dp", scatter_dimension=1, tiled=True
        ).astype(jnp.float32),
        lax.psum_scatter(
            tile_done[5].astype(jnp.bfloat16), "dp", scatter_dimension=1, tiled=True
        ).astype(jnp.float32),
        lax.psum_scatter(
            tile_done[6].astype(jnp.bfloat16), "dp", scatter_dimension=1, tiled=True
        ).astype(jnp.float32),
        lax.psum_scatter(
            tile_done[7].astype(jnp.bfloat16), "dp", scatter_dimension=1, tiled=True
        ).astype(jnp.float32),
        lax.psum_scatter(
            tile_done[8].astype(jnp.bfloat16), "dp", scatter_dimension=1, tiled=True
        ).astype(jnp.float32),
        lax.psum_scatter(
            tile_done[9].astype(jnp.bfloat16), "dp", scatter_dimension=1, tiled=True
        ).astype(jnp.float32),
        lax.psum_scatter(
            d_time_w.astype(jnp.bfloat16), "dp", scatter_dimension=1, tiled=True
        ).astype(jnp.float32),
        lax.psum_scatter(
            d_shift_w.astype(jnp.bfloat16), "dp", scatter_dimension=1, tiled=True
        ).astype(jnp.float32),
        lax.psum_scatter(
            d_text_w.astype(jnp.bfloat16), "dp", scatter_dimension=1, tiled=True
        ).astype(jnp.float32),
    )
    return (
        prediction,
        latent_grad,
        skip_grad,
        text_grad,
        reduced[0],
        reduced[1],
        reduced[10],
        reduced[11],
        reduced[2],
        reduced[3],
        reduced[4],
        reduced[12],
        reduced[5],
        reduced[6],
        reduced[7],
        reduced[8],
        reduced[9],
    )


TILE = ("row", "col")
EVERY = ("dp", "row", "col")
LOG2E = math.log2(math.e)
F32 = jnp.float32
BF16 = jnp.bfloat16
VMEM_BYTES = 56 * 2**20


def kernel_call(body, flops, moved, **options):
    return pl.pallas_call(
        body,
        compiler_params=pltpu.CompilerParams(vmem_limit_bytes=VMEM_BYTES),
        cost_estimate=pl.CostEstimate(flops=flops, bytes_accessed=moved, transcendentals=0),
        **options,
    )


def pair_swap(values_in):
    quarter = values_in.shape[0] // 4
    parts = [values_in[at * quarter : (at + 1) * quarter] for at in (1, 0, 3, 2)]
    return jnp.concatenate(parts, axis=0)


def column_norm(values_in):
    centred = values_in - jnp.mean(values_in, axis=0, keepdims=True)
    inverse = lax.rsqrt(jnp.mean(centred * centred, axis=0, keepdims=True) + EPSILON)
    return (centred * inverse, inverse)


def column_norm_back(grad_normed, normed, inverse):
    mean_grad = jnp.mean(grad_normed, axis=0, keepdims=True)
    mean_cross = jnp.mean(grad_normed * normed, axis=0, keepdims=True)
    return inverse * (grad_normed - mean_grad - normed * mean_cross)


def minus_pieces(row_values):
    high = row_values.astype(BF16).astype(F32)
    rest = row_values - high
    middle = rest.astype(BF16).astype(F32)
    lower = rest - middle
    at = lax.broadcasted_iota(jnp.int32, (8, row_values.shape[1]), 0)
    zero = jnp.zeros((8, row_values.shape[1]), F32)
    picked = jnp.where(at == 0, high, jnp.where(at == 1, middle, jnp.where(at == 2, lower, zero)))
    return -picked


def piece_flags(width):
    return (lax.broadcasted_iota(jnp.int32, (8, width), 0) < 3).astype(F32)


def head_norm_body(
    query_scale, rows_ref, weight_ref, cos_ref, sin_ref, ok_ref, out_ref, inv_ref
):
    groups, _, heads, head_dim, _ = out_ref.shape
    part = pl.program_id(0)
    made = jnp.dot(rows_ref[...], weight_ref[...], preferred_element_type=F32).T
    valid = ok_ref[...]

    @pl.when(part < 2)
    def _():
        factor = jnp.where(part == 0, query_scale, valid)
        cosine, sine = cos_ref[...] * factor, sin_ref[...] * factor
        for group in range(groups):
            for head in range(heads):
                at = (group * heads + head) * head_dim
                normed, inverse = column_norm(made[at : at + head_dim])
                turned = normed * cosine + pair_swap(normed) * sine
                out_ref[group, 0, head] = turned.astype(BF16)
                inv_ref[group, 0, head : head + 1] = inverse

    @pl.when(part == 2)
    def _():
        for group in range(groups):
            for head in range(heads):
                at = (group * heads + head) * head_dim
                out_ref[group, 0, head] = (made[at : at + head_dim] * valid).astype(BF16)
                inv_ref[group, 0, head : head + 1] = valid


def head_norm(rows, weight, tables, valid, groups, head_dim, query_scale):
    tile_len, depth = rows.shape
    width = weight.shape[1] // 3
    heads = width // groups // head_dim
    table = pl.BlockSpec((head_dim, tile_len), lambda p: (0, 0))
    return kernel_call(
        functools.partial(head_norm_body, query_scale),
        6 * tile_len * depth * width,
        6 * depth * width,
        grid=(3,),
        in_specs=[
            pl.BlockSpec((tile_len, depth), lambda p: (0, 0)),
            pl.BlockSpec((depth, width), lambda p: (0, p)),
            table,
            table,
            pl.BlockSpec((1, tile_len), lambda p: (0, 0)),
        ],
        out_specs=[
            pl.BlockSpec((groups, 1, heads, head_dim, tile_len), lambda p: (0, p, 0, 0, 0)),
            pl.BlockSpec((groups, 1, heads, tile_len), lambda p: (0, p, 0, 0)),
        ],
        out_shape=[
            jax.ShapeDtypeStruct((groups, 3, heads, head_dim, tile_len), BF16),
            jax.ShapeDtypeStruct((groups, 3, heads, tile_len), F32),
        ],
    )(rows, weight, *tables, valid)


def head_back_body(
    query_scale, grad_ref, own_ref, inv_ref, cos_ref, sin_ref, ok_ref, *others
):
    out_ref = others[-1]
    heads, head_dim = own_ref.shape[2], own_ref.shape[3]
    cosine, sine, valid = cos_ref[...], sin_ref[...], ok_ref[...]

    def unturn(values_in):
        return values_in * cosine - pair_swap(values_in) * sine

    for part in range(3):
        pieces = []
        for head in range(heads):
            grad = grad_ref[0, part, head].astype(F32)
            if part > 0:
                grad = grad * valid
            if part < 2:
                normed = unturn(own_ref[0, part, head].astype(F32))
                if part == 0:
                    normed = normed * (1.0 / query_scale)
                inverse = inv_ref[0, part, head : head + 1]
                grad = column_norm_back(unturn(grad), normed, inverse)
            pieces.append(grad)
        out_ref[part, 0] = jnp.concatenate(pieces, axis=0).astype(BF16)


def head_back(grads, own, inverses, tables, valid, query_scale, image, images, before):
    groups, _, heads, head_dim, tile_len = own.shape
    group_rows = heads * head_dim
    stacked = pl.BlockSpec((1, 3, heads, head_dim, tile_len), lambda g: (g, 0, 0, 0, 0))
    table = pl.BlockSpec((head_dim, tile_len), lambda g: (0, 0))
    earlier = () if before is None else (before,)
    return kernel_call(
        functools.partial(head_back_body, query_scale),
        0,
        6 * own.size,
        grid=(groups,),
        in_specs=[
            stacked,
            stacked,
            pl.BlockSpec((1, 3, heads, tile_len), lambda g: (g, 0, 0, 0)),
            table,
            table,
            pl.BlockSpec((1, tile_len), lambda g: (0, 0)),
        ]
        + [pl.BlockSpec(memory_space=pl.ANY)] * len(earlier),
        out_specs=pl.BlockSpec((3, 1, group_rows, tile_len), lambda g: (0, g, 0, image)),
        out_shape=jax.ShapeDtypeStruct((3, groups, group_rows, images * tile_len), BF16),
        input_output_aliases={6: 0} if earlier else {},
    )(grads, own, inverses, *tables, valid, *earlier)


def attend_body(query_ref, key_ref, value_ref, ok_ref, out_ref, lse_ref, key_nat, value_ext):
    tiles, tile_len, head_dim = key_ref.shape[0], key_ref.shape[-1], key_ref.shape[-2]

    @pl.when(pl.program_id(1) == 0)
    def _():
        for tile in range(tiles):
            key_nat[tile * tile_len : (tile + 1) * tile_len, :] = key_ref[tile, 0, 0].T
            value_ext[tile] = jnp.concatenate(
                [value_ref[tile, 0, 0].astype(F32), ok_ref[tile]], axis=0
            ).astype(BF16)

    query = query_ref[0, 0, 0]

    def step(tile, total):
        rows = pl.ds(pl.multiple_of(tile * tile_len, tile_len), tile_len)
        scores = jnp.dot(key_nat[rows, :], query, preferred_element_type=F32)
        weight = jnp.exp2(scores).astype(BF16)
        return total + jnp.dot(value_ext[tile], weight, preferred_element_type=F32)

    start = jnp.zeros((head_dim + 8, tile_len), F32)
    total = lax.fori_loop(0, tiles, step, start, unroll=8)
    weight_sum = total[head_dim : head_dim + 1]
    out_ref[0, 0] = (total[:head_dim] / weight_sum).astype(BF16)
    lse_ref[0, 0] = jnp.log2(weight_sum)


def attend(qkv, flags):
    tiles, _, heads, head_dim, tile_len = qkv.shape
    return kernel_call(
        attend_body,
        1024 * heads * tiles**2 * tile_len**2,
        8 * qkv.size,
        grid=(heads, tiles),
        in_specs=[
            pl.BlockSpec((1, 1, 1, head_dim, tile_len), lambda h, t: (t, 0, h, 0, 0)),
            pl.BlockSpec((tiles, 1, 1, head_dim, tile_len), lambda h, t: (0, 1, h, 0, 0)),
            pl.BlockSpec((tiles, 1, 1, head_dim, tile_len), lambda h, t: (0, 2, h, 0, 0)),
            pl.BlockSpec((tiles, 8, tile_len), lambda h, t: (0, 0, 0)),
        ],
        out_specs=[
            pl.BlockSpec((1, 1, head_dim, tile_len), lambda h, t: (t, h, 0, 0)),
            pl.BlockSpec((1, 1, 1, tile_len), lambda h, t: (t, h, 0, 0)),
        ],
        out_shape=[
            jax.ShapeDtypeStruct((tiles, heads, head_dim, tile_len), BF16),
            jax.ShapeDtypeStruct((tiles, heads, 1, tile_len), F32),
        ],
        scratch_shapes=[
            pltpu.VMEM((tiles * tile_len, head_dim), BF16),
            pltpu.VMEM((tiles, head_dim + 8, tile_len), BF16),
        ],
    )(qkv, qkv, qkv, flags)


def attend_back_body(
    score_scale,
    query_ref,
    key_ref,
    value_ref,
    grad_ref,
    att_ref,
    lse_ref,
    out_ref,
    key_nat,
    value_nat,
    key_sum,
    value_sum,
):
    tiles, tile_len, head_dim = key_ref.shape[0], key_ref.shape[-1], key_ref.shape[-2]
    at = pl.program_id(1)

    @pl.when(at == 0)
    def _():
        ones = piece_flags(tile_len)
        for tile in range(tiles):
            rows = slice(tile * tile_len, (tile + 1) * tile_len)
            for source, kept in ((key_ref, key_nat), (value_ref, value_nat)):
                wide = jnp.concatenate([source[tile, 0, 0].astype(F32), ones], axis=0)
                kept[rows, :] = wide.T.astype(BF16)
        key_sum[...] = jnp.zeros_like(key_sum)
        value_sum[...] = jnp.zeros_like(value_sum)

    query = query_ref[0, 0, 0].astype(F32)
    grad = grad_ref[0, 0].astype(F32)
    delta = jnp.sum(grad * att_ref[0, 0].astype(F32), axis=0, keepdims=True)
    query_ext = jnp.concatenate([query, minus_pieces(lse_ref[0, 0])], axis=0)
    grad_ext = jnp.concatenate([grad, minus_pieces(delta)], axis=0)
    query_cols, grad_cols = query_ext.astype(BF16), grad_ext.astype(BF16)
    query_nat, grad_nat = query_ext.T.astype(BF16), grad_ext.T.astype(BF16)

    def step(tile, total):
        rows = pl.ds(pl.multiple_of(tile * tile_len, tile_len), tile_len)
        scores = jnp.dot(key_nat[rows, :], query_cols, preferred_element_type=F32)
        probs = jnp.exp2(scores)
        grad_probs = jnp.dot(value_nat[rows, :], grad_cols, preferred_element_type=F32)
        grad_scores = (probs * grad_probs).astype(BF16)
        value_sum[rows, :] += jnp.dot(probs.astype(BF16), grad_nat, preferred_element_type=F32)
        key_sum[rows, :] += jnp.dot(grad_scores, query_nat, preferred_element_type=F32)
        return total + jnp.dot(key_ref[tile, 0, 0], grad_scores, preferred_element_type=F32)

    start = jnp.zeros((head_dim, tile_len), F32)
    total = lax.fori_loop(0, tiles, step, start, unroll=8)
    out_ref[at, 0, 0] = (total * score_scale).astype(BF16)

    @pl.when(at == tiles - 1)
    def _():
        for tile in range(tiles):
            rows = slice(tile * tile_len, (tile + 1) * tile_len)
            key_grad = key_sum[rows, :].T[:head_dim] * (1.0 / LOG2E)
            out_ref[tile, 1, 0] = key_grad.astype(BF16)
            out_ref[tile, 2, 0] = value_sum[rows, :].T[:head_dim].astype(BF16)


def attend_back(qkv, grad_att, att, lse, score_scale):
    tiles, _, heads, head_dim, tile_len = qkv.shape
    one = pl.BlockSpec((1, 1, head_dim, tile_len), lambda h, t: (t, h, 0, 0))
    return kernel_call(
        functools.partial(attend_back_body, score_scale),
        2560 * heads * tiles**2 * tile_len**2,
        8 * qkv.size,
        grid=(heads, tiles),
        in_specs=[
            pl.BlockSpec((1, 1, 1, head_dim, tile_len), lambda h, t: (t, 0, h, 0, 0)),
            pl.BlockSpec((tiles, 1, 1, head_dim, tile_len), lambda h, t: (0, 1, h, 0, 0)),
            pl.BlockSpec((tiles, 1, 1, head_dim, tile_len), lambda h, t: (0, 2, h, 0, 0)),
            one,
            one,
            pl.BlockSpec((1, 1, 1, tile_len), lambda h, t: (t, h, 0, 0)),
        ],
        out_specs=pl.BlockSpec(
            (tiles, 3, 1, head_dim, tile_len), lambda h, t: (0, 0, h, 0, 0)
        ),
        out_shape=jax.ShapeDtypeStruct(qkv.shape, BF16),
        scratch_shapes=[
            pltpu.VMEM((tiles * tile_len, head_dim + 8), BF16),
            pltpu.VMEM((tiles * tile_len, head_dim + 8), BF16),
            pltpu.VMEM((tiles * tile_len, head_dim + 8), F32),
            pltpu.VMEM((tiles * tile_len, head_dim + 8), F32),
        ],
    )(qkv, qkv, qkv, grad_att, att, lse)


def cross_body(text_len, query_scale, pre_ref, kv_ref, att_ref, query_ref, inv_ref, lse_ref):
    head_dim, text_pad = kv_ref.shape[2], kv_ref.shape[3]
    normed, inverse = column_norm(pre_ref[0])
    query = (normed * query_scale).astype(BF16)
    query_ref[0] = query
    inv_ref[0] = inverse
    key = column_norm(kv_ref[0, 0])[0].astype(BF16)
    at = lax.broadcasted_iota(jnp.int32, (8, text_pad), 0)
    text_at = lax.broadcasted_iota(jnp.int32, (8, text_pad), 1)
    flags = ((at == 0) & (text_at < text_len)).astype(F32)
    value_ext = jnp.concatenate([kv_ref[1, 0], flags], axis=0).astype(BF16)
    scores = jnp.dot(key.T, query, preferred_element_type=F32)
    weight = jnp.exp2(scores).astype(BF16)
    total = jnp.dot(value_ext, weight, preferred_element_type=F32)
    weight_sum = total[head_dim : head_dim + 1]
    att_ref[0] = (total[:head_dim] / weight_sum).astype(BF16)
    lse_ref[0] = jnp.log2(weight_sum)


def cross_attend(pre, text_kv, images, text_len, query_scale):
    heads, head_dim, tokens = pre.shape
    tile_len, text_pad = tokens // images, text_kv.shape[3] // images
    wide = pl.BlockSpec((1, head_dim, tile_len), lambda i, h: (h, 0, i))
    row = pl.BlockSpec((1, 1, tile_len), lambda i, h: (h, 0, i))
    return kernel_call(
        functools.partial(cross_body, text_len, query_scale),
        1024 * heads * tokens * text_pad,
        8 * pre.size,
        grid=(images, heads),
        in_specs=[wide, pl.BlockSpec((2, 1, head_dim, text_pad), lambda i, h: (0, h, 0, i))],
        out_specs=[wide, wide, row, row],
        out_shape=[
            jax.ShapeDtypeStruct(pre.shape, BF16),
            jax.ShapeDtypeStruct(pre.shape, BF16),
            jax.ShapeDtypeStruct((heads, 1, tokens), F32),
            jax.ShapeDtypeStruct((heads, 1, tokens), F32),
        ],
    )(pre, text_kv)


def cross_back_body(
    query_scale,
    score_scale,
    query_ref,
    kv_ref,
    grad_ref,
    att_ref,
    inv_ref,
    lse_ref,
    out_ref,
    key_ref,
    value_ref,
):
    head_dim, text_pad = kv_ref.shape[2], kv_ref.shape[3]
    query = query_ref[0].astype(F32)
    grad = grad_ref[0].astype(F32)
    delta = jnp.sum(grad * att_ref[0].astype(F32), axis=0, keepdims=True)
    query_ext = jnp.concatenate([query, minus_pieces(lse_ref[0])], axis=0).astype(BF16)
    grad_ext = jnp.concatenate([grad, minus_pieces(delta)], axis=0).astype(BF16)
    ones = piece_flags(text_pad)
    key = column_norm(kv_ref[0, 0])[0].astype(BF16)
    key_ext = jnp.concatenate([key.astype(F32), ones], axis=0).T.astype(BF16)
    value_ext = jnp.concatenate([kv_ref[1, 0], ones], axis=0).T.astype(BF16)
    probs = jnp.exp2(jnp.dot(key_ext, query_ext, preferred_element_type=F32))
    grad_probs = jnp.dot(value_ext, grad_ext, preferred_element_type=F32)
    grad_scores = (probs * grad_probs).astype(BF16)
    value_grad = right_dot(grad_ext, probs.astype(BF16))[:head_dim]
    key_grad = right_dot(query_ext, grad_scores)[:head_dim]
    key_ref[0] = (key_grad * (1.0 / LOG2E)).astype(BF16)
    value_ref[0] = value_grad.astype(BF16)
    query_grad = jnp.dot(key, grad_scores, preferred_element_type=F32) * score_scale
    normed = query * (1.0 / query_scale)
    out_ref[0] = column_norm_back(query_grad, normed, inv_ref[0]).astype(BF16)


def cross_back(query, text_kv, grad, att, inverse, lse, images, query_scale, score_scale):
    heads, head_dim, tokens = query.shape
    tile_len, text_pad = tokens // images, text_kv.shape[3] // images
    wide = pl.BlockSpec((1, head_dim, tile_len), lambda i, h: (h, 0, i))
    row = pl.BlockSpec((1, 1, tile_len), lambda i, h: (h, 0, i))
    text = pl.BlockSpec((2, 1, head_dim, text_pad), lambda i, h: (0, h, 0, i))
    text_out = pl.BlockSpec((1, head_dim, text_pad), lambda i, h: (h, 0, i))
    return kernel_call(
        functools.partial(cross_back_body, query_scale, score_scale),
        2560 * heads * tokens * text_pad,
        16 * query.size,
        grid=(images, heads),
        in_specs=[wide, text, wide, wide, row, row],
        out_specs=[
            wide,
            text_out,
            text_out,
        ],
        out_shape=[
            jax.ShapeDtypeStruct(query.shape, BF16),
            jax.ShapeDtypeStruct((heads, head_dim, images * text_pad), BF16),
            jax.ShapeDtypeStruct((heads, head_dim, images * text_pad), BF16),
        ],
    )(query, text_kv, grad, att, inverse, lse)


def swap_tiles(values_in):
    return lax.all_to_all(values_in, TILE, split_axis=0, concat_axis=0, tiled=True)


def shift_pairs(devices, step):
    return [(at, (at + step) % devices) for at in range(devices)]


def fetch(weight):
    devices = lax.axis_size("dp")
    return [weight] + [
        lax.ppermute(weight, "dp", shift_pairs(devices, step)) for step in range(1, devices)
    ]


def widen(pieces, first=None):
    devices, me = lax.axis_size("dp"), lax.axis_index("dp")
    if first is not None:
        pieces = after(first, *pieces)
    return jnp.concatenate(
        [lax.select_n((me - at) % devices, *pieces) for at in range(devices)], axis=1
    )


def narrow_blocks(blocks):
    devices, me = lax.axis_size("dp"), lax.axis_index("dp")
    total = lax.select_n(me, *blocks).astype(F32)
    for step in range(1, devices):
        sent = lax.select_n((me + step) % devices, *blocks)
        total = total + lax.ppermute(sent, "dp", shift_pairs(devices, step)).astype(F32)
    return total


def narrow(weight_grad):
    return narrow_blocks(jnp.split(weight_grad, lax.axis_size("dp"), axis=1))


def narrow_three(weight_grads):
    devices = lax.axis_size("dp")
    weight_grads = jnp.split(weight_grads, 3, axis=1)
    split = [jnp.split(weight_grad, devices, axis=1) for weight_grad in weight_grads]
    return narrow_blocks([jnp.concatenate(blocks, axis=1) for blocks in zip(*split)])


def sum_tiles(part_sums):
    devices, me = lax.axis_size(TILE), lax.axis_index(TILE)
    blocks = jnp.split(part_sums, devices, axis=0)
    total = lax.select_n(me, *blocks)
    for step in range(1, devices):
        sent = lax.select_n((me + step) % devices, *blocks)
        total = total + lax.ppermute(sent, TILE, shift_pairs(devices, step))
    return total


def total_tiles(part_sum):
    devices = lax.axis_size(TILE)
    total = part_sum
    for step in range(1, devices):
        total = total + lax.ppermute(part_sum, TILE, shift_pairs(devices, step))
    return total


def over_tiles(weight_grad):
    return lax.optimization_barrier(
        lax.psum_scatter(weight_grad, TILE, scatter_dimension=0, tiled=True)
    )


def tiles_whole(weight):
    return lax.all_gather(weight, TILE, axis=0, tiled=True)


def after(first, *values_in):
    return lax.optimization_barrier((first, *values_in))[1:]


def dot_over(left_mat, right_mat, left_axis, right_axis):
    return lax.dot_general(
        left_mat,
        right_mat,
        (((left_axis,), (right_axis,)), ((), ())),
        preferred_element_type=F32,
    )


def local_heads(
    latent,
    skip_input,
    text_states,
    timesteps,
    image_sides,
    cotangent,
    w_patch,
    w_skip,
    w_time,
    w_shift,
    w_qkv,
    w_out,
    w_query,
    w_text,
    w_cross,
    w_up,
    w_down,
    w_final,
    norm_params,
):
    dp_devices = lax.axis_size("dp")
    grid_devices = lax.axis_size(TILE)
    col_devices = lax.axis_size("col")
    grid_at = lax.axis_index(TILE)
    row_at = lax.axis_index("row")
    col_at = lax.axis_index("col")
    images, rows_tile, cols_tile, patch_width = latent.shape
    tile_len = rows_tile * cols_tile
    row_count = images * tile_len
    out_width = cotangent.shape[3]

    part_skip = widen(fetch(w_skip))
    small = jnp.concatenate([w_patch, w_final, norm_params], axis=1)
    small_widths = (w_patch.shape[1], w_final.shape[1], norm_params.shape[1])
    cuts = (0, small_widths[0], sum(small_widths[:2]), sum(small_widths))
    part_small = widen(fetch(small))
    part_time, part_shift_w = widen(fetch(w_time)), widen(fetch(w_shift))
    f_small = tiles_whole(part_small).reshape(-1, dp_devices, sum(small_widths))
    f_patch, f_final, f_norms = (
        f_small[:, :, cuts[at] : cuts[at + 1]].reshape(f_small.shape[0], -1) for at in range(3)
    )
    f_skip = tiles_whole(part_skip)
    held_qkv = fetch(w_qkv)
    held_out, held_query, held_cross = fetch(w_out), fetch(w_query), fetch(w_cross)
    held_text = fetch(w_text)
    held_up, held_down = fetch(w_up), fetch(w_down)
    model_width = skip_input.shape[3]
    head_count = HEADS
    head_dim = model_width // head_count
    text_len = text_states.shape[1]
    text_pad = -(-text_len // 128) * 128
    score_scale = head_dim ** (-0.5)
    query_scale = score_scale * LOG2E
    positions = jnp.arange(tile_len, dtype=jnp.int32)
    row_pos = row_at * rows_tile + positions // cols_tile
    col_pos = col_at * cols_tile + positions % cols_tile
    query_ok = (row_pos[None, :] < image_sides[:, None]) & (col_pos[None, :] < image_sides[:, None])
    valid = query_ok.astype(F32)
    keep_rows = query_ok.astype(F32).reshape(row_count, 1)
    tile_list = jnp.arange(grid_devices, dtype=jnp.int32)[:, None]
    key_row = tile_list // col_devices * rows_tile + (positions // cols_tile)[None, :]
    key_col = tile_list % col_devices * cols_tile + (positions % cols_tile)[None, :]
    sides = image_sides[:, None, None]
    key_ok = ((key_row[None] < sides) & (key_col[None] < sides)).astype(F32)
    flags = jnp.concatenate(
        [key_ok[:, :, None, :], jnp.zeros((images, grid_devices, 7, tile_len), F32)], axis=2
    )
    cos_row, sin_row, cos_col, sin_col = (
        jnp.transpose(table[:, 0, :]) for table in rope_tables(row_pos, col_pos, head_dim)
    )
    tables = (
        jnp.concatenate([cos_row, cos_row, cos_col, cos_col], axis=0),
        jnp.concatenate([-sin_row, sin_row, -sin_col, sin_col], axis=0),
    )
    norm_f = f_norms.astype(F32)

    embedding = time_embed(timesteps, FREQ).astype(BF16)
    freq_slice = part_time.shape[0]
    shift_slice = part_shift_w.shape[0]
    embed_cols = lax.dynamic_slice_in_dim(embedding, grid_at * freq_slice, freq_slice, 1)
    time_pre = total_tiles(plain_dot(embed_cols, part_time))
    time_float, silu_pull = jax.vjp(jax.nn.silu, time_pre)
    time_act = time_float.astype(BF16)
    act_cols = lax.dynamic_slice_in_dim(time_act, grid_at * shift_slice, shift_slice, 1)
    time_shift = total_tiles(plain_dot(act_cols, part_shift_w))

    patch_rows = latent.reshape(row_count, patch_width)
    patch_feat = right_dot(patch_rows, f_patch)
    skip_rows = skip_input.reshape(row_count, model_width).astype(F32)
    gain_skip = jnp.concatenate([norm_f[:, 8], norm_f[:, 10]])
    bias_skip = jnp.concatenate([norm_f[:, 9], norm_f[:, 11]])
    joined, joined_inv = layer_norm(jnp.concatenate([patch_feat, skip_rows], axis=-1))
    skip_in = (joined * gain_skip + bias_skip).astype(BF16)
    f_qkv = tiles_whole(widen(held_qkv, skip_in))
    part_three = [widen(held, skip_in) for held in (held_out, held_query, held_cross)]
    f_three = tiles_whole(jnp.concatenate(part_three, axis=1))
    f_out, f_query, f_cross = jnp.split(f_three, 3, axis=1)
    residual = plain_dot(skip_in, f_skip)
    first_z, first_inv = layer_norm(residual)
    first_pre = (first_z * norm_f[:, 0] + norm_f[:, 1]).reshape(
        images, tile_len, model_width
    ) + time_shift[:, None, :]
    first_in = first_pre.reshape(row_count, model_width).astype(BF16)
    f_up = tiles_whole(widen(held_up, first_in))
    part_text = widen(held_text, first_in)
    f_text = tiles_whole(part_text)
    first_rows = first_in.reshape(images, tile_len, model_width)
    own_qkv, qk_inv, tile_qkv, tile_att, tile_lse, att_rows = [], [], [], [], [], []
    for image in range(images):
        rows = first_rows[image]
        own, inverses = head_norm(
            rows,
            f_qkv,
            tables,
            valid[image : image + 1],
            grid_devices,
            head_dim,
            query_scale,
        )
        own_qkv.append(own)
        qk_inv.append(inverses)
        tile_qkv.append(swap_tiles(own))
    for image in range(images):
        att, lse = attend(tile_qkv[image], flags[image])
        tile_att.append(att)
        tile_lse.append(lse)
        own_att = swap_tiles(att).reshape(model_width, tile_len)
        att_rows.append(jnp.transpose(own_att))
    att_low = jnp.concatenate(att_rows, axis=0)
    residual_two = residual + plain_dot(att_low, f_out)
    f_down = tiles_whole(widen(held_down, residual_two))

    third_z, third_inv = layer_norm(residual_two)
    third_in = (third_z * norm_f[:, 2] + norm_f[:, 3]).astype(BF16)
    cross_pre = dot_over(f_query, third_in, 0, 1).reshape(head_count, head_dim, row_count)
    text_rows = jnp.pad(text_states, ((0, 0), (0, text_pad - text_len), (0, 0)))
    text_rows = text_rows.reshape(images * text_pad, -1)
    text_kv = dot_over(f_text, text_rows, 0, 1).reshape(2, head_count, head_dim, images * text_pad)
    crossed, cross_queries, cq_inv, cross_lse = cross_attend(
        cross_pre, text_kv, images, text_len, query_scale
    )
    cross_cols = crossed.reshape(model_width, row_count)
    residual_three = residual_two + left_dot(cross_cols, f_cross)
    second_z, second_inv = layer_norm(residual_three)
    second_in = (second_z * norm_f[:, 4] + norm_f[:, 5]).astype(BF16)
    up_pre = plain_dot(second_in, f_up)
    hidden_float, gelu_pull = jax.vjp(gelu_tanh, up_pre)
    hidden_act = hidden_float.astype(BF16)
    residual_four = residual_three + plain_dot(hidden_act, f_down)
    last_z, last_inv = layer_norm(residual_four)
    last_in = (last_z * norm_f[:, 6] + norm_f[:, 7]).astype(BF16)
    produced = plain_dot(last_in, f_final)
    prediction = (
        (produced * keep_rows).astype(BF16).reshape(images, rows_tile, cols_tile, out_width)
    )

    grad_out = (cotangent.reshape(row_count, out_width).astype(F32) * keep_rows).astype(BF16)
    d_final = left_dot(last_in, grad_out)
    grad_last = right_dot(grad_out, f_final)
    gain_final = jnp.sum(grad_last * last_z, axis=0)
    bias_final = jnp.sum(grad_last, axis=0)
    grad_four = norm_back(grad_last * norm_f[:, 6], last_z, last_inv)
    low_four = grad_four.astype(BF16)
    d_down = left_dot(hidden_act, low_four).astype(BF16)
    d_down, low_four = lax.optimization_barrier((d_down, low_four))
    t_down = over_tiles(d_down)
    grad_hidden = right_dot(low_four, f_down)
    grad_up = gelu_pull(grad_hidden)[0].astype(BF16)
    d_up = left_dot(second_in, grad_up).astype(BF16)
    d_up, grad_up = lax.optimization_barrier((d_up, grad_up))
    t_up = over_tiles(d_up)
    grad_second = right_dot(grad_up, f_up)
    gain_second = jnp.sum(grad_second * second_z, axis=0)
    bias_second = jnp.sum(grad_second, axis=0)
    grad_three = grad_four + norm_back(grad_second * norm_f[:, 4], second_z, second_inv)
    low_three = grad_three.astype(BF16)
    d_cross = plain_dot(cross_cols, low_three).astype(BF16)
    down_grad = narrow(t_down)
    grad_crossed = dot_over(f_cross, low_three, 1, 1).astype(BF16)
    t_down, grad_crossed = lax.optimization_barrier((t_down, grad_crossed))
    grad_cross_q, d_text_key, d_text_value = cross_back(
        cross_queries,
        text_kv,
        grad_crossed.reshape(head_count, head_dim, row_count),
        crossed,
        cq_inv,
        cross_lse,
        images,
        query_scale,
        score_scale,
    )
    grad_cross_q = grad_cross_q.reshape(model_width, row_count)
    d_query = dot_over(third_in, grad_cross_q, 0, 1).astype(BF16)
    grad_third = dot_over(grad_cross_q, f_query, 0, 1)
    gain_third = jnp.sum(grad_third * third_z, axis=0)
    bias_third = jnp.sum(grad_third, axis=0)
    grad_two = grad_three + norm_back(grad_third * norm_f[:, 2], third_z, third_inv)
    low_two = grad_two.astype(BF16)
    low_two_rows = low_two.reshape(images, tile_len, model_width)
    tile_grads = []
    for image in range(images):
        grad_att = dot_over(f_out, low_two_rows[image], 1, 1).astype(BF16)
        tile_grads.append(swap_tiles(grad_att.reshape(tile_att[image].shape)))
    d_out = left_dot(att_low, low_two).astype(BF16)
    d_joint = jnp.concatenate(
        [
            d_out,
            d_query,
            d_cross,
            d_text_key.reshape(model_width, -1),
            d_text_value.reshape(model_width, -1),
        ],
        axis=1,
    )
    t_joint = over_tiles(d_joint)
    own_grads = []
    tile_back = None
    for image in range(images):
        if tile_back is not None:
            t_up, down_grad, tile_grads[image], tile_back = lax.optimization_barrier(
                (t_up, down_grad, tile_grads[image], tile_back)
            )
            own_grads.append(swap_tiles(tile_back))
        tile_back = attend_back(
            tile_qkv[image], tile_grads[image], tile_att[image], tile_lse[image], score_scale
        )
    own_grads.append(swap_tiles(tile_back))
    up_grad = narrow(t_up)
    t_joint, up_grad, own_grads[-1] = lax.optimization_barrier((t_joint, up_grad, own_grads[-1]))
    joint_grad = narrow_three(t_joint[:, : 3 * model_width])
    sum_text_kv = t_joint[:, 3 * model_width :].astype(F32)
    sum_text_kv = jnp.transpose(
        sum_text_kv.reshape(-1, head_dim, 2, images * text_pad), (2, 0, 1, 3)
    )
    group_heads = head_count // grid_devices
    own_key = lax.dynamic_slice_in_dim(text_kv[0], grid_at * group_heads, group_heads, 0)
    ck_z, ck_inv = layer_norm(jnp.swapaxes(own_key, 1, 2))
    grad_ckey = jnp.swapaxes(norm_back(jnp.swapaxes(sum_text_kv[0], 1, 2), ck_z, ck_inv), 1, 2)
    grad_kv = tiles_whole(jnp.stack([grad_ckey, sum_text_kv[1]]).astype(BF16)[None])
    grad_qkv = None
    for image in range(images):
        grad_qkv = head_back(
            own_grads[image],
            own_qkv[image],
            qk_inv[image],
            tables,
            valid[image : image + 1],
            query_scale,
            image,
            images,
            grad_qkv,
        )
    grad_qkv = grad_qkv.reshape(3 * model_width, row_count)
    d_qkv = dot_over(first_in, grad_qkv, 0, 1).astype(BF16)
    d_qkv, grad_qkv = lax.optimization_barrier((d_qkv, grad_qkv))
    t_qkv = over_tiles(d_qkv)
    grad_first = dot_over(grad_qkv, f_qkv, 0, 1)
    joint_grad, grad_first = lax.optimization_barrier((joint_grad, grad_first))
    out_grad, query_w_grad, cross_grad = jnp.split(joint_grad, 3, axis=1)
    gain_first = jnp.sum(grad_first * first_z, axis=0)
    bias_first = jnp.sum(grad_first, axis=0)
    part_shift = jnp.sum(grad_first.reshape(images, tile_len, model_width), axis=1)
    grad_one = grad_two + norm_back(grad_first * norm_f[:, 0], first_z, first_inv)

    low_one = grad_one.astype(BF16)
    d_skip_w = left_dot(skip_in, low_one).astype(BF16)
    d_skip_w, low_one = lax.optimization_barrier((d_skip_w, low_one))
    t_qkv, d_skip_w = lax.optimization_barrier((t_qkv, d_skip_w))
    qkv_grad = narrow(t_qkv)
    t_skip = over_tiles(d_skip_w)

    grad_kv = jnp.transpose(grad_kv, (1, 0, 2, 3, 4)).reshape(2 * model_width, images * text_pad)
    text_slice = text_states.shape[2] // grid_devices
    text_cols = lax.dynamic_slice_in_dim(text_rows, grid_at * text_slice, text_slice, 1)
    text_w_grad = narrow(dot_over(text_cols, grad_kv, 0, 1).astype(BF16))
    text_grad = dot_over(grad_kv, part_text, 0, 1).reshape(images, text_pad, text_slice)
    text_grad = text_grad[:, :text_len]

    shift_low = total_tiles(part_shift).astype(BF16)
    shift_w_grad = narrow(left_dot(act_cols, shift_low).astype(BF16))
    grad_time_act = lax.all_gather(right_dot(shift_low, part_shift_w), TILE, axis=1, tiled=True)
    grad_time_pre = silu_pull(grad_time_act)[0].astype(BF16)
    time_w_grad = narrow(left_dot(embed_cols, grad_time_pre).astype(BF16))

    grad_skip_in = right_dot(low_one, f_skip)
    gain_skips = jnp.sum(grad_skip_in * joined, axis=0)
    bias_skips = jnp.sum(grad_skip_in, axis=0)
    grad_joined = norm_back(grad_skip_in * gain_skip, joined, joined_inv)
    qkv_grad, grad_joined = lax.optimization_barrier((qkv_grad, grad_joined))
    skip_grad = grad_joined[:, model_width:].reshape(images, rows_tile, cols_tile, model_width)
    grad_patch = grad_joined[:, :model_width].astype(BF16)
    d_patch = left_dot(grad_patch, patch_rows)
    latent_grad = plain_dot(grad_patch, f_patch).reshape(images, rows_tile, cols_tile, patch_width)
    d_norms = jnp.stack(
        [
            gain_first,
            bias_first,
            gain_third,
            bias_third,
            gain_second,
            bias_second,
            gain_final,
            bias_final,
            gain_skips[:model_width],
            bias_skips[:model_width],
            gain_skips[model_width:],
            bias_skips[model_width:],
        ],
        axis=1,
    )
    small_grads = jnp.concatenate(
        [
            grad.reshape(model_width, dp_devices, -1)
            for grad in (d_patch, d_final, d_norms)
        ],
        axis=2,
    )
    small_grads = narrow(sum_tiles(small_grads.reshape(model_width, -1)))
    skip_w_grad = narrow(t_skip)
    patch_grad, final_grad, norms_grad = (
        small_grads[:, cuts[at] : cuts[at + 1]] for at in range(3)
    )
    return (
        prediction,
        latent_grad,
        skip_grad,
        text_grad,
        patch_grad,
        skip_w_grad,
        time_w_grad,
        shift_w_grad,
        qkv_grad,
        out_grad,
        query_w_grad,
        text_w_grad,
        cross_grad,
        up_grad,
        down_grad,
        final_grad,
        norms_grad,
    )


def local(sizes, latent, *others):
    grid_devices = sizes["row"] * sizes["col"]
    tile_len = latent.shape[1] * latent.shape[2]
    if HEADS % grid_devices == 0 and tile_len % 128 == 0:
        return local_heads(latent, *others)
    return local_gathered(latent, *others)


def solution(mesh):
    return jax.shard_map(
        functools.partial(local, mesh.shape),
        mesh=mesh,
        in_specs=(
            P("dp", "row", "col", None),
            P("dp", "row", "col", None),
            P("dp", None, None),
            P("dp"),
            P("dp"),
            P("dp", "row", "col", None),
            P(("row", "col"), "dp"),
            P(("row", "col"), "dp"),
            P(("row", "col"), "dp"),
            P(("row", "col"), "dp"),
            P(("row", "col"), "dp"),
            P(("row", "col"), "dp"),
            P(("row", "col"), "dp"),
            P(("row", "col"), "dp"),
            P(("row", "col"), "dp"),
            P(("row", "col"), "dp"),
            P(("row", "col"), "dp"),
            P(("row", "col"), "dp"),
            P(("row", "col"), "dp"),
        ),
        out_specs=(
            P("dp", "row", "col", None),
            P("dp", "row", "col", None),
            P("dp", "row", "col", None),
            P("dp", None, ("row", "col")),
            P(("row", "col"), "dp"),
            P(("row", "col"), "dp"),
            P(("row", "col"), "dp"),
            P(("row", "col"), "dp"),
            P(("row", "col"), "dp"),
            P(("row", "col"), "dp"),
            P(("row", "col"), "dp"),
            P(("row", "col"), "dp"),
            P(("row", "col"), "dp"),
            P(("row", "col"), "dp"),
            P(("row", "col"), "dp"),
            P(("row", "col"), "dp"),
            P(("row", "col"), "dp"),
        ),
        check_vma=False,
    )
```

```python
import functools
import math

import jax
import jax.numpy as jnp
from jax import lax
from jax.experimental import pallas as pl
from jax.experimental.layout import Layout, with_layout_constraint
from jax.experimental.pallas import tpu as pltpu
from jax.sharding import PartitionSpec as P

HEADS = 16
FREQ = 256


EPSILON = 1e-06


def layer_norm(values_in):
    centred = values_in - jnp.mean(values_in, axis=-1, keepdims=True)
    inverse = lax.rsqrt(jnp.mean(centred * centred, axis=-1, keepdims=True) + EPSILON)
    return (centred * inverse, inverse)


def norm_back(grad_normed, normed, inverse):
    mean_grad = jnp.mean(grad_normed, axis=-1, keepdims=True)
    mean_cross = jnp.mean(grad_normed * normed, axis=-1, keepdims=True)
    return inverse * (grad_normed - mean_grad - normed * mean_cross)


def turn_half(piece_half, cosine, sine_tab):
    quarter = cosine.shape[-1]
    lower = piece_half[..., :quarter]
    higher = piece_half[..., quarter:]
    return jnp.concatenate(
        [lower * cosine - higher * sine_tab, higher * cosine + lower * sine_tab], axis=-1
    )


def rotate(values_in, tables, signum):
    cos_row, sin_row, cos_col, sin_col = tables
    half_dim = values_in.shape[-1] // 2
    return jnp.concatenate(
        [
            turn_half(values_in[..., :half_dim], cos_row, signum * sin_row),
            turn_half(values_in[..., half_dim:], cos_col, signum * sin_col),
        ],
        axis=-1,
    )


def rope_tables(row_pos, col_pos, head_size):
    quarter = head_size // 4
    frequency = jnp.exp(jnp.arange(quarter, dtype=jnp.float32) * (-math.log(10000.0) / quarter))
    row_ang = row_pos.astype(jnp.float32)[:, None, None] * frequency
    col_ang = col_pos.astype(jnp.float32)[:, None, None] * frequency
    return (jnp.cos(row_ang), jnp.sin(row_ang), jnp.cos(col_ang), jnp.sin(col_ang))


def time_embed(step_values, freq_count):
    half_dim = freq_count // 2
    rate_list = jnp.exp(jnp.arange(half_dim, dtype=jnp.float32) * (-math.log(10000.0) / half_dim))
    angles = step_values.astype(jnp.float32)[..., None] * rate_list
    return jnp.concatenate([jnp.cos(angles), jnp.sin(angles)], axis=-1)


def gelu_tanh(inputs):
    return jax.nn.gelu(inputs, approximate=True)


def plain_dot(left_mat, right_mat):
    return jnp.dot(left_mat, right_mat, preferred_element_type=jnp.float32)


def left_dot(left_mat, right_mat):
    return lax.dot_general(
        left_mat, right_mat, (((0,), (0,)), ((), ())), preferred_element_type=jnp.float32
    )


def right_dot(left_mat, right_mat):
    return lax.dot_general(
        left_mat, right_mat, (((1,), (1,)), ((), ())), preferred_element_type=jnp.float32
    )


def block_size(key_count):
    block_len = key_count
    while block_len > 1024 and block_len % 2 == 0:
        block_len = block_len // 2
    return block_len


def local_gathered(
    latent,
    skip_input,
    text_states,
    timesteps,
    image_sides,
    cotangent,
    w_patch,
    w_skip,
    w_time,
    w_shift,
    w_qkv,
    w_out,
    w_query,
    w_text,
    w_cross,
    w_up,
    w_down,
    w_final,
    norm_params,
):
    widened = (
        lax.all_gather(w_patch, "dp", axis=1, tiled=True),
        lax.all_gather(w_skip, "dp", axis=1, tiled=True),
        lax.all_gather(w_time, "dp", axis=1, tiled=True),
        lax.all_gather(w_shift, "dp", axis=1, tiled=True),
        lax.all_gather(w_qkv, "dp", axis=1, tiled=True),
        lax.all_gather(w_out, "dp", axis=1, tiled=True),
        lax.all_gather(w_query, "dp", axis=1, tiled=True),
        lax.all_gather(w_text, "dp", axis=1, tiled=True),
        lax.all_gather(w_cross, "dp", axis=1, tiled=True),
        lax.all_gather(w_up, "dp", axis=1, tiled=True),
        lax.all_gather(w_down, "dp", axis=1, tiled=True),
        lax.all_gather(w_final, "dp", axis=1, tiled=True),
        lax.all_gather(norm_params, "dp", axis=1, tiled=True),
    )
    gathered = (
        lax.all_gather(widened[0], ("row", "col"), axis=0, tiled=True),
        lax.all_gather(widened[1], ("row", "col"), axis=0, tiled=True),
        lax.all_gather(widened[2], ("row", "col"), axis=0, tiled=True),
        lax.all_gather(widened[3], ("row", "col"), axis=0, tiled=True),
        lax.all_gather(widened[4], ("row", "col"), axis=0, tiled=True),
        lax.all_gather(widened[5], ("row", "col"), axis=0, tiled=True),
        lax.all_gather(widened[6], ("row", "col"), axis=0, tiled=True),
        lax.all_gather(widened[7], ("row", "col"), axis=0, tiled=True),
        lax.all_gather(widened[8], ("row", "col"), axis=0, tiled=True),
        lax.all_gather(widened[9], ("row", "col"), axis=0, tiled=True),
        lax.all_gather(widened[10], ("row", "col"), axis=0, tiled=True),
        lax.all_gather(widened[11], ("row", "col"), axis=0, tiled=True),
        lax.all_gather(widened[12], ("row", "col"), axis=0, tiled=True),
    )
    (
        f_patch,
        f_skip,
        f_time,
        f_shift,
        f_qkv,
        f_out,
        f_query,
        f_text,
        f_cross,
        f_up,
        f_down,
        f_final,
        f_norms,
    ) = gathered
    part_text = widened[7]
    images, rows_tile, cols_tile, patch_width = latent.shape
    tile_len = rows_tile * cols_tile
    row_count = images * tile_len
    model_width = f_qkv.shape[0]
    head_count = HEADS
    head_dim = model_width // head_count
    text_len = text_states.shape[1]
    grid_devices = lax.axis_size(("row", "col"))
    col_devices = lax.axis_size("col")
    grid_at = lax.axis_index(("row", "col"))
    row_at = lax.axis_index("row")
    col_at = lax.axis_index("col")
    score_scale = head_dim ** (-0.5)
    positions = jnp.arange(tile_len, dtype=jnp.int32)
    row_pos = row_at * rows_tile + positions // cols_tile
    col_pos = col_at * cols_tile + positions % cols_tile
    query_ok = (row_pos[None, :] < image_sides[:, None]) & (col_pos[None, :] < image_sides[:, None])
    keep_rows = query_ok.astype(jnp.float32).reshape(row_count, 1)
    tables = rope_tables(row_pos, col_pos, head_dim)
    norm_f = f_norms.astype(jnp.float32)

    def valid_keys(offset, block_len):
        index_list = offset + jnp.arange(block_len, dtype=jnp.int32)
        source = index_list // tile_len
        within = index_list % tile_len
        key_row = source // col_devices * rows_tile + within // cols_tile
        key_col = source % col_devices * cols_tile + within % cols_tile
        return (key_row[None, :] < image_sides[:, None]) & (key_col[None, :] < image_sides[:, None])

    patch_rows = latent.reshape(row_count, patch_width)
    patch_feat = right_dot(patch_rows, f_patch)
    skip_rows = skip_input.reshape(row_count, model_width).astype(jnp.float32)
    gain_skip = jnp.concatenate([norm_f[:, 8], norm_f[:, 10]])
    bias_skip = jnp.concatenate([norm_f[:, 9], norm_f[:, 11]])
    joined, joined_inv = layer_norm(jnp.concatenate([patch_feat, skip_rows], axis=-1))
    skip_in = (joined * gain_skip + bias_skip).astype(jnp.bfloat16)
    residual = plain_dot(skip_in, f_skip)
    embedding = time_embed(timesteps, FREQ).astype(jnp.bfloat16)
    time_pre = plain_dot(embedding, f_time)
    time_float, silu_pull = jax.vjp(jax.nn.silu, time_pre)
    time_act = time_float.astype(jnp.bfloat16)
    time_shift = plain_dot(time_act, f_shift)
    first_z, first_inv = layer_norm(residual)
    first_pre = (first_z * norm_f[:, 0] + norm_f[:, 1]).reshape(
        images, tile_len, model_width
    ) + time_shift[:, None, :]
    first_in = first_pre.reshape(row_count, model_width).astype(jnp.bfloat16)
    qkv = plain_dot(first_in, f_qkv)
    query_z, query_inv = layer_norm(
        qkv[:, :model_width].reshape(images, tile_len, head_count, head_dim)
    )
    key_z, key_inv = layer_norm(
        qkv[:, model_width : 2 * model_width].reshape(images, tile_len, head_count, head_dim)
    )
    queries = rotate(query_z, tables, 1.0).astype(jnp.bfloat16)
    queries_h = jnp.transpose(queries, (0, 2, 1, 3))
    keys = rotate(key_z, tables, 1.0).astype(jnp.bfloat16).reshape(images, tile_len, model_width)
    values = qkv[:, 2 * model_width :].astype(jnp.bfloat16).reshape(images, tile_len, model_width)
    start_carry = (
        jnp.full((images, head_count, tile_len), -1e30, jnp.float32),
        jnp.zeros((images, head_count, tile_len), jnp.float32),
        jnp.zeros((images, head_count, tile_len, head_dim), jnp.float32),
    )
    key_rows = lax.all_gather(keys, ("row", "col"), axis=1, tiled=True)
    value_rows = lax.all_gather(values, ("row", "col"), axis=1, tiled=True)
    key_count = key_rows.shape[1]
    block_len = block_size(key_count)

    def forward_block_step(block_index, running):
        running_max, weight_sum, accum_sum = running
        offset = block_index * block_len
        key_blk = lax.dynamic_slice_in_dim(key_rows, offset, block_len, 1).reshape(
            images, block_len, head_count, head_dim
        )
        value_blk = lax.dynamic_slice_in_dim(value_rows, offset, block_len, 1).reshape(
            images, block_len, head_count, head_dim
        )
        key_ok = valid_keys(offset, block_len)
        scores = (
            jnp.einsum("ihqe,ikhe->ihqk", queries_h, key_blk, preferred_element_type=jnp.float32)
            * score_scale
        )
        scores = jnp.where(key_ok[:, None, None, :], scores, -jnp.inf)
        new_max = jnp.maximum(running_max, jnp.max(scores, axis=-1))
        weight = jnp.exp(scores - new_max[..., None])
        rescale = jnp.exp(running_max - new_max)
        weight_sum = weight_sum * rescale + jnp.sum(weight, axis=-1)
        accum_sum = accum_sum * rescale[..., None] + jnp.einsum(
            "ihqk,ikhe->ihqe",
            weight.astype(jnp.bfloat16),
            value_blk,
            preferred_element_type=jnp.float32,
        )
        return (new_max, weight_sum, accum_sum)

    running_max, weight_sum, accum_sum = lax.fori_loop(
        0, key_count // block_len, forward_block_step, start_carry
    )
    attended = accum_sum / weight_sum[..., None]
    log_sum = running_max + jnp.log(weight_sum)
    att_low = (
        jnp.transpose(attended, (0, 2, 1, 3)).reshape(row_count, model_width).astype(jnp.bfloat16)
    )
    residual_two = residual + plain_dot(att_low, f_out)
    third_z, third_inv = layer_norm(residual_two)
    third_in = (third_z * norm_f[:, 2] + norm_f[:, 3]).astype(jnp.bfloat16)
    cross_pre = plain_dot(third_in, f_query)
    cq_z, cq_inv = layer_norm(cross_pre.reshape(images, tile_len, head_count, head_dim))
    cross_queries = cq_z.astype(jnp.bfloat16)
    text_kv = jnp.einsum("itc,cd->itd", text_states, f_text, preferred_element_type=jnp.float32)
    ck_z, ck_inv = layer_norm(
        text_kv[..., :model_width].reshape(images, text_len, head_count, head_dim)
    )
    cross_keys = ck_z.astype(jnp.bfloat16)
    cross_values = (
        text_kv[..., model_width:]
        .astype(jnp.bfloat16)
        .reshape(images, text_len, head_count, head_dim)
    )

    def cross_softmax():
        scores = (
            jnp.einsum(
                "iqhe,ikhe->ihqk", cross_queries, cross_keys, preferred_element_type=jnp.float32
            )
            * score_scale
        )
        return jax.nn.softmax(scores, axis=-1)

    crossed = jnp.einsum(
        "ihqk,ikhe->iqhe",
        cross_softmax().astype(jnp.bfloat16),
        cross_values,
        preferred_element_type=jnp.float32,
    )
    cross_low = crossed.reshape(row_count, model_width).astype(jnp.bfloat16)
    residual_three = residual_two + plain_dot(cross_low, f_cross)
    second_z, second_inv = layer_norm(residual_three)
    second_in = (second_z * norm_f[:, 4] + norm_f[:, 5]).astype(jnp.bfloat16)
    up_pre = plain_dot(second_in, f_up)
    hidden_float, gelu_pull = jax.vjp(gelu_tanh, up_pre)
    hidden_act = hidden_float.astype(jnp.bfloat16)
    residual_four = residual_three + plain_dot(hidden_act, f_down)
    last_z, last_inv = layer_norm(residual_four)
    last_in = (last_z * norm_f[:, 6] + norm_f[:, 7]).astype(jnp.bfloat16)
    produced = plain_dot(last_in, f_final)
    prediction = (
        (produced * keep_rows)
        .astype(jnp.bfloat16)
        .reshape(images, rows_tile, cols_tile, produced.shape[1])
    )
    grad_out = (
        cotangent.reshape(row_count, produced.shape[1]).astype(jnp.float32) * keep_rows
    ).astype(jnp.bfloat16)
    d_final = left_dot(last_in, grad_out)
    grad_last = right_dot(grad_out, f_final)
    gain_final = jnp.sum(grad_last * last_z, axis=0)
    bias_final = jnp.sum(grad_last, axis=0)
    grad_four = norm_back(grad_last * norm_f[:, 6], last_z, last_inv)
    low_four = grad_four.astype(jnp.bfloat16)
    d_down = left_dot(hidden_act, low_four)
    grad_hidden = right_dot(low_four, f_down)
    grad_up = gelu_pull(grad_hidden)[0].astype(jnp.bfloat16)
    d_up = left_dot(second_in, grad_up)
    grad_second = right_dot(grad_up, f_up)
    gain_second = jnp.sum(grad_second * second_z, axis=0)
    bias_second = jnp.sum(grad_second, axis=0)
    grad_three = grad_four + norm_back(grad_second * norm_f[:, 4], second_z, second_inv)
    low_three = grad_three.astype(jnp.bfloat16)
    d_cross = left_dot(cross_low, low_three)
    grad_crossed = (
        right_dot(low_three, f_cross)
        .astype(jnp.bfloat16)
        .reshape(images, tile_len, head_count, head_dim)
    )
    cross_probs = cross_softmax()
    cross_delta = jnp.transpose(
        jnp.sum(grad_crossed.astype(jnp.float32) * crossed, axis=-1), (0, 2, 1)
    )
    grad_probs = jnp.einsum(
        "iqhe,ikhe->ihqk", grad_crossed, cross_values, preferred_element_type=jnp.float32
    )
    grad_cscore = (cross_probs * (grad_probs - cross_delta[..., None])).astype(jnp.bfloat16)
    grad_cq = score_scale * jnp.einsum(
        "ihqk,ikhe->iqhe", grad_cscore, cross_keys, preferred_element_type=jnp.float32
    )
    part_ckey = score_scale * jnp.einsum(
        "ihqk,iqhe->ikhe", grad_cscore, cross_queries, preferred_element_type=jnp.float32
    )
    part_cvalue = jnp.einsum(
        "ihqk,iqhe->ikhe",
        cross_probs.astype(jnp.bfloat16),
        grad_crossed,
        preferred_element_type=jnp.float32,
    )
    grad_cross_q = (
        norm_back(grad_cq, cq_z, cq_inv).reshape(row_count, model_width).astype(jnp.bfloat16)
    )
    d_query = left_dot(third_in, grad_cross_q)
    grad_third = right_dot(grad_cross_q, f_query)
    gain_third = jnp.sum(grad_third * third_z, axis=0)
    bias_third = jnp.sum(grad_third, axis=0)
    grad_two = grad_three + norm_back(grad_third * norm_f[:, 2], third_z, third_inv)
    sum_ckey, sum_cvalue = lax.psum((part_ckey, part_cvalue), ("row", "col"))
    low_two = grad_two.astype(jnp.bfloat16)
    d_out = left_dot(att_low, low_two)
    grad_att = (
        right_dot(low_two, f_out)
        .astype(jnp.bfloat16)
        .reshape(images, tile_len, head_count, head_dim)
    )
    grad_att_h = jnp.transpose(grad_att, (0, 2, 1, 3))
    delta_rows = jnp.sum(grad_att_h.astype(jnp.float32) * attended, axis=-1)
    back_carry = (
        jnp.zeros((images, head_count, tile_len, head_dim), jnp.float32),
        jnp.zeros((images, tile_len * grid_devices, model_width), jnp.float32),
        jnp.zeros((images, tile_len * grid_devices, model_width), jnp.float32),
    )
    backward_key_rows = lax.all_gather(keys, ("row", "col"), axis=1, tiled=True)
    backward_value_rows = lax.all_gather(values, ("row", "col"), axis=1, tiled=True)
    key_count = backward_key_rows.shape[1]
    backward_block_len = block_size(key_count)

    def backward_block_step(block_index, running):
        grad_query, grad_key_all, grad_value_all = running
        offset = block_index * backward_block_len
        key_blk = lax.dynamic_slice_in_dim(
            backward_key_rows, offset, backward_block_len, 1
        ).reshape(images, backward_block_len, head_count, head_dim)
        value_blk = lax.dynamic_slice_in_dim(
            backward_value_rows, offset, backward_block_len, 1
        ).reshape(images, backward_block_len, head_count, head_dim)
        key_ok = valid_keys(offset, backward_block_len)
        scores = (
            jnp.einsum("ihqe,ikhe->ihqk", queries_h, key_blk, preferred_element_type=jnp.float32)
            * score_scale
        )
        scores = jnp.where(key_ok[:, None, None, :], scores, -jnp.inf)
        attn_probs = jnp.exp(scores - log_sum[..., None])
        grad_prob = jnp.einsum(
            "ihqe,ikhe->ihqk", grad_att_h, value_blk, preferred_element_type=jnp.float32
        )
        grad_score = (attn_probs * (grad_prob - delta_rows[..., None])).astype(jnp.bfloat16)
        grad_query = grad_query + score_scale * jnp.einsum(
            "ihqk,ikhe->ihqe", grad_score, key_blk, preferred_element_type=jnp.float32
        )
        key_part = score_scale * jnp.einsum(
            "ihqk,ihqe->ikhe", grad_score, queries_h, preferred_element_type=jnp.float32
        )
        value_part = jnp.einsum(
            "ihqk,ihqe->ikhe",
            attn_probs.astype(jnp.bfloat16),
            grad_att_h,
            preferred_element_type=jnp.float32,
        )
        grad_key_all = lax.dynamic_update_slice_in_dim(
            grad_key_all, key_part.reshape(images, backward_block_len, model_width), offset, 1
        )
        grad_value_all = lax.dynamic_update_slice_in_dim(
            grad_value_all, value_part.reshape(images, backward_block_len, model_width), offset, 1
        )
        return (grad_query, grad_key_all, grad_value_all)

    grad_query, grad_key_all, grad_value_all = lax.fori_loop(
        0, key_count // backward_block_len, backward_block_step, back_carry
    )
    grad_key_own, grad_value_own = (
        lax.psum_scatter(grad_key_all, ("row", "col"), scatter_dimension=1, tiled=True),
        lax.psum_scatter(grad_value_all, ("row", "col"), scatter_dimension=1, tiled=True),
    )
    grad_qn = rotate(jnp.transpose(grad_query, (0, 2, 1, 3)), tables, -1.0)
    grad_kn = rotate(grad_key_own.reshape(images, tile_len, head_count, head_dim), tables, -1.0)
    grad_qkv = jnp.concatenate(
        [
            norm_back(grad_qn, query_z, query_inv).reshape(row_count, model_width),
            norm_back(grad_kn, key_z, key_inv).reshape(row_count, model_width),
            grad_value_own.reshape(row_count, model_width),
        ],
        axis=-1,
    ).astype(jnp.bfloat16)
    d_qkv = left_dot(first_in, grad_qkv)
    grad_first = right_dot(grad_qkv, f_qkv)
    gain_first = jnp.sum(grad_first * first_z, axis=0)
    bias_first = jnp.sum(grad_first, axis=0)
    part_shift = jnp.sum(grad_first.reshape(images, tile_len, model_width), axis=1)
    grad_one = grad_two + norm_back(grad_first * norm_f[:, 0], first_z, first_inv)
    shift_grad = lax.psum(part_shift, ("row", "col"))
    grad_ckey = norm_back(sum_ckey, ck_z, ck_inv).reshape(images, text_len, model_width)
    grad_kv = jnp.concatenate(
        [grad_ckey, sum_cvalue.reshape(images, text_len, model_width)], axis=-1
    ).astype(jnp.bfloat16)
    text_slice = text_states.shape[2] // grid_devices
    text_cols = lax.dynamic_slice_in_dim(text_states, grid_at * text_slice, text_slice, 2)
    d_text_w = jnp.einsum("itc,itd->cd", text_cols, grad_kv, preferred_element_type=jnp.float32)
    text_grad = jnp.einsum("itd,cd->itc", grad_kv, part_text, preferred_element_type=jnp.float32)
    shift_low = shift_grad.astype(jnp.bfloat16)
    shift_slice = model_width // grid_devices
    act_cols = lax.dynamic_slice_in_dim(time_act, grid_at * shift_slice, shift_slice, 1)
    d_shift_w = jnp.einsum("ic,id->cd", act_cols, shift_low, preferred_element_type=jnp.float32)
    grad_time_act = right_dot(shift_low, f_shift)
    grad_time_pre = silu_pull(grad_time_act)[0].astype(jnp.bfloat16)
    freq_slice = embedding.shape[1] // grid_devices
    embed_cols = lax.dynamic_slice_in_dim(embedding, grid_at * freq_slice, freq_slice, 1)
    d_time_w = jnp.einsum(
        "ic,id->cd", embed_cols, grad_time_pre, preferred_element_type=jnp.float32
    )
    low_one = grad_one.astype(jnp.bfloat16)
    d_skip_w = left_dot(skip_in, low_one)
    grad_skip_in = right_dot(low_one, f_skip)
    gain_skips = jnp.sum(grad_skip_in * joined, axis=0)
    bias_skips = jnp.sum(grad_skip_in, axis=0)
    grad_joined = norm_back(grad_skip_in * gain_skip, joined, joined_inv)
    skip_grad = grad_joined[:, model_width:].reshape(images, rows_tile, cols_tile, model_width)
    grad_patch = grad_joined[:, :model_width].astype(jnp.bfloat16)
    d_patch = left_dot(grad_patch, patch_rows)
    latent_grad = plain_dot(grad_patch, f_patch).reshape(images, rows_tile, cols_tile, patch_width)
    d_norms = jnp.stack(
        [
            gain_first,
            bias_first,
            gain_third,
            bias_third,
            gain_second,
            bias_second,
            gain_final,
            bias_final,
            gain_skips[:model_width],
            bias_skips[:model_width],
            gain_skips[model_width:],
            bias_skips[model_width:],
        ],
        axis=1,
    )
    tile_done = (
        lax.psum_scatter(d_patch, ("row", "col"), scatter_dimension=0, tiled=True),
        lax.psum_scatter(d_skip_w, ("row", "col"), scatter_dimension=0, tiled=True),
        lax.psum_scatter(d_qkv, ("row", "col"), scatter_dimension=0, tiled=True),
        lax.psum_scatter(d_out, ("row", "col"), scatter_dimension=0, tiled=True),
        lax.psum_scatter(d_query, ("row", "col"), scatter_dimension=0, tiled=True),
        lax.psum_scatter(d_cross, ("row", "col"), scatter_dimension=0, tiled=True),
        lax.psum_scatter(d_up, ("row", "col"), scatter_dimension=0, tiled=True),
        lax.psum_scatter(d_down, ("row", "col"), scatter_dimension=0, tiled=True),
        lax.psum_scatter(d_final, ("row", "col"), scatter_dimension=0, tiled=True),
        lax.psum_scatter(d_norms, ("row", "col"), scatter_dimension=0, tiled=True),
    )
    reduced = (
        lax.psum_scatter(
            tile_done[0].astype(jnp.bfloat16), "dp", scatter_dimension=1, tiled=True
        ).astype(jnp.float32),
        lax.psum_scatter(
            tile_done[1].astype(jnp.bfloat16), "dp", scatter_dimension=1, tiled=True
        ).astype(jnp.float32),
        lax.psum_scatter(
            tile_done[2].astype(jnp.bfloat16), "dp", scatter_dimension=1, tiled=True
        ).astype(jnp.float32),
        lax.psum_scatter(
            tile_done[3].astype(jnp.bfloat16), "dp", scatter_dimension=1, tiled=True
        ).astype(jnp.float32),
        lax.psum_scatter(
            tile_done[4].astype(jnp.bfloat16), "dp", scatter_dimension=1, tiled=True
        ).astype(jnp.float32),
        lax.psum_scatter(
            tile_done[5].astype(jnp.bfloat16), "dp", scatter_dimension=1, tiled=True
        ).astype(jnp.float32),
        lax.psum_scatter(
            tile_done[6].astype(jnp.bfloat16), "dp", scatter_dimension=1, tiled=True
        ).astype(jnp.float32),
        lax.psum_scatter(
            tile_done[7].astype(jnp.bfloat16), "dp", scatter_dimension=1, tiled=True
        ).astype(jnp.float32),
        lax.psum_scatter(
            tile_done[8].astype(jnp.bfloat16), "dp", scatter_dimension=1, tiled=True
        ).astype(jnp.float32),
        lax.psum_scatter(
            tile_done[9].astype(jnp.bfloat16), "dp", scatter_dimension=1, tiled=True
        ).astype(jnp.float32),
        lax.psum_scatter(
            d_time_w.astype(jnp.bfloat16), "dp", scatter_dimension=1, tiled=True
        ).astype(jnp.float32),
        lax.psum_scatter(
            d_shift_w.astype(jnp.bfloat16), "dp", scatter_dimension=1, tiled=True
        ).astype(jnp.float32),
        lax.psum_scatter(
            d_text_w.astype(jnp.bfloat16), "dp", scatter_dimension=1, tiled=True
        ).astype(jnp.float32),
    )
    return (
        prediction,
        latent_grad,
        skip_grad,
        text_grad,
        reduced[0],
        reduced[1],
        reduced[10],
        reduced[11],
        reduced[2],
        reduced[3],
        reduced[4],
        reduced[12],
        reduced[5],
        reduced[6],
        reduced[7],
        reduced[8],
        reduced[9],
    )


TILE = ("row", "col")
EVERY = ("dp", "row", "col")
LOG2E = math.log2(math.e)
F32 = jnp.float32
BF16 = jnp.bfloat16
VMEM_BYTES = 56 * 2**20


def kernel_call(body, flops, moved, **options):
    return pl.pallas_call(
        body,
        compiler_params=pltpu.CompilerParams(vmem_limit_bytes=VMEM_BYTES),
        cost_estimate=pl.CostEstimate(flops=flops, bytes_accessed=moved, transcendentals=0),
        **options,
    )


def pair_swap(values_in):
    quarter = values_in.shape[0] // 4
    parts = [values_in[at * quarter : (at + 1) * quarter] for at in (1, 0, 3, 2)]
    return jnp.concatenate(parts, axis=0)


def column_norm(values_in):
    centred = values_in - jnp.mean(values_in, axis=0, keepdims=True)
    inverse = lax.rsqrt(jnp.mean(centred * centred, axis=0, keepdims=True) + EPSILON)
    return (centred * inverse, inverse)


def column_norm_back(grad_normed, normed, inverse):
    mean_grad = jnp.mean(grad_normed, axis=0, keepdims=True)
    mean_cross = jnp.mean(grad_normed * normed, axis=0, keepdims=True)
    return inverse * (grad_normed - mean_grad - normed * mean_cross)


def minus_pieces(row_values):
    high = row_values.astype(BF16).astype(F32)
    rest = row_values - high
    middle = rest.astype(BF16).astype(F32)
    lower = rest - middle
    at = lax.broadcasted_iota(jnp.int32, (8, row_values.shape[1]), 0)
    zero = jnp.zeros((8, row_values.shape[1]), F32)
    picked = jnp.where(at == 0, high, jnp.where(at == 1, middle, jnp.where(at == 2, lower, zero)))
    return -picked


def piece_flags(width):
    return (lax.broadcasted_iota(jnp.int32, (8, width), 0) < 3).astype(F32)


def head_norm_body(
    query_scale, rows_ref, weight_ref, cos_ref, sin_ref, ok_ref, out_ref, inv_ref
):
    groups, _, heads, head_dim, _ = out_ref.shape
    part = pl.program_id(0)
    made = jnp.dot(rows_ref[...], weight_ref[...], preferred_element_type=F32).T
    valid = ok_ref[...]

    @pl.when(part < 2)
    def _():
        factor = jnp.where(part == 0, query_scale, valid)
        cosine, sine = cos_ref[...] * factor, sin_ref[...] * factor
        for group in range(groups):
            for head in range(heads):
                at = (group * heads + head) * head_dim
                normed, inverse = column_norm(made[at : at + head_dim])
                turned = normed * cosine + pair_swap(normed) * sine
                out_ref[group, 0, head] = turned.astype(BF16)
                inv_ref[group, 0, head : head + 1] = inverse

    @pl.when(part == 2)
    def _():
        for group in range(groups):
            for head in range(heads):
                at = (group * heads + head) * head_dim
                out_ref[group, 0, head] = (made[at : at + head_dim] * valid).astype(BF16)
                inv_ref[group, 0, head : head + 1] = valid


def head_norm(rows, weight, tables, valid, groups, head_dim, query_scale):
    tile_len, depth = rows.shape
    width = weight.shape[1] // 3
    heads = width // groups // head_dim
    table = pl.BlockSpec((head_dim, tile_len), lambda p: (0, 0))
    return kernel_call(
        functools.partial(head_norm_body, query_scale),
        6 * tile_len * depth * width,
        6 * depth * width,
        grid=(3,),
        in_specs=[
            pl.BlockSpec((tile_len, depth), lambda p: (0, 0)),
            pl.BlockSpec((depth, width), lambda p: (0, p)),
            table,
            table,
            pl.BlockSpec((1, tile_len), lambda p: (0, 0)),
        ],
        out_specs=[
            pl.BlockSpec((groups, 1, heads, head_dim, tile_len), lambda p: (0, p, 0, 0, 0)),
            pl.BlockSpec((groups, 1, heads, tile_len), lambda p: (0, p, 0, 0)),
        ],
        out_shape=[
            jax.ShapeDtypeStruct((groups, 3, heads, head_dim, tile_len), BF16),
            jax.ShapeDtypeStruct((groups, 3, heads, tile_len), F32),
        ],
    )(rows, weight, *tables, valid)


def head_back_body(
    query_scale, grad_ref, own_ref, inv_ref, cos_ref, sin_ref, ok_ref, *others
):
    out_ref = others[-1]
    heads, head_dim = own_ref.shape[2], own_ref.shape[3]
    cosine, sine, valid = cos_ref[...], sin_ref[...], ok_ref[...]

    def unturn(values_in):
        return values_in * cosine - pair_swap(values_in) * sine

    for part in range(3):
        pieces = []
        for head in range(heads):
            grad = grad_ref[0, part, head].astype(F32)
            if part > 0:
                grad = grad * valid
            if part < 2:
                normed = unturn(own_ref[0, part, head].astype(F32))
                if part == 0:
                    normed = normed * (1.0 / query_scale)
                inverse = inv_ref[0, part, head : head + 1]
                grad = column_norm_back(unturn(grad), normed, inverse)
            pieces.append(grad)
        out_ref[part, 0] = jnp.concatenate(pieces, axis=0).astype(BF16)


def head_back(grads, own, inverses, tables, valid, query_scale, image, images, before):
    groups, _, heads, head_dim, tile_len = own.shape
    group_rows = heads * head_dim
    stacked = pl.BlockSpec((1, 3, heads, head_dim, tile_len), lambda g: (g, 0, 0, 0, 0))
    table = pl.BlockSpec((head_dim, tile_len), lambda g: (0, 0))
    earlier = () if before is None else (before,)
    return kernel_call(
        functools.partial(head_back_body, query_scale),
        0,
        6 * own.size,
        grid=(groups,),
        in_specs=[
            stacked,
            stacked,
            pl.BlockSpec((1, 3, heads, tile_len), lambda g: (g, 0, 0, 0)),
            table,
            table,
            pl.BlockSpec((1, tile_len), lambda g: (0, 0)),
        ]
        + [pl.BlockSpec(memory_space=pl.ANY)] * len(earlier),
        out_specs=pl.BlockSpec((3, 1, group_rows, tile_len), lambda g: (0, g, 0, image)),
        out_shape=jax.ShapeDtypeStruct((3, groups, group_rows, images * tile_len), BF16),
        input_output_aliases={6: 0} if earlier else {},
    )(grads, own, inverses, *tables, valid, *earlier)


def attend_body(query_ref, key_ref, value_ref, ok_ref, out_ref, lse_ref, key_nat, value_ext):
    tiles, tile_len, head_dim = key_ref.shape[0], key_ref.shape[-1], key_ref.shape[-2]

    @pl.when(pl.program_id(1) == 0)
    def _():
        for tile in range(tiles):
            key_nat[tile * tile_len : (tile + 1) * tile_len, :] = key_ref[tile, 0, 0].T
            value_ext[tile] = jnp.concatenate(
                [value_ref[tile, 0, 0].astype(F32), ok_ref[tile]], axis=0
            ).astype(BF16)

    query = query_ref[0, 0, 0]
    total = jnp.zeros((head_dim + 8, tile_len), F32)
    held = None
    for tile in range(tiles + 1):
        scores = None
        if tile < tiles:
            rows = slice(tile * tile_len, (tile + 1) * tile_len)
            scores = jnp.dot(key_nat[rows, :], query, preferred_element_type=F32)
        if held is not None:
            weight = jnp.exp2(held).astype(BF16)
            total = total + jnp.dot(value_ext[tile - 1], weight, preferred_element_type=F32)
        held = scores
    weight_sum = total[head_dim : head_dim + 1]
    out_ref[0, 0] = (total[:head_dim] / weight_sum).astype(BF16)
    lse_ref[0, 0] = jnp.log2(weight_sum)


def attend(qkv, flags):
    tiles, _, heads, head_dim, tile_len = qkv.shape
    return kernel_call(
        attend_body,
        1024 * heads * tiles**2 * tile_len**2,
        8 * qkv.size,
        grid=(heads, tiles),
        in_specs=[
            pl.BlockSpec((1, 1, 1, head_dim, tile_len), lambda h, t: (t, 0, h, 0, 0)),
            pl.BlockSpec((tiles, 1, 1, head_dim, tile_len), lambda h, t: (0, 1, h, 0, 0)),
            pl.BlockSpec((tiles, 1, 1, head_dim, tile_len), lambda h, t: (0, 2, h, 0, 0)),
            pl.BlockSpec((tiles, 8, tile_len), lambda h, t: (0, 0, 0)),
        ],
        out_specs=[
            pl.BlockSpec((1, 1, head_dim, tile_len), lambda h, t: (t, h, 0, 0)),
            pl.BlockSpec((1, 1, 1, tile_len), lambda h, t: (t, h, 0, 0)),
        ],
        out_shape=[
            jax.ShapeDtypeStruct((tiles, heads, head_dim, tile_len), BF16),
            jax.ShapeDtypeStruct((tiles, heads, 1, tile_len), F32),
        ],
        scratch_shapes=[
            pltpu.VMEM((tiles * tile_len, head_dim), BF16),
            pltpu.VMEM((tiles, head_dim + 8, tile_len), BF16),
        ],
    )(qkv, qkv, qkv, flags)


def attend_back_body(
    score_scale,
    query_ref,
    key_ref,
    value_ref,
    grad_ref,
    att_ref,
    lse_ref,
    out_ref,
    key_nat,
    value_nat,
    key_sum,
    value_sum,
):
    tiles, tile_len, head_dim = key_ref.shape[0], key_ref.shape[-1], key_ref.shape[-2]
    at = pl.program_id(1)

    @pl.when(at == 0)
    def _():
        ones = piece_flags(tile_len)
        for tile in range(tiles):
            rows = slice(tile * tile_len, (tile + 1) * tile_len)
            for source, kept in ((key_ref, key_nat), (value_ref, value_nat)):
                wide = jnp.concatenate([source[tile, 0, 0].astype(F32), ones], axis=0)
                kept[rows, :] = wide.T.astype(BF16)
        key_sum[...] = jnp.zeros_like(key_sum)
        value_sum[...] = jnp.zeros_like(value_sum)

    query = query_ref[0, 0, 0].astype(F32)
    grad = grad_ref[0, 0].astype(F32)
    delta = jnp.sum(grad * att_ref[0, 0].astype(F32), axis=0, keepdims=True)
    query_ext = jnp.concatenate([query, minus_pieces(lse_ref[0, 0])], axis=0)
    grad_ext = jnp.concatenate([grad, minus_pieces(delta)], axis=0)
    query_cols, grad_cols = query_ext.astype(BF16), grad_ext.astype(BF16)
    query_nat, grad_nat = query_ext.T.astype(BF16), grad_ext.T.astype(BF16)

    def step(tile, total):
        rows = pl.ds(pl.multiple_of(tile * tile_len, tile_len), tile_len)
        scores = jnp.dot(key_nat[rows, :], query_cols, preferred_element_type=F32)
        probs = jnp.exp2(scores)
        grad_probs = jnp.dot(value_nat[rows, :], grad_cols, preferred_element_type=F32)
        grad_scores = (probs * grad_probs).astype(BF16)
        value_sum[rows, :] += jnp.dot(probs.astype(BF16), grad_nat, preferred_element_type=F32)
        key_sum[rows, :] += jnp.dot(grad_scores, query_nat, preferred_element_type=F32)
        return total + jnp.dot(key_ref[tile, 0, 0], grad_scores, preferred_element_type=F32)

    start = jnp.zeros((head_dim, tile_len), F32)
    total = lax.fori_loop(0, tiles, step, start, unroll=8)
    out_ref[at, 0, 0] = (total * score_scale).astype(BF16)

    @pl.when(at == tiles - 1)
    def _():
        for tile in range(tiles):
            rows = slice(tile * tile_len, (tile + 1) * tile_len)
            key_grad = key_sum[rows, :].T[:head_dim] * (1.0 / LOG2E)
            out_ref[tile, 1, 0] = key_grad.astype(BF16)
            out_ref[tile, 2, 0] = value_sum[rows, :].T[:head_dim].astype(BF16)


def attend_back(qkv, grad_att, att, lse, score_scale):
    tiles, _, heads, head_dim, tile_len = qkv.shape
    one = pl.BlockSpec((1, 1, head_dim, tile_len), lambda h, t: (t, h, 0, 0))
    return kernel_call(
        functools.partial(attend_back_body, score_scale),
        2560 * heads * tiles**2 * tile_len**2,
        8 * qkv.size,
        grid=(heads, tiles),
        in_specs=[
            pl.BlockSpec((1, 1, 1, head_dim, tile_len), lambda h, t: (t, 0, h, 0, 0)),
            pl.BlockSpec((tiles, 1, 1, head_dim, tile_len), lambda h, t: (0, 1, h, 0, 0)),
            pl.BlockSpec((tiles, 1, 1, head_dim, tile_len), lambda h, t: (0, 2, h, 0, 0)),
            one,
            one,
            pl.BlockSpec((1, 1, 1, tile_len), lambda h, t: (t, h, 0, 0)),
        ],
        out_specs=pl.BlockSpec(
            (tiles, 3, 1, head_dim, tile_len), lambda h, t: (0, 0, h, 0, 0)
        ),
        out_shape=jax.ShapeDtypeStruct(qkv.shape, BF16),
        scratch_shapes=[
            pltpu.VMEM((tiles * tile_len, head_dim + 8), BF16),
            pltpu.VMEM((tiles * tile_len, head_dim + 8), BF16),
            pltpu.VMEM((tiles * tile_len, head_dim + 8), F32),
            pltpu.VMEM((tiles * tile_len, head_dim + 8), F32),
        ],
    )(qkv, qkv, qkv, grad_att, att, lse)


def cross_body(text_len, query_scale, pre_ref, kv_ref, att_ref, query_ref, inv_ref, lse_ref):
    head_dim, text_pad = kv_ref.shape[2], kv_ref.shape[3]
    at = lax.broadcasted_iota(jnp.int32, (8, text_pad), 0)
    text_at = lax.broadcasted_iota(jnp.int32, (8, text_pad), 1)
    flags = ((at == 0) & (text_at < text_len)).astype(F32)
    for head in range(pre_ref.shape[0]):
        normed, inverse = column_norm(pre_ref[head])
        query = (normed * query_scale).astype(BF16)
        query_ref[head] = query
        inv_ref[head] = inverse
        key = column_norm(kv_ref[0, head])[0].astype(BF16)
        value_ext = jnp.concatenate([kv_ref[1, head], flags], axis=0).astype(BF16)
        scores = jnp.dot(key.T, query, preferred_element_type=F32)
        weight = jnp.exp2(scores).astype(BF16)
        total = jnp.dot(value_ext, weight, preferred_element_type=F32)
        weight_sum = total[head_dim : head_dim + 1]
        att_ref[head] = (total[:head_dim] / weight_sum).astype(BF16)
        lse_ref[head] = jnp.log2(weight_sum)


def cross_attend(pre, text_kv, images, text_len, query_scale):
    heads, head_dim, tokens = pre.shape
    tile_len, text_pad = tokens // images, text_kv.shape[3] // images
    block = math.gcd(heads, 4)
    wide = pl.BlockSpec((block, head_dim, tile_len), lambda i, h: (h, 0, i))
    row = pl.BlockSpec((block, 1, tile_len), lambda i, h: (h, 0, i))
    return kernel_call(
        functools.partial(cross_body, text_len, query_scale),
        1024 * heads * tokens * text_pad,
        8 * pre.size,
        grid=(images, heads // block),
        in_specs=[wide, pl.BlockSpec((2, block, head_dim, text_pad), lambda i, h: (0, h, 0, i))],
        out_specs=[wide, wide, row, row],
        out_shape=[
            jax.ShapeDtypeStruct(pre.shape, BF16),
            jax.ShapeDtypeStruct(pre.shape, BF16),
            jax.ShapeDtypeStruct((heads, 1, tokens), F32),
            jax.ShapeDtypeStruct((heads, 1, tokens), F32),
        ],
    )(pre, text_kv)


def cross_back_body(
    query_scale,
    score_scale,
    query_ref,
    kv_ref,
    grad_ref,
    att_ref,
    inv_ref,
    lse_ref,
    out_ref,
    key_ref,
    value_ref,
):
    head_dim, text_pad = kv_ref.shape[2], kv_ref.shape[3]
    ones = piece_flags(text_pad)
    for head in range(query_ref.shape[0]):
        query = query_ref[head].astype(F32)
        grad = grad_ref[head].astype(F32)
        delta = jnp.sum(grad * att_ref[head].astype(F32), axis=0, keepdims=True)
        query_ext = jnp.concatenate([query, minus_pieces(lse_ref[head])], axis=0).astype(BF16)
        grad_ext = jnp.concatenate([grad, minus_pieces(delta)], axis=0).astype(BF16)
        key = column_norm(kv_ref[0, head])[0].astype(BF16)
        key_ext = jnp.concatenate([key.astype(F32), ones], axis=0).T.astype(BF16)
        value_ext = jnp.concatenate([kv_ref[1, head], ones], axis=0).T.astype(BF16)
        probs = jnp.exp2(jnp.dot(key_ext, query_ext, preferred_element_type=F32))
        grad_probs = jnp.dot(value_ext, grad_ext, preferred_element_type=F32)
        grad_scores = (probs * grad_probs).astype(BF16)
        value_grad = right_dot(grad_ext, probs.astype(BF16))[:head_dim]
        key_grad = right_dot(query_ext, grad_scores)[:head_dim]
        key_ref[head] = (key_grad * (1.0 / LOG2E)).astype(BF16)
        value_ref[head] = value_grad.astype(BF16)
        query_grad = jnp.dot(key, grad_scores, preferred_element_type=F32) * score_scale
        normed = query * (1.0 / query_scale)
        out_ref[head] = column_norm_back(query_grad, normed, inv_ref[head]).astype(BF16)


def cross_back(query, text_kv, grad, att, inverse, lse, images, query_scale, score_scale):
    heads, head_dim, tokens = query.shape
    tile_len, text_pad = tokens // images, text_kv.shape[3] // images
    block = math.gcd(heads, 4)
    wide = pl.BlockSpec((block, head_dim, tile_len), lambda i, h: (h, 0, i))
    row = pl.BlockSpec((block, 1, tile_len), lambda i, h: (h, 0, i))
    text = pl.BlockSpec((2, block, head_dim, text_pad), lambda i, h: (0, h, 0, i))
    text_out = pl.BlockSpec((block, head_dim, text_pad), lambda i, h: (h, 0, i))
    return kernel_call(
        functools.partial(cross_back_body, query_scale, score_scale),
        2560 * heads * tokens * text_pad,
        16 * query.size,
        grid=(images, heads // block),
        in_specs=[wide, text, wide, wide, row, row],
        out_specs=[
            wide,
            text_out,
            text_out,
        ],
        out_shape=[
            jax.ShapeDtypeStruct(query.shape, BF16),
            jax.ShapeDtypeStruct((heads, head_dim, images * text_pad), BF16),
            jax.ShapeDtypeStruct((heads, head_dim, images * text_pad), BF16),
        ],
    )(query, text_kv, grad, att, inverse, lse)


def join_norm_body(patch_ref, skip_ref, weight_ref, gain_ref, bias_ref, z_ref, inv_ref, in_ref):
    width = skip_ref.shape[1]
    patch_feat = right_dot(patch_ref[...], weight_ref[...])
    joined = jnp.concatenate([patch_feat, skip_ref[...].astype(F32)], axis=1)
    normed, inverse = layer_norm(joined)
    z_ref[...] = normed
    inv_ref[...] = inverse
    in_ref[...] = (normed * gain_ref[...] + bias_ref[...]).astype(BF16)


def join_norm(patch_rows, skip_rows, f_patch, gain, bias):
    tokens, width = skip_rows.shape
    block = math.gcd(tokens, 256)
    rows = lambda columns: pl.BlockSpec((block, columns), lambda t: (t, 0))
    fixed = lambda shape: pl.BlockSpec(shape, lambda t: (0, 0))
    return kernel_call(
        join_norm_body,
        64 * tokens * width,
        16 * tokens * width,
        grid=(tokens // block,),
        in_specs=[
            rows(patch_rows.shape[1]),
            rows(width),
            fixed(f_patch.shape),
            fixed(gain.shape),
            fixed(bias.shape),
        ],
        out_specs=[rows(2 * width), rows(1), rows(2 * width)],
        out_shape=[
            jax.ShapeDtypeStruct((tokens, 2 * width), F32),
            jax.ShapeDtypeStruct((tokens, 1), F32),
            jax.ShapeDtypeStruct((tokens, 2 * width), BF16),
        ],
    )(patch_rows, skip_rows, f_patch, gain, bias)


def join_back_body(low_ref, weight_ref, z_ref, inv_ref, gain_ref, skip_ref, patch_ref, sums_ref):
    width = skip_ref.shape[1]
    grad, normed = right_dot(low_ref[...], weight_ref[...]), z_ref[...]

    @pl.when(pl.program_id(0) == 0)
    def _():
        sums_ref[...] = jnp.zeros_like(sums_ref)

    sums_ref[0:1] += jnp.sum(grad * normed, axis=0, keepdims=True)
    sums_ref[1:2] += jnp.sum(grad, axis=0, keepdims=True)
    back = norm_back(grad * gain_ref[...], normed, inv_ref[...])
    patch_ref[...] = back[:, :width].astype(BF16)
    skip_ref[...] = back[:, width:]


def join_back(low_rows, f_skip, normed, inverse, gain):
    tokens, width = low_rows.shape
    block = math.gcd(tokens, 256)
    rows = lambda columns: pl.BlockSpec((block, columns), lambda t: (t, 0))
    fixed = lambda shape: pl.BlockSpec(shape, lambda t: (0, 0))
    return kernel_call(
        join_back_body,
        4 * tokens * width * width,
        18 * tokens * width,
        grid=(tokens // block,),
        in_specs=[rows(width), fixed(f_skip.shape), rows(2 * width), rows(1), fixed(gain.shape)],
        out_specs=[rows(width), rows(width), fixed((2, 2 * width))],
        out_shape=[
            jax.ShapeDtypeStruct((tokens, width), F32),
            jax.ShapeDtypeStruct((tokens, width), BF16),
            jax.ShapeDtypeStruct((2, 2 * width), F32),
        ],
    )(low_rows, f_skip, normed, inverse, gain)


def gelu_and_slope(inputs):
    scale, cubic = math.sqrt(2.0 / math.pi), 0.044715
    square = inputs * inputs
    curve = jnp.tanh(scale * inputs * (1.0 + cubic * square))
    half = 0.5 * (1.0 + curve)
    bend = 0.5 * inputs * (1.0 - curve * curve) * (scale * (1.0 + 3.0 * cubic * square))
    return ((inputs * half).astype(BF16), (half + bend).astype(BF16))


def swap_tiles(values_in):
    return lax.all_to_all(values_in, TILE, split_axis=0, concat_axis=0, tiled=True)


def shift_pairs(devices, step):
    return [(at, (at + step) % devices) for at in range(devices)]


def fetch(weight):
    devices = lax.axis_size("dp")
    return [weight] + [
        lax.ppermute(weight, "dp", shift_pairs(devices, step)) for step in range(1, devices)
    ]


def widen(pieces, first=None):
    devices, me = lax.axis_size("dp"), lax.axis_index("dp")
    if first is not None:
        pieces = after(first, *pieces)
    return jnp.concatenate(
        [lax.select_n((me - at) % devices, *pieces) for at in range(devices)], axis=1
    )


def narrow_blocks(blocks, first=None):
    devices, me = lax.axis_size("dp"), lax.axis_index("dp")
    received = []
    for step in range(1, devices):
        sent = lax.select_n((me + step) % devices, *blocks)
        received.append(lax.ppermute(sent, "dp", shift_pairs(devices, step)))
    if first is not None:
        received = after(first, *received)
    total = lax.select_n(me, *blocks).astype(F32)
    for piece in received:
        total = total + piece.astype(F32)
    return total


def narrow(weight_grad, first=None):
    return narrow_blocks(jnp.split(weight_grad, lax.axis_size("dp"), axis=1), first)


def by_device(weight_grads, parts):
    devices = lax.axis_size("dp")
    split = [jnp.split(weight_grad, devices, axis=1) for weight_grad in weight_grads]
    return [jnp.concatenate(blocks, axis=parts) for blocks in zip(*split)]


def sum_tiles(part_sums):
    devices, me = lax.axis_size(TILE), lax.axis_index(TILE)
    total, step = part_sums, devices // 2
    while step > 0:
        pairs = [(at, at ^ step) for at in range(devices)]
        lower, upper = jnp.split(total, 2, axis=0)
        high = (me // step) % 2 == 1
        sent = jnp.where(high, lower, upper)
        total = jnp.where(high, upper, lower) + lax.ppermute(sent, TILE, pairs)
        step //= 2
    return total


def total_tiles(part_sum):
    devices = lax.axis_size(TILE)
    total, step = part_sum, 1
    while step < devices:
        pairs = [(at, at ^ step) for at in range(devices)]
        total = total + lax.ppermute(total, TILE, pairs)
        step *= 2
    return total


def over_tiles(weight_grad):
    return lax.optimization_barrier(
        lax.psum_scatter(weight_grad, TILE, scatter_dimension=0, tiled=True)
    )


def tiles_whole(weight):
    return lax.all_gather(weight, TILE, axis=0, tiled=True)


def after(first, *values_in):
    return lax.optimization_barrier((first, *values_in))[1:]


def dot_over(left_mat, right_mat, left_axis, right_axis):
    return lax.dot_general(
        left_mat,
        right_mat,
        (((left_axis,), (right_axis,)), ((), ())),
        preferred_element_type=F32,
    )


def local_heads(
    latent,
    skip_input,
    text_states,
    timesteps,
    image_sides,
    cotangent,
    w_patch,
    w_skip,
    w_time,
    w_shift,
    w_qkv,
    w_out,
    w_query,
    w_text,
    w_cross,
    w_up,
    w_down,
    w_final,
    norm_params,
):
    dp_devices = lax.axis_size("dp")
    grid_devices = lax.axis_size(TILE)
    col_devices = lax.axis_size("col")
    grid_at = lax.axis_index(TILE)
    row_at = lax.axis_index("row")
    col_at = lax.axis_index("col")
    images, rows_tile, cols_tile, patch_width = latent.shape
    tile_len = rows_tile * cols_tile
    row_count = images * tile_len
    out_width = cotangent.shape[3]

    part_skip = widen(fetch(w_skip))
    small = jnp.concatenate([w_patch, w_final, norm_params], axis=1)
    small_widths = (w_patch.shape[1], w_final.shape[1], norm_params.shape[1])
    cuts = (0, small_widths[0], sum(small_widths[:2]), sum(small_widths))
    early = [jnp.pad(small, ((0, 0), (0, w_shift.shape[1] - small.shape[1]))), w_time, w_shift]
    ends = (small.shape[0], small.shape[0] + w_time.shape[0])
    part_small, part_time, part_shift_w = jnp.split(
        widen(fetch(jnp.concatenate(early, axis=0))), ends, axis=0
    )
    part_small = part_small.reshape(small.shape[0], dp_devices, -1)[:, :, : small.shape[1]]
    part_small = part_small.reshape(small.shape[0], -1)
    f_small = tiles_whole(part_small).reshape(-1, dp_devices, sum(small_widths))
    f_patch, f_final, f_norms = (
        f_small[:, :, cuts[at] : cuts[at + 1]].reshape(f_small.shape[0], -1) for at in range(3)
    )
    f_skip = tiles_whole(part_skip)
    held_qkv = fetch(w_qkv)
    held_three = fetch(jnp.concatenate([w_out, w_query, w_cross], axis=1))
    held_text = fetch(w_text)
    held_up, held_down = fetch(w_up), fetch(w_down)
    model_width = skip_input.shape[3]
    head_count = HEADS
    head_dim = model_width // head_count
    text_len = text_states.shape[1]
    text_pad = -(-text_len // 128) * 128
    score_scale = head_dim ** (-0.5)
    query_scale = score_scale * LOG2E
    positions = jnp.arange(tile_len, dtype=jnp.int32)
    row_pos = row_at * rows_tile + positions // cols_tile
    col_pos = col_at * cols_tile + positions % cols_tile
    query_ok = (row_pos[None, :] < image_sides[:, None]) & (col_pos[None, :] < image_sides[:, None])
    valid = query_ok.astype(F32)
    keep_rows = query_ok.astype(F32).reshape(row_count, 1)
    tile_list = jnp.arange(grid_devices, dtype=jnp.int32)[:, None]
    key_row = tile_list // col_devices * rows_tile + (positions // cols_tile)[None, :]
    key_col = tile_list % col_devices * cols_tile + (positions % cols_tile)[None, :]
    sides = image_sides[:, None, None]
    key_ok = ((key_row[None] < sides) & (key_col[None] < sides)).astype(F32)
    flags = jnp.concatenate(
        [key_ok[:, :, None, :], jnp.zeros((images, grid_devices, 7, tile_len), F32)], axis=2
    )
    cos_row, sin_row, cos_col, sin_col = (
        jnp.transpose(table[:, 0, :]) for table in rope_tables(row_pos, col_pos, head_dim)
    )
    tables = (
        jnp.concatenate([cos_row, cos_row, cos_col, cos_col], axis=0),
        jnp.concatenate([-sin_row, sin_row, -sin_col, sin_col], axis=0),
    )
    norm_f = f_norms.astype(F32)

    embedding = time_embed(timesteps, FREQ).astype(BF16)
    freq_slice = part_time.shape[0]
    shift_slice = part_shift_w.shape[0]
    embed_cols = lax.dynamic_slice_in_dim(embedding, grid_at * freq_slice, freq_slice, 1)
    time_pre = total_tiles(plain_dot(embed_cols, part_time))
    time_float, silu_pull = jax.vjp(jax.nn.silu, time_pre)
    time_act = time_float.astype(BF16)
    act_cols = lax.dynamic_slice_in_dim(time_act, grid_at * shift_slice, shift_slice, 1)
    time_shift = total_tiles(plain_dot(act_cols, part_shift_w))

    patch_rows = latent.reshape(row_count, patch_width)
    skip_rows = skip_input.reshape(row_count, model_width)
    gain_skip = jnp.concatenate([norm_f[:, 8], norm_f[:, 10]])[None]
    bias_skip = jnp.concatenate([norm_f[:, 9], norm_f[:, 11]])[None]
    joined, joined_inv, skip_in = join_norm(patch_rows, skip_rows, f_patch, gain_skip, bias_skip)
    f_qkv = tiles_whole(widen(held_qkv, skip_in))
    part_three = widen(held_three, skip_in).reshape(-1, dp_devices, 3, w_out.shape[1])
    part_three = jnp.swapaxes(part_three, 1, 2).reshape(part_three.shape[0], -1)
    f_three = tiles_whole(part_three)
    f_out, f_query, f_cross = jnp.split(f_three, 3, axis=1)
    residual = plain_dot(skip_in, f_skip)
    first_z, first_inv = layer_norm(residual)
    first_pre = (first_z * norm_f[:, 0] + norm_f[:, 1]).reshape(
        images, tile_len, model_width
    ) + time_shift[:, None, :]
    first_in = first_pre.reshape(row_count, model_width).astype(BF16)
    part_text = widen(held_text, first_in)
    f_text = tiles_whole(part_text)
    first_rows = first_in.reshape(images, tile_len, model_width)
    own_qkv, qk_inv, tile_qkv, tile_att, tile_lse, att_rows = [], [], [], [], [], []
    for image in range(images):
        rows = first_rows[image]
        own, inverses = head_norm(
            rows,
            f_qkv,
            tables,
            valid[image : image + 1],
            grid_devices,
            head_dim,
            query_scale,
        )
        own_qkv.append(own)
        qk_inv.append(inverses)
        tile_qkv.append(swap_tiles(own))
    f_up = tiles_whole(widen(held_up, tile_qkv[0]))
    for image in range(images):
        att, lse = attend(tile_qkv[image], flags[image])
        tile_att.append(att)
        tile_lse.append(lse)
        own_att = swap_tiles(att).reshape(model_width, tile_len)
        att_rows.append(jnp.transpose(own_att))
    att_low = jnp.concatenate(att_rows, axis=0)
    residual_two = residual + plain_dot(att_low, f_out)
    f_down = tiles_whole(widen(held_down, residual_two))

    third_z, third_inv = layer_norm(residual_two)
    third_in = (third_z * norm_f[:, 2] + norm_f[:, 3]).astype(BF16)
    cross_pre = dot_over(f_query, third_in, 0, 1).reshape(head_count, head_dim, row_count)
    text_rows = jnp.pad(text_states, ((0, 0), (0, text_pad - text_len), (0, 0)))
    text_rows = text_rows.reshape(images * text_pad, -1)
    text_kv = dot_over(f_text, text_rows, 0, 1).reshape(2, head_count, head_dim, images * text_pad)
    crossed, cross_queries, cq_inv, cross_lse = cross_attend(
        cross_pre, text_kv, images, text_len, query_scale
    )
    cross_cols = crossed.reshape(model_width, row_count)
    residual_three = residual_two + left_dot(cross_cols, f_cross)
    second_z, second_inv = layer_norm(residual_three)
    second_in = (second_z * norm_f[:, 4] + norm_f[:, 5]).astype(BF16)
    up_pre = plain_dot(second_in, f_up)
    hidden_act, slope = lax.optimization_barrier(gelu_and_slope(up_pre))
    residual_four = residual_three + plain_dot(hidden_act, f_down)
    last_z, last_inv = layer_norm(residual_four)
    last_in = (last_z * norm_f[:, 6] + norm_f[:, 7]).astype(BF16)
    produced = plain_dot(last_in, f_final)
    prediction = (
        (produced * keep_rows).astype(BF16).reshape(images, rows_tile, cols_tile, out_width)
    )

    grad_out = (cotangent.reshape(row_count, out_width).astype(F32) * keep_rows).astype(BF16)
    d_final = left_dot(last_in, grad_out)
    grad_last = right_dot(grad_out, f_final)
    gain_final = jnp.sum(grad_last * last_z, axis=0)
    bias_final = jnp.sum(grad_last, axis=0)
    grad_four = norm_back(grad_last * norm_f[:, 6], last_z, last_inv)
    low_four = grad_four.astype(BF16)
    d_down = left_dot(hidden_act, low_four).astype(BF16)
    d_down, low_four = lax.optimization_barrier((d_down, low_four))
    t_down = over_tiles(d_down)
    grad_hidden = right_dot(low_four, f_down)
    grad_up = (grad_hidden * slope).astype(BF16)
    d_up = left_dot(second_in, grad_up).astype(BF16)
    d_up, grad_up = lax.optimization_barrier((d_up, grad_up))
    t_up = over_tiles(d_up)
    grad_second = right_dot(grad_up, f_up)
    gain_second = jnp.sum(grad_second * second_z, axis=0)
    bias_second = jnp.sum(grad_second, axis=0)
    grad_three = grad_four + norm_back(grad_second * norm_f[:, 4], second_z, second_inv)
    low_three = grad_three.astype(BF16)
    d_cross = plain_dot(cross_cols, low_three).astype(BF16)
    grad_crossed = dot_over(f_cross, low_three, 1, 1).astype(BF16)
    t_down, grad_crossed = lax.optimization_barrier((t_down, grad_crossed))
    grad_cross_q, d_text_key, d_text_value = cross_back(
        cross_queries,
        text_kv,
        grad_crossed.reshape(head_count, head_dim, row_count),
        crossed,
        cq_inv,
        cross_lse,
        images,
        query_scale,
        score_scale,
    )
    grad_cross_q = grad_cross_q.reshape(model_width, row_count)
    d_query = dot_over(third_in, grad_cross_q, 0, 1).astype(BF16)
    grad_third = dot_over(grad_cross_q, f_query, 0, 1)
    gain_third = jnp.sum(grad_third * third_z, axis=0)
    bias_third = jnp.sum(grad_third, axis=0)
    grad_two = grad_three + norm_back(grad_third * norm_f[:, 2], third_z, third_inv)
    low_two = grad_two.astype(BF16)
    low_two_rows = low_two.reshape(images, tile_len, model_width)
    tile_grads = []
    for image in range(images):
        grad_att = dot_over(f_out, low_two_rows[image], 1, 1).astype(BF16)
        tile_grads.append(swap_tiles(grad_att.reshape(tile_att[image].shape)))
    d_out = left_dot(att_low, low_two).astype(BF16)
    d_joint = jnp.concatenate(
        [
            d_out,
            d_query,
            d_cross,
            d_text_key.reshape(model_width, -1),
            d_text_value.reshape(model_width, -1),
        ],
        axis=1,
    )
    d_joint = with_layout_constraint(d_joint, Layout(major_to_minor=(0, 1)))
    d_joint, tile_grads[0] = lax.optimization_barrier((d_joint, tile_grads[0]))
    t_joint = over_tiles(d_joint)
    own_grads, grad_qkv, tile_back = [], None, None
    for image in range(images):
        if tile_back is not None:
            down_grad = narrow(t_down, tile_back)
            down_grad, tile_grads[image], tile_back = lax.optimization_barrier(
                (down_grad, tile_grads[image], tile_back)
            )
            own_grads.append(swap_tiles(tile_back))
        tile_back = attend_back(
            tile_qkv[image], tile_grads[image], tile_att[image], tile_lse[image], score_scale
        )
    own_grads.append(swap_tiles(tile_back))
    for image in range(images):
        if image == images - 1:
            up_grad = narrow(t_up, tile_back)
            t_joint, up_grad, own_grads[-1], grad_qkv = lax.optimization_barrier(
                (t_joint, up_grad, own_grads[-1], grad_qkv)
            )
        grad_qkv = head_back(
            own_grads[image],
            own_qkv[image],
            qk_inv[image],
            tables,
            valid[image : image + 1],
            query_scale,
            image,
            images,
            grad_qkv,
        )
    sum_text_kv = t_joint[:, 3 * model_width :].astype(F32)
    sum_text_kv = jnp.transpose(
        sum_text_kv.reshape(-1, head_dim, 2, images * text_pad), (2, 0, 1, 3)
    )
    group_heads = head_count // grid_devices
    own_key = lax.dynamic_slice_in_dim(text_kv[0], grid_at * group_heads, group_heads, 0)
    ck_z, ck_inv = layer_norm(jnp.swapaxes(own_key, 1, 2))
    grad_ckey = jnp.swapaxes(norm_back(jnp.swapaxes(sum_text_kv[0], 1, 2), ck_z, ck_inv), 1, 2)
    grad_kv = tiles_whole(jnp.stack([grad_ckey, sum_text_kv[1]]).astype(BF16)[None])
    grad_kv, grad_qkv = lax.optimization_barrier((grad_kv, grad_qkv))
    grad_qkv = grad_qkv.reshape(3 * model_width, row_count)
    d_qkv = dot_over(first_in, grad_qkv, 0, 1).astype(BF16)
    d_qkv, grad_qkv = lax.optimization_barrier((d_qkv, grad_qkv))
    t_qkv = over_tiles(d_qkv)
    grad_first = dot_over(grad_qkv, f_qkv, 0, 1)
    joint_blocks = by_device(jnp.split(t_joint[:, : 3 * model_width], 3, axis=1), 1)
    joint_grad = narrow_blocks(joint_blocks, grad_first)
    gain_first = jnp.sum(grad_first * first_z, axis=0)
    bias_first = jnp.sum(grad_first, axis=0)
    part_shift = jnp.sum(grad_first.reshape(images, tile_len, model_width), axis=1)
    grad_one = grad_two + norm_back(grad_first * norm_f[:, 0], first_z, first_inv)

    low_one = grad_one.astype(BF16)
    d_skip_w = left_dot(skip_in, low_one).astype(BF16)
    d_skip_w, low_one = lax.optimization_barrier((d_skip_w, low_one))
    skip_grad, grad_patch, skip_sums = join_back(low_one, f_skip, joined, joined_inv, gain_skip)
    t_qkv, d_skip_w, joint_grad, skip_sums = lax.optimization_barrier(
        (t_qkv, d_skip_w, joint_grad, skip_sums)
    )
    out_grad, query_w_grad, cross_grad = jnp.split(joint_grad, 3, axis=1)
    t_skip = over_tiles(d_skip_w)

    grad_kv = jnp.transpose(grad_kv, (1, 0, 2, 3, 4)).reshape(2 * model_width, images * text_pad)
    text_slice = text_states.shape[2] // grid_devices
    text_cols = lax.dynamic_slice_in_dim(text_rows, grid_at * text_slice, text_slice, 1)
    d_text = dot_over(text_cols, grad_kv, 0, 1).astype(BF16)
    text_grad = dot_over(grad_kv, part_text, 0, 1).reshape(images, text_pad, text_slice)
    text_grad = text_grad[:, :text_len]

    shift_low = total_tiles(part_shift).astype(BF16)
    d_shift = left_dot(act_cols, shift_low).astype(BF16)
    grad_time_act = total_tiles(
        lax.dynamic_update_slice_in_dim(
            jnp.zeros_like(time_pre), right_dot(shift_low, part_shift_w), grid_at * shift_slice, 1
        )
    )
    grad_time_pre = silu_pull(grad_time_act)[0].astype(BF16)
    d_time = left_dot(embed_cols, grad_time_pre).astype(BF16)
    late, width = [], w_shift.shape[1]
    for at in range(dp_devices):
        pair = d_text[:, 2 * at * width : 2 * (at + 1) * width]
        own = slice(at * width, (at + 1) * width)
        late.append(
            jnp.concatenate([pair[:, :width], pair[:, width:], d_time[:, own], d_shift[:, own]])
        )
    late = narrow_blocks(late)
    qkv_grad = narrow(t_qkv, late)
    rows = d_text.shape[0]
    text_w_grad = jnp.concatenate([late[:rows], late[rows : 2 * rows]], axis=1)
    time_w_grad, shift_w_grad = jnp.split(late[2 * rows :], [d_time.shape[0]], axis=0)

    skip_grad = skip_grad.reshape(images, rows_tile, cols_tile, model_width)
    gain_skips, bias_skips = skip_sums[0], skip_sums[1]
    d_patch = left_dot(grad_patch, patch_rows)
    latent_grad = plain_dot(grad_patch, f_patch).reshape(images, rows_tile, cols_tile, patch_width)
    d_norms = jnp.stack(
        [
            gain_first,
            bias_first,
            gain_third,
            bias_third,
            gain_second,
            bias_second,
            gain_final,
            bias_final,
            gain_skips[:model_width],
            bias_skips[:model_width],
            gain_skips[model_width:],
            bias_skips[model_width:],
        ],
        axis=1,
    )
    small_grads = jnp.concatenate(
        [
            grad.reshape(model_width, dp_devices, -1)
            for grad in (d_patch, d_final, d_norms)
        ],
        axis=2,
    )
    small_grads = narrow(sum_tiles(small_grads.reshape(model_width, -1)))
    skip_w_grad = narrow(t_skip)
    patch_grad, final_grad, norms_grad = (
        small_grads[:, cuts[at] : cuts[at + 1]] for at in range(3)
    )
    return (
        prediction,
        latent_grad,
        skip_grad,
        text_grad,
        patch_grad,
        skip_w_grad,
        time_w_grad,
        shift_w_grad,
        qkv_grad,
        out_grad,
        query_w_grad,
        text_w_grad,
        cross_grad,
        up_grad,
        down_grad,
        final_grad,
        norms_grad,
    )


def local(sizes, latent, *others):
    grid_devices = sizes["row"] * sizes["col"]
    tile_len = latent.shape[1] * latent.shape[2]
    if HEADS % grid_devices == 0 and tile_len % 128 == 0:
        return local_heads(latent, *others)
    return local_gathered(latent, *others)


def solution(mesh):
    return jax.shard_map(
        functools.partial(local, mesh.shape),
        mesh=mesh,
        in_specs=(
            P("dp", "row", "col", None),
            P("dp", "row", "col", None),
            P("dp", None, None),
            P("dp"),
            P("dp"),
            P("dp", "row", "col", None),
            P(("row", "col"), "dp"),
            P(("row", "col"), "dp"),
            P(("row", "col"), "dp"),
            P(("row", "col"), "dp"),
            P(("row", "col"), "dp"),
            P(("row", "col"), "dp"),
            P(("row", "col"), "dp"),
            P(("row", "col"), "dp"),
            P(("row", "col"), "dp"),
            P(("row", "col"), "dp"),
            P(("row", "col"), "dp"),
            P(("row", "col"), "dp"),
            P(("row", "col"), "dp"),
        ),
        out_specs=(
            P("dp", "row", "col", None),
            P("dp", "row", "col", None),
            P("dp", "row", "col", None),
            P("dp", None, ("row", "col")),
            P(("row", "col"), "dp"),
            P(("row", "col"), "dp"),
            P(("row", "col"), "dp"),
            P(("row", "col"), "dp"),
            P(("row", "col"), "dp"),
            P(("row", "col"), "dp"),
            P(("row", "col"), "dp"),
            P(("row", "col"), "dp"),
            P(("row", "col"), "dp"),
            P(("row", "col"), "dp"),
            P(("row", "col"), "dp"),
            P(("row", "col"), "dp"),
            P(("row", "col"), "dp"),
        ),
        check_vma=False,
    )
```

```python
import functools
import math

import jax
import jax.numpy as jnp
from jax import lax
from jax.experimental import pallas as pl
from jax.experimental.layout import Layout, with_layout_constraint
from jax.experimental.pallas import tpu as pltpu
from jax.sharding import PartitionSpec as P

HEADS = 16
FREQ = 256


EPSILON = 1e-06


def layer_norm(values_in):
    centred = values_in - jnp.mean(values_in, axis=-1, keepdims=True)
    inverse = lax.rsqrt(jnp.mean(centred * centred, axis=-1, keepdims=True) + EPSILON)
    return (centred * inverse, inverse)


def norm_back(grad_normed, normed, inverse):
    mean_grad = jnp.mean(grad_normed, axis=-1, keepdims=True)
    mean_cross = jnp.mean(grad_normed * normed, axis=-1, keepdims=True)
    return inverse * (grad_normed - mean_grad - normed * mean_cross)


def turn_half(piece_half, cosine, sine_tab):
    quarter = cosine.shape[-1]
    lower = piece_half[..., :quarter]
    higher = piece_half[..., quarter:]
    return jnp.concatenate(
        [lower * cosine - higher * sine_tab, higher * cosine + lower * sine_tab], axis=-1
    )


def rotate(values_in, tables, signum):
    cos_row, sin_row, cos_col, sin_col = tables
    half_dim = values_in.shape[-1] // 2
    return jnp.concatenate(
        [
            turn_half(values_in[..., :half_dim], cos_row, signum * sin_row),
            turn_half(values_in[..., half_dim:], cos_col, signum * sin_col),
        ],
        axis=-1,
    )


def rope_tables(row_pos, col_pos, head_size):
    quarter = head_size // 4
    frequency = jnp.exp(jnp.arange(quarter, dtype=jnp.float32) * (-math.log(10000.0) / quarter))
    row_ang = row_pos.astype(jnp.float32)[:, None, None] * frequency
    col_ang = col_pos.astype(jnp.float32)[:, None, None] * frequency
    return (jnp.cos(row_ang), jnp.sin(row_ang), jnp.cos(col_ang), jnp.sin(col_ang))


def time_embed(step_values, freq_count):
    half_dim = freq_count // 2
    rate_list = jnp.exp(jnp.arange(half_dim, dtype=jnp.float32) * (-math.log(10000.0) / half_dim))
    angles = step_values.astype(jnp.float32)[..., None] * rate_list
    return jnp.concatenate([jnp.cos(angles), jnp.sin(angles)], axis=-1)


def gelu_tanh(inputs):
    return jax.nn.gelu(inputs, approximate=True)


def plain_dot(left_mat, right_mat):
    return jnp.dot(left_mat, right_mat, preferred_element_type=jnp.float32)


def left_dot(left_mat, right_mat):
    return lax.dot_general(
        left_mat, right_mat, (((0,), (0,)), ((), ())), preferred_element_type=jnp.float32
    )


def right_dot(left_mat, right_mat):
    return lax.dot_general(
        left_mat, right_mat, (((1,), (1,)), ((), ())), preferred_element_type=jnp.float32
    )


def block_size(key_count):
    block_len = key_count
    while block_len > 1024 and block_len % 2 == 0:
        block_len = block_len // 2
    return block_len


def local_gathered(
    latent,
    skip_input,
    text_states,
    timesteps,
    image_sides,
    cotangent,
    w_patch,
    w_skip,
    w_time,
    w_shift,
    w_qkv,
    w_out,
    w_query,
    w_text,
    w_cross,
    w_up,
    w_down,
    w_final,
    norm_params,
):
    widened = (
        lax.all_gather(w_patch, "dp", axis=1, tiled=True),
        lax.all_gather(w_skip, "dp", axis=1, tiled=True),
        lax.all_gather(w_time, "dp", axis=1, tiled=True),
        lax.all_gather(w_shift, "dp", axis=1, tiled=True),
        lax.all_gather(w_qkv, "dp", axis=1, tiled=True),
        lax.all_gather(w_out, "dp", axis=1, tiled=True),
        lax.all_gather(w_query, "dp", axis=1, tiled=True),
        lax.all_gather(w_text, "dp", axis=1, tiled=True),
        lax.all_gather(w_cross, "dp", axis=1, tiled=True),
        lax.all_gather(w_up, "dp", axis=1, tiled=True),
        lax.all_gather(w_down, "dp", axis=1, tiled=True),
        lax.all_gather(w_final, "dp", axis=1, tiled=True),
        lax.all_gather(norm_params, "dp", axis=1, tiled=True),
    )
    gathered = (
        lax.all_gather(widened[0], ("row", "col"), axis=0, tiled=True),
        lax.all_gather(widened[1], ("row", "col"), axis=0, tiled=True),
        lax.all_gather(widened[2], ("row", "col"), axis=0, tiled=True),
        lax.all_gather(widened[3], ("row", "col"), axis=0, tiled=True),
        lax.all_gather(widened[4], ("row", "col"), axis=0, tiled=True),
        lax.all_gather(widened[5], ("row", "col"), axis=0, tiled=True),
        lax.all_gather(widened[6], ("row", "col"), axis=0, tiled=True),
        lax.all_gather(widened[7], ("row", "col"), axis=0, tiled=True),
        lax.all_gather(widened[8], ("row", "col"), axis=0, tiled=True),
        lax.all_gather(widened[9], ("row", "col"), axis=0, tiled=True),
        lax.all_gather(widened[10], ("row", "col"), axis=0, tiled=True),
        lax.all_gather(widened[11], ("row", "col"), axis=0, tiled=True),
        lax.all_gather(widened[12], ("row", "col"), axis=0, tiled=True),
    )
    (
        f_patch,
        f_skip,
        f_time,
        f_shift,
        f_qkv,
        f_out,
        f_query,
        f_text,
        f_cross,
        f_up,
        f_down,
        f_final,
        f_norms,
    ) = gathered
    part_text = widened[7]
    images, rows_tile, cols_tile, patch_width = latent.shape
    tile_len = rows_tile * cols_tile
    row_count = images * tile_len
    model_width = f_qkv.shape[0]
    head_count = HEADS
    head_dim = model_width // head_count
    text_len = text_states.shape[1]
    grid_devices = lax.axis_size(("row", "col"))
    col_devices = lax.axis_size("col")
    grid_at = lax.axis_index(("row", "col"))
    row_at = lax.axis_index("row")
    col_at = lax.axis_index("col")
    score_scale = head_dim ** (-0.5)
    positions = jnp.arange(tile_len, dtype=jnp.int32)
    row_pos = row_at * rows_tile + positions // cols_tile
    col_pos = col_at * cols_tile + positions % cols_tile
    query_ok = (row_pos[None, :] < image_sides[:, None]) & (col_pos[None, :] < image_sides[:, None])
    keep_rows = query_ok.astype(jnp.float32).reshape(row_count, 1)
    tables = rope_tables(row_pos, col_pos, head_dim)
    norm_f = f_norms.astype(jnp.float32)

    def valid_keys(offset, block_len):
        index_list = offset + jnp.arange(block_len, dtype=jnp.int32)
        source = index_list // tile_len
        within = index_list % tile_len
        key_row = source // col_devices * rows_tile + within // cols_tile
        key_col = source % col_devices * cols_tile + within % cols_tile
        return (key_row[None, :] < image_sides[:, None]) & (key_col[None, :] < image_sides[:, None])

    patch_rows = latent.reshape(row_count, patch_width)
    patch_feat = right_dot(patch_rows, f_patch)
    skip_rows = skip_input.reshape(row_count, model_width).astype(jnp.float32)
    gain_skip = jnp.concatenate([norm_f[:, 8], norm_f[:, 10]])
    bias_skip = jnp.concatenate([norm_f[:, 9], norm_f[:, 11]])
    joined, joined_inv = layer_norm(jnp.concatenate([patch_feat, skip_rows], axis=-1))
    skip_in = (joined * gain_skip + bias_skip).astype(jnp.bfloat16)
    residual = plain_dot(skip_in, f_skip)
    embedding = time_embed(timesteps, FREQ).astype(jnp.bfloat16)
    time_pre = plain_dot(embedding, f_time)
    time_float, silu_pull = jax.vjp(jax.nn.silu, time_pre)
    time_act = time_float.astype(jnp.bfloat16)
    time_shift = plain_dot(time_act, f_shift)
    first_z, first_inv = layer_norm(residual)
    first_pre = (first_z * norm_f[:, 0] + norm_f[:, 1]).reshape(
        images, tile_len, model_width
    ) + time_shift[:, None, :]
    first_in = first_pre.reshape(row_count, model_width).astype(jnp.bfloat16)
    qkv = plain_dot(first_in, f_qkv)
    query_z, query_inv = layer_norm(
        qkv[:, :model_width].reshape(images, tile_len, head_count, head_dim)
    )
    key_z, key_inv = layer_norm(
        qkv[:, model_width : 2 * model_width].reshape(images, tile_len, head_count, head_dim)
    )
    queries = rotate(query_z, tables, 1.0).astype(jnp.bfloat16)
    queries_h = jnp.transpose(queries, (0, 2, 1, 3))
    keys = rotate(key_z, tables, 1.0).astype(jnp.bfloat16).reshape(images, tile_len, model_width)
    values = qkv[:, 2 * model_width :].astype(jnp.bfloat16).reshape(images, tile_len, model_width)
    start_carry = (
        jnp.full((images, head_count, tile_len), -1e30, jnp.float32),
        jnp.zeros((images, head_count, tile_len), jnp.float32),
        jnp.zeros((images, head_count, tile_len, head_dim), jnp.float32),
    )
    key_rows = lax.all_gather(keys, ("row", "col"), axis=1, tiled=True)
    value_rows = lax.all_gather(values, ("row", "col"), axis=1, tiled=True)
    key_count = key_rows.shape[1]
    block_len = block_size(key_count)

    def forward_block_step(block_index, running):
        running_max, weight_sum, accum_sum = running
        offset = block_index * block_len
        key_blk = lax.dynamic_slice_in_dim(key_rows, offset, block_len, 1).reshape(
            images, block_len, head_count, head_dim
        )
        value_blk = lax.dynamic_slice_in_dim(value_rows, offset, block_len, 1).reshape(
            images, block_len, head_count, head_dim
        )
        key_ok = valid_keys(offset, block_len)
        scores = (
            jnp.einsum("ihqe,ikhe->ihqk", queries_h, key_blk, preferred_element_type=jnp.float32)
            * score_scale
        )
        scores = jnp.where(key_ok[:, None, None, :], scores, -jnp.inf)
        new_max = jnp.maximum(running_max, jnp.max(scores, axis=-1))
        weight = jnp.exp(scores - new_max[..., None])
        rescale = jnp.exp(running_max - new_max)
        weight_sum = weight_sum * rescale + jnp.sum(weight, axis=-1)
        accum_sum = accum_sum * rescale[..., None] + jnp.einsum(
            "ihqk,ikhe->ihqe",
            weight.astype(jnp.bfloat16),
            value_blk,
            preferred_element_type=jnp.float32,
        )
        return (new_max, weight_sum, accum_sum)

    running_max, weight_sum, accum_sum = lax.fori_loop(
        0, key_count // block_len, forward_block_step, start_carry
    )
    attended = accum_sum / weight_sum[..., None]
    log_sum = running_max + jnp.log(weight_sum)
    att_low = (
        jnp.transpose(attended, (0, 2, 1, 3)).reshape(row_count, model_width).astype(jnp.bfloat16)
    )
    residual_two = residual + plain_dot(att_low, f_out)
    third_z, third_inv = layer_norm(residual_two)
    third_in = (third_z * norm_f[:, 2] + norm_f[:, 3]).astype(jnp.bfloat16)
    cross_pre = plain_dot(third_in, f_query)
    cq_z, cq_inv = layer_norm(cross_pre.reshape(images, tile_len, head_count, head_dim))
    cross_queries = cq_z.astype(jnp.bfloat16)
    text_kv = jnp.einsum("itc,cd->itd", text_states, f_text, preferred_element_type=jnp.float32)
    ck_z, ck_inv = layer_norm(
        text_kv[..., :model_width].reshape(images, text_len, head_count, head_dim)
    )
    cross_keys = ck_z.astype(jnp.bfloat16)
    cross_values = (
        text_kv[..., model_width:]
        .astype(jnp.bfloat16)
        .reshape(images, text_len, head_count, head_dim)
    )

    def cross_softmax():
        scores = (
            jnp.einsum(
                "iqhe,ikhe->ihqk", cross_queries, cross_keys, preferred_element_type=jnp.float32
            )
            * score_scale
        )
        return jax.nn.softmax(scores, axis=-1)

    crossed = jnp.einsum(
        "ihqk,ikhe->iqhe",
        cross_softmax().astype(jnp.bfloat16),
        cross_values,
        preferred_element_type=jnp.float32,
    )
    cross_low = crossed.reshape(row_count, model_width).astype(jnp.bfloat16)
    residual_three = residual_two + plain_dot(cross_low, f_cross)
    second_z, second_inv = layer_norm(residual_three)
    second_in = (second_z * norm_f[:, 4] + norm_f[:, 5]).astype(jnp.bfloat16)
    up_pre = plain_dot(second_in, f_up)
    hidden_float, gelu_pull = jax.vjp(gelu_tanh, up_pre)
    hidden_act = hidden_float.astype(jnp.bfloat16)
    residual_four = residual_three + plain_dot(hidden_act, f_down)
    last_z, last_inv = layer_norm(residual_four)
    last_in = (last_z * norm_f[:, 6] + norm_f[:, 7]).astype(jnp.bfloat16)
    produced = plain_dot(last_in, f_final)
    prediction = (
        (produced * keep_rows)
        .astype(jnp.bfloat16)
        .reshape(images, rows_tile, cols_tile, produced.shape[1])
    )
    grad_out = (
        cotangent.reshape(row_count, produced.shape[1]).astype(jnp.float32) * keep_rows
    ).astype(jnp.bfloat16)
    d_final = left_dot(last_in, grad_out)
    grad_last = right_dot(grad_out, f_final)
    gain_final = jnp.sum(grad_last * last_z, axis=0)
    bias_final = jnp.sum(grad_last, axis=0)
    grad_four = norm_back(grad_last * norm_f[:, 6], last_z, last_inv)
    low_four = grad_four.astype(jnp.bfloat16)
    d_down = left_dot(hidden_act, low_four)
    grad_hidden = right_dot(low_four, f_down)
    grad_up = gelu_pull(grad_hidden)[0].astype(jnp.bfloat16)
    d_up = left_dot(second_in, grad_up)
    grad_second = right_dot(grad_up, f_up)
    gain_second = jnp.sum(grad_second * second_z, axis=0)
    bias_second = jnp.sum(grad_second, axis=0)
    grad_three = grad_four + norm_back(grad_second * norm_f[:, 4], second_z, second_inv)
    low_three = grad_three.astype(jnp.bfloat16)
    d_cross = left_dot(cross_low, low_three)
    grad_crossed = (
        right_dot(low_three, f_cross)
        .astype(jnp.bfloat16)
        .reshape(images, tile_len, head_count, head_dim)
    )
    cross_probs = cross_softmax()
    cross_delta = jnp.transpose(
        jnp.sum(grad_crossed.astype(jnp.float32) * crossed, axis=-1), (0, 2, 1)
    )
    grad_probs = jnp.einsum(
        "iqhe,ikhe->ihqk", grad_crossed, cross_values, preferred_element_type=jnp.float32
    )
    grad_cscore = (cross_probs * (grad_probs - cross_delta[..., None])).astype(jnp.bfloat16)
    grad_cq = score_scale * jnp.einsum(
        "ihqk,ikhe->iqhe", grad_cscore, cross_keys, preferred_element_type=jnp.float32
    )
    part_ckey = score_scale * jnp.einsum(
        "ihqk,iqhe->ikhe", grad_cscore, cross_queries, preferred_element_type=jnp.float32
    )
    part_cvalue = jnp.einsum(
        "ihqk,iqhe->ikhe",
        cross_probs.astype(jnp.bfloat16),
        grad_crossed,
        preferred_element_type=jnp.float32,
    )
    grad_cross_q = (
        norm_back(grad_cq, cq_z, cq_inv).reshape(row_count, model_width).astype(jnp.bfloat16)
    )
    d_query = left_dot(third_in, grad_cross_q)
    grad_third = right_dot(grad_cross_q, f_query)
    gain_third = jnp.sum(grad_third * third_z, axis=0)
    bias_third = jnp.sum(grad_third, axis=0)
    grad_two = grad_three + norm_back(grad_third * norm_f[:, 2], third_z, third_inv)
    sum_ckey, sum_cvalue = lax.psum((part_ckey, part_cvalue), ("row", "col"))
    low_two = grad_two.astype(jnp.bfloat16)
    d_out = left_dot(att_low, low_two)
    grad_att = (
        right_dot(low_two, f_out)
        .astype(jnp.bfloat16)
        .reshape(images, tile_len, head_count, head_dim)
    )
    grad_att_h = jnp.transpose(grad_att, (0, 2, 1, 3))
    delta_rows = jnp.sum(grad_att_h.astype(jnp.float32) * attended, axis=-1)
    back_carry = (
        jnp.zeros((images, head_count, tile_len, head_dim), jnp.float32),
        jnp.zeros((images, tile_len * grid_devices, model_width), jnp.float32),
        jnp.zeros((images, tile_len * grid_devices, model_width), jnp.float32),
    )
    backward_key_rows = lax.all_gather(keys, ("row", "col"), axis=1, tiled=True)
    backward_value_rows = lax.all_gather(values, ("row", "col"), axis=1, tiled=True)
    key_count = backward_key_rows.shape[1]
    backward_block_len = block_size(key_count)

    def backward_block_step(block_index, running):
        grad_query, grad_key_all, grad_value_all = running
        offset = block_index * backward_block_len
        key_blk = lax.dynamic_slice_in_dim(
            backward_key_rows, offset, backward_block_len, 1
        ).reshape(images, backward_block_len, head_count, head_dim)
        value_blk = lax.dynamic_slice_in_dim(
            backward_value_rows, offset, backward_block_len, 1
        ).reshape(images, backward_block_len, head_count, head_dim)
        key_ok = valid_keys(offset, backward_block_len)
        scores = (
            jnp.einsum("ihqe,ikhe->ihqk", queries_h, key_blk, preferred_element_type=jnp.float32)
            * score_scale
        )
        scores = jnp.where(key_ok[:, None, None, :], scores, -jnp.inf)
        attn_probs = jnp.exp(scores - log_sum[..., None])
        grad_prob = jnp.einsum(
            "ihqe,ikhe->ihqk", grad_att_h, value_blk, preferred_element_type=jnp.float32
        )
        grad_score = (attn_probs * (grad_prob - delta_rows[..., None])).astype(jnp.bfloat16)
        grad_query = grad_query + score_scale * jnp.einsum(
            "ihqk,ikhe->ihqe", grad_score, key_blk, preferred_element_type=jnp.float32
        )
        key_part = score_scale * jnp.einsum(
            "ihqk,ihqe->ikhe", grad_score, queries_h, preferred_element_type=jnp.float32
        )
        value_part = jnp.einsum(
            "ihqk,ihqe->ikhe",
            attn_probs.astype(jnp.bfloat16),
            grad_att_h,
            preferred_element_type=jnp.float32,
        )
        grad_key_all = lax.dynamic_update_slice_in_dim(
            grad_key_all, key_part.reshape(images, backward_block_len, model_width), offset, 1
        )
        grad_value_all = lax.dynamic_update_slice_in_dim(
            grad_value_all, value_part.reshape(images, backward_block_len, model_width), offset, 1
        )
        return (grad_query, grad_key_all, grad_value_all)

    grad_query, grad_key_all, grad_value_all = lax.fori_loop(
        0, key_count // backward_block_len, backward_block_step, back_carry
    )
    grad_key_own, grad_value_own = (
        lax.psum_scatter(grad_key_all, ("row", "col"), scatter_dimension=1, tiled=True),
        lax.psum_scatter(grad_value_all, ("row", "col"), scatter_dimension=1, tiled=True),
    )
    grad_qn = rotate(jnp.transpose(grad_query, (0, 2, 1, 3)), tables, -1.0)
    grad_kn = rotate(grad_key_own.reshape(images, tile_len, head_count, head_dim), tables, -1.0)
    grad_qkv = jnp.concatenate(
        [
            norm_back(grad_qn, query_z, query_inv).reshape(row_count, model_width),
            norm_back(grad_kn, key_z, key_inv).reshape(row_count, model_width),
            grad_value_own.reshape(row_count, model_width),
        ],
        axis=-1,
    ).astype(jnp.bfloat16)
    d_qkv = left_dot(first_in, grad_qkv)
    grad_first = right_dot(grad_qkv, f_qkv)
    gain_first = jnp.sum(grad_first * first_z, axis=0)
    bias_first = jnp.sum(grad_first, axis=0)
    part_shift = jnp.sum(grad_first.reshape(images, tile_len, model_width), axis=1)
    grad_one = grad_two + norm_back(grad_first * norm_f[:, 0], first_z, first_inv)
    shift_grad = lax.psum(part_shift, ("row", "col"))
    grad_ckey = norm_back(sum_ckey, ck_z, ck_inv).reshape(images, text_len, model_width)
    grad_kv = jnp.concatenate(
        [grad_ckey, sum_cvalue.reshape(images, text_len, model_width)], axis=-1
    ).astype(jnp.bfloat16)
    text_slice = text_states.shape[2] // grid_devices
    text_cols = lax.dynamic_slice_in_dim(text_states, grid_at * text_slice, text_slice, 2)
    d_text_w = jnp.einsum("itc,itd->cd", text_cols, grad_kv, preferred_element_type=jnp.float32)
    text_grad = jnp.einsum("itd,cd->itc", grad_kv, part_text, preferred_element_type=jnp.float32)
    shift_low = shift_grad.astype(jnp.bfloat16)
    shift_slice = model_width // grid_devices
    act_cols = lax.dynamic_slice_in_dim(time_act, grid_at * shift_slice, shift_slice, 1)
    d_shift_w = jnp.einsum("ic,id->cd", act_cols, shift_low, preferred_element_type=jnp.float32)
    grad_time_act = right_dot(shift_low, f_shift)
    grad_time_pre = silu_pull(grad_time_act)[0].astype(jnp.bfloat16)
    freq_slice = embedding.shape[1] // grid_devices
    embed_cols = lax.dynamic_slice_in_dim(embedding, grid_at * freq_slice, freq_slice, 1)
    d_time_w = jnp.einsum(
        "ic,id->cd", embed_cols, grad_time_pre, preferred_element_type=jnp.float32
    )
    low_one = grad_one.astype(jnp.bfloat16)
    d_skip_w = left_dot(skip_in, low_one)
    grad_skip_in = right_dot(low_one, f_skip)
    gain_skips = jnp.sum(grad_skip_in * joined, axis=0)
    bias_skips = jnp.sum(grad_skip_in, axis=0)
    grad_joined = norm_back(grad_skip_in * gain_skip, joined, joined_inv)
    skip_grad = grad_joined[:, model_width:].reshape(images, rows_tile, cols_tile, model_width)
    grad_patch = grad_joined[:, :model_width].astype(jnp.bfloat16)
    d_patch = left_dot(grad_patch, patch_rows)
    latent_grad = plain_dot(grad_patch, f_patch).reshape(images, rows_tile, cols_tile, patch_width)
    d_norms = jnp.stack(
        [
            gain_first,
            bias_first,
            gain_third,
            bias_third,
            gain_second,
            bias_second,
            gain_final,
            bias_final,
            gain_skips[:model_width],
            bias_skips[:model_width],
            gain_skips[model_width:],
            bias_skips[model_width:],
        ],
        axis=1,
    )
    tile_done = (
        lax.psum_scatter(d_patch, ("row", "col"), scatter_dimension=0, tiled=True),
        lax.psum_scatter(d_skip_w, ("row", "col"), scatter_dimension=0, tiled=True),
        lax.psum_scatter(d_qkv, ("row", "col"), scatter_dimension=0, tiled=True),
        lax.psum_scatter(d_out, ("row", "col"), scatter_dimension=0, tiled=True),
        lax.psum_scatter(d_query, ("row", "col"), scatter_dimension=0, tiled=True),
        lax.psum_scatter(d_cross, ("row", "col"), scatter_dimension=0, tiled=True),
        lax.psum_scatter(d_up, ("row", "col"), scatter_dimension=0, tiled=True),
        lax.psum_scatter(d_down, ("row", "col"), scatter_dimension=0, tiled=True),
        lax.psum_scatter(d_final, ("row", "col"), scatter_dimension=0, tiled=True),
        lax.psum_scatter(d_norms, ("row", "col"), scatter_dimension=0, tiled=True),
    )
    reduced = (
        lax.psum_scatter(
            tile_done[0].astype(jnp.bfloat16), "dp", scatter_dimension=1, tiled=True
        ).astype(jnp.float32),
        lax.psum_scatter(
            tile_done[1].astype(jnp.bfloat16), "dp", scatter_dimension=1, tiled=True
        ).astype(jnp.float32),
        lax.psum_scatter(
            tile_done[2].astype(jnp.bfloat16), "dp", scatter_dimension=1, tiled=True
        ).astype(jnp.float32),
        lax.psum_scatter(
            tile_done[3].astype(jnp.bfloat16), "dp", scatter_dimension=1, tiled=True
        ).astype(jnp.float32),
        lax.psum_scatter(
            tile_done[4].astype(jnp.bfloat16), "dp", scatter_dimension=1, tiled=True
        ).astype(jnp.float32),
        lax.psum_scatter(
            tile_done[5].astype(jnp.bfloat16), "dp", scatter_dimension=1, tiled=True
        ).astype(jnp.float32),
        lax.psum_scatter(
            tile_done[6].astype(jnp.bfloat16), "dp", scatter_dimension=1, tiled=True
        ).astype(jnp.float32),
        lax.psum_scatter(
            tile_done[7].astype(jnp.bfloat16), "dp", scatter_dimension=1, tiled=True
        ).astype(jnp.float32),
        lax.psum_scatter(
            tile_done[8].astype(jnp.bfloat16), "dp", scatter_dimension=1, tiled=True
        ).astype(jnp.float32),
        lax.psum_scatter(
            tile_done[9].astype(jnp.bfloat16), "dp", scatter_dimension=1, tiled=True
        ).astype(jnp.float32),
        lax.psum_scatter(
            d_time_w.astype(jnp.bfloat16), "dp", scatter_dimension=1, tiled=True
        ).astype(jnp.float32),
        lax.psum_scatter(
            d_shift_w.astype(jnp.bfloat16), "dp", scatter_dimension=1, tiled=True
        ).astype(jnp.float32),
        lax.psum_scatter(
            d_text_w.astype(jnp.bfloat16), "dp", scatter_dimension=1, tiled=True
        ).astype(jnp.float32),
    )
    return (
        prediction,
        latent_grad,
        skip_grad,
        text_grad,
        reduced[0],
        reduced[1],
        reduced[10],
        reduced[11],
        reduced[2],
        reduced[3],
        reduced[4],
        reduced[12],
        reduced[5],
        reduced[6],
        reduced[7],
        reduced[8],
        reduced[9],
    )


TILE = ("row", "col")
EVERY = ("dp", "row", "col")
LOG2E = math.log2(math.e)
F32 = jnp.float32
BF16 = jnp.bfloat16
VMEM_BYTES = 56 * 2**20


def kernel_call(body, flops, moved, **options):
    return pl.pallas_call(
        body,
        compiler_params=pltpu.CompilerParams(vmem_limit_bytes=VMEM_BYTES),
        cost_estimate=pl.CostEstimate(flops=flops, bytes_accessed=moved, transcendentals=0),
        **options,
    )


def pair_swap(values_in):
    quarter = values_in.shape[0] // 4
    parts = [values_in[at * quarter : (at + 1) * quarter] for at in (1, 0, 3, 2)]
    return jnp.concatenate(parts, axis=0)


def column_norm(values_in):
    centred = values_in - jnp.mean(values_in, axis=0, keepdims=True)
    inverse = lax.rsqrt(jnp.mean(centred * centred, axis=0, keepdims=True) + EPSILON)
    return (centred * inverse, inverse)


def column_norm_back(grad_normed, normed, inverse):
    mean_grad = jnp.mean(grad_normed, axis=0, keepdims=True)
    mean_cross = jnp.mean(grad_normed * normed, axis=0, keepdims=True)
    return inverse * (grad_normed - mean_grad - normed * mean_cross)


def minus_pieces(row_values):
    high = row_values.astype(BF16).astype(F32)
    rest = row_values - high
    middle = rest.astype(BF16).astype(F32)
    lower = rest - middle
    at = lax.broadcasted_iota(jnp.int32, (8, row_values.shape[1]), 0)
    zero = jnp.zeros((8, row_values.shape[1]), F32)
    picked = jnp.where(at == 0, high, jnp.where(at == 1, middle, jnp.where(at == 2, lower, zero)))
    return -picked


def piece_flags(width):
    return (lax.broadcasted_iota(jnp.int32, (8, width), 0) < 3).astype(F32)


def head_norm_body(
    query_scale, rows_ref, weight_ref, cos_ref, sin_ref, ok_ref, out_ref, inv_ref
):
    groups, _, heads, head_dim, _ = out_ref.shape
    part = pl.program_id(0)
    made = jnp.dot(rows_ref[...], weight_ref[...], preferred_element_type=F32).T
    valid = ok_ref[...]

    @pl.when(part < 2)
    def _():
        factor = jnp.where(part == 0, query_scale, valid)
        cosine, sine = cos_ref[...] * factor, sin_ref[...] * factor
        for group in range(groups):
            for head in range(heads):
                at = (group * heads + head) * head_dim
                normed, inverse = column_norm(made[at : at + head_dim])
                turned = normed * cosine + pair_swap(normed) * sine
                out_ref[group, 0, head] = turned.astype(BF16)
                inv_ref[group, 0, head : head + 1] = inverse

    @pl.when(part == 2)
    def _():
        for group in range(groups):
            for head in range(heads):
                at = (group * heads + head) * head_dim
                out_ref[group, 0, head] = (made[at : at + head_dim] * valid).astype(BF16)
                inv_ref[group, 0, head : head + 1] = valid


def head_norm(rows, weight, tables, valid, groups, head_dim, query_scale):
    tile_len, depth = rows.shape
    width = weight.shape[1] // 3
    heads = width // groups // head_dim
    table = pl.BlockSpec((head_dim, tile_len), lambda p: (0, 0))
    return kernel_call(
        functools.partial(head_norm_body, query_scale),
        6 * tile_len * depth * width,
        6 * depth * width,
        grid=(3,),
        in_specs=[
            pl.BlockSpec((tile_len, depth), lambda p: (0, 0)),
            pl.BlockSpec((depth, width), lambda p: (0, p)),
            table,
            table,
            pl.BlockSpec((1, tile_len), lambda p: (0, 0)),
        ],
        out_specs=[
            pl.BlockSpec((groups, 1, heads, head_dim, tile_len), lambda p: (0, p, 0, 0, 0)),
            pl.BlockSpec((groups, 1, heads, tile_len), lambda p: (0, p, 0, 0)),
        ],
        out_shape=[
            jax.ShapeDtypeStruct((groups, 3, heads, head_dim, tile_len), BF16),
            jax.ShapeDtypeStruct((groups, 3, heads, tile_len), F32),
        ],
    )(rows, weight, *tables, valid)


def head_back_body(
    query_scale, grad_ref, own_ref, inv_ref, cos_ref, sin_ref, ok_ref, *others
):
    out_ref = others[-1]
    heads, head_dim = own_ref.shape[2], own_ref.shape[3]
    cosine, sine, valid = cos_ref[...], sin_ref[...], ok_ref[...]

    def unturn(values_in):
        return values_in * cosine - pair_swap(values_in) * sine

    for part in range(3):
        pieces = []
        for head in range(heads):
            grad = grad_ref[0, part, head].astype(F32)
            if part > 0:
                grad = grad * valid
            if part < 2:
                normed = unturn(own_ref[0, part, head].astype(F32))
                if part == 0:
                    normed = normed * (1.0 / query_scale)
                inverse = inv_ref[0, part, head : head + 1]
                grad = column_norm_back(unturn(grad), normed, inverse)
            pieces.append(grad)
        out_ref[part, 0] = jnp.concatenate(pieces, axis=0).astype(BF16)


def head_back(grads, own, inverses, tables, valid, query_scale, image, images, before):
    groups, _, heads, head_dim, tile_len = own.shape
    group_rows = heads * head_dim
    stacked = pl.BlockSpec((1, 3, heads, head_dim, tile_len), lambda g: (g, 0, 0, 0, 0))
    table = pl.BlockSpec((head_dim, tile_len), lambda g: (0, 0))
    earlier = () if before is None else (before,)
    return kernel_call(
        functools.partial(head_back_body, query_scale),
        0,
        6 * own.size,
        grid=(groups,),
        in_specs=[
            stacked,
            stacked,
            pl.BlockSpec((1, 3, heads, tile_len), lambda g: (g, 0, 0, 0)),
            table,
            table,
            pl.BlockSpec((1, tile_len), lambda g: (0, 0)),
        ]
        + [pl.BlockSpec(memory_space=pl.ANY)] * len(earlier),
        out_specs=pl.BlockSpec((3, 1, group_rows, tile_len), lambda g: (0, g, 0, image)),
        out_shape=jax.ShapeDtypeStruct((3, groups, group_rows, images * tile_len), BF16),
        input_output_aliases={6: 0} if earlier else {},
    )(grads, own, inverses, *tables, valid, *earlier)


def attend_body(query_ref, key_ref, value_ref, ok_ref, out_ref, lse_ref, key_nat, value_ext):
    tiles, tile_len, head_dim = key_ref.shape[0], key_ref.shape[-1], key_ref.shape[-2]

    @pl.when(pl.program_id(1) == 0)
    def _():
        for tile in range(tiles):
            key_nat[tile * tile_len : (tile + 1) * tile_len, :] = key_ref[tile, 0, 0].T
            value_ext[tile] = jnp.concatenate(
                [value_ref[tile, 0, 0].astype(F32), ok_ref[tile]], axis=0
            ).astype(BF16)

    query = query_ref[0, 0, 0]
    total = jnp.zeros((head_dim + 8, tile_len), F32)
    held = None
    for tile in range(tiles + 1):
        scores = None
        if tile < tiles:
            rows = slice(tile * tile_len, (tile + 1) * tile_len)
            scores = jnp.dot(key_nat[rows, :], query, preferred_element_type=F32)
        if held is not None:
            weight = jnp.exp2(held).astype(BF16)
            total = total + jnp.dot(value_ext[tile - 1], weight, preferred_element_type=F32)
        held = scores
    weight_sum = total[head_dim : head_dim + 1]
    out_ref[0, 0] = (total[:head_dim] / weight_sum).astype(BF16)
    lse_ref[0, 0] = jnp.log2(weight_sum)


def attend(qkv, flags):
    tiles, _, heads, head_dim, tile_len = qkv.shape
    return kernel_call(
        attend_body,
        1024 * heads * tiles**2 * tile_len**2,
        8 * qkv.size,
        grid=(heads, tiles),
        in_specs=[
            pl.BlockSpec((1, 1, 1, head_dim, tile_len), lambda h, t: (t, 0, h, 0, 0)),
            pl.BlockSpec((tiles, 1, 1, head_dim, tile_len), lambda h, t: (0, 1, h, 0, 0)),
            pl.BlockSpec((tiles, 1, 1, head_dim, tile_len), lambda h, t: (0, 2, h, 0, 0)),
            pl.BlockSpec((tiles, 8, tile_len), lambda h, t: (0, 0, 0)),
        ],
        out_specs=[
            pl.BlockSpec((1, 1, head_dim, tile_len), lambda h, t: (t, h, 0, 0)),
            pl.BlockSpec((1, 1, 1, tile_len), lambda h, t: (t, h, 0, 0)),
        ],
        out_shape=[
            jax.ShapeDtypeStruct((tiles, heads, head_dim, tile_len), BF16),
            jax.ShapeDtypeStruct((tiles, heads, 1, tile_len), F32),
        ],
        scratch_shapes=[
            pltpu.VMEM((tiles * tile_len, head_dim), BF16),
            pltpu.VMEM((tiles, head_dim + 8, tile_len), BF16),
        ],
    )(qkv, qkv, qkv, flags)


def attend_back_body(
    score_scale,
    query_ref,
    key_ref,
    value_ref,
    grad_ref,
    att_ref,
    lse_ref,
    out_ref,
    key_nat,
    value_nat,
    key_sum,
    value_sum,
):
    tiles, tile_len, head_dim = key_ref.shape[0], key_ref.shape[-1], key_ref.shape[-2]
    at = pl.program_id(1)

    @pl.when(at == 0)
    def _():
        ones = piece_flags(tile_len)
        for tile in range(tiles):
            rows = slice(tile * tile_len, (tile + 1) * tile_len)
            for source, kept in ((key_ref, key_nat), (value_ref, value_nat)):
                wide = jnp.concatenate([source[tile, 0, 0].astype(F32), ones], axis=0)
                kept[rows, :] = wide.T.astype(BF16)
        key_sum[...] = jnp.zeros_like(key_sum)
        value_sum[...] = jnp.zeros_like(value_sum)

    query = query_ref[0, 0, 0].astype(F32)
    grad = grad_ref[0, 0].astype(F32)
    delta = jnp.sum(grad * att_ref[0, 0].astype(F32), axis=0, keepdims=True)
    query_ext = jnp.concatenate([query, minus_pieces(lse_ref[0, 0])], axis=0)
    grad_ext = jnp.concatenate([grad, minus_pieces(delta)], axis=0)
    query_cols, grad_cols = query_ext.astype(BF16), grad_ext.astype(BF16)
    query_nat, grad_nat = query_ext.T.astype(BF16), grad_ext.T.astype(BF16)

    def step(tile, total):
        rows = pl.ds(pl.multiple_of(tile * tile_len, tile_len), tile_len)
        scores = jnp.dot(key_nat[rows, :], query_cols, preferred_element_type=F32)
        probs = jnp.exp2(scores)
        grad_probs = jnp.dot(value_nat[rows, :], grad_cols, preferred_element_type=F32)
        grad_scores = (probs * grad_probs).astype(BF16)
        value_sum[rows, :] += jnp.dot(probs.astype(BF16), grad_nat, preferred_element_type=F32)
        key_sum[rows, :] += jnp.dot(grad_scores, query_nat, preferred_element_type=F32)
        return total + jnp.dot(key_ref[tile, 0, 0], grad_scores, preferred_element_type=F32)

    start = jnp.zeros((head_dim, tile_len), F32)
    total = lax.fori_loop(0, tiles, step, start, unroll=8)
    out_ref[at, 0, 0] = (total * score_scale).astype(BF16)

    @pl.when(at == tiles - 1)
    def _():
        for tile in range(tiles):
            rows = slice(tile * tile_len, (tile + 1) * tile_len)
            key_grad = key_sum[rows, :].T[:head_dim] * (1.0 / LOG2E)
            out_ref[tile, 1, 0] = key_grad.astype(BF16)
            out_ref[tile, 2, 0] = value_sum[rows, :].T[:head_dim].astype(BF16)


def attend_back(qkv, grad_att, att, lse, score_scale):
    tiles, _, heads, head_dim, tile_len = qkv.shape
    one = pl.BlockSpec((1, 1, head_dim, tile_len), lambda h, t: (t, h, 0, 0))
    return kernel_call(
        functools.partial(attend_back_body, score_scale),
        2560 * heads * tiles**2 * tile_len**2,
        8 * qkv.size,
        grid=(heads, tiles),
        in_specs=[
            pl.BlockSpec((1, 1, 1, head_dim, tile_len), lambda h, t: (t, 0, h, 0, 0)),
            pl.BlockSpec((tiles, 1, 1, head_dim, tile_len), lambda h, t: (0, 1, h, 0, 0)),
            pl.BlockSpec((tiles, 1, 1, head_dim, tile_len), lambda h, t: (0, 2, h, 0, 0)),
            one,
            one,
            pl.BlockSpec((1, 1, 1, tile_len), lambda h, t: (t, h, 0, 0)),
        ],
        out_specs=pl.BlockSpec(
            (tiles, 3, 1, head_dim, tile_len), lambda h, t: (0, 0, h, 0, 0)
        ),
        out_shape=jax.ShapeDtypeStruct(qkv.shape, BF16),
        scratch_shapes=[
            pltpu.VMEM((tiles * tile_len, head_dim + 8), BF16),
            pltpu.VMEM((tiles * tile_len, head_dim + 8), BF16),
            pltpu.VMEM((tiles * tile_len, head_dim + 8), F32),
            pltpu.VMEM((tiles * tile_len, head_dim + 8), F32),
        ],
    )(qkv, qkv, qkv, grad_att, att, lse)


def cross_body(text_len, query_scale, pre_ref, kv_ref, att_ref, query_ref, inv_ref, lse_ref):
    head_dim, text_pad = kv_ref.shape[2], kv_ref.shape[3]
    at = lax.broadcasted_iota(jnp.int32, (8, text_pad), 0)
    text_at = lax.broadcasted_iota(jnp.int32, (8, text_pad), 1)
    flags = ((at == 0) & (text_at < text_len)).astype(F32)
    for head in range(pre_ref.shape[0]):
        normed, inverse = column_norm(pre_ref[head])
        query = (normed * query_scale).astype(BF16)
        query_ref[head] = query
        inv_ref[head] = inverse
        key = column_norm(kv_ref[0, head])[0].astype(BF16)
        value_ext = jnp.concatenate([kv_ref[1, head], flags], axis=0).astype(BF16)
        scores = jnp.dot(key.T, query, preferred_element_type=F32)
        weight = jnp.exp2(scores).astype(BF16)
        total = jnp.dot(value_ext, weight, preferred_element_type=F32)
        weight_sum = total[head_dim : head_dim + 1]
        att_ref[head] = (total[:head_dim] / weight_sum).astype(BF16)
        lse_ref[head] = jnp.log2(weight_sum)


def cross_attend(pre, text_kv, images, text_len, query_scale):
    heads, head_dim, tokens = pre.shape
    tile_len, text_pad = tokens // images, text_kv.shape[3] // images
    block = math.gcd(heads, 4)
    wide = pl.BlockSpec((block, head_dim, tile_len), lambda i, h: (h, 0, i))
    row = pl.BlockSpec((block, 1, tile_len), lambda i, h: (h, 0, i))
    return kernel_call(
        functools.partial(cross_body, text_len, query_scale),
        1024 * heads * tokens * text_pad,
        8 * pre.size,
        grid=(images, heads // block),
        in_specs=[wide, pl.BlockSpec((2, block, head_dim, text_pad), lambda i, h: (0, h, 0, i))],
        out_specs=[wide, wide, row, row],
        out_shape=[
            jax.ShapeDtypeStruct(pre.shape, BF16),
            jax.ShapeDtypeStruct(pre.shape, BF16),
            jax.ShapeDtypeStruct((heads, 1, tokens), F32),
            jax.ShapeDtypeStruct((heads, 1, tokens), F32),
        ],
    )(pre, text_kv)


def cross_back_body(
    query_scale,
    score_scale,
    query_ref,
    kv_ref,
    grad_ref,
    att_ref,
    inv_ref,
    lse_ref,
    out_ref,
    key_ref,
    value_ref,
):
    head_dim, text_pad = kv_ref.shape[2], kv_ref.shape[3]
    ones = piece_flags(text_pad)
    for head in range(query_ref.shape[0]):
        query = query_ref[head].astype(F32)
        grad = grad_ref[head].astype(F32)
        delta = jnp.sum(grad * att_ref[head].astype(F32), axis=0, keepdims=True)
        query_ext = jnp.concatenate([query, minus_pieces(lse_ref[head])], axis=0).astype(BF16)
        grad_ext = jnp.concatenate([grad, minus_pieces(delta)], axis=0).astype(BF16)
        key = column_norm(kv_ref[0, head])[0].astype(BF16)
        key_ext = jnp.concatenate([key.astype(F32), ones], axis=0).T.astype(BF16)
        value_ext = jnp.concatenate([kv_ref[1, head], ones], axis=0).T.astype(BF16)
        probs = jnp.exp2(jnp.dot(key_ext, query_ext, preferred_element_type=F32))
        grad_probs = jnp.dot(value_ext, grad_ext, preferred_element_type=F32)
        grad_scores = (probs * grad_probs).astype(BF16)
        value_grad = right_dot(grad_ext, probs.astype(BF16))[:head_dim]
        key_grad = right_dot(query_ext, grad_scores)[:head_dim]
        key_ref[head] = (key_grad * (1.0 / LOG2E)).astype(BF16)
        value_ref[head] = value_grad.astype(BF16)
        query_grad = jnp.dot(key, grad_scores, preferred_element_type=F32) * score_scale
        normed = query * (1.0 / query_scale)
        out_ref[head] = column_norm_back(query_grad, normed, inv_ref[head]).astype(BF16)


def cross_back(query, text_kv, grad, att, inverse, lse, images, query_scale, score_scale):
    heads, head_dim, tokens = query.shape
    tile_len, text_pad = tokens // images, text_kv.shape[3] // images
    block = math.gcd(heads, 4)
    wide = pl.BlockSpec((block, head_dim, tile_len), lambda i, h: (h, 0, i))
    row = pl.BlockSpec((block, 1, tile_len), lambda i, h: (h, 0, i))
    text = pl.BlockSpec((2, block, head_dim, text_pad), lambda i, h: (0, h, 0, i))
    text_out = pl.BlockSpec((block, head_dim, text_pad), lambda i, h: (h, 0, i))
    return kernel_call(
        functools.partial(cross_back_body, query_scale, score_scale),
        2560 * heads * tokens * text_pad,
        16 * query.size,
        grid=(images, heads // block),
        in_specs=[wide, text, wide, wide, row, row],
        out_specs=[
            wide,
            text_out,
            text_out,
        ],
        out_shape=[
            jax.ShapeDtypeStruct(query.shape, BF16),
            jax.ShapeDtypeStruct((heads, head_dim, images * text_pad), BF16),
            jax.ShapeDtypeStruct((heads, head_dim, images * text_pad), BF16),
        ],
    )(query, text_kv, grad, att, inverse, lse)


def join_norm_body(patch_ref, skip_ref, weight_ref, gain_ref, bias_ref, z_ref, inv_ref, in_ref):
    width = skip_ref.shape[1]
    patch_feat = right_dot(patch_ref[...], weight_ref[...])
    joined = jnp.concatenate([patch_feat, skip_ref[...].astype(F32)], axis=1)
    normed, inverse = layer_norm(joined)
    z_ref[...] = normed
    inv_ref[...] = inverse
    in_ref[...] = (normed * gain_ref[...] + bias_ref[...]).astype(BF16)


def join_norm(patch_rows, skip_rows, f_patch, gain, bias):
    tokens, width = skip_rows.shape
    block = math.gcd(tokens, 256)
    rows = lambda columns: pl.BlockSpec((block, columns), lambda t: (t, 0))
    fixed = lambda shape: pl.BlockSpec(shape, lambda t: (0, 0))
    return kernel_call(
        join_norm_body,
        64 * tokens * width,
        16 * tokens * width,
        grid=(tokens // block,),
        in_specs=[
            rows(patch_rows.shape[1]),
            rows(width),
            fixed(f_patch.shape),
            fixed(gain.shape),
            fixed(bias.shape),
        ],
        out_specs=[rows(2 * width), rows(1), rows(2 * width)],
        out_shape=[
            jax.ShapeDtypeStruct((tokens, 2 * width), F32),
            jax.ShapeDtypeStruct((tokens, 1), F32),
            jax.ShapeDtypeStruct((tokens, 2 * width), BF16),
        ],
    )(patch_rows, skip_rows, f_patch, gain, bias)


def join_back_body(low_ref, weight_ref, z_ref, inv_ref, gain_ref, skip_ref, patch_ref, sums_ref):
    width = skip_ref.shape[1]
    grad, normed = right_dot(low_ref[...], weight_ref[...]), z_ref[...]

    @pl.when(pl.program_id(0) == 0)
    def _():
        sums_ref[...] = jnp.zeros_like(sums_ref)

    sums_ref[0:1] += jnp.sum(grad * normed, axis=0, keepdims=True)
    sums_ref[1:2] += jnp.sum(grad, axis=0, keepdims=True)
    back = norm_back(grad * gain_ref[...], normed, inv_ref[...])
    patch_ref[...] = back[:, :width].astype(BF16)
    skip_ref[...] = back[:, width:]


def join_back(low_rows, f_skip, normed, inverse, gain):
    tokens, width = low_rows.shape
    block = math.gcd(tokens, 256)
    rows = lambda columns: pl.BlockSpec((block, columns), lambda t: (t, 0))
    fixed = lambda shape: pl.BlockSpec(shape, lambda t: (0, 0))
    return kernel_call(
        join_back_body,
        4 * tokens * width * width,
        18 * tokens * width,
        grid=(tokens // block,),
        in_specs=[rows(width), fixed(f_skip.shape), rows(2 * width), rows(1), fixed(gain.shape)],
        out_specs=[rows(width), rows(width), fixed((2, 2 * width))],
        out_shape=[
            jax.ShapeDtypeStruct((tokens, width), F32),
            jax.ShapeDtypeStruct((tokens, width), BF16),
            jax.ShapeDtypeStruct((2, 2 * width), F32),
        ],
    )(low_rows, f_skip, normed, inverse, gain)


def gelu_and_slope(inputs):
    scale, cubic = math.sqrt(2.0 / math.pi), 0.044715
    square = inputs * inputs
    curve = jnp.tanh(scale * inputs * (1.0 + cubic * square))
    half = 0.5 * (1.0 + curve)
    bend = 0.5 * inputs * (1.0 - curve * curve) * (scale * (1.0 + 3.0 * cubic * square))
    return ((inputs * half).astype(BF16), (half + bend).astype(BF16))


def swap_tiles(values_in):
    return lax.all_to_all(values_in, TILE, split_axis=0, concat_axis=0, tiled=True)


def shift_pairs(devices, step):
    return [(at, (at + step) % devices) for at in range(devices)]


def fetch(weight):
    devices = lax.axis_size("dp")
    return [weight] + [
        lax.ppermute(weight, "dp", shift_pairs(devices, step)) for step in range(1, devices)
    ]


def widen(pieces, first=None, joined=1):
    devices, me = lax.axis_size("dp"), lax.axis_index("dp")
    if first is not None:
        pieces = after(first, *pieces)
    slots = [lax.select_n((me - at) % devices, *pieces) for at in range(devices)]
    if joined > 1:
        split = [jnp.split(slot, joined, axis=1) for slot in slots]
        slots = [each for group in zip(*split) for each in group]
    return jnp.concatenate(slots, axis=1)


def narrow_blocks(blocks, first=None):
    devices, me = lax.axis_size("dp"), lax.axis_index("dp")
    received = []
    for step in range(1, devices):
        sent = lax.select_n((me + step) % devices, *blocks)
        received.append(lax.ppermute(sent, "dp", shift_pairs(devices, step)))
    if first is not None:
        received = after(first, *received)
    total = lax.select_n(me, *blocks).astype(F32)
    for piece in received:
        total = total + piece.astype(F32)
    return total


def narrow(weight_grad, first=None):
    return narrow_blocks(jnp.split(weight_grad, lax.axis_size("dp"), axis=1), first)


def by_device(weight_grads, parts):
    devices = lax.axis_size("dp")
    split = [jnp.split(weight_grad, devices, axis=1) for weight_grad in weight_grads]
    return [jnp.concatenate(blocks, axis=parts) for blocks in zip(*split)]


def sum_tiles(part_sums):
    devices, me = lax.axis_size(TILE), lax.axis_index(TILE)
    total, step = part_sums, devices // 2
    while step > 0:
        pairs = [(at, at ^ step) for at in range(devices)]
        lower, upper = jnp.split(total, 2, axis=0)
        high = (me // step) % 2 == 1
        sent = jnp.where(high, lower, upper)
        total = jnp.where(high, upper, lower) + lax.ppermute(sent, TILE, pairs)
        step //= 2
    return total


def total_tiles(part_sum):
    devices = lax.axis_size(TILE)
    total, step = part_sum, 1
    while step < devices:
        pairs = [(at, at ^ step) for at in range(devices)]
        total = total + lax.ppermute(total, TILE, pairs)
        step *= 2
    return total


def over_tiles(weight_grad):
    return lax.optimization_barrier(
        lax.psum_scatter(weight_grad, TILE, scatter_dimension=0, tiled=True)
    )


def tiles_whole(weight):
    return lax.all_gather(weight, TILE, axis=0, tiled=True)


def after(first, *values_in):
    return lax.optimization_barrier((first, *values_in))[1:]


def dot_over(left_mat, right_mat, left_axis, right_axis):
    return lax.dot_general(
        left_mat,
        right_mat,
        (((left_axis,), (right_axis,)), ((), ())),
        preferred_element_type=F32,
    )


def local_heads(
    latent,
    skip_input,
    text_states,
    timesteps,
    image_sides,
    cotangent,
    w_patch,
    w_skip,
    w_time,
    w_shift,
    w_qkv,
    w_out,
    w_query,
    w_text,
    w_cross,
    w_up,
    w_down,
    w_final,
    norm_params,
):
    dp_devices = lax.axis_size("dp")
    grid_devices = lax.axis_size(TILE)
    col_devices = lax.axis_size("col")
    grid_at = lax.axis_index(TILE)
    row_at = lax.axis_index("row")
    col_at = lax.axis_index("col")
    images, rows_tile, cols_tile, patch_width = latent.shape
    tile_len = rows_tile * cols_tile
    row_count = images * tile_len
    out_width = cotangent.shape[3]

    f_skip = lax.all_gather(w_skip, EVERY, axis=0, tiled=True).reshape(
        dp_devices, -1, w_skip.shape[1]
    )
    f_skip = jnp.swapaxes(f_skip, 0, 1).reshape(f_skip.shape[1], -1)
    small = jnp.concatenate([w_patch, w_final, norm_params], axis=1)
    small_widths = (w_patch.shape[1], w_final.shape[1], norm_params.shape[1])
    cuts = (0, small_widths[0], sum(small_widths[:2]), sum(small_widths))
    early = [jnp.pad(small, ((0, 0), (0, w_shift.shape[1] - small.shape[1]))), w_time, w_shift]
    ends = (small.shape[0], small.shape[0] + w_time.shape[0])
    part_small, part_time, part_shift_w = jnp.split(
        widen(fetch(jnp.concatenate(early, axis=0))), ends, axis=0
    )
    part_small = part_small.reshape(small.shape[0], dp_devices, -1)[:, :, : small.shape[1]]
    part_small = part_small.reshape(small.shape[0], -1)
    f_small = tiles_whole(part_small).reshape(-1, dp_devices, sum(small_widths))
    f_patch, f_final, f_norms = (
        f_small[:, :, cuts[at] : cuts[at + 1]].reshape(f_small.shape[0], -1) for at in range(3)
    )
    held_qkv = fetch(w_qkv)
    held_three = fetch(jnp.concatenate([w_out, w_query, w_cross], axis=1))
    held_text = fetch(w_text)
    held_up, held_down = fetch(w_up), fetch(w_down)
    model_width = skip_input.shape[3]
    head_count = HEADS
    head_dim = model_width // head_count
    text_len = text_states.shape[1]
    text_pad = -(-text_len // 128) * 128
    score_scale = head_dim ** (-0.5)
    query_scale = score_scale * LOG2E
    positions = jnp.arange(tile_len, dtype=jnp.int32)
    row_pos = row_at * rows_tile + positions // cols_tile
    col_pos = col_at * cols_tile + positions % cols_tile
    query_ok = (row_pos[None, :] < image_sides[:, None]) & (col_pos[None, :] < image_sides[:, None])
    valid = query_ok.astype(F32)
    keep_rows = query_ok.astype(F32).reshape(row_count, 1)
    tile_list = jnp.arange(grid_devices, dtype=jnp.int32)[:, None]
    key_row = tile_list // col_devices * rows_tile + (positions // cols_tile)[None, :]
    key_col = tile_list % col_devices * cols_tile + (positions % cols_tile)[None, :]
    sides = image_sides[:, None, None]
    key_ok = ((key_row[None] < sides) & (key_col[None] < sides)).astype(F32)
    flags = jnp.concatenate(
        [key_ok[:, :, None, :], jnp.zeros((images, grid_devices, 7, tile_len), F32)], axis=2
    )
    cos_row, sin_row, cos_col, sin_col = (
        jnp.transpose(table[:, 0, :]) for table in rope_tables(row_pos, col_pos, head_dim)
    )
    tables = (
        jnp.concatenate([cos_row, cos_row, cos_col, cos_col], axis=0),
        jnp.concatenate([-sin_row, sin_row, -sin_col, sin_col], axis=0),
    )
    norm_f = f_norms.astype(F32)

    embedding = time_embed(timesteps, FREQ).astype(BF16)
    freq_slice = part_time.shape[0]
    shift_slice = part_shift_w.shape[0]
    embed_cols = lax.dynamic_slice_in_dim(embedding, grid_at * freq_slice, freq_slice, 1)
    time_pre = total_tiles(plain_dot(embed_cols, part_time))
    time_float, silu_pull = jax.vjp(jax.nn.silu, time_pre)
    time_act = time_float.astype(BF16)
    act_cols = lax.dynamic_slice_in_dim(time_act, grid_at * shift_slice, shift_slice, 1)
    time_shift = total_tiles(plain_dot(act_cols, part_shift_w))

    patch_rows = latent.reshape(row_count, patch_width)
    skip_rows = skip_input.reshape(row_count, model_width)
    gain_skip = jnp.concatenate([norm_f[:, 8], norm_f[:, 10]])[None]
    bias_skip = jnp.concatenate([norm_f[:, 9], norm_f[:, 11]])[None]
    joined, joined_inv, skip_in = join_norm(patch_rows, skip_rows, f_patch, gain_skip, bias_skip)
    f_qkv = tiles_whole(widen(held_qkv, skip_in))
    part_three = widen(held_three, skip_in, 3)
    f_three = tiles_whole(part_three)
    f_out, f_query, f_cross = jnp.split(f_three, 3, axis=1)
    residual = plain_dot(skip_in, f_skip)
    first_z, first_inv = layer_norm(residual)
    first_pre = (first_z * norm_f[:, 0] + norm_f[:, 1]).reshape(
        images, tile_len, model_width
    ) + time_shift[:, None, :]
    first_in = first_pre.reshape(row_count, model_width).astype(BF16)
    part_text = widen(held_text, first_in)
    f_text = tiles_whole(part_text)
    first_rows = first_in.reshape(images, tile_len, model_width)
    own_qkv, qk_inv, tile_qkv, tile_att, tile_lse, att_rows = [], [], [], [], [], []
    for image in range(images):
        rows = first_rows[image]
        own, inverses = head_norm(
            rows,
            f_qkv,
            tables,
            valid[image : image + 1],
            grid_devices,
            head_dim,
            query_scale,
        )
        own_qkv.append(own)
        qk_inv.append(inverses)
        tile_qkv.append(swap_tiles(own))
    f_up = tiles_whole(widen(held_up, tile_qkv[0]))
    for image in range(images):
        att, lse = attend(tile_qkv[image], flags[image])
        tile_att.append(att)
        tile_lse.append(lse)
        own_att = swap_tiles(att).reshape(model_width, tile_len)
        att_rows.append(jnp.transpose(own_att))
    att_low = jnp.concatenate(att_rows, axis=0)
    residual_two = residual + plain_dot(att_low, f_out)
    f_down = tiles_whole(widen(held_down, residual_two))

    third_z, third_inv = layer_norm(residual_two)
    third_in = (third_z * norm_f[:, 2] + norm_f[:, 3]).astype(BF16)
    cross_pre = dot_over(f_query, third_in, 0, 1).reshape(head_count, head_dim, row_count)
    text_rows = jnp.pad(text_states, ((0, 0), (0, text_pad - text_len), (0, 0)))
    text_rows = text_rows.reshape(images * text_pad, -1)
    text_kv = dot_over(f_text, text_rows, 0, 1).reshape(2, head_count, head_dim, images * text_pad)
    crossed, cross_queries, cq_inv, cross_lse = cross_attend(
        cross_pre, text_kv, images, text_len, query_scale
    )
    cross_cols = crossed.reshape(model_width, row_count)
    residual_three = residual_two + left_dot(cross_cols, f_cross)
    second_z, second_inv = layer_norm(residual_three)
    second_in = (second_z * norm_f[:, 4] + norm_f[:, 5]).astype(BF16)
    up_pre = plain_dot(second_in, f_up)
    hidden_act, slope = lax.optimization_barrier(gelu_and_slope(up_pre))
    residual_four = residual_three + plain_dot(hidden_act, f_down)
    last_z, last_inv = layer_norm(residual_four)
    last_in = (last_z * norm_f[:, 6] + norm_f[:, 7]).astype(BF16)
    produced = plain_dot(last_in, f_final)
    prediction = (
        (produced * keep_rows).astype(BF16).reshape(images, rows_tile, cols_tile, out_width)
    )

    grad_out = (cotangent.reshape(row_count, out_width).astype(F32) * keep_rows).astype(BF16)
    d_final = left_dot(last_in, grad_out)
    grad_last = right_dot(grad_out, f_final)
    gain_final = jnp.sum(grad_last * last_z, axis=0)
    bias_final = jnp.sum(grad_last, axis=0)
    grad_four = norm_back(grad_last * norm_f[:, 6], last_z, last_inv)
    low_four = grad_four.astype(BF16)
    d_down = left_dot(hidden_act, low_four).astype(BF16)
    d_down, low_four = lax.optimization_barrier((d_down, low_four))
    t_down = over_tiles(d_down)
    grad_hidden = right_dot(low_four, f_down)
    grad_up = (grad_hidden * slope).astype(BF16)
    d_up = left_dot(second_in, grad_up).astype(BF16)
    d_up, grad_up = lax.optimization_barrier((d_up, grad_up))
    t_up = over_tiles(d_up)
    grad_second = right_dot(grad_up, f_up)
    gain_second = jnp.sum(grad_second * second_z, axis=0)
    bias_second = jnp.sum(grad_second, axis=0)
    grad_three = grad_four + norm_back(grad_second * norm_f[:, 4], second_z, second_inv)
    low_three = grad_three.astype(BF16)
    d_cross = plain_dot(cross_cols, low_three).astype(BF16)
    grad_crossed = dot_over(f_cross, low_three, 1, 1).astype(BF16)
    grad_cross_q, d_text_key, d_text_value = cross_back(
        cross_queries,
        text_kv,
        grad_crossed.reshape(head_count, head_dim, row_count),
        crossed,
        cq_inv,
        cross_lse,
        images,
        query_scale,
        score_scale,
    )
    t_down, grad_cross_q = lax.optimization_barrier((t_down, grad_cross_q))
    grad_cross_q = grad_cross_q.reshape(model_width, row_count)
    d_query = dot_over(third_in, grad_cross_q, 0, 1).astype(BF16)
    grad_third = dot_over(grad_cross_q, f_query, 0, 1)
    gain_third = jnp.sum(grad_third * third_z, axis=0)
    bias_third = jnp.sum(grad_third, axis=0)
    grad_two = grad_three + norm_back(grad_third * norm_f[:, 2], third_z, third_inv)
    low_two = grad_two.astype(BF16)
    low_two_rows = low_two.reshape(images, tile_len, model_width)
    tile_grads = []
    for image in range(images):
        grad_att = dot_over(f_out, low_two_rows[image], 1, 1).astype(BF16)
        tile_grads.append(swap_tiles(grad_att.reshape(tile_att[image].shape)))
    d_out = left_dot(att_low, low_two).astype(BF16)
    d_joint = jnp.concatenate(
        [
            d_out,
            d_query,
            d_cross,
            d_text_key.reshape(model_width, -1),
            d_text_value.reshape(model_width, -1),
        ],
        axis=1,
    )
    d_joint = with_layout_constraint(d_joint, Layout(major_to_minor=(0, 1)))
    d_joint, tile_grads[0] = lax.optimization_barrier((d_joint, tile_grads[0]))
    t_joint = over_tiles(d_joint)
    own_grads, grad_qkv, tile_back = [], None, None
    for image in range(images):
        if tile_back is not None:
            down_grad = narrow(t_down, tile_back)
            down_grad, tile_grads[image], tile_back = lax.optimization_barrier(
                (down_grad, tile_grads[image], tile_back)
            )
            own_grads.append(swap_tiles(tile_back))
        tile_back = attend_back(
            tile_qkv[image], tile_grads[image], tile_att[image], tile_lse[image], score_scale
        )
    own_grads.append(swap_tiles(tile_back))
    for image in range(images):
        if image == images - 1:
            up_grad = narrow(t_up, tile_back)
            up_grad, own_grads[-1], grad_qkv = lax.optimization_barrier(
                (up_grad, own_grads[-1], grad_qkv)
            )
        grad_qkv = head_back(
            own_grads[image],
            own_qkv[image],
            qk_inv[image],
            tables,
            valid[image : image + 1],
            query_scale,
            image,
            images,
            grad_qkv,
        )
    sum_text_kv = t_joint[:, 3 * model_width :].astype(F32)
    sum_text_kv = jnp.transpose(
        sum_text_kv.reshape(-1, head_dim, 2, images * text_pad), (2, 0, 1, 3)
    )
    group_heads = head_count // grid_devices
    own_key = lax.dynamic_slice_in_dim(text_kv[0], grid_at * group_heads, group_heads, 0)
    ck_z, ck_inv = layer_norm(jnp.swapaxes(own_key, 1, 2))
    grad_ckey = jnp.swapaxes(norm_back(jnp.swapaxes(sum_text_kv[0], 1, 2), ck_z, ck_inv), 1, 2)
    grad_kv = jnp.stack([grad_ckey, sum_text_kv[1]]).astype(BF16)
    grad_kv = tiles_whole(grad_kv.reshape(-1, images * text_pad))
    grad_qkv = grad_qkv.reshape(3 * model_width, row_count)
    d_qkv = dot_over(first_in, grad_qkv, 0, 1).astype(BF16)
    d_qkv, grad_qkv = lax.optimization_barrier((d_qkv, grad_qkv))
    t_qkv = over_tiles(d_qkv)
    grad_first = dot_over(grad_qkv, f_qkv, 0, 1)
    joint_blocks = by_device(jnp.split(t_joint[:, : 3 * model_width], 3, axis=1), 1)
    joint_grad = narrow_blocks(joint_blocks, grad_first)
    gain_first = jnp.sum(grad_first * first_z, axis=0)
    bias_first = jnp.sum(grad_first, axis=0)
    part_shift = jnp.sum(grad_first.reshape(images, tile_len, model_width), axis=1)
    grad_one = grad_two + norm_back(grad_first * norm_f[:, 0], first_z, first_inv)

    low_one = grad_one.astype(BF16)
    d_skip_w = left_dot(skip_in, low_one).astype(BF16)
    d_skip_w, low_one = lax.optimization_barrier((d_skip_w, low_one))
    skip_grad, grad_patch, skip_sums = join_back(low_one, f_skip, joined, joined_inv, gain_skip)
    t_qkv, d_skip_w, joint_grad, skip_sums = lax.optimization_barrier(
        (t_qkv, d_skip_w, joint_grad, skip_sums)
    )
    out_grad, query_w_grad, cross_grad = jnp.split(joint_grad, 3, axis=1)
    t_skip = over_tiles(d_skip_w)

    group_shape = (-1, 2, grid_devices, model_width // grid_devices)
    text_slice = text_states.shape[2] // grid_devices
    text_cols = lax.dynamic_slice_in_dim(text_rows, grid_at * text_slice, text_slice, 1)
    d_text = dot_over(text_cols, grad_kv, 0, 1).astype(BF16)
    d_text = jnp.swapaxes(d_text.reshape(text_slice, grid_devices, 2, -1), 1, 2)
    d_text = d_text.reshape(text_slice, -1)
    grouped_text = jnp.swapaxes(part_text.reshape(group_shape), 1, 2).reshape(part_text.shape)
    text_grad = dot_over(grad_kv, grouped_text, 0, 1).reshape(images, text_pad, text_slice)
    text_grad = text_grad[:, :text_len]

    shift_low = total_tiles(part_shift).astype(BF16)
    d_shift = left_dot(act_cols, shift_low).astype(BF16)
    grad_time_act = total_tiles(
        lax.dynamic_update_slice_in_dim(
            jnp.zeros_like(time_pre), right_dot(shift_low, part_shift_w), grid_at * shift_slice, 1
        )
    )
    grad_time_pre = silu_pull(grad_time_act)[0].astype(BF16)
    d_time = left_dot(embed_cols, grad_time_pre).astype(BF16)
    late, width = [], w_shift.shape[1]
    for at in range(dp_devices):
        pair = d_text[:, 2 * at * width : 2 * (at + 1) * width]
        own = slice(at * width, (at + 1) * width)
        late.append(
            jnp.concatenate([pair[:, :width], pair[:, width:], d_time[:, own], d_shift[:, own]])
        )
    qkv_grad = narrow(t_qkv, d_text)
    qkv_grad, *late = lax.optimization_barrier((qkv_grad, *late))
    late = narrow_blocks(late)
    rows = d_text.shape[0]
    text_w_grad = jnp.concatenate([late[:rows], late[rows : 2 * rows]], axis=1)
    time_w_grad, shift_w_grad = jnp.split(late[2 * rows :], [d_time.shape[0]], axis=0)

    skip_grad = skip_grad.reshape(images, rows_tile, cols_tile, model_width)
    gain_skips, bias_skips = skip_sums[0], skip_sums[1]
    d_patch = left_dot(grad_patch, patch_rows)
    latent_grad = plain_dot(grad_patch, f_patch).reshape(images, rows_tile, cols_tile, patch_width)
    d_norms = jnp.stack(
        [
            gain_first,
            bias_first,
            gain_third,
            bias_third,
            gain_second,
            bias_second,
            gain_final,
            bias_final,
            gain_skips[:model_width],
            bias_skips[:model_width],
            gain_skips[model_width:],
            bias_skips[model_width:],
        ],
        axis=1,
    )
    small_grads = jnp.concatenate(
        [
            grad.reshape(model_width, dp_devices, -1)
            for grad in (d_patch, d_final, d_norms)
        ],
        axis=2,
    )
    small_grads = narrow(sum_tiles(small_grads.reshape(model_width, -1)))
    skip_w_grad = narrow(t_skip)
    patch_grad, final_grad, norms_grad = (
        small_grads[:, cuts[at] : cuts[at + 1]] for at in range(3)
    )
    return (
        prediction,
        latent_grad,
        skip_grad,
        text_grad,
        patch_grad,
        skip_w_grad,
        time_w_grad,
        shift_w_grad,
        qkv_grad,
        out_grad,
        query_w_grad,
        text_w_grad,
        cross_grad,
        up_grad,
        down_grad,
        final_grad,
        norms_grad,
    )


def local(sizes, latent, *others):
    grid_devices = sizes["row"] * sizes["col"]
    tile_len = latent.shape[1] * latent.shape[2]
    if HEADS % grid_devices == 0 and tile_len % 128 == 0:
        return local_heads(latent, *others)
    return local_gathered(latent, *others)


def solution(mesh):
    return jax.shard_map(
        functools.partial(local, mesh.shape),
        mesh=mesh,
        in_specs=(
            P("dp", "row", "col", None),
            P("dp", "row", "col", None),
            P("dp", None, None),
            P("dp"),
            P("dp"),
            P("dp", "row", "col", None),
            P(("row", "col"), "dp"),
            P(("row", "col"), "dp"),
            P(("row", "col"), "dp"),
            P(("row", "col"), "dp"),
            P(("row", "col"), "dp"),
            P(("row", "col"), "dp"),
            P(("row", "col"), "dp"),
            P(("row", "col"), "dp"),
            P(("row", "col"), "dp"),
            P(("row", "col"), "dp"),
            P(("row", "col"), "dp"),
            P(("row", "col"), "dp"),
            P(("row", "col"), "dp"),
        ),
        out_specs=(
            P("dp", "row", "col", None),
            P("dp", "row", "col", None),
            P("dp", "row", "col", None),
            P("dp", None, ("row", "col")),
            P(("row", "col"), "dp"),
            P(("row", "col"), "dp"),
            P(("row", "col"), "dp"),
            P(("row", "col"), "dp"),
            P(("row", "col"), "dp"),
            P(("row", "col"), "dp"),
            P(("row", "col"), "dp"),
            P(("row", "col"), "dp"),
            P(("row", "col"), "dp"),
            P(("row", "col"), "dp"),
            P(("row", "col"), "dp"),
            P(("row", "col"), "dp"),
            P(("row", "col"), "dp"),
        ),
        check_vma=False,
    )
```

```python
import functools
import math

import jax
import jax.numpy as jnp
from jax import lax
from jax.experimental import pallas as pl
from jax.experimental.layout import Layout, with_layout_constraint
from jax.experimental.pallas import tpu as pltpu
from jax.sharding import PartitionSpec as P

HEADS = 16
FREQ = 256


EPSILON = 1e-06


def layer_norm(values_in):
    centred = values_in - jnp.mean(values_in, axis=-1, keepdims=True)
    inverse = lax.rsqrt(jnp.mean(centred * centred, axis=-1, keepdims=True) + EPSILON)
    return (centred * inverse, inverse)


def norm_back(grad_normed, normed, inverse):
    mean_grad = jnp.mean(grad_normed, axis=-1, keepdims=True)
    mean_cross = jnp.mean(grad_normed * normed, axis=-1, keepdims=True)
    return inverse * (grad_normed - mean_grad - normed * mean_cross)


def turn_half(piece_half, cosine, sine_tab):
    quarter = cosine.shape[-1]
    lower = piece_half[..., :quarter]
    higher = piece_half[..., quarter:]
    return jnp.concatenate(
        [lower * cosine - higher * sine_tab, higher * cosine + lower * sine_tab], axis=-1
    )


def rotate(values_in, tables, signum):
    cos_row, sin_row, cos_col, sin_col = tables
    half_dim = values_in.shape[-1] // 2
    return jnp.concatenate(
        [
            turn_half(values_in[..., :half_dim], cos_row, signum * sin_row),
            turn_half(values_in[..., half_dim:], cos_col, signum * sin_col),
        ],
        axis=-1,
    )


def rope_tables(row_pos, col_pos, head_size):
    quarter = head_size // 4
    frequency = jnp.exp(jnp.arange(quarter, dtype=jnp.float32) * (-math.log(10000.0) / quarter))
    row_ang = row_pos.astype(jnp.float32)[:, None, None] * frequency
    col_ang = col_pos.astype(jnp.float32)[:, None, None] * frequency
    return (jnp.cos(row_ang), jnp.sin(row_ang), jnp.cos(col_ang), jnp.sin(col_ang))


def time_embed(step_values, freq_count):
    half_dim = freq_count // 2
    rate_list = jnp.exp(jnp.arange(half_dim, dtype=jnp.float32) * (-math.log(10000.0) / half_dim))
    angles = step_values.astype(jnp.float32)[..., None] * rate_list
    return jnp.concatenate([jnp.cos(angles), jnp.sin(angles)], axis=-1)


def gelu_tanh(inputs):
    return jax.nn.gelu(inputs, approximate=True)


def plain_dot(left_mat, right_mat):
    return jnp.dot(left_mat, right_mat, preferred_element_type=jnp.float32)


def left_dot(left_mat, right_mat):
    return lax.dot_general(
        left_mat, right_mat, (((0,), (0,)), ((), ())), preferred_element_type=jnp.float32
    )


def right_dot(left_mat, right_mat):
    return lax.dot_general(
        left_mat, right_mat, (((1,), (1,)), ((), ())), preferred_element_type=jnp.float32
    )


def block_size(key_count):
    block_len = key_count
    while block_len > 1024 and block_len % 2 == 0:
        block_len = block_len // 2
    return block_len


def local_gathered(
    latent,
    skip_input,
    text_states,
    timesteps,
    image_sides,
    cotangent,
    w_patch,
    w_skip,
    w_time,
    w_shift,
    w_qkv,
    w_out,
    w_query,
    w_text,
    w_cross,
    w_up,
    w_down,
    w_final,
    norm_params,
):
    widened = (
        lax.all_gather(w_patch, "dp", axis=1, tiled=True),
        lax.all_gather(w_skip, "dp", axis=1, tiled=True),
        lax.all_gather(w_time, "dp", axis=1, tiled=True),
        lax.all_gather(w_shift, "dp", axis=1, tiled=True),
        lax.all_gather(w_qkv, "dp", axis=1, tiled=True),
        lax.all_gather(w_out, "dp", axis=1, tiled=True),
        lax.all_gather(w_query, "dp", axis=1, tiled=True),
        lax.all_gather(w_text, "dp", axis=1, tiled=True),
        lax.all_gather(w_cross, "dp", axis=1, tiled=True),
        lax.all_gather(w_up, "dp", axis=1, tiled=True),
        lax.all_gather(w_down, "dp", axis=1, tiled=True),
        lax.all_gather(w_final, "dp", axis=1, tiled=True),
        lax.all_gather(norm_params, "dp", axis=1, tiled=True),
    )
    gathered = (
        lax.all_gather(widened[0], ("row", "col"), axis=0, tiled=True),
        lax.all_gather(widened[1], ("row", "col"), axis=0, tiled=True),
        lax.all_gather(widened[2], ("row", "col"), axis=0, tiled=True),
        lax.all_gather(widened[3], ("row", "col"), axis=0, tiled=True),
        lax.all_gather(widened[4], ("row", "col"), axis=0, tiled=True),
        lax.all_gather(widened[5], ("row", "col"), axis=0, tiled=True),
        lax.all_gather(widened[6], ("row", "col"), axis=0, tiled=True),
        lax.all_gather(widened[7], ("row", "col"), axis=0, tiled=True),
        lax.all_gather(widened[8], ("row", "col"), axis=0, tiled=True),
        lax.all_gather(widened[9], ("row", "col"), axis=0, tiled=True),
        lax.all_gather(widened[10], ("row", "col"), axis=0, tiled=True),
        lax.all_gather(widened[11], ("row", "col"), axis=0, tiled=True),
        lax.all_gather(widened[12], ("row", "col"), axis=0, tiled=True),
    )
    (
        f_patch,
        f_skip,
        f_time,
        f_shift,
        f_qkv,
        f_out,
        f_query,
        f_text,
        f_cross,
        f_up,
        f_down,
        f_final,
        f_norms,
    ) = gathered
    part_text = widened[7]
    images, rows_tile, cols_tile, patch_width = latent.shape
    tile_len = rows_tile * cols_tile
    row_count = images * tile_len
    model_width = f_qkv.shape[0]
    head_count = HEADS
    head_dim = model_width // head_count
    text_len = text_states.shape[1]
    grid_devices = lax.axis_size(("row", "col"))
    col_devices = lax.axis_size("col")
    grid_at = lax.axis_index(("row", "col"))
    row_at = lax.axis_index("row")
    col_at = lax.axis_index("col")
    score_scale = head_dim ** (-0.5)
    positions = jnp.arange(tile_len, dtype=jnp.int32)
    row_pos = row_at * rows_tile + positions // cols_tile
    col_pos = col_at * cols_tile + positions % cols_tile
    query_ok = (row_pos[None, :] < image_sides[:, None]) & (col_pos[None, :] < image_sides[:, None])
    keep_rows = query_ok.astype(jnp.float32).reshape(row_count, 1)
    tables = rope_tables(row_pos, col_pos, head_dim)
    norm_f = f_norms.astype(jnp.float32)

    def valid_keys(offset, block_len):
        index_list = offset + jnp.arange(block_len, dtype=jnp.int32)
        source = index_list // tile_len
        within = index_list % tile_len
        key_row = source // col_devices * rows_tile + within // cols_tile
        key_col = source % col_devices * cols_tile + within % cols_tile
        return (key_row[None, :] < image_sides[:, None]) & (key_col[None, :] < image_sides[:, None])

    patch_rows = latent.reshape(row_count, patch_width)
    patch_feat = right_dot(patch_rows, f_patch)
    skip_rows = skip_input.reshape(row_count, model_width).astype(jnp.float32)
    gain_skip = jnp.concatenate([norm_f[:, 8], norm_f[:, 10]])
    bias_skip = jnp.concatenate([norm_f[:, 9], norm_f[:, 11]])
    joined, joined_inv = layer_norm(jnp.concatenate([patch_feat, skip_rows], axis=-1))
    skip_in = (joined * gain_skip + bias_skip).astype(jnp.bfloat16)
    residual = plain_dot(skip_in, f_skip)
    embedding = time_embed(timesteps, FREQ).astype(jnp.bfloat16)
    time_pre = plain_dot(embedding, f_time)
    time_float, silu_pull = jax.vjp(jax.nn.silu, time_pre)
    time_act = time_float.astype(jnp.bfloat16)
    time_shift = plain_dot(time_act, f_shift)
    first_z, first_inv = layer_norm(residual)
    first_pre = (first_z * norm_f[:, 0] + norm_f[:, 1]).reshape(
        images, tile_len, model_width
    ) + time_shift[:, None, :]
    first_in = first_pre.reshape(row_count, model_width).astype(jnp.bfloat16)
    qkv = plain_dot(first_in, f_qkv)
    query_z, query_inv = layer_norm(
        qkv[:, :model_width].reshape(images, tile_len, head_count, head_dim)
    )
    key_z, key_inv = layer_norm(
        qkv[:, model_width : 2 * model_width].reshape(images, tile_len, head_count, head_dim)
    )
    queries = rotate(query_z, tables, 1.0).astype(jnp.bfloat16)
    queries_h = jnp.transpose(queries, (0, 2, 1, 3))
    keys = rotate(key_z, tables, 1.0).astype(jnp.bfloat16).reshape(images, tile_len, model_width)
    values = qkv[:, 2 * model_width :].astype(jnp.bfloat16).reshape(images, tile_len, model_width)
    start_carry = (
        jnp.full((images, head_count, tile_len), -1e30, jnp.float32),
        jnp.zeros((images, head_count, tile_len), jnp.float32),
        jnp.zeros((images, head_count, tile_len, head_dim), jnp.float32),
    )
    key_rows = lax.all_gather(keys, ("row", "col"), axis=1, tiled=True)
    value_rows = lax.all_gather(values, ("row", "col"), axis=1, tiled=True)
    key_count = key_rows.shape[1]
    block_len = block_size(key_count)

    def forward_block_step(block_index, running):
        running_max, weight_sum, accum_sum = running
        offset = block_index * block_len
        key_blk = lax.dynamic_slice_in_dim(key_rows, offset, block_len, 1).reshape(
            images, block_len, head_count, head_dim
        )
        value_blk = lax.dynamic_slice_in_dim(value_rows, offset, block_len, 1).reshape(
            images, block_len, head_count, head_dim
        )
        key_ok = valid_keys(offset, block_len)
        scores = (
            jnp.einsum("ihqe,ikhe->ihqk", queries_h, key_blk, preferred_element_type=jnp.float32)
            * score_scale
        )
        scores = jnp.where(key_ok[:, None, None, :], scores, -jnp.inf)
        new_max = jnp.maximum(running_max, jnp.max(scores, axis=-1))
        weight = jnp.exp(scores - new_max[..., None])
        rescale = jnp.exp(running_max - new_max)
        weight_sum = weight_sum * rescale + jnp.sum(weight, axis=-1)
        accum_sum = accum_sum * rescale[..., None] + jnp.einsum(
            "ihqk,ikhe->ihqe",
            weight.astype(jnp.bfloat16),
            value_blk,
            preferred_element_type=jnp.float32,
        )
        return (new_max, weight_sum, accum_sum)

    running_max, weight_sum, accum_sum = lax.fori_loop(
        0, key_count // block_len, forward_block_step, start_carry
    )
    attended = accum_sum / weight_sum[..., None]
    log_sum = running_max + jnp.log(weight_sum)
    att_low = (
        jnp.transpose(attended, (0, 2, 1, 3)).reshape(row_count, model_width).astype(jnp.bfloat16)
    )
    residual_two = residual + plain_dot(att_low, f_out)
    third_z, third_inv = layer_norm(residual_two)
    third_in = (third_z * norm_f[:, 2] + norm_f[:, 3]).astype(jnp.bfloat16)
    cross_pre = plain_dot(third_in, f_query)
    cq_z, cq_inv = layer_norm(cross_pre.reshape(images, tile_len, head_count, head_dim))
    cross_queries = cq_z.astype(jnp.bfloat16)
    text_kv = jnp.einsum("itc,cd->itd", text_states, f_text, preferred_element_type=jnp.float32)
    ck_z, ck_inv = layer_norm(
        text_kv[..., :model_width].reshape(images, text_len, head_count, head_dim)
    )
    cross_keys = ck_z.astype(jnp.bfloat16)
    cross_values = (
        text_kv[..., model_width:]
        .astype(jnp.bfloat16)
        .reshape(images, text_len, head_count, head_dim)
    )

    def cross_softmax():
        scores = (
            jnp.einsum(
                "iqhe,ikhe->ihqk", cross_queries, cross_keys, preferred_element_type=jnp.float32
            )
            * score_scale
        )
        return jax.nn.softmax(scores, axis=-1)

    crossed = jnp.einsum(
        "ihqk,ikhe->iqhe",
        cross_softmax().astype(jnp.bfloat16),
        cross_values,
        preferred_element_type=jnp.float32,
    )
    cross_low = crossed.reshape(row_count, model_width).astype(jnp.bfloat16)
    residual_three = residual_two + plain_dot(cross_low, f_cross)
    second_z, second_inv = layer_norm(residual_three)
    second_in = (second_z * norm_f[:, 4] + norm_f[:, 5]).astype(jnp.bfloat16)
    up_pre = plain_dot(second_in, f_up)
    hidden_float, gelu_pull = jax.vjp(gelu_tanh, up_pre)
    hidden_act = hidden_float.astype(jnp.bfloat16)
    residual_four = residual_three + plain_dot(hidden_act, f_down)
    last_z, last_inv = layer_norm(residual_four)
    last_in = (last_z * norm_f[:, 6] + norm_f[:, 7]).astype(jnp.bfloat16)
    produced = plain_dot(last_in, f_final)
    prediction = (
        (produced * keep_rows)
        .astype(jnp.bfloat16)
        .reshape(images, rows_tile, cols_tile, produced.shape[1])
    )
    grad_out = (
        cotangent.reshape(row_count, produced.shape[1]).astype(jnp.float32) * keep_rows
    ).astype(jnp.bfloat16)
    d_final = left_dot(last_in, grad_out)
    grad_last = right_dot(grad_out, f_final)
    gain_final = jnp.sum(grad_last * last_z, axis=0)
    bias_final = jnp.sum(grad_last, axis=0)
    grad_four = norm_back(grad_last * norm_f[:, 6], last_z, last_inv)
    low_four = grad_four.astype(jnp.bfloat16)
    d_down = left_dot(hidden_act, low_four)
    grad_hidden = right_dot(low_four, f_down)
    grad_up = gelu_pull(grad_hidden)[0].astype(jnp.bfloat16)
    d_up = left_dot(second_in, grad_up)
    grad_second = right_dot(grad_up, f_up)
    gain_second = jnp.sum(grad_second * second_z, axis=0)
    bias_second = jnp.sum(grad_second, axis=0)
    grad_three = grad_four + norm_back(grad_second * norm_f[:, 4], second_z, second_inv)
    low_three = grad_three.astype(jnp.bfloat16)
    d_cross = left_dot(cross_low, low_three)
    grad_crossed = (
        right_dot(low_three, f_cross)
        .astype(jnp.bfloat16)
        .reshape(images, tile_len, head_count, head_dim)
    )
    cross_probs = cross_softmax()
    cross_delta = jnp.transpose(
        jnp.sum(grad_crossed.astype(jnp.float32) * crossed, axis=-1), (0, 2, 1)
    )
    grad_probs = jnp.einsum(
        "iqhe,ikhe->ihqk", grad_crossed, cross_values, preferred_element_type=jnp.float32
    )
    grad_cscore = (cross_probs * (grad_probs - cross_delta[..., None])).astype(jnp.bfloat16)
    grad_cq = score_scale * jnp.einsum(
        "ihqk,ikhe->iqhe", grad_cscore, cross_keys, preferred_element_type=jnp.float32
    )
    part_ckey = score_scale * jnp.einsum(
        "ihqk,iqhe->ikhe", grad_cscore, cross_queries, preferred_element_type=jnp.float32
    )
    part_cvalue = jnp.einsum(
        "ihqk,iqhe->ikhe",
        cross_probs.astype(jnp.bfloat16),
        grad_crossed,
        preferred_element_type=jnp.float32,
    )
    grad_cross_q = (
        norm_back(grad_cq, cq_z, cq_inv).reshape(row_count, model_width).astype(jnp.bfloat16)
    )
    d_query = left_dot(third_in, grad_cross_q)
    grad_third = right_dot(grad_cross_q, f_query)
    gain_third = jnp.sum(grad_third * third_z, axis=0)
    bias_third = jnp.sum(grad_third, axis=0)
    grad_two = grad_three + norm_back(grad_third * norm_f[:, 2], third_z, third_inv)
    sum_ckey, sum_cvalue = lax.psum((part_ckey, part_cvalue), ("row", "col"))
    low_two = grad_two.astype(jnp.bfloat16)
    d_out = left_dot(att_low, low_two)
    grad_att = (
        right_dot(low_two, f_out)
        .astype(jnp.bfloat16)
        .reshape(images, tile_len, head_count, head_dim)
    )
    grad_att_h = jnp.transpose(grad_att, (0, 2, 1, 3))
    delta_rows = jnp.sum(grad_att_h.astype(jnp.float32) * attended, axis=-1)
    back_carry = (
        jnp.zeros((images, head_count, tile_len, head_dim), jnp.float32),
        jnp.zeros((images, tile_len * grid_devices, model_width), jnp.float32),
        jnp.zeros((images, tile_len * grid_devices, model_width), jnp.float32),
    )
    backward_key_rows = lax.all_gather(keys, ("row", "col"), axis=1, tiled=True)
    backward_value_rows = lax.all_gather(values, ("row", "col"), axis=1, tiled=True)
    key_count = backward_key_rows.shape[1]
    backward_block_len = block_size(key_count)

    def backward_block_step(block_index, running):
        grad_query, grad_key_all, grad_value_all = running
        offset = block_index * backward_block_len
        key_blk = lax.dynamic_slice_in_dim(
            backward_key_rows, offset, backward_block_len, 1
        ).reshape(images, backward_block_len, head_count, head_dim)
        value_blk = lax.dynamic_slice_in_dim(
            backward_value_rows, offset, backward_block_len, 1
        ).reshape(images, backward_block_len, head_count, head_dim)
        key_ok = valid_keys(offset, backward_block_len)
        scores = (
            jnp.einsum("ihqe,ikhe->ihqk", queries_h, key_blk, preferred_element_type=jnp.float32)
            * score_scale
        )
        scores = jnp.where(key_ok[:, None, None, :], scores, -jnp.inf)
        attn_probs = jnp.exp(scores - log_sum[..., None])
        grad_prob = jnp.einsum(
            "ihqe,ikhe->ihqk", grad_att_h, value_blk, preferred_element_type=jnp.float32
        )
        grad_score = (attn_probs * (grad_prob - delta_rows[..., None])).astype(jnp.bfloat16)
        grad_query = grad_query + score_scale * jnp.einsum(
            "ihqk,ikhe->ihqe", grad_score, key_blk, preferred_element_type=jnp.float32
        )
        key_part = score_scale * jnp.einsum(
            "ihqk,ihqe->ikhe", grad_score, queries_h, preferred_element_type=jnp.float32
        )
        value_part = jnp.einsum(
            "ihqk,ihqe->ikhe",
            attn_probs.astype(jnp.bfloat16),
            grad_att_h,
            preferred_element_type=jnp.float32,
        )
        grad_key_all = lax.dynamic_update_slice_in_dim(
            grad_key_all, key_part.reshape(images, backward_block_len, model_width), offset, 1
        )
        grad_value_all = lax.dynamic_update_slice_in_dim(
            grad_value_all, value_part.reshape(images, backward_block_len, model_width), offset, 1
        )
        return (grad_query, grad_key_all, grad_value_all)

    grad_query, grad_key_all, grad_value_all = lax.fori_loop(
        0, key_count // backward_block_len, backward_block_step, back_carry
    )
    grad_key_own, grad_value_own = (
        lax.psum_scatter(grad_key_all, ("row", "col"), scatter_dimension=1, tiled=True),
        lax.psum_scatter(grad_value_all, ("row", "col"), scatter_dimension=1, tiled=True),
    )
    grad_qn = rotate(jnp.transpose(grad_query, (0, 2, 1, 3)), tables, -1.0)
    grad_kn = rotate(grad_key_own.reshape(images, tile_len, head_count, head_dim), tables, -1.0)
    grad_qkv = jnp.concatenate(
        [
            norm_back(grad_qn, query_z, query_inv).reshape(row_count, model_width),
            norm_back(grad_kn, key_z, key_inv).reshape(row_count, model_width),
            grad_value_own.reshape(row_count, model_width),
        ],
        axis=-1,
    ).astype(jnp.bfloat16)
    d_qkv = left_dot(first_in, grad_qkv)
    grad_first = right_dot(grad_qkv, f_qkv)
    gain_first = jnp.sum(grad_first * first_z, axis=0)
    bias_first = jnp.sum(grad_first, axis=0)
    part_shift = jnp.sum(grad_first.reshape(images, tile_len, model_width), axis=1)
    grad_one = grad_two + norm_back(grad_first * norm_f[:, 0], first_z, first_inv)
    shift_grad = lax.psum(part_shift, ("row", "col"))
    grad_ckey = norm_back(sum_ckey, ck_z, ck_inv).reshape(images, text_len, model_width)
    grad_kv = jnp.concatenate(
        [grad_ckey, sum_cvalue.reshape(images, text_len, model_width)], axis=-1
    ).astype(jnp.bfloat16)
    text_slice = text_states.shape[2] // grid_devices
    text_cols = lax.dynamic_slice_in_dim(text_states, grid_at * text_slice, text_slice, 2)
    d_text_w = jnp.einsum("itc,itd->cd", text_cols, grad_kv, preferred_element_type=jnp.float32)
    text_grad = jnp.einsum("itd,cd->itc", grad_kv, part_text, preferred_element_type=jnp.float32)
    shift_low = shift_grad.astype(jnp.bfloat16)
    shift_slice = model_width // grid_devices
    act_cols = lax.dynamic_slice_in_dim(time_act, grid_at * shift_slice, shift_slice, 1)
    d_shift_w = jnp.einsum("ic,id->cd", act_cols, shift_low, preferred_element_type=jnp.float32)
    grad_time_act = right_dot(shift_low, f_shift)
    grad_time_pre = silu_pull(grad_time_act)[0].astype(jnp.bfloat16)
    freq_slice = embedding.shape[1] // grid_devices
    embed_cols = lax.dynamic_slice_in_dim(embedding, grid_at * freq_slice, freq_slice, 1)
    d_time_w = jnp.einsum(
        "ic,id->cd", embed_cols, grad_time_pre, preferred_element_type=jnp.float32
    )
    low_one = grad_one.astype(jnp.bfloat16)
    d_skip_w = left_dot(skip_in, low_one)
    grad_skip_in = right_dot(low_one, f_skip)
    gain_skips = jnp.sum(grad_skip_in * joined, axis=0)
    bias_skips = jnp.sum(grad_skip_in, axis=0)
    grad_joined = norm_back(grad_skip_in * gain_skip, joined, joined_inv)
    skip_grad = grad_joined[:, model_width:].reshape(images, rows_tile, cols_tile, model_width)
    grad_patch = grad_joined[:, :model_width].astype(jnp.bfloat16)
    d_patch = left_dot(grad_patch, patch_rows)
    latent_grad = plain_dot(grad_patch, f_patch).reshape(images, rows_tile, cols_tile, patch_width)
    d_norms = jnp.stack(
        [
            gain_first,
            bias_first,
            gain_third,
            bias_third,
            gain_second,
            bias_second,
            gain_final,
            bias_final,
            gain_skips[:model_width],
            bias_skips[:model_width],
            gain_skips[model_width:],
            bias_skips[model_width:],
        ],
        axis=1,
    )
    tile_done = (
        lax.psum_scatter(d_patch, ("row", "col"), scatter_dimension=0, tiled=True),
        lax.psum_scatter(d_skip_w, ("row", "col"), scatter_dimension=0, tiled=True),
        lax.psum_scatter(d_qkv, ("row", "col"), scatter_dimension=0, tiled=True),
        lax.psum_scatter(d_out, ("row", "col"), scatter_dimension=0, tiled=True),
        lax.psum_scatter(d_query, ("row", "col"), scatter_dimension=0, tiled=True),
        lax.psum_scatter(d_cross, ("row", "col"), scatter_dimension=0, tiled=True),
        lax.psum_scatter(d_up, ("row", "col"), scatter_dimension=0, tiled=True),
        lax.psum_scatter(d_down, ("row", "col"), scatter_dimension=0, tiled=True),
        lax.psum_scatter(d_final, ("row", "col"), scatter_dimension=0, tiled=True),
        lax.psum_scatter(d_norms, ("row", "col"), scatter_dimension=0, tiled=True),
    )
    reduced = (
        lax.psum_scatter(
            tile_done[0].astype(jnp.bfloat16), "dp", scatter_dimension=1, tiled=True
        ).astype(jnp.float32),
        lax.psum_scatter(
            tile_done[1].astype(jnp.bfloat16), "dp", scatter_dimension=1, tiled=True
        ).astype(jnp.float32),
        lax.psum_scatter(
            tile_done[2].astype(jnp.bfloat16), "dp", scatter_dimension=1, tiled=True
        ).astype(jnp.float32),
        lax.psum_scatter(
            tile_done[3].astype(jnp.bfloat16), "dp", scatter_dimension=1, tiled=True
        ).astype(jnp.float32),
        lax.psum_scatter(
            tile_done[4].astype(jnp.bfloat16), "dp", scatter_dimension=1, tiled=True
        ).astype(jnp.float32),
        lax.psum_scatter(
            tile_done[5].astype(jnp.bfloat16), "dp", scatter_dimension=1, tiled=True
        ).astype(jnp.float32),
        lax.psum_scatter(
            tile_done[6].astype(jnp.bfloat16), "dp", scatter_dimension=1, tiled=True
        ).astype(jnp.float32),
        lax.psum_scatter(
            tile_done[7].astype(jnp.bfloat16), "dp", scatter_dimension=1, tiled=True
        ).astype(jnp.float32),
        lax.psum_scatter(
            tile_done[8].astype(jnp.bfloat16), "dp", scatter_dimension=1, tiled=True
        ).astype(jnp.float32),
        lax.psum_scatter(
            tile_done[9].astype(jnp.bfloat16), "dp", scatter_dimension=1, tiled=True
        ).astype(jnp.float32),
        lax.psum_scatter(
            d_time_w.astype(jnp.bfloat16), "dp", scatter_dimension=1, tiled=True
        ).astype(jnp.float32),
        lax.psum_scatter(
            d_shift_w.astype(jnp.bfloat16), "dp", scatter_dimension=1, tiled=True
        ).astype(jnp.float32),
        lax.psum_scatter(
            d_text_w.astype(jnp.bfloat16), "dp", scatter_dimension=1, tiled=True
        ).astype(jnp.float32),
    )
    return (
        prediction,
        latent_grad,
        skip_grad,
        text_grad,
        reduced[0],
        reduced[1],
        reduced[10],
        reduced[11],
        reduced[2],
        reduced[3],
        reduced[4],
        reduced[12],
        reduced[5],
        reduced[6],
        reduced[7],
        reduced[8],
        reduced[9],
    )


TILE = ("row", "col")
EVERY = ("dp", "row", "col")
LOG2E = math.log2(math.e)
F32 = jnp.float32
BF16 = jnp.bfloat16
VMEM_BYTES = 56 * 2**20


def kernel_call(body, flops, moved, **options):
    return pl.pallas_call(
        body,
        compiler_params=pltpu.CompilerParams(vmem_limit_bytes=VMEM_BYTES),
        cost_estimate=pl.CostEstimate(flops=flops, bytes_accessed=moved, transcendentals=0),
        **options,
    )


def pair_swap(values_in):
    quarter = values_in.shape[0] // 4
    parts = [values_in[at * quarter : (at + 1) * quarter] for at in (1, 0, 3, 2)]
    return jnp.concatenate(parts, axis=0)


def column_norm(values_in):
    centred = values_in - jnp.mean(values_in, axis=0, keepdims=True)
    inverse = lax.rsqrt(jnp.mean(centred * centred, axis=0, keepdims=True) + EPSILON)
    return (centred * inverse, inverse)


def column_norm_back(grad_normed, normed, inverse):
    mean_grad = jnp.mean(grad_normed, axis=0, keepdims=True)
    mean_cross = jnp.mean(grad_normed * normed, axis=0, keepdims=True)
    return inverse * (grad_normed - mean_grad - normed * mean_cross)


def minus_pieces(row_values):
    high = row_values.astype(BF16).astype(F32)
    rest = row_values - high
    middle = rest.astype(BF16).astype(F32)
    lower = rest - middle
    at = lax.broadcasted_iota(jnp.int32, (8, row_values.shape[1]), 0)
    zero = jnp.zeros((8, row_values.shape[1]), F32)
    picked = jnp.where(at == 0, high, jnp.where(at == 1, middle, jnp.where(at == 2, lower, zero)))
    return -picked


def piece_flags(width):
    return (lax.broadcasted_iota(jnp.int32, (8, width), 0) < 3).astype(F32)


def head_norm_body(
    query_scale, rows_ref, weight_ref, cos_ref, sin_ref, ok_ref, out_ref, inv_ref
):
    groups, _, heads, head_dim, _ = out_ref.shape
    part = pl.program_id(0)
    made = jnp.dot(rows_ref[...], weight_ref[...], preferred_element_type=F32).T
    valid = ok_ref[...]

    @pl.when(part < 2)
    def _():
        factor = jnp.where(part == 0, query_scale, valid)
        cosine, sine = cos_ref[...] * factor, sin_ref[...] * factor
        for group in range(groups):
            for head in range(heads):
                at = (group * heads + head) * head_dim
                normed, inverse = column_norm(made[at : at + head_dim])
                turned = normed * cosine + pair_swap(normed) * sine
                out_ref[group, 0, head] = turned.astype(BF16)
                inv_ref[group, 0, head : head + 1] = inverse

    @pl.when(part == 2)
    def _():
        for group in range(groups):
            for head in range(heads):
                at = (group * heads + head) * head_dim
                out_ref[group, 0, head] = (made[at : at + head_dim] * valid).astype(BF16)
                inv_ref[group, 0, head : head + 1] = valid


def head_norm(rows, weight, tables, valid, groups, head_dim, query_scale):
    tile_len, depth = rows.shape
    width = weight.shape[1] // 3
    heads = width // groups // head_dim
    table = pl.BlockSpec((head_dim, tile_len), lambda p: (0, 0))
    return kernel_call(
        functools.partial(head_norm_body, query_scale),
        6 * tile_len * depth * width,
        6 * depth * width,
        grid=(3,),
        in_specs=[
            pl.BlockSpec((tile_len, depth), lambda p: (0, 0)),
            pl.BlockSpec((depth, width), lambda p: (0, p)),
            table,
            table,
            pl.BlockSpec((1, tile_len), lambda p: (0, 0)),
        ],
        out_specs=[
            pl.BlockSpec((groups, 1, heads, head_dim, tile_len), lambda p: (0, p, 0, 0, 0)),
            pl.BlockSpec((groups, 1, heads, tile_len), lambda p: (0, p, 0, 0)),
        ],
        out_shape=[
            jax.ShapeDtypeStruct((groups, 3, heads, head_dim, tile_len), BF16),
            jax.ShapeDtypeStruct((groups, 3, heads, tile_len), F32),
        ],
    )(rows, weight, *tables, valid)


def head_back_body(
    query_scale, grad_ref, own_ref, inv_ref, cos_ref, sin_ref, ok_ref, *others
):
    out_ref = others[-1]
    heads, head_dim = own_ref.shape[2], own_ref.shape[3]
    cosine, sine, valid = cos_ref[...], sin_ref[...], ok_ref[...]

    def unturn(values_in):
        return values_in * cosine - pair_swap(values_in) * sine

    for part in range(3):
        pieces = []
        for head in range(heads):
            grad = grad_ref[0, part, head].astype(F32)
            if part > 0:
                grad = grad * valid
            if part < 2:
                normed = unturn(own_ref[0, part, head].astype(F32))
                if part == 0:
                    normed = normed * (1.0 / query_scale)
                inverse = inv_ref[0, part, head : head + 1]
                grad = column_norm_back(unturn(grad), normed, inverse)
            pieces.append(grad)
        out_ref[part, 0] = jnp.concatenate(pieces, axis=0).astype(BF16)


def head_back(grads, own, inverses, tables, valid, query_scale, image, images, before):
    groups, _, heads, head_dim, tile_len = own.shape
    group_rows = heads * head_dim
    stacked = pl.BlockSpec((1, 3, heads, head_dim, tile_len), lambda g: (g, 0, 0, 0, 0))
    table = pl.BlockSpec((head_dim, tile_len), lambda g: (0, 0))
    earlier = () if before is None else (before,)
    return kernel_call(
        functools.partial(head_back_body, query_scale),
        0,
        6 * own.size,
        grid=(groups,),
        in_specs=[
            stacked,
            stacked,
            pl.BlockSpec((1, 3, heads, tile_len), lambda g: (g, 0, 0, 0)),
            table,
            table,
            pl.BlockSpec((1, tile_len), lambda g: (0, 0)),
        ]
        + [pl.BlockSpec(memory_space=pl.ANY)] * len(earlier),
        out_specs=pl.BlockSpec((3, 1, group_rows, tile_len), lambda g: (0, g, 0, image)),
        out_shape=jax.ShapeDtypeStruct((3, groups, group_rows, images * tile_len), BF16),
        input_output_aliases={6: 0} if earlier else {},
    )(grads, own, inverses, *tables, valid, *earlier)


def attend_body(query_ref, key_ref, value_ref, ok_ref, out_ref, lse_ref, key_nat, value_ext):
    tiles, tile_len, head_dim = key_ref.shape[0], key_ref.shape[-1], key_ref.shape[-2]

    @pl.when(pl.program_id(1) == 0)
    def _():
        for tile in range(tiles):
            key_nat[tile * tile_len : (tile + 1) * tile_len, :] = key_ref[tile, 0, 0].T
            value_ext[tile] = jnp.concatenate(
                [value_ref[tile, 0, 0].astype(F32), ok_ref[tile]], axis=0
            ).astype(BF16)

    query = query_ref[0, 0, 0]
    total = jnp.zeros((head_dim + 8, tile_len), F32)
    held = None
    for tile in range(tiles + 1):
        scores = None
        if tile < tiles:
            rows = slice(tile * tile_len, (tile + 1) * tile_len)
            scores = jnp.dot(key_nat[rows, :], query, preferred_element_type=F32)
        if held is not None:
            weight = jnp.exp2(held).astype(BF16)
            total = total + jnp.dot(value_ext[tile - 1], weight, preferred_element_type=F32)
        held = scores
    weight_sum = total[head_dim : head_dim + 1]
    out_ref[0, 0] = (total[:head_dim] / weight_sum).astype(BF16)
    lse_ref[0, 0] = jnp.log2(weight_sum)


def attend(qkv, flags):
    tiles, _, heads, head_dim, tile_len = qkv.shape
    return kernel_call(
        attend_body,
        1024 * heads * tiles**2 * tile_len**2,
        8 * qkv.size,
        grid=(heads, tiles),
        in_specs=[
            pl.BlockSpec((1, 1, 1, head_dim, tile_len), lambda h, t: (t, 0, h, 0, 0)),
            pl.BlockSpec((tiles, 1, 1, head_dim, tile_len), lambda h, t: (0, 1, h, 0, 0)),
            pl.BlockSpec((tiles, 1, 1, head_dim, tile_len), lambda h, t: (0, 2, h, 0, 0)),
            pl.BlockSpec((tiles, 8, tile_len), lambda h, t: (0, 0, 0)),
        ],
        out_specs=[
            pl.BlockSpec((1, 1, head_dim, tile_len), lambda h, t: (t, h, 0, 0)),
            pl.BlockSpec((1, 1, 1, tile_len), lambda h, t: (t, h, 0, 0)),
        ],
        out_shape=[
            jax.ShapeDtypeStruct((tiles, heads, head_dim, tile_len), BF16),
            jax.ShapeDtypeStruct((tiles, heads, 1, tile_len), F32),
        ],
        scratch_shapes=[
            pltpu.VMEM((tiles * tile_len, head_dim), BF16),
            pltpu.VMEM((tiles, head_dim + 8, tile_len), BF16),
        ],
    )(qkv, qkv, qkv, flags)


def attend_back_body(
    score_scale,
    query_ref,
    key_ref,
    value_ref,
    grad_ref,
    att_ref,
    lse_ref,
    out_ref,
    key_nat,
    value_nat,
    key_sum,
    value_sum,
):
    tiles, tile_len, head_dim = key_ref.shape[0], key_ref.shape[-1], key_ref.shape[-2]
    at = pl.program_id(1)

    @pl.when(at == 0)
    def _():
        ones = piece_flags(tile_len)
        for tile in range(tiles):
            rows = slice(tile * tile_len, (tile + 1) * tile_len)
            for source, kept in ((key_ref, key_nat), (value_ref, value_nat)):
                wide = jnp.concatenate([source[tile, 0, 0].astype(F32), ones], axis=0)
                kept[rows, :] = wide.T.astype(BF16)
        key_sum[...] = jnp.zeros_like(key_sum)
        value_sum[...] = jnp.zeros_like(value_sum)

    query = query_ref[0, 0, 0].astype(F32)
    grad = grad_ref[0, 0].astype(F32)
    delta = jnp.sum(grad * att_ref[0, 0].astype(F32), axis=0, keepdims=True)
    query_ext = jnp.concatenate([query, minus_pieces(lse_ref[0, 0])], axis=0)
    grad_ext = jnp.concatenate([grad, minus_pieces(delta)], axis=0)
    query_cols, grad_cols = query_ext.astype(BF16), grad_ext.astype(BF16)
    query_nat, grad_nat = query_ext.T.astype(BF16), grad_ext.T.astype(BF16)

    def step(tile, total):
        rows = pl.ds(pl.multiple_of(tile * tile_len, tile_len), tile_len)
        scores = jnp.dot(key_nat[rows, :], query_cols, preferred_element_type=F32)
        probs = jnp.exp2(scores)
        grad_probs = jnp.dot(value_nat[rows, :], grad_cols, preferred_element_type=F32)
        grad_scores = (probs * grad_probs).astype(BF16)
        value_sum[rows, :] += jnp.dot(probs.astype(BF16), grad_nat, preferred_element_type=F32)
        key_sum[rows, :] += jnp.dot(grad_scores, query_nat, preferred_element_type=F32)
        return total + jnp.dot(key_ref[tile, 0, 0], grad_scores, preferred_element_type=F32)

    start = jnp.zeros((head_dim, tile_len), F32)
    total = lax.fori_loop(0, tiles, step, start, unroll=8)
    out_ref[at, 0, 0] = (total * score_scale).astype(BF16)

    @pl.when(at == tiles - 1)
    def _():
        for tile in range(tiles):
            rows = slice(tile * tile_len, (tile + 1) * tile_len)
            key_grad = key_sum[rows, :].T[:head_dim] * (1.0 / LOG2E)
            out_ref[tile, 1, 0] = key_grad.astype(BF16)
            out_ref[tile, 2, 0] = value_sum[rows, :].T[:head_dim].astype(BF16)


def attend_back(qkv, grad_att, att, lse, score_scale):
    tiles, _, heads, head_dim, tile_len = qkv.shape
    one = pl.BlockSpec((1, 1, head_dim, tile_len), lambda h, t: (t, h, 0, 0))
    return kernel_call(
        functools.partial(attend_back_body, score_scale),
        2560 * heads * tiles**2 * tile_len**2,
        8 * qkv.size,
        grid=(heads, tiles),
        in_specs=[
            pl.BlockSpec((1, 1, 1, head_dim, tile_len), lambda h, t: (t, 0, h, 0, 0)),
            pl.BlockSpec((tiles, 1, 1, head_dim, tile_len), lambda h, t: (0, 1, h, 0, 0)),
            pl.BlockSpec((tiles, 1, 1, head_dim, tile_len), lambda h, t: (0, 2, h, 0, 0)),
            one,
            one,
            pl.BlockSpec((1, 1, 1, tile_len), lambda h, t: (t, h, 0, 0)),
        ],
        out_specs=pl.BlockSpec(
            (tiles, 3, 1, head_dim, tile_len), lambda h, t: (0, 0, h, 0, 0)
        ),
        out_shape=jax.ShapeDtypeStruct(qkv.shape, BF16),
        scratch_shapes=[
            pltpu.VMEM((tiles * tile_len, head_dim + 8), BF16),
            pltpu.VMEM((tiles * tile_len, head_dim + 8), BF16),
            pltpu.VMEM((tiles * tile_len, head_dim + 8), F32),
            pltpu.VMEM((tiles * tile_len, head_dim + 8), F32),
        ],
    )(qkv, qkv, qkv, grad_att, att, lse)


def cross_body(text_len, query_scale, pre_ref, kv_ref, att_ref, query_ref, inv_ref, lse_ref):
    head_dim, text_pad = kv_ref.shape[2], kv_ref.shape[3]
    at = lax.broadcasted_iota(jnp.int32, (8, text_pad), 0)
    text_at = lax.broadcasted_iota(jnp.int32, (8, text_pad), 1)
    flags = ((at == 0) & (text_at < text_len)).astype(F32)
    for head in range(pre_ref.shape[0]):
        normed, inverse = column_norm(pre_ref[head])
        query = (normed * query_scale).astype(BF16)
        query_ref[head] = query
        inv_ref[head] = inverse
        key = column_norm(kv_ref[0, head])[0].astype(BF16)
        value_ext = jnp.concatenate([kv_ref[1, head], flags], axis=0).astype(BF16)
        scores = jnp.dot(key.T, query, preferred_element_type=F32)
        weight = jnp.exp2(scores).astype(BF16)
        total = jnp.dot(value_ext, weight, preferred_element_type=F32)
        weight_sum = total[head_dim : head_dim + 1]
        att_ref[head] = (total[:head_dim] / weight_sum).astype(BF16)
        lse_ref[head] = jnp.log2(weight_sum)


def cross_attend(pre, text_kv, images, text_len, query_scale):
    heads, head_dim, tokens = pre.shape
    tile_len, text_pad = tokens // images, text_kv.shape[3] // images
    block = math.gcd(heads, 4)
    wide = pl.BlockSpec((block, head_dim, tile_len), lambda i, h: (h, 0, i))
    row = pl.BlockSpec((block, 1, tile_len), lambda i, h: (h, 0, i))
    return kernel_call(
        functools.partial(cross_body, text_len, query_scale),
        1024 * heads * tokens * text_pad,
        8 * pre.size,
        grid=(images, heads // block),
        in_specs=[wide, pl.BlockSpec((2, block, head_dim, text_pad), lambda i, h: (0, h, 0, i))],
        out_specs=[wide, wide, row, row],
        out_shape=[
            jax.ShapeDtypeStruct(pre.shape, BF16),
            jax.ShapeDtypeStruct(pre.shape, BF16),
            jax.ShapeDtypeStruct((heads, 1, tokens), F32),
            jax.ShapeDtypeStruct((heads, 1, tokens), F32),
        ],
    )(pre, text_kv)


def cross_back_body(
    query_scale,
    score_scale,
    query_ref,
    kv_ref,
    grad_ref,
    att_ref,
    inv_ref,
    lse_ref,
    out_ref,
    key_ref,
    value_ref,
):
    head_dim, text_pad = kv_ref.shape[2], kv_ref.shape[3]
    ones = piece_flags(text_pad)
    for head in range(query_ref.shape[0]):
        query = query_ref[head].astype(F32)
        grad = grad_ref[head].astype(F32)
        delta = jnp.sum(grad * att_ref[head].astype(F32), axis=0, keepdims=True)
        query_ext = jnp.concatenate([query, minus_pieces(lse_ref[head])], axis=0).astype(BF16)
        grad_ext = jnp.concatenate([grad, minus_pieces(delta)], axis=0).astype(BF16)
        key = column_norm(kv_ref[0, head])[0].astype(BF16)
        key_ext = jnp.concatenate([key.astype(F32), ones], axis=0).T.astype(BF16)
        value_ext = jnp.concatenate([kv_ref[1, head], ones], axis=0).T.astype(BF16)
        probs = jnp.exp2(jnp.dot(key_ext, query_ext, preferred_element_type=F32))
        grad_probs = jnp.dot(value_ext, grad_ext, preferred_element_type=F32)
        grad_scores = (probs * grad_probs).astype(BF16)
        value_grad = right_dot(grad_ext, probs.astype(BF16))[:head_dim]
        key_grad = right_dot(query_ext, grad_scores)[:head_dim]
        key_ref[head] = (key_grad * (1.0 / LOG2E)).astype(BF16)
        value_ref[head] = value_grad.astype(BF16)
        query_grad = jnp.dot(key, grad_scores, preferred_element_type=F32) * score_scale
        normed = query * (1.0 / query_scale)
        out_ref[head] = column_norm_back(query_grad, normed, inv_ref[head]).astype(BF16)


def cross_back(query, text_kv, grad, att, inverse, lse, images, query_scale, score_scale):
    heads, head_dim, tokens = query.shape
    tile_len, text_pad = tokens // images, text_kv.shape[3] // images
    block = math.gcd(heads, 4)
    wide = pl.BlockSpec((block, head_dim, tile_len), lambda i, h: (h, 0, i))
    row = pl.BlockSpec((block, 1, tile_len), lambda i, h: (h, 0, i))
    text = pl.BlockSpec((2, block, head_dim, text_pad), lambda i, h: (0, h, 0, i))
    text_out = pl.BlockSpec((block, head_dim, text_pad), lambda i, h: (h, 0, i))
    return kernel_call(
        functools.partial(cross_back_body, query_scale, score_scale),
        2560 * heads * tokens * text_pad,
        16 * query.size,
        grid=(images, heads // block),
        in_specs=[wide, text, wide, wide, row, row],
        out_specs=[
            wide,
            text_out,
            text_out,
        ],
        out_shape=[
            jax.ShapeDtypeStruct(query.shape, BF16),
            jax.ShapeDtypeStruct((heads, head_dim, images * text_pad), BF16),
            jax.ShapeDtypeStruct((heads, head_dim, images * text_pad), BF16),
        ],
    )(query, text_kv, grad, att, inverse, lse)


def join_norm_body(patch_ref, skip_ref, weight_ref, gain_ref, bias_ref, z_ref, inv_ref, in_ref):
    width = skip_ref.shape[1]
    patch_feat = right_dot(patch_ref[...], weight_ref[...])
    joined = jnp.concatenate([patch_feat, skip_ref[...].astype(F32)], axis=1)
    normed, inverse = layer_norm(joined)
    z_ref[...] = normed
    inv_ref[...] = inverse
    in_ref[...] = (normed * gain_ref[...] + bias_ref[...]).astype(BF16)


def join_norm(patch_rows, skip_rows, f_patch, gain, bias):
    tokens, width = skip_rows.shape
    block = math.gcd(tokens, 256)
    rows = lambda columns: pl.BlockSpec((block, columns), lambda t: (t, 0))
    fixed = lambda shape: pl.BlockSpec(shape, lambda t: (0, 0))
    return kernel_call(
        join_norm_body,
        64 * tokens * width,
        16 * tokens * width,
        grid=(tokens // block,),
        in_specs=[
            rows(patch_rows.shape[1]),
            rows(width),
            fixed(f_patch.shape),
            fixed(gain.shape),
            fixed(bias.shape),
        ],
        out_specs=[rows(2 * width), rows(1), rows(2 * width)],
        out_shape=[
            jax.ShapeDtypeStruct((tokens, 2 * width), F32),
            jax.ShapeDtypeStruct((tokens, 1), F32),
            jax.ShapeDtypeStruct((tokens, 2 * width), BF16),
        ],
    )(patch_rows, skip_rows, f_patch, gain, bias)


def join_back_body(low_ref, weight_ref, z_ref, inv_ref, gain_ref, skip_ref, patch_ref, sums_ref):
    width = skip_ref.shape[1]
    grad, normed = right_dot(low_ref[...], weight_ref[...]), z_ref[...]

    @pl.when(pl.program_id(0) == 0)
    def _():
        sums_ref[...] = jnp.zeros_like(sums_ref)

    sums_ref[0:1] += jnp.sum(grad * normed, axis=0, keepdims=True)
    sums_ref[1:2] += jnp.sum(grad, axis=0, keepdims=True)
    back = norm_back(grad * gain_ref[...], normed, inv_ref[...])
    patch_ref[...] = back[:, :width].astype(BF16)
    skip_ref[...] = back[:, width:]


def join_back(low_rows, f_skip, normed, inverse, gain):
    tokens, width = low_rows.shape
    block = math.gcd(tokens, 256)
    rows = lambda columns: pl.BlockSpec((block, columns), lambda t: (t, 0))
    fixed = lambda shape: pl.BlockSpec(shape, lambda t: (0, 0))
    return kernel_call(
        join_back_body,
        4 * tokens * width * width,
        18 * tokens * width,
        grid=(tokens // block,),
        in_specs=[rows(width), fixed(f_skip.shape), rows(2 * width), rows(1), fixed(gain.shape)],
        out_specs=[rows(width), rows(width), fixed((2, 2 * width))],
        out_shape=[
            jax.ShapeDtypeStruct((tokens, width), F32),
            jax.ShapeDtypeStruct((tokens, width), BF16),
            jax.ShapeDtypeStruct((2, 2 * width), F32),
        ],
    )(low_rows, f_skip, normed, inverse, gain)


def gelu_and_slope(inputs):
    scale, cubic = math.sqrt(2.0 / math.pi), 0.044715
    square = inputs * inputs
    curve = jnp.tanh(scale * inputs * (1.0 + cubic * square))
    half = 0.5 * (1.0 + curve)
    bend = 0.5 * inputs * (1.0 - curve * curve) * (scale * (1.0 + 3.0 * cubic * square))
    return ((inputs * half).astype(BF16), (half + bend).astype(BF16))


def swap_tiles(values_in):
    return lax.all_to_all(values_in, TILE, split_axis=0, concat_axis=0, tiled=True)


def shift_pairs(devices, step):
    return [(at, (at + step) % devices) for at in range(devices)]


def fetch(weight):
    devices = lax.axis_size("dp")
    return [weight] + [
        lax.ppermute(weight, "dp", shift_pairs(devices, step)) for step in range(1, devices)
    ]


def widen(pieces, first=None, joined=1):
    devices, me = lax.axis_size("dp"), lax.axis_index("dp")
    if first is not None:
        pieces = after(first, *pieces)
    slots = [lax.select_n((me - at) % devices, *pieces) for at in range(devices)]
    if joined > 1:
        split = [jnp.split(slot, joined, axis=1) for slot in slots]
        slots = [each for group in zip(*split) for each in group]
    return jnp.concatenate(slots, axis=1)


def narrow_blocks(blocks, first=None):
    devices, me = lax.axis_size("dp"), lax.axis_index("dp")
    received = []
    for step in range(1, devices):
        sent = lax.select_n((me + step) % devices, *blocks)
        received.append(lax.ppermute(sent, "dp", shift_pairs(devices, step)))
    if first is not None:
        received = after(first, *received)
    total = lax.select_n(me, *blocks).astype(F32)
    for piece in received:
        total = total + piece.astype(F32)
    return total


def narrow(weight_grad, first=None):
    return narrow_blocks(jnp.split(weight_grad, lax.axis_size("dp"), axis=1), first)


def by_device(weight_grads, parts):
    devices = lax.axis_size("dp")
    split = [jnp.split(weight_grad, devices, axis=1) for weight_grad in weight_grads]
    return [jnp.concatenate(blocks, axis=parts) for blocks in zip(*split)]


def sum_tiles(part_sums):
    devices, me = lax.axis_size(TILE), lax.axis_index(TILE)
    total, step = part_sums, devices // 2
    while step > 0:
        pairs = [(at, at ^ step) for at in range(devices)]
        lower, upper = jnp.split(total, 2, axis=0)
        high = (me // step) % 2 == 1
        sent = jnp.where(high, lower, upper)
        total = jnp.where(high, upper, lower) + lax.ppermute(sent, TILE, pairs)
        step //= 2
    return total


def total_tiles(part_sum):
    devices = lax.axis_size(TILE)
    total, step = part_sum, 1
    while step < devices:
        pairs = [(at, at ^ step) for at in range(devices)]
        total = total + lax.ppermute(total, TILE, pairs)
        step *= 2
    return total


def over_tiles(weight_grad):
    return lax.optimization_barrier(
        lax.psum_scatter(weight_grad, TILE, scatter_dimension=0, tiled=True)
    )


def tiles_whole(weight):
    return lax.all_gather(weight, TILE, axis=0, tiled=True)


def after(first, *values_in):
    return lax.optimization_barrier((first, *values_in))[1:]


def dot_over(left_mat, right_mat, left_axis, right_axis):
    return lax.dot_general(
        left_mat,
        right_mat,
        (((left_axis,), (right_axis,)), ((), ())),
        preferred_element_type=F32,
    )


def local_heads(
    latent,
    skip_input,
    text_states,
    timesteps,
    image_sides,
    cotangent,
    w_patch,
    w_skip,
    w_time,
    w_shift,
    w_qkv,
    w_out,
    w_query,
    w_text,
    w_cross,
    w_up,
    w_down,
    w_final,
    norm_params,
):
    dp_devices = lax.axis_size("dp")
    grid_devices = lax.axis_size(TILE)
    col_devices = lax.axis_size("col")
    grid_at = lax.axis_index(TILE)
    row_at = lax.axis_index("row")
    col_at = lax.axis_index("col")
    images, rows_tile, cols_tile, patch_width = latent.shape
    tile_len = rows_tile * cols_tile
    row_count = images * tile_len
    out_width = cotangent.shape[3]

    f_skip = tiles_whole(widen(fetch(w_skip)))
    small = jnp.concatenate([w_patch, w_final, norm_params], axis=1)
    small_widths = (w_patch.shape[1], w_final.shape[1], norm_params.shape[1])
    cuts = (0, small_widths[0], sum(small_widths[:2]), sum(small_widths))
    early = [jnp.pad(small, ((0, 0), (0, w_shift.shape[1] - small.shape[1]))), w_time, w_shift]
    ends = (small.shape[0], small.shape[0] + w_time.shape[0])
    part_small, part_time, part_shift_w = jnp.split(
        widen(fetch(jnp.concatenate(early, axis=0))), ends, axis=0
    )
    part_small = part_small.reshape(small.shape[0], dp_devices, -1)[:, :, : small.shape[1]]
    part_small = part_small.reshape(small.shape[0], -1)
    f_small = tiles_whole(part_small).reshape(-1, dp_devices, sum(small_widths))
    f_patch, f_final, f_norms = (
        f_small[:, :, cuts[at] : cuts[at + 1]].reshape(f_small.shape[0], -1) for at in range(3)
    )
    held_qkv = fetch(w_qkv)
    held_three = fetch(jnp.concatenate([w_out, w_query, w_cross], axis=1))
    held_text = fetch(w_text)
    held_up, held_down = fetch(w_up), fetch(w_down)
    model_width = skip_input.shape[3]
    head_count = HEADS
    head_dim = model_width // head_count
    text_len = text_states.shape[1]
    text_pad = -(-text_len // 128) * 128
    score_scale = head_dim ** (-0.5)
    query_scale = score_scale * LOG2E
    positions = jnp.arange(tile_len, dtype=jnp.int32)
    row_pos = row_at * rows_tile + positions // cols_tile
    col_pos = col_at * cols_tile + positions % cols_tile
    query_ok = (row_pos[None, :] < image_sides[:, None]) & (col_pos[None, :] < image_sides[:, None])
    valid = query_ok.astype(F32)
    keep_rows = query_ok.astype(F32).reshape(row_count, 1)
    tile_list = jnp.arange(grid_devices, dtype=jnp.int32)[:, None]
    key_row = tile_list // col_devices * rows_tile + (positions // cols_tile)[None, :]
    key_col = tile_list % col_devices * cols_tile + (positions % cols_tile)[None, :]
    sides = image_sides[:, None, None]
    key_ok = ((key_row[None] < sides) & (key_col[None] < sides)).astype(F32)
    flags = jnp.concatenate(
        [key_ok[:, :, None, :], jnp.zeros((images, grid_devices, 7, tile_len), F32)], axis=2
    )
    cos_row, sin_row, cos_col, sin_col = (
        jnp.transpose(table[:, 0, :]) for table in rope_tables(row_pos, col_pos, head_dim)
    )
    tables = (
        jnp.concatenate([cos_row, cos_row, cos_col, cos_col], axis=0),
        jnp.concatenate([-sin_row, sin_row, -sin_col, sin_col], axis=0),
    )
    norm_f = f_norms.astype(F32)

    embedding = time_embed(timesteps, FREQ).astype(BF16)
    freq_slice = part_time.shape[0]
    shift_slice = part_shift_w.shape[0]
    embed_cols = lax.dynamic_slice_in_dim(embedding, grid_at * freq_slice, freq_slice, 1)
    time_pre = total_tiles(plain_dot(embed_cols, part_time))
    time_float, silu_pull = jax.vjp(jax.nn.silu, time_pre)
    time_act = time_float.astype(BF16)
    act_cols = lax.dynamic_slice_in_dim(time_act, grid_at * shift_slice, shift_slice, 1)
    time_shift = total_tiles(plain_dot(act_cols, part_shift_w))

    patch_rows = latent.reshape(row_count, patch_width)
    skip_rows = skip_input.reshape(row_count, model_width)
    gain_skip = jnp.concatenate([norm_f[:, 8], norm_f[:, 10]])[None]
    bias_skip = jnp.concatenate([norm_f[:, 9], norm_f[:, 11]])[None]
    joined, joined_inv, skip_in = join_norm(patch_rows, skip_rows, f_patch, gain_skip, bias_skip)
    f_qkv = tiles_whole(widen(held_qkv, skip_in))
    residual = plain_dot(skip_in, f_skip)
    first_z, first_inv = layer_norm(residual)
    first_pre = (first_z * norm_f[:, 0] + norm_f[:, 1]).reshape(
        images, tile_len, model_width
    ) + time_shift[:, None, :]
    first_in = first_pre.reshape(row_count, model_width).astype(BF16)
    f_three = tiles_whole(widen(held_three, first_in, 3))
    f_out, f_query, f_cross = jnp.split(f_three, 3, axis=1)
    part_text = widen(held_text, first_in)
    f_text = tiles_whole(part_text)
    first_rows = first_in.reshape(images, tile_len, model_width)
    own_qkv, qk_inv, tile_qkv, tile_att, tile_lse, att_rows = [], [], [], [], [], []
    for image in range(images):
        rows = first_rows[image]
        own, inverses = head_norm(
            rows,
            f_qkv,
            tables,
            valid[image : image + 1],
            grid_devices,
            head_dim,
            query_scale,
        )
        own_qkv.append(own)
        qk_inv.append(inverses)
        tile_qkv.append(swap_tiles(own))
    tile_qkv[0], own_qkv[-1] = lax.optimization_barrier((tile_qkv[0], own_qkv[-1]))
    f_up = tiles_whole(widen(held_up, tile_qkv[0]))
    for image in range(images):
        att, lse = attend(tile_qkv[image], flags[image])
        tile_att.append(att)
        tile_lse.append(lse)
        own_att = swap_tiles(att).reshape(model_width, tile_len)
        att_rows.append(jnp.transpose(own_att))
    att_low = jnp.concatenate(att_rows, axis=0)
    residual_two = residual + plain_dot(att_low, f_out)
    f_down = tiles_whole(widen(held_down, residual_two))

    third_z, third_inv = layer_norm(residual_two)
    third_in = (third_z * norm_f[:, 2] + norm_f[:, 3]).astype(BF16)
    cross_pre = dot_over(f_query, third_in, 0, 1).reshape(head_count, head_dim, row_count)
    text_rows = jnp.pad(text_states, ((0, 0), (0, text_pad - text_len), (0, 0)))
    text_rows = text_rows.reshape(images * text_pad, -1)
    text_kv = dot_over(f_text, text_rows, 0, 1).reshape(2, head_count, head_dim, images * text_pad)
    crossed, cross_queries, cq_inv, cross_lse = cross_attend(
        cross_pre, text_kv, images, text_len, query_scale
    )
    cross_cols = crossed.reshape(model_width, row_count)
    residual_three = residual_two + left_dot(cross_cols, f_cross)
    second_z, second_inv = layer_norm(residual_three)
    second_in = (second_z * norm_f[:, 4] + norm_f[:, 5]).astype(BF16)
    up_pre = plain_dot(second_in, f_up)
    hidden_act, slope = lax.optimization_barrier(gelu_and_slope(up_pre))
    residual_four = residual_three + plain_dot(hidden_act, f_down)
    last_z, last_inv = layer_norm(residual_four)
    last_in = (last_z * norm_f[:, 6] + norm_f[:, 7]).astype(BF16)
    produced = plain_dot(last_in, f_final)
    prediction = (
        (produced * keep_rows).astype(BF16).reshape(images, rows_tile, cols_tile, out_width)
    )

    grad_out = (cotangent.reshape(row_count, out_width).astype(F32) * keep_rows).astype(BF16)
    d_final = left_dot(last_in, grad_out)
    grad_last = right_dot(grad_out, f_final)
    gain_final = jnp.sum(grad_last * last_z, axis=0)
    bias_final = jnp.sum(grad_last, axis=0)
    grad_four = norm_back(grad_last * norm_f[:, 6], last_z, last_inv)
    low_four = grad_four.astype(BF16)
    d_down = left_dot(hidden_act, low_four).astype(BF16)
    d_down, low_four = lax.optimization_barrier((d_down, low_four))
    t_down = over_tiles(d_down)
    grad_hidden = right_dot(low_four, f_down)
    grad_up = (grad_hidden * slope).astype(BF16)
    d_up = left_dot(second_in, grad_up).astype(BF16)
    d_up, grad_up = lax.optimization_barrier((d_up, grad_up))
    t_up = over_tiles(d_up)
    grad_second = right_dot(grad_up, f_up)
    gain_second = jnp.sum(grad_second * second_z, axis=0)
    bias_second = jnp.sum(grad_second, axis=0)
    grad_three = grad_four + norm_back(grad_second * norm_f[:, 4], second_z, second_inv)
    low_three = grad_three.astype(BF16)
    d_cross = plain_dot(cross_cols, low_three).astype(BF16)
    grad_crossed = dot_over(f_cross, low_three, 1, 1).astype(BF16)
    grad_cross_q, d_text_key, d_text_value = cross_back(
        cross_queries,
        text_kv,
        grad_crossed.reshape(head_count, head_dim, row_count),
        crossed,
        cq_inv,
        cross_lse,
        images,
        query_scale,
        score_scale,
    )
    t_down, grad_cross_q = lax.optimization_barrier((t_down, grad_cross_q))
    grad_cross_q = grad_cross_q.reshape(model_width, row_count)
    d_query = dot_over(third_in, grad_cross_q, 0, 1).astype(BF16)
    grad_third = dot_over(grad_cross_q, f_query, 0, 1)
    gain_third = jnp.sum(grad_third * third_z, axis=0)
    bias_third = jnp.sum(grad_third, axis=0)
    grad_two = grad_three + norm_back(grad_third * norm_f[:, 2], third_z, third_inv)
    low_two = grad_two.astype(BF16)
    low_two_rows = low_two.reshape(images, tile_len, model_width)
    tile_grads = []
    for image in range(images):
        grad_att = dot_over(f_out, low_two_rows[image], 1, 1).astype(BF16)
        tile_grads.append(swap_tiles(grad_att.reshape(tile_att[image].shape)))
    d_out = left_dot(att_low, low_two).astype(BF16)
    d_joint = jnp.concatenate(
        [
            d_out,
            d_query,
            d_cross,
            d_text_key.reshape(model_width, -1),
            d_text_value.reshape(model_width, -1),
        ],
        axis=1,
    )
    d_joint = with_layout_constraint(d_joint, Layout(major_to_minor=(0, 1)))
    d_joint, tile_grads[0] = lax.optimization_barrier((d_joint, tile_grads[0]))
    t_joint = over_tiles(d_joint)
    own_grads, grad_qkv, tile_back = [], None, None
    for image in range(images):
        if tile_back is not None:
            down_grad = narrow(t_down, tile_back)
            down_grad, tile_grads[image], tile_back = lax.optimization_barrier(
                (down_grad, tile_grads[image], tile_back)
            )
            own_grads.append(swap_tiles(tile_back))
        tile_back = attend_back(
            tile_qkv[image], tile_grads[image], tile_att[image], tile_lse[image], score_scale
        )
    own_grads.append(swap_tiles(tile_back))
    for image in range(images):
        if image == images - 1:
            up_grad = narrow(t_up, tile_back)
            up_grad, own_grads[-1], grad_qkv = lax.optimization_barrier(
                (up_grad, own_grads[-1], grad_qkv)
            )
        grad_qkv = head_back(
            own_grads[image],
            own_qkv[image],
            qk_inv[image],
            tables,
            valid[image : image + 1],
            query_scale,
            image,
            images,
            grad_qkv,
        )
    sum_text_kv = t_joint[:, 3 * model_width :].astype(F32)
    sum_text_kv = jnp.transpose(
        sum_text_kv.reshape(-1, head_dim, 2, images * text_pad), (2, 0, 1, 3)
    )
    group_heads = head_count // grid_devices
    own_key = lax.dynamic_slice_in_dim(text_kv[0], grid_at * group_heads, group_heads, 0)
    ck_z, ck_inv = layer_norm(jnp.swapaxes(own_key, 1, 2))
    grad_ckey = jnp.swapaxes(norm_back(jnp.swapaxes(sum_text_kv[0], 1, 2), ck_z, ck_inv), 1, 2)
    grad_kv = jnp.stack([grad_ckey, sum_text_kv[1]]).astype(BF16)
    grad_kv = grad_kv.reshape(-1, images * text_pad)
    grad_qkv = grad_qkv.reshape(3 * model_width, row_count)
    d_qkv = dot_over(first_in, grad_qkv, 0, 1).astype(BF16)
    d_qkv, grad_qkv = lax.optimization_barrier((d_qkv, grad_qkv))
    t_qkv = over_tiles(d_qkv)
    grad_first = dot_over(grad_qkv, f_qkv, 0, 1)
    joint_blocks = by_device(jnp.split(t_joint[:, : 3 * model_width], 3, axis=1), 1)
    joint_grad = narrow_blocks(joint_blocks, grad_first)
    gain_first = jnp.sum(grad_first * first_z, axis=0)
    bias_first = jnp.sum(grad_first, axis=0)
    part_shift = jnp.sum(grad_first.reshape(images, tile_len, model_width), axis=1)
    grad_one = grad_two + norm_back(grad_first * norm_f[:, 0], first_z, first_inv)

    low_one = grad_one.astype(BF16)
    d_skip_w = left_dot(skip_in, low_one).astype(BF16)
    d_skip_w, low_one = lax.optimization_barrier((d_skip_w, low_one))
    skip_grad, grad_patch, skip_sums = join_back(low_one, f_skip, joined, joined_inv, gain_skip)
    t_qkv, d_skip_w, joint_grad = lax.optimization_barrier((t_qkv, d_skip_w, joint_grad))
    out_grad, query_w_grad, cross_grad = jnp.split(joint_grad, 3, axis=1)
    t_skip = over_tiles(d_skip_w)

    text_slice = text_states.shape[2] // grid_devices
    own_cols = lax.dynamic_slice_in_dim(
        f_text.reshape(f_text.shape[0], 2, -1), grid_at * group_heads * head_dim, group_heads * head_dim, 2
    ).reshape(f_text.shape[0], -1)
    text_parts = jnp.concatenate(
        [dot_over(text_rows, grad_kv, 0, 1).astype(BF16), plain_dot(own_cols, grad_kv).astype(BF16)],
        axis=1,
    )
    text_parts = swap_tiles(text_parts.reshape(grid_devices, text_slice, -1))
    own_width = own_cols.shape[1]
    d_text = text_parts[:, :, :own_width].reshape(grid_devices, text_slice, 2, -1)
    d_text = jnp.transpose(d_text, (1, 2, 0, 3)).reshape(text_slice, -1)
    text_grad = jnp.sum(text_parts[:, :, own_width:].astype(F32), axis=0)
    text_grad = jnp.transpose(text_grad).reshape(images, text_pad, text_slice)
    text_grad = text_grad[:, :text_len]

    shift_low = total_tiles(part_shift).astype(BF16)
    d_shift = left_dot(act_cols, shift_low).astype(BF16)
    grad_time_act = total_tiles(
        lax.dynamic_update_slice_in_dim(
            jnp.zeros_like(time_pre), right_dot(shift_low, part_shift_w), grid_at * shift_slice, 1
        )
    )
    grad_time_pre = silu_pull(grad_time_act)[0].astype(BF16)
    d_time = left_dot(embed_cols, grad_time_pre).astype(BF16)
    skip_grad = skip_grad.reshape(images, rows_tile, cols_tile, model_width)
    gain_skips, bias_skips = skip_sums[0], skip_sums[1]
    d_patch = left_dot(grad_patch, patch_rows)
    latent_grad = plain_dot(grad_patch, f_patch).reshape(images, rows_tile, cols_tile, patch_width)
    d_norms = jnp.stack(
        [
            gain_first,
            bias_first,
            gain_third,
            bias_third,
            gain_second,
            bias_second,
            gain_final,
            bias_final,
            gain_skips[:model_width],
            bias_skips[:model_width],
            gain_skips[model_width:],
            bias_skips[model_width:],
        ],
        axis=1,
    )
    small_grads = jnp.concatenate(
        [
            grad.reshape(model_width, dp_devices, -1)
            for grad in (d_patch, d_final, d_norms)
        ],
        axis=2,
    )
    small_grads = sum_tiles(small_grads.reshape(model_width, -1))
    late, width = [], w_shift.shape[1]
    small_width = sum(small_widths)
    for at in range(dp_devices):
        pair = d_text[:, 2 * at * width : 2 * (at + 1) * width]
        own = slice(at * width, (at + 1) * width)
        few = small_grads[:, at * small_width : (at + 1) * small_width].astype(BF16)
        few = jnp.pad(few, ((0, 0), (0, width - small_width)))
        late.append(
            jnp.concatenate([pair[:, :width], pair[:, width:], d_time[:, own], d_shift[:, own], few])
        )
    qkv_grad = narrow(t_qkv, d_text)
    qkv_grad, *late = lax.optimization_barrier((qkv_grad, *late))
    late = narrow_blocks(late)
    rows = d_text.shape[0]
    text_w_grad = jnp.concatenate([late[:rows], late[rows : 2 * rows]], axis=1)
    ends = (d_time.shape[0], d_time.shape[0] + d_shift.shape[0])
    time_w_grad, shift_w_grad, few = jnp.split(late[2 * rows :], ends, axis=0)
    skip_w_grad = narrow(t_skip)
    patch_grad, final_grad, norms_grad = (few[:, cuts[at] : cuts[at + 1]] for at in range(3))
    return (
        prediction,
        latent_grad,
        skip_grad,
        text_grad,
        patch_grad,
        skip_w_grad,
        time_w_grad,
        shift_w_grad,
        qkv_grad,
        out_grad,
        query_w_grad,
        text_w_grad,
        cross_grad,
        up_grad,
        down_grad,
        final_grad,
        norms_grad,
    )


def local(sizes, latent, *others):
    grid_devices = sizes["row"] * sizes["col"]
    tile_len = latent.shape[1] * latent.shape[2]
    if HEADS % grid_devices == 0 and tile_len % 128 == 0:
        return local_heads(latent, *others)
    return local_gathered(latent, *others)


def solution(mesh):
    return jax.shard_map(
        functools.partial(local, mesh.shape),
        mesh=mesh,
        in_specs=(
            P("dp", "row", "col", None),
            P("dp", "row", "col", None),
            P("dp", None, None),
            P("dp"),
            P("dp"),
            P("dp", "row", "col", None),
            P(("row", "col"), "dp"),
            P(("row", "col"), "dp"),
            P(("row", "col"), "dp"),
            P(("row", "col"), "dp"),
            P(("row", "col"), "dp"),
            P(("row", "col"), "dp"),
            P(("row", "col"), "dp"),
            P(("row", "col"), "dp"),
            P(("row", "col"), "dp"),
            P(("row", "col"), "dp"),
            P(("row", "col"), "dp"),
            P(("row", "col"), "dp"),
            P(("row", "col"), "dp"),
        ),
        out_specs=(
            P("dp", "row", "col", None),
            P("dp", "row", "col", None),
            P("dp", "row", "col", None),
            P("dp", None, ("row", "col")),
            P(("row", "col"), "dp"),
            P(("row", "col"), "dp"),
            P(("row", "col"), "dp"),
            P(("row", "col"), "dp"),
            P(("row", "col"), "dp"),
            P(("row", "col"), "dp"),
            P(("row", "col"), "dp"),
            P(("row", "col"), "dp"),
            P(("row", "col"), "dp"),
            P(("row", "col"), "dp"),
            P(("row", "col"), "dp"),
            P(("row", "col"), "dp"),
            P(("row", "col"), "dp"),
        ),
        check_vma=False,
    )
```

```python
import functools
import math

import jax
import jax.numpy as jnp
from jax import lax
from jax.experimental import pallas as pl
from jax.experimental.layout import Layout, with_layout_constraint
from jax.experimental.pallas import tpu as pltpu
from jax.sharding import PartitionSpec as P

HEADS = 16
FREQ = 256


EPSILON = 1e-06


def layer_norm(values_in):
    centred = values_in - jnp.mean(values_in, axis=-1, keepdims=True)
    inverse = lax.rsqrt(jnp.mean(centred * centred, axis=-1, keepdims=True) + EPSILON)
    return (centred * inverse, inverse)


def norm_back(grad_normed, normed, inverse):
    mean_grad = jnp.mean(grad_normed, axis=-1, keepdims=True)
    mean_cross = jnp.mean(grad_normed * normed, axis=-1, keepdims=True)
    return inverse * (grad_normed - mean_grad - normed * mean_cross)


def turn_half(piece_half, cosine, sine_tab):
    quarter = cosine.shape[-1]
    lower = piece_half[..., :quarter]
    higher = piece_half[..., quarter:]
    return jnp.concatenate(
        [lower * cosine - higher * sine_tab, higher * cosine + lower * sine_tab], axis=-1
    )


def rotate(values_in, tables, signum):
    cos_row, sin_row, cos_col, sin_col = tables
    half_dim = values_in.shape[-1] // 2
    return jnp.concatenate(
        [
            turn_half(values_in[..., :half_dim], cos_row, signum * sin_row),
            turn_half(values_in[..., half_dim:], cos_col, signum * sin_col),
        ],
        axis=-1,
    )


def rope_tables(row_pos, col_pos, head_size):
    quarter = head_size // 4
    frequency = jnp.exp(jnp.arange(quarter, dtype=jnp.float32) * (-math.log(10000.0) / quarter))
    row_ang = row_pos.astype(jnp.float32)[:, None, None] * frequency
    col_ang = col_pos.astype(jnp.float32)[:, None, None] * frequency
    return (jnp.cos(row_ang), jnp.sin(row_ang), jnp.cos(col_ang), jnp.sin(col_ang))


def time_embed(step_values, freq_count):
    half_dim = freq_count // 2
    rate_list = jnp.exp(jnp.arange(half_dim, dtype=jnp.float32) * (-math.log(10000.0) / half_dim))
    angles = step_values.astype(jnp.float32)[..., None] * rate_list
    return jnp.concatenate([jnp.cos(angles), jnp.sin(angles)], axis=-1)


def gelu_tanh(inputs):
    return jax.nn.gelu(inputs, approximate=True)


def plain_dot(left_mat, right_mat):
    return jnp.dot(left_mat, right_mat, preferred_element_type=jnp.float32)


def left_dot(left_mat, right_mat):
    return lax.dot_general(
        left_mat, right_mat, (((0,), (0,)), ((), ())), preferred_element_type=jnp.float32
    )


def right_dot(left_mat, right_mat):
    return lax.dot_general(
        left_mat, right_mat, (((1,), (1,)), ((), ())), preferred_element_type=jnp.float32
    )


def block_size(key_count):
    block_len = key_count
    while block_len > 1024 and block_len % 2 == 0:
        block_len = block_len // 2
    return block_len


def local_gathered(
    latent,
    skip_input,
    text_states,
    timesteps,
    image_sides,
    cotangent,
    w_patch,
    w_skip,
    w_time,
    w_shift,
    w_qkv,
    w_out,
    w_query,
    w_text,
    w_cross,
    w_up,
    w_down,
    w_final,
    norm_params,
):
    widened = (
        lax.all_gather(w_patch, "dp", axis=1, tiled=True),
        lax.all_gather(w_skip, "dp", axis=1, tiled=True),
        lax.all_gather(w_time, "dp", axis=1, tiled=True),
        lax.all_gather(w_shift, "dp", axis=1, tiled=True),
        lax.all_gather(w_qkv, "dp", axis=1, tiled=True),
        lax.all_gather(w_out, "dp", axis=1, tiled=True),
        lax.all_gather(w_query, "dp", axis=1, tiled=True),
        lax.all_gather(w_text, "dp", axis=1, tiled=True),
        lax.all_gather(w_cross, "dp", axis=1, tiled=True),
        lax.all_gather(w_up, "dp", axis=1, tiled=True),
        lax.all_gather(w_down, "dp", axis=1, tiled=True),
        lax.all_gather(w_final, "dp", axis=1, tiled=True),
        lax.all_gather(norm_params, "dp", axis=1, tiled=True),
    )
    gathered = (
        lax.all_gather(widened[0], ("row", "col"), axis=0, tiled=True),
        lax.all_gather(widened[1], ("row", "col"), axis=0, tiled=True),
        lax.all_gather(widened[2], ("row", "col"), axis=0, tiled=True),
        lax.all_gather(widened[3], ("row", "col"), axis=0, tiled=True),
        lax.all_gather(widened[4], ("row", "col"), axis=0, tiled=True),
        lax.all_gather(widened[5], ("row", "col"), axis=0, tiled=True),
        lax.all_gather(widened[6], ("row", "col"), axis=0, tiled=True),
        lax.all_gather(widened[7], ("row", "col"), axis=0, tiled=True),
        lax.all_gather(widened[8], ("row", "col"), axis=0, tiled=True),
        lax.all_gather(widened[9], ("row", "col"), axis=0, tiled=True),
        lax.all_gather(widened[10], ("row", "col"), axis=0, tiled=True),
        lax.all_gather(widened[11], ("row", "col"), axis=0, tiled=True),
        lax.all_gather(widened[12], ("row", "col"), axis=0, tiled=True),
    )
    (
        f_patch,
        f_skip,
        f_time,
        f_shift,
        f_qkv,
        f_out,
        f_query,
        f_text,
        f_cross,
        f_up,
        f_down,
        f_final,
        f_norms,
    ) = gathered
    part_text = widened[7]
    images, rows_tile, cols_tile, patch_width = latent.shape
    tile_len = rows_tile * cols_tile
    row_count = images * tile_len
    model_width = f_qkv.shape[0]
    head_count = HEADS
    head_dim = model_width // head_count
    text_len = text_states.shape[1]
    grid_devices = lax.axis_size(("row", "col"))
    col_devices = lax.axis_size("col")
    grid_at = lax.axis_index(("row", "col"))
    row_at = lax.axis_index("row")
    col_at = lax.axis_index("col")
    score_scale = head_dim ** (-0.5)
    positions = jnp.arange(tile_len, dtype=jnp.int32)
    row_pos = row_at * rows_tile + positions // cols_tile
    col_pos = col_at * cols_tile + positions % cols_tile
    query_ok = (row_pos[None, :] < image_sides[:, None]) & (col_pos[None, :] < image_sides[:, None])
    keep_rows = query_ok.astype(jnp.float32).reshape(row_count, 1)
    tables = rope_tables(row_pos, col_pos, head_dim)
    norm_f = f_norms.astype(jnp.float32)

    def valid_keys(offset, block_len):
        index_list = offset + jnp.arange(block_len, dtype=jnp.int32)
        source = index_list // tile_len
        within = index_list % tile_len
        key_row = source // col_devices * rows_tile + within // cols_tile
        key_col = source % col_devices * cols_tile + within % cols_tile
        return (key_row[None, :] < image_sides[:, None]) & (key_col[None, :] < image_sides[:, None])

    patch_rows = latent.reshape(row_count, patch_width)
    patch_feat = right_dot(patch_rows, f_patch)
    skip_rows = skip_input.reshape(row_count, model_width).astype(jnp.float32)
    gain_skip = jnp.concatenate([norm_f[:, 8], norm_f[:, 10]])
    bias_skip = jnp.concatenate([norm_f[:, 9], norm_f[:, 11]])
    joined, joined_inv = layer_norm(jnp.concatenate([patch_feat, skip_rows], axis=-1))
    skip_in = (joined * gain_skip + bias_skip).astype(jnp.bfloat16)
    residual = plain_dot(skip_in, f_skip)
    embedding = time_embed(timesteps, FREQ).astype(jnp.bfloat16)
    time_pre = plain_dot(embedding, f_time)
    time_float, silu_pull = jax.vjp(jax.nn.silu, time_pre)
    time_act = time_float.astype(jnp.bfloat16)
    time_shift = plain_dot(time_act, f_shift)
    first_z, first_inv = layer_norm(residual)
    first_pre = (first_z * norm_f[:, 0] + norm_f[:, 1]).reshape(
        images, tile_len, model_width
    ) + time_shift[:, None, :]
    first_in = first_pre.reshape(row_count, model_width).astype(jnp.bfloat16)
    qkv = plain_dot(first_in, f_qkv)
    query_z, query_inv = layer_norm(
        qkv[:, :model_width].reshape(images, tile_len, head_count, head_dim)
    )
    key_z, key_inv = layer_norm(
        qkv[:, model_width : 2 * model_width].reshape(images, tile_len, head_count, head_dim)
    )
    queries = rotate(query_z, tables, 1.0).astype(jnp.bfloat16)
    queries_h = jnp.transpose(queries, (0, 2, 1, 3))
    keys = rotate(key_z, tables, 1.0).astype(jnp.bfloat16).reshape(images, tile_len, model_width)
    values = qkv[:, 2 * model_width :].astype(jnp.bfloat16).reshape(images, tile_len, model_width)
    start_carry = (
        jnp.full((images, head_count, tile_len), -1e30, jnp.float32),
        jnp.zeros((images, head_count, tile_len), jnp.float32),
        jnp.zeros((images, head_count, tile_len, head_dim), jnp.float32),
    )
    key_rows = lax.all_gather(keys, ("row", "col"), axis=1, tiled=True)
    value_rows = lax.all_gather(values, ("row", "col"), axis=1, tiled=True)
    key_count = key_rows.shape[1]
    block_len = block_size(key_count)

    def forward_block_step(block_index, running):
        running_max, weight_sum, accum_sum = running
        offset = block_index * block_len
        key_blk = lax.dynamic_slice_in_dim(key_rows, offset, block_len, 1).reshape(
            images, block_len, head_count, head_dim
        )
        value_blk = lax.dynamic_slice_in_dim(value_rows, offset, block_len, 1).reshape(
            images, block_len, head_count, head_dim
        )
        key_ok = valid_keys(offset, block_len)
        scores = (
            jnp.einsum("ihqe,ikhe->ihqk", queries_h, key_blk, preferred_element_type=jnp.float32)
            * score_scale
        )
        scores = jnp.where(key_ok[:, None, None, :], scores, -jnp.inf)
        new_max = jnp.maximum(running_max, jnp.max(scores, axis=-1))
        weight = jnp.exp(scores - new_max[..., None])
        rescale = jnp.exp(running_max - new_max)
        weight_sum = weight_sum * rescale + jnp.sum(weight, axis=-1)
        accum_sum = accum_sum * rescale[..., None] + jnp.einsum(
            "ihqk,ikhe->ihqe",
            weight.astype(jnp.bfloat16),
            value_blk,
            preferred_element_type=jnp.float32,
        )
        return (new_max, weight_sum, accum_sum)

    running_max, weight_sum, accum_sum = lax.fori_loop(
        0, key_count // block_len, forward_block_step, start_carry
    )
    attended = accum_sum / weight_sum[..., None]
    log_sum = running_max + jnp.log(weight_sum)
    att_low = (
        jnp.transpose(attended, (0, 2, 1, 3)).reshape(row_count, model_width).astype(jnp.bfloat16)
    )
    residual_two = residual + plain_dot(att_low, f_out)
    third_z, third_inv = layer_norm(residual_two)
    third_in = (third_z * norm_f[:, 2] + norm_f[:, 3]).astype(jnp.bfloat16)
    cross_pre = plain_dot(third_in, f_query)
    cq_z, cq_inv = layer_norm(cross_pre.reshape(images, tile_len, head_count, head_dim))
    cross_queries = cq_z.astype(jnp.bfloat16)
    text_kv = jnp.einsum("itc,cd->itd", text_states, f_text, preferred_element_type=jnp.float32)
    ck_z, ck_inv = layer_norm(
        text_kv[..., :model_width].reshape(images, text_len, head_count, head_dim)
    )
    cross_keys = ck_z.astype(jnp.bfloat16)
    cross_values = (
        text_kv[..., model_width:]
        .astype(jnp.bfloat16)
        .reshape(images, text_len, head_count, head_dim)
    )

    def cross_softmax():
        scores = (
            jnp.einsum(
                "iqhe,ikhe->ihqk", cross_queries, cross_keys, preferred_element_type=jnp.float32
            )
            * score_scale
        )
        return jax.nn.softmax(scores, axis=-1)

    crossed = jnp.einsum(
        "ihqk,ikhe->iqhe",
        cross_softmax().astype(jnp.bfloat16),
        cross_values,
        preferred_element_type=jnp.float32,
    )
    cross_low = crossed.reshape(row_count, model_width).astype(jnp.bfloat16)
    residual_three = residual_two + plain_dot(cross_low, f_cross)
    second_z, second_inv = layer_norm(residual_three)
    second_in = (second_z * norm_f[:, 4] + norm_f[:, 5]).astype(jnp.bfloat16)
    up_pre = plain_dot(second_in, f_up)
    hidden_float, gelu_pull = jax.vjp(gelu_tanh, up_pre)
    hidden_act = hidden_float.astype(jnp.bfloat16)
    residual_four = residual_three + plain_dot(hidden_act, f_down)
    last_z, last_inv = layer_norm(residual_four)
    last_in = (last_z * norm_f[:, 6] + norm_f[:, 7]).astype(jnp.bfloat16)
    produced = plain_dot(last_in, f_final)
    prediction = (
        (produced * keep_rows)
        .astype(jnp.bfloat16)
        .reshape(images, rows_tile, cols_tile, produced.shape[1])
    )
    grad_out = (
        cotangent.reshape(row_count, produced.shape[1]).astype(jnp.float32) * keep_rows
    ).astype(jnp.bfloat16)
    d_final = left_dot(last_in, grad_out)
    grad_last = right_dot(grad_out, f_final)
    gain_final = jnp.sum(grad_last * last_z, axis=0)
    bias_final = jnp.sum(grad_last, axis=0)
    grad_four = norm_back(grad_last * norm_f[:, 6], last_z, last_inv)
    low_four = grad_four.astype(jnp.bfloat16)
    d_down = left_dot(hidden_act, low_four)
    grad_hidden = right_dot(low_four, f_down)
    grad_up = gelu_pull(grad_hidden)[0].astype(jnp.bfloat16)
    d_up = left_dot(second_in, grad_up)
    grad_second = right_dot(grad_up, f_up)
    gain_second = jnp.sum(grad_second * second_z, axis=0)
    bias_second = jnp.sum(grad_second, axis=0)
    grad_three = grad_four + norm_back(grad_second * norm_f[:, 4], second_z, second_inv)
    low_three = grad_three.astype(jnp.bfloat16)
    d_cross = left_dot(cross_low, low_three)
    grad_crossed = (
        right_dot(low_three, f_cross)
        .astype(jnp.bfloat16)
        .reshape(images, tile_len, head_count, head_dim)
    )
    cross_probs = cross_softmax()
    cross_delta = jnp.transpose(
        jnp.sum(grad_crossed.astype(jnp.float32) * crossed, axis=-1), (0, 2, 1)
    )
    grad_probs = jnp.einsum(
        "iqhe,ikhe->ihqk", grad_crossed, cross_values, preferred_element_type=jnp.float32
    )
    grad_cscore = (cross_probs * (grad_probs - cross_delta[..., None])).astype(jnp.bfloat16)
    grad_cq = score_scale * jnp.einsum(
        "ihqk,ikhe->iqhe", grad_cscore, cross_keys, preferred_element_type=jnp.float32
    )
    part_ckey = score_scale * jnp.einsum(
        "ihqk,iqhe->ikhe", grad_cscore, cross_queries, preferred_element_type=jnp.float32
    )
    part_cvalue = jnp.einsum(
        "ihqk,iqhe->ikhe",
        cross_probs.astype(jnp.bfloat16),
        grad_crossed,
        preferred_element_type=jnp.float32,
    )
    grad_cross_q = (
        norm_back(grad_cq, cq_z, cq_inv).reshape(row_count, model_width).astype(jnp.bfloat16)
    )
    d_query = left_dot(third_in, grad_cross_q)
    grad_third = right_dot(grad_cross_q, f_query)
    gain_third = jnp.sum(grad_third * third_z, axis=0)
    bias_third = jnp.sum(grad_third, axis=0)
    grad_two = grad_three + norm_back(grad_third * norm_f[:, 2], third_z, third_inv)
    sum_ckey, sum_cvalue = lax.psum((part_ckey, part_cvalue), ("row", "col"))
    low_two = grad_two.astype(jnp.bfloat16)
    d_out = left_dot(att_low, low_two)
    grad_att = (
        right_dot(low_two, f_out)
        .astype(jnp.bfloat16)
        .reshape(images, tile_len, head_count, head_dim)
    )
    grad_att_h = jnp.transpose(grad_att, (0, 2, 1, 3))
    delta_rows = jnp.sum(grad_att_h.astype(jnp.float32) * attended, axis=-1)
    back_carry = (
        jnp.zeros((images, head_count, tile_len, head_dim), jnp.float32),
        jnp.zeros((images, tile_len * grid_devices, model_width), jnp.float32),
        jnp.zeros((images, tile_len * grid_devices, model_width), jnp.float32),
    )
    backward_key_rows = lax.all_gather(keys, ("row", "col"), axis=1, tiled=True)
    backward_value_rows = lax.all_gather(values, ("row", "col"), axis=1, tiled=True)
    key_count = backward_key_rows.shape[1]
    backward_block_len = block_size(key_count)

    def backward_block_step(block_index, running):
        grad_query, grad_key_all, grad_value_all = running
        offset = block_index * backward_block_len
        key_blk = lax.dynamic_slice_in_dim(
            backward_key_rows, offset, backward_block_len, 1
        ).reshape(images, backward_block_len, head_count, head_dim)
        value_blk = lax.dynamic_slice_in_dim(
            backward_value_rows, offset, backward_block_len, 1
        ).reshape(images, backward_block_len, head_count, head_dim)
        key_ok = valid_keys(offset, backward_block_len)
        scores = (
            jnp.einsum("ihqe,ikhe->ihqk", queries_h, key_blk, preferred_element_type=jnp.float32)
            * score_scale
        )
        scores = jnp.where(key_ok[:, None, None, :], scores, -jnp.inf)
        attn_probs = jnp.exp(scores - log_sum[..., None])
        grad_prob = jnp.einsum(
            "ihqe,ikhe->ihqk", grad_att_h, value_blk, preferred_element_type=jnp.float32
        )
        grad_score = (attn_probs * (grad_prob - delta_rows[..., None])).astype(jnp.bfloat16)
        grad_query = grad_query + score_scale * jnp.einsum(
            "ihqk,ikhe->ihqe", grad_score, key_blk, preferred_element_type=jnp.float32
        )
        key_part = score_scale * jnp.einsum(
            "ihqk,ihqe->ikhe", grad_score, queries_h, preferred_element_type=jnp.float32
        )
        value_part = jnp.einsum(
            "ihqk,ihqe->ikhe",
            attn_probs.astype(jnp.bfloat16),
            grad_att_h,
            preferred_element_type=jnp.float32,
        )
        grad_key_all = lax.dynamic_update_slice_in_dim(
            grad_key_all, key_part.reshape(images, backward_block_len, model_width), offset, 1
        )
        grad_value_all = lax.dynamic_update_slice_in_dim(
            grad_value_all, value_part.reshape(images, backward_block_len, model_width), offset, 1
        )
        return (grad_query, grad_key_all, grad_value_all)

    grad_query, grad_key_all, grad_value_all = lax.fori_loop(
        0, key_count // backward_block_len, backward_block_step, back_carry
    )
    grad_key_own, grad_value_own = (
        lax.psum_scatter(grad_key_all, ("row", "col"), scatter_dimension=1, tiled=True),
        lax.psum_scatter(grad_value_all, ("row", "col"), scatter_dimension=1, tiled=True),
    )
    grad_qn = rotate(jnp.transpose(grad_query, (0, 2, 1, 3)), tables, -1.0)
    grad_kn = rotate(grad_key_own.reshape(images, tile_len, head_count, head_dim), tables, -1.0)
    grad_qkv = jnp.concatenate(
        [
            norm_back(grad_qn, query_z, query_inv).reshape(row_count, model_width),
            norm_back(grad_kn, key_z, key_inv).reshape(row_count, model_width),
            grad_value_own.reshape(row_count, model_width),
        ],
        axis=-1,
    ).astype(jnp.bfloat16)
    d_qkv = left_dot(first_in, grad_qkv)
    grad_first = right_dot(grad_qkv, f_qkv)
    gain_first = jnp.sum(grad_first * first_z, axis=0)
    bias_first = jnp.sum(grad_first, axis=0)
    part_shift = jnp.sum(grad_first.reshape(images, tile_len, model_width), axis=1)
    grad_one = grad_two + norm_back(grad_first * norm_f[:, 0], first_z, first_inv)
    shift_grad = lax.psum(part_shift, ("row", "col"))
    grad_ckey = norm_back(sum_ckey, ck_z, ck_inv).reshape(images, text_len, model_width)
    grad_kv = jnp.concatenate(
        [grad_ckey, sum_cvalue.reshape(images, text_len, model_width)], axis=-1
    ).astype(jnp.bfloat16)
    text_slice = text_states.shape[2] // grid_devices
    text_cols = lax.dynamic_slice_in_dim(text_states, grid_at * text_slice, text_slice, 2)
    d_text_w = jnp.einsum("itc,itd->cd", text_cols, grad_kv, preferred_element_type=jnp.float32)
    text_grad = jnp.einsum("itd,cd->itc", grad_kv, part_text, preferred_element_type=jnp.float32)
    shift_low = shift_grad.astype(jnp.bfloat16)
    shift_slice = model_width // grid_devices
    act_cols = lax.dynamic_slice_in_dim(time_act, grid_at * shift_slice, shift_slice, 1)
    d_shift_w = jnp.einsum("ic,id->cd", act_cols, shift_low, preferred_element_type=jnp.float32)
    grad_time_act = right_dot(shift_low, f_shift)
    grad_time_pre = silu_pull(grad_time_act)[0].astype(jnp.bfloat16)
    freq_slice = embedding.shape[1] // grid_devices
    embed_cols = lax.dynamic_slice_in_dim(embedding, grid_at * freq_slice, freq_slice, 1)
    d_time_w = jnp.einsum(
        "ic,id->cd", embed_cols, grad_time_pre, preferred_element_type=jnp.float32
    )
    low_one = grad_one.astype(jnp.bfloat16)
    d_skip_w = left_dot(skip_in, low_one)
    grad_skip_in = right_dot(low_one, f_skip)
    gain_skips = jnp.sum(grad_skip_in * joined, axis=0)
    bias_skips = jnp.sum(grad_skip_in, axis=0)
    grad_joined = norm_back(grad_skip_in * gain_skip, joined, joined_inv)
    skip_grad = grad_joined[:, model_width:].reshape(images, rows_tile, cols_tile, model_width)
    grad_patch = grad_joined[:, :model_width].astype(jnp.bfloat16)
    d_patch = left_dot(grad_patch, patch_rows)
    latent_grad = plain_dot(grad_patch, f_patch).reshape(images, rows_tile, cols_tile, patch_width)
    d_norms = jnp.stack(
        [
            gain_first,
            bias_first,
            gain_third,
            bias_third,
            gain_second,
            bias_second,
            gain_final,
            bias_final,
            gain_skips[:model_width],
            bias_skips[:model_width],
            gain_skips[model_width:],
            bias_skips[model_width:],
        ],
        axis=1,
    )
    tile_done = (
        lax.psum_scatter(d_patch, ("row", "col"), scatter_dimension=0, tiled=True),
        lax.psum_scatter(d_skip_w, ("row", "col"), scatter_dimension=0, tiled=True),
        lax.psum_scatter(d_qkv, ("row", "col"), scatter_dimension=0, tiled=True),
        lax.psum_scatter(d_out, ("row", "col"), scatter_dimension=0, tiled=True),
        lax.psum_scatter(d_query, ("row", "col"), scatter_dimension=0, tiled=True),
        lax.psum_scatter(d_cross, ("row", "col"), scatter_dimension=0, tiled=True),
        lax.psum_scatter(d_up, ("row", "col"), scatter_dimension=0, tiled=True),
        lax.psum_scatter(d_down, ("row", "col"), scatter_dimension=0, tiled=True),
        lax.psum_scatter(d_final, ("row", "col"), scatter_dimension=0, tiled=True),
        lax.psum_scatter(d_norms, ("row", "col"), scatter_dimension=0, tiled=True),
    )
    reduced = (
        lax.psum_scatter(
            tile_done[0].astype(jnp.bfloat16), "dp", scatter_dimension=1, tiled=True
        ).astype(jnp.float32),
        lax.psum_scatter(
            tile_done[1].astype(jnp.bfloat16), "dp", scatter_dimension=1, tiled=True
        ).astype(jnp.float32),
        lax.psum_scatter(
            tile_done[2].astype(jnp.bfloat16), "dp", scatter_dimension=1, tiled=True
        ).astype(jnp.float32),
        lax.psum_scatter(
            tile_done[3].astype(jnp.bfloat16), "dp", scatter_dimension=1, tiled=True
        ).astype(jnp.float32),
        lax.psum_scatter(
            tile_done[4].astype(jnp.bfloat16), "dp", scatter_dimension=1, tiled=True
        ).astype(jnp.float32),
        lax.psum_scatter(
            tile_done[5].astype(jnp.bfloat16), "dp", scatter_dimension=1, tiled=True
        ).astype(jnp.float32),
        lax.psum_scatter(
            tile_done[6].astype(jnp.bfloat16), "dp", scatter_dimension=1, tiled=True
        ).astype(jnp.float32),
        lax.psum_scatter(
            tile_done[7].astype(jnp.bfloat16), "dp", scatter_dimension=1, tiled=True
        ).astype(jnp.float32),
        lax.psum_scatter(
            tile_done[8].astype(jnp.bfloat16), "dp", scatter_dimension=1, tiled=True
        ).astype(jnp.float32),
        lax.psum_scatter(
            tile_done[9].astype(jnp.bfloat16), "dp", scatter_dimension=1, tiled=True
        ).astype(jnp.float32),
        lax.psum_scatter(
            d_time_w.astype(jnp.bfloat16), "dp", scatter_dimension=1, tiled=True
        ).astype(jnp.float32),
        lax.psum_scatter(
            d_shift_w.astype(jnp.bfloat16), "dp", scatter_dimension=1, tiled=True
        ).astype(jnp.float32),
        lax.psum_scatter(
            d_text_w.astype(jnp.bfloat16), "dp", scatter_dimension=1, tiled=True
        ).astype(jnp.float32),
    )
    return (
        prediction,
        latent_grad,
        skip_grad,
        text_grad,
        reduced[0],
        reduced[1],
        reduced[10],
        reduced[11],
        reduced[2],
        reduced[3],
        reduced[4],
        reduced[12],
        reduced[5],
        reduced[6],
        reduced[7],
        reduced[8],
        reduced[9],
    )


TILE = ("row", "col")
EVERY = ("dp", "row", "col")
LOG2E = math.log2(math.e)
F32 = jnp.float32
BF16 = jnp.bfloat16
VMEM_BYTES = 56 * 2**20


def kernel_call(body, flops, moved, **options):
    return pl.pallas_call(
        body,
        compiler_params=pltpu.CompilerParams(vmem_limit_bytes=VMEM_BYTES),
        cost_estimate=pl.CostEstimate(flops=flops, bytes_accessed=moved, transcendentals=0),
        **options,
    )


def pair_swap(values_in):
    quarter = values_in.shape[0] // 4
    parts = [values_in[at * quarter : (at + 1) * quarter] for at in (1, 0, 3, 2)]
    return jnp.concatenate(parts, axis=0)


def column_norm(values_in):
    centred = values_in - jnp.mean(values_in, axis=0, keepdims=True)
    inverse = lax.rsqrt(jnp.mean(centred * centred, axis=0, keepdims=True) + EPSILON)
    return (centred * inverse, inverse)


def column_norm_back(grad_normed, normed, inverse):
    mean_grad = jnp.mean(grad_normed, axis=0, keepdims=True)
    mean_cross = jnp.mean(grad_normed * normed, axis=0, keepdims=True)
    return inverse * (grad_normed - mean_grad - normed * mean_cross)


def minus_pieces(row_values):
    high = row_values.astype(BF16).astype(F32)
    rest = row_values - high
    middle = rest.astype(BF16).astype(F32)
    lower = rest - middle
    at = lax.broadcasted_iota(jnp.int32, (8, row_values.shape[1]), 0)
    zero = jnp.zeros((8, row_values.shape[1]), F32)
    picked = jnp.where(at == 0, high, jnp.where(at == 1, middle, jnp.where(at == 2, lower, zero)))
    return -picked


def piece_flags(width):
    return (lax.broadcasted_iota(jnp.int32, (8, width), 0) < 3).astype(F32)


def head_norm_body(
    query_scale, rows_ref, weight_ref, cos_ref, sin_ref, ok_ref, out_ref, inv_ref
):
    groups, _, heads, head_dim, _ = out_ref.shape
    part = pl.program_id(0)
    made = jnp.dot(rows_ref[...], weight_ref[...], preferred_element_type=F32).T
    valid = ok_ref[...]

    @pl.when(part < 2)
    def _():
        factor = jnp.where(part == 0, query_scale, valid)
        cosine, sine = cos_ref[...] * factor, sin_ref[...] * factor
        for group in range(groups):
            for head in range(heads):
                at = (group * heads + head) * head_dim
                normed, inverse = column_norm(made[at : at + head_dim])
                turned = normed * cosine + pair_swap(normed) * sine
                out_ref[group, 0, head] = turned.astype(BF16)
                inv_ref[group, 0, head : head + 1] = inverse

    @pl.when(part == 2)
    def _():
        for group in range(groups):
            for head in range(heads):
                at = (group * heads + head) * head_dim
                out_ref[group, 0, head] = (made[at : at + head_dim] * valid).astype(BF16)
                inv_ref[group, 0, head : head + 1] = valid


def head_norm(rows, weight, tables, valid, groups, head_dim, query_scale):
    tile_len, depth = rows.shape
    width = weight.shape[1] // 3
    heads = width // groups // head_dim
    table = pl.BlockSpec((head_dim, tile_len), lambda p: (0, 0))
    return kernel_call(
        functools.partial(head_norm_body, query_scale),
        6 * tile_len * depth * width,
        6 * depth * width,
        grid=(3,),
        in_specs=[
            pl.BlockSpec((tile_len, depth), lambda p: (0, 0)),
            pl.BlockSpec((depth, width), lambda p: (0, p)),
            table,
            table,
            pl.BlockSpec((1, tile_len), lambda p: (0, 0)),
        ],
        out_specs=[
            pl.BlockSpec((groups, 1, heads, head_dim, tile_len), lambda p: (0, p, 0, 0, 0)),
            pl.BlockSpec((groups, 1, heads, tile_len), lambda p: (0, p, 0, 0)),
        ],
        out_shape=[
            jax.ShapeDtypeStruct((groups, 3, heads, head_dim, tile_len), BF16),
            jax.ShapeDtypeStruct((groups, 3, heads, tile_len), F32),
        ],
    )(rows, weight, *tables, valid)


def head_back_body(
    query_scale, grad_ref, own_ref, inv_ref, cos_ref, sin_ref, ok_ref, *others
):
    out_ref = others[-1]
    heads, head_dim = own_ref.shape[2], own_ref.shape[3]
    cosine, sine, valid = cos_ref[...], sin_ref[...], ok_ref[...]

    def unturn(values_in):
        return values_in * cosine - pair_swap(values_in) * sine

    for part in range(3):
        pieces = []
        for head in range(heads):
            grad = grad_ref[0, part, head].astype(F32)
            if part > 0:
                grad = grad * valid
            if part < 2:
                normed = unturn(own_ref[0, part, head].astype(F32))
                if part == 0:
                    normed = normed * (1.0 / query_scale)
                inverse = inv_ref[0, part, head : head + 1]
                grad = column_norm_back(unturn(grad), normed, inverse)
            pieces.append(grad)
        out_ref[part, 0] = jnp.concatenate(pieces, axis=0).astype(BF16)


def head_back(grads, own, inverses, tables, valid, query_scale, image, images, before):
    groups, _, heads, head_dim, tile_len = own.shape
    group_rows = heads * head_dim
    stacked = pl.BlockSpec((1, 3, heads, head_dim, tile_len), lambda g: (g, 0, 0, 0, 0))
    table = pl.BlockSpec((head_dim, tile_len), lambda g: (0, 0))
    earlier = () if before is None else (before,)
    return kernel_call(
        functools.partial(head_back_body, query_scale),
        0,
        6 * own.size,
        grid=(groups,),
        in_specs=[
            stacked,
            stacked,
            pl.BlockSpec((1, 3, heads, tile_len), lambda g: (g, 0, 0, 0)),
            table,
            table,
            pl.BlockSpec((1, tile_len), lambda g: (0, 0)),
        ]
        + [pl.BlockSpec(memory_space=pl.ANY)] * len(earlier),
        out_specs=pl.BlockSpec((3, 1, group_rows, tile_len), lambda g: (0, g, 0, image)),
        out_shape=jax.ShapeDtypeStruct((3, groups, group_rows, images * tile_len), BF16),
        input_output_aliases={6: 0} if earlier else {},
    )(grads, own, inverses, *tables, valid, *earlier)


def attend_body(query_ref, key_ref, value_ref, ok_ref, out_ref, lse_ref, key_nat, value_ext):
    tiles, tile_len, head_dim = key_ref.shape[0], key_ref.shape[-1], key_ref.shape[-2]

    @pl.when(pl.program_id(1) == 0)
    def _():
        for tile in range(tiles):
            key_nat[tile * tile_len : (tile + 1) * tile_len, :] = key_ref[tile, 0, 0].T
            value_ext[tile] = jnp.concatenate(
                [value_ref[tile, 0, 0].astype(F32), ok_ref[tile]], axis=0
            ).astype(BF16)

    query = query_ref[0, 0, 0]
    total = jnp.zeros((head_dim + 8, tile_len), F32)
    held = None
    for tile in range(tiles + 1):
        scores = None
        if tile < tiles:
            rows = slice(tile * tile_len, (tile + 1) * tile_len)
            scores = jnp.dot(key_nat[rows, :], query, preferred_element_type=F32)
        if held is not None:
            weight = jnp.exp2(held).astype(BF16)
            total = total + jnp.dot(value_ext[tile - 1], weight, preferred_element_type=F32)
        held = scores
    weight_sum = total[head_dim : head_dim + 1]
    out_ref[0, 0] = (total[:head_dim] / weight_sum).astype(BF16)
    lse_ref[0, 0] = jnp.log2(weight_sum)


def attend(qkv, flags):
    tiles, _, heads, head_dim, tile_len = qkv.shape
    return kernel_call(
        attend_body,
        1024 * heads * tiles**2 * tile_len**2,
        8 * qkv.size,
        grid=(heads, tiles),
        in_specs=[
            pl.BlockSpec((1, 1, 1, head_dim, tile_len), lambda h, t: (t, 0, h, 0, 0)),
            pl.BlockSpec((tiles, 1, 1, head_dim, tile_len), lambda h, t: (0, 1, h, 0, 0)),
            pl.BlockSpec((tiles, 1, 1, head_dim, tile_len), lambda h, t: (0, 2, h, 0, 0)),
            pl.BlockSpec((tiles, 8, tile_len), lambda h, t: (0, 0, 0)),
        ],
        out_specs=[
            pl.BlockSpec((1, 1, head_dim, tile_len), lambda h, t: (t, h, 0, 0)),
            pl.BlockSpec((1, 1, 1, tile_len), lambda h, t: (t, h, 0, 0)),
        ],
        out_shape=[
            jax.ShapeDtypeStruct((tiles, heads, head_dim, tile_len), BF16),
            jax.ShapeDtypeStruct((tiles, heads, 1, tile_len), F32),
        ],
        scratch_shapes=[
            pltpu.VMEM((tiles * tile_len, head_dim), BF16),
            pltpu.VMEM((tiles, head_dim + 8, tile_len), BF16),
        ],
    )(qkv, qkv, qkv, flags)


def attend_back_body(
    score_scale,
    query_ref,
    key_ref,
    value_ref,
    grad_ref,
    att_ref,
    lse_ref,
    out_ref,
    key_nat,
    value_nat,
    key_sum,
    value_sum,
):
    tiles, tile_len, head_dim = key_ref.shape[0], key_ref.shape[-1], key_ref.shape[-2]
    at = pl.program_id(1)

    @pl.when(at == 0)
    def _():
        ones = piece_flags(tile_len)
        for tile in range(tiles):
            rows = slice(tile * tile_len, (tile + 1) * tile_len)
            for source, kept in ((key_ref, key_nat), (value_ref, value_nat)):
                wide = jnp.concatenate([source[tile, 0, 0].astype(F32), ones], axis=0)
                kept[rows, :] = wide.T.astype(BF16)
        key_sum[...] = jnp.zeros_like(key_sum)
        value_sum[...] = jnp.zeros_like(value_sum)

    query = query_ref[0, 0, 0].astype(F32)
    grad = grad_ref[0, 0].astype(F32)
    delta = jnp.sum(grad * att_ref[0, 0].astype(F32), axis=0, keepdims=True)
    query_ext = jnp.concatenate([query, minus_pieces(lse_ref[0, 0])], axis=0)
    grad_ext = jnp.concatenate([grad, minus_pieces(delta)], axis=0)
    query_cols, grad_cols = query_ext.astype(BF16), grad_ext.astype(BF16)
    query_nat, grad_nat = query_ext.T.astype(BF16), grad_ext.T.astype(BF16)

    def step(tile, total):
        rows = pl.ds(pl.multiple_of(tile * tile_len, tile_len), tile_len)
        scores = jnp.dot(key_nat[rows, :], query_cols, preferred_element_type=F32)
        probs = jnp.exp2(scores)
        grad_probs = jnp.dot(value_nat[rows, :], grad_cols, preferred_element_type=F32)
        grad_scores = (probs * grad_probs).astype(BF16)
        value_sum[rows, :] += jnp.dot(probs.astype(BF16), grad_nat, preferred_element_type=F32)
        key_sum[rows, :] += jnp.dot(grad_scores, query_nat, preferred_element_type=F32)
        return total + jnp.dot(key_ref[tile, 0, 0], grad_scores, preferred_element_type=F32)

    start = jnp.zeros((head_dim, tile_len), F32)
    total = lax.fori_loop(0, tiles, step, start, unroll=8)
    out_ref[at, 0, 0] = (total * score_scale).astype(BF16)

    @pl.when(at == tiles - 1)
    def _():
        for tile in range(tiles):
            rows = slice(tile * tile_len, (tile + 1) * tile_len)
            key_grad = key_sum[rows, :].T[:head_dim] * (1.0 / LOG2E)
            out_ref[tile, 1, 0] = key_grad.astype(BF16)
            out_ref[tile, 2, 0] = value_sum[rows, :].T[:head_dim].astype(BF16)


def attend_back(qkv, grad_att, att, lse, score_scale):
    tiles, _, heads, head_dim, tile_len = qkv.shape
    one = pl.BlockSpec((1, 1, head_dim, tile_len), lambda h, t: (t, h, 0, 0))
    return kernel_call(
        functools.partial(attend_back_body, score_scale),
        2560 * heads * tiles**2 * tile_len**2,
        8 * qkv.size,
        grid=(heads, tiles),
        in_specs=[
            pl.BlockSpec((1, 1, 1, head_dim, tile_len), lambda h, t: (t, 0, h, 0, 0)),
            pl.BlockSpec((tiles, 1, 1, head_dim, tile_len), lambda h, t: (0, 1, h, 0, 0)),
            pl.BlockSpec((tiles, 1, 1, head_dim, tile_len), lambda h, t: (0, 2, h, 0, 0)),
            one,
            one,
            pl.BlockSpec((1, 1, 1, tile_len), lambda h, t: (t, h, 0, 0)),
        ],
        out_specs=pl.BlockSpec(
            (tiles, 3, 1, head_dim, tile_len), lambda h, t: (0, 0, h, 0, 0)
        ),
        out_shape=jax.ShapeDtypeStruct(qkv.shape, BF16),
        scratch_shapes=[
            pltpu.VMEM((tiles * tile_len, head_dim + 8), BF16),
            pltpu.VMEM((tiles * tile_len, head_dim + 8), BF16),
            pltpu.VMEM((tiles * tile_len, head_dim + 8), F32),
            pltpu.VMEM((tiles * tile_len, head_dim + 8), F32),
        ],
    )(qkv, qkv, qkv, grad_att, att, lse)


def cross_body(text_len, query_scale, pre_ref, kv_ref, att_ref, query_ref, inv_ref, lse_ref):
    head_dim, text_pad = kv_ref.shape[2], kv_ref.shape[3]
    at = lax.broadcasted_iota(jnp.int32, (8, text_pad), 0)
    text_at = lax.broadcasted_iota(jnp.int32, (8, text_pad), 1)
    flags = ((at == 0) & (text_at < text_len)).astype(F32)
    for head in range(pre_ref.shape[0]):
        normed, inverse = column_norm(pre_ref[head])
        query = (normed * query_scale).astype(BF16)
        query_ref[head] = query
        inv_ref[head] = inverse
        key = column_norm(kv_ref[0, head])[0].astype(BF16)
        value_ext = jnp.concatenate([kv_ref[1, head], flags], axis=0).astype(BF16)
        scores = jnp.dot(key.T, query, preferred_element_type=F32)
        weight = jnp.exp2(scores).astype(BF16)
        total = jnp.dot(value_ext, weight, preferred_element_type=F32)
        weight_sum = total[head_dim : head_dim + 1]
        att_ref[head] = (total[:head_dim] / weight_sum).astype(BF16)
        lse_ref[head] = jnp.log2(weight_sum)


def cross_attend(pre, text_kv, images, text_len, query_scale):
    heads, head_dim, tokens = pre.shape
    tile_len, text_pad = tokens // images, text_kv.shape[3] // images
    block = math.gcd(heads, 4)
    wide = pl.BlockSpec((block, head_dim, tile_len), lambda i, h: (h, 0, i))
    row = pl.BlockSpec((block, 1, tile_len), lambda i, h: (h, 0, i))
    return kernel_call(
        functools.partial(cross_body, text_len, query_scale),
        1024 * heads * tokens * text_pad,
        8 * pre.size,
        grid=(images, heads // block),
        in_specs=[wide, pl.BlockSpec((2, block, head_dim, text_pad), lambda i, h: (0, h, 0, i))],
        out_specs=[wide, wide, row, row],
        out_shape=[
            jax.ShapeDtypeStruct(pre.shape, BF16),
            jax.ShapeDtypeStruct(pre.shape, BF16),
            jax.ShapeDtypeStruct((heads, 1, tokens), F32),
            jax.ShapeDtypeStruct((heads, 1, tokens), F32),
        ],
    )(pre, text_kv)


def cross_back_body(
    query_scale,
    score_scale,
    query_ref,
    kv_ref,
    grad_ref,
    att_ref,
    inv_ref,
    lse_ref,
    out_ref,
    key_ref,
    value_ref,
):
    head_dim, text_pad = kv_ref.shape[2], kv_ref.shape[3]
    ones = piece_flags(text_pad)
    for head in range(query_ref.shape[0]):
        query = query_ref[head].astype(F32)
        grad = grad_ref[head].astype(F32)
        delta = jnp.sum(grad * att_ref[head].astype(F32), axis=0, keepdims=True)
        query_ext = jnp.concatenate([query, minus_pieces(lse_ref[head])], axis=0).astype(BF16)
        grad_ext = jnp.concatenate([grad, minus_pieces(delta)], axis=0).astype(BF16)
        key = column_norm(kv_ref[0, head])[0].astype(BF16)
        key_ext = jnp.concatenate([key.astype(F32), ones], axis=0).T.astype(BF16)
        value_ext = jnp.concatenate([kv_ref[1, head], ones], axis=0).T.astype(BF16)
        probs = jnp.exp2(jnp.dot(key_ext, query_ext, preferred_element_type=F32))
        grad_probs = jnp.dot(value_ext, grad_ext, preferred_element_type=F32)
        grad_scores = (probs * grad_probs).astype(BF16)
        value_grad = right_dot(grad_ext, probs.astype(BF16))[:head_dim]
        key_grad = right_dot(query_ext, grad_scores)[:head_dim]
        key_ref[head] = (key_grad * (1.0 / LOG2E)).astype(BF16)
        value_ref[head] = value_grad.astype(BF16)
        query_grad = jnp.dot(key, grad_scores, preferred_element_type=F32) * score_scale
        normed = query * (1.0 / query_scale)
        out_ref[head] = column_norm_back(query_grad, normed, inv_ref[head]).astype(BF16)


def cross_back(query, text_kv, grad, att, inverse, lse, images, query_scale, score_scale):
    heads, head_dim, tokens = query.shape
    tile_len, text_pad = tokens // images, text_kv.shape[3] // images
    block = math.gcd(heads, 4)
    wide = pl.BlockSpec((block, head_dim, tile_len), lambda i, h: (h, 0, i))
    row = pl.BlockSpec((block, 1, tile_len), lambda i, h: (h, 0, i))
    text = pl.BlockSpec((2, block, head_dim, text_pad), lambda i, h: (0, h, 0, i))
    text_out = pl.BlockSpec((block, head_dim, text_pad), lambda i, h: (h, 0, i))
    return kernel_call(
        functools.partial(cross_back_body, query_scale, score_scale),
        2560 * heads * tokens * text_pad,
        16 * query.size,
        grid=(images, heads // block),
        in_specs=[wide, text, wide, wide, row, row],
        out_specs=[
            wide,
            text_out,
            text_out,
        ],
        out_shape=[
            jax.ShapeDtypeStruct(query.shape, BF16),
            jax.ShapeDtypeStruct((heads, head_dim, images * text_pad), BF16),
            jax.ShapeDtypeStruct((heads, head_dim, images * text_pad), BF16),
        ],
    )(query, text_kv, grad, att, inverse, lse)


def join_norm_body(patch_ref, skip_ref, weight_ref, gain_ref, bias_ref, z_ref, inv_ref, in_ref):
    width = skip_ref.shape[1]
    patch_feat = right_dot(patch_ref[...], weight_ref[...])
    joined = jnp.concatenate([patch_feat, skip_ref[...].astype(F32)], axis=1)
    normed, inverse = layer_norm(joined)
    z_ref[...] = normed
    inv_ref[...] = inverse
    in_ref[...] = (normed * gain_ref[...] + bias_ref[...]).astype(BF16)


def join_norm(patch_rows, skip_rows, f_patch, gain, bias):
    tokens, width = skip_rows.shape
    block = math.gcd(tokens, 256)
    rows = lambda columns: pl.BlockSpec((block, columns), lambda t: (t, 0))
    fixed = lambda shape: pl.BlockSpec(shape, lambda t: (0, 0))
    return kernel_call(
        join_norm_body,
        64 * tokens * width,
        16 * tokens * width,
        grid=(tokens // block,),
        in_specs=[
            rows(patch_rows.shape[1]),
            rows(width),
            fixed(f_patch.shape),
            fixed(gain.shape),
            fixed(bias.shape),
        ],
        out_specs=[rows(2 * width), rows(1), rows(2 * width)],
        out_shape=[
            jax.ShapeDtypeStruct((tokens, 2 * width), F32),
            jax.ShapeDtypeStruct((tokens, 1), F32),
            jax.ShapeDtypeStruct((tokens, 2 * width), BF16),
        ],
    )(patch_rows, skip_rows, f_patch, gain, bias)


def join_back_body(low_ref, weight_ref, z_ref, inv_ref, gain_ref, skip_ref, patch_ref, sums_ref):
    width = skip_ref.shape[1]
    grad, normed = right_dot(low_ref[...], weight_ref[...]), z_ref[...]

    @pl.when(pl.program_id(0) == 0)
    def _():
        sums_ref[...] = jnp.zeros_like(sums_ref)

    sums_ref[0:1] += jnp.sum(grad * normed, axis=0, keepdims=True)
    sums_ref[1:2] += jnp.sum(grad, axis=0, keepdims=True)
    back = norm_back(grad * gain_ref[...], normed, inv_ref[...])
    patch_ref[...] = back[:, :width].astype(BF16)
    skip_ref[...] = back[:, width:]


def join_back(low_rows, f_skip, normed, inverse, gain):
    tokens, width = low_rows.shape
    block = math.gcd(tokens, 256)
    rows = lambda columns: pl.BlockSpec((block, columns), lambda t: (t, 0))
    fixed = lambda shape: pl.BlockSpec(shape, lambda t: (0, 0))
    return kernel_call(
        join_back_body,
        64 * tokens * width * width,
        18 * tokens * width,
        grid=(tokens // block,),
        in_specs=[rows(width), fixed(f_skip.shape), rows(2 * width), rows(1), fixed(gain.shape)],
        out_specs=[rows(width), rows(width), fixed((2, 2 * width))],
        out_shape=[
            jax.ShapeDtypeStruct((tokens, width), F32),
            jax.ShapeDtypeStruct((tokens, width), BF16),
            jax.ShapeDtypeStruct((2, 2 * width), F32),
        ],
    )(low_rows, f_skip, normed, inverse, gain)


def gelu_and_slope(inputs):
    scale, cubic = math.sqrt(2.0 / math.pi), 0.044715
    square = inputs * inputs
    curve = jnp.tanh(scale * inputs * (1.0 + cubic * square))
    half = 0.5 * (1.0 + curve)
    bend = 0.5 * inputs * (1.0 - curve * curve) * (scale * (1.0 + 3.0 * cubic * square))
    return ((inputs * half).astype(BF16), (half + bend).astype(BF16))


def swap_tiles(values_in):
    return lax.all_to_all(values_in, TILE, split_axis=0, concat_axis=0, tiled=True)


def shift_pairs(devices, step):
    return [(at, (at + step) % devices) for at in range(devices)]


def fetch(weight):
    devices = lax.axis_size("dp")
    return [weight] + [
        lax.ppermute(weight, "dp", shift_pairs(devices, step)) for step in range(1, devices)
    ]


def widen(pieces, first=None, joined=1):
    devices, me = lax.axis_size("dp"), lax.axis_index("dp")
    if first is not None:
        pieces = after(first, *pieces)
    slots = [lax.select_n((me - at) % devices, *pieces) for at in range(devices)]
    if joined > 1:
        split = [jnp.split(slot, joined, axis=1) for slot in slots]
        slots = [each for group in zip(*split) for each in group]
    return jnp.concatenate(slots, axis=1)


def narrow_blocks(blocks, first=None):
    devices, me = lax.axis_size("dp"), lax.axis_index("dp")
    received = []
    for step in range(1, devices):
        sent = lax.select_n((me + step) % devices, *blocks)
        received.append(lax.ppermute(sent, "dp", shift_pairs(devices, step)))
    if first is not None:
        received = after(first, *received)
    total = lax.select_n(me, *blocks).astype(F32)
    for piece in received:
        total = total + piece.astype(F32)
    return total


def narrow(weight_grad, first=None):
    return narrow_blocks(jnp.split(weight_grad, lax.axis_size("dp"), axis=1), first)


def by_device(weight_grads, parts):
    devices = lax.axis_size("dp")
    split = [jnp.split(weight_grad, devices, axis=1) for weight_grad in weight_grads]
    return [jnp.concatenate(blocks, axis=parts) for blocks in zip(*split)]


def sum_tiles(part_sums):
    devices, me = lax.axis_size(TILE), lax.axis_index(TILE)
    total, step = part_sums, devices // 2
    while step > 0:
        pairs = [(at, at ^ step) for at in range(devices)]
        lower, upper = jnp.split(total, 2, axis=0)
        high = (me // step) % 2 == 1
        sent = jnp.where(high, lower, upper)
        total = jnp.where(high, upper, lower) + lax.ppermute(sent, TILE, pairs)
        step //= 2
    return total


def total_tiles(part_sum):
    devices = lax.axis_size(TILE)
    total, step = part_sum, 1
    while step < devices:
        pairs = [(at, at ^ step) for at in range(devices)]
        total = total + lax.ppermute(total, TILE, pairs)
        step *= 2
    return total


def over_tiles(weight_grad):
    return lax.optimization_barrier(
        lax.psum_scatter(weight_grad, TILE, scatter_dimension=0, tiled=True)
    )


def tiles_whole(weight):
    return lax.all_gather(weight, TILE, axis=0, tiled=True)


def after(first, *values_in):
    return lax.optimization_barrier((first, *values_in))[1:]


def dot_over(left_mat, right_mat, left_axis, right_axis):
    return lax.dot_general(
        left_mat,
        right_mat,
        (((left_axis,), (right_axis,)), ((), ())),
        preferred_element_type=F32,
    )


def local_heads(
    latent,
    skip_input,
    text_states,
    timesteps,
    image_sides,
    cotangent,
    w_patch,
    w_skip,
    w_time,
    w_shift,
    w_qkv,
    w_out,
    w_query,
    w_text,
    w_cross,
    w_up,
    w_down,
    w_final,
    norm_params,
):
    dp_devices = lax.axis_size("dp")
    grid_devices = lax.axis_size(TILE)
    col_devices = lax.axis_size("col")
    grid_at = lax.axis_index(TILE)
    row_at = lax.axis_index("row")
    col_at = lax.axis_index("col")
    images, rows_tile, cols_tile, patch_width = latent.shape
    tile_len = rows_tile * cols_tile
    row_count = images * tile_len
    out_width = cotangent.shape[3]

    f_skip = tiles_whole(widen(fetch(w_skip)))
    small = jnp.concatenate([w_patch, w_final, norm_params], axis=1)
    small_widths = (w_patch.shape[1], w_final.shape[1], norm_params.shape[1])
    cuts = (0, small_widths[0], sum(small_widths[:2]), sum(small_widths))
    early = [jnp.pad(small, ((0, 0), (0, w_shift.shape[1] - small.shape[1]))), w_time, w_shift]
    ends = (small.shape[0], small.shape[0] + w_time.shape[0])
    part_small, part_time, part_shift_w = jnp.split(
        widen(fetch(jnp.concatenate(early, axis=0))), ends, axis=0
    )
    part_small = part_small.reshape(small.shape[0], dp_devices, -1)[:, :, : small.shape[1]]
    part_small = part_small.reshape(small.shape[0], -1)
    f_small = tiles_whole(part_small).reshape(-1, dp_devices, sum(small_widths))
    f_patch, f_final, f_norms = (
        f_small[:, :, cuts[at] : cuts[at + 1]].reshape(f_small.shape[0], -1) for at in range(3)
    )
    held_qkv = fetch(w_qkv)
    held_three = fetch(jnp.concatenate([w_out, w_query, w_cross], axis=1))
    held_text = fetch(w_text)
    held_up, held_down = fetch(w_up), fetch(w_down)
    model_width = skip_input.shape[3]
    head_count = HEADS
    head_dim = model_width // head_count
    text_len = text_states.shape[1]
    text_pad = -(-text_len // 128) * 128
    score_scale = head_dim ** (-0.5)
    query_scale = score_scale * LOG2E
    positions = jnp.arange(tile_len, dtype=jnp.int32)
    row_pos = row_at * rows_tile + positions // cols_tile
    col_pos = col_at * cols_tile + positions % cols_tile
    query_ok = (row_pos[None, :] < image_sides[:, None]) & (col_pos[None, :] < image_sides[:, None])
    valid = query_ok.astype(F32)
    keep_rows = query_ok.astype(F32).reshape(row_count, 1)
    tile_list = jnp.arange(grid_devices, dtype=jnp.int32)[:, None]
    key_row = tile_list // col_devices * rows_tile + (positions // cols_tile)[None, :]
    key_col = tile_list % col_devices * cols_tile + (positions % cols_tile)[None, :]
    sides = image_sides[:, None, None]
    key_ok = ((key_row[None] < sides) & (key_col[None] < sides)).astype(F32)
    flags = jnp.concatenate(
        [key_ok[:, :, None, :], jnp.zeros((images, grid_devices, 7, tile_len), F32)], axis=2
    )
    cos_row, sin_row, cos_col, sin_col = (
        jnp.transpose(table[:, 0, :]) for table in rope_tables(row_pos, col_pos, head_dim)
    )
    tables = (
        jnp.concatenate([cos_row, cos_row, cos_col, cos_col], axis=0),
        jnp.concatenate([-sin_row, sin_row, -sin_col, sin_col], axis=0),
    )
    norm_f = f_norms.astype(F32)

    embedding = time_embed(timesteps, FREQ).astype(BF16)
    freq_slice = part_time.shape[0]
    shift_slice = part_shift_w.shape[0]
    embed_cols = lax.dynamic_slice_in_dim(embedding, grid_at * freq_slice, freq_slice, 1)
    time_pre = total_tiles(plain_dot(embed_cols, part_time))
    time_float, silu_pull = jax.vjp(jax.nn.silu, time_pre)
    time_act = time_float.astype(BF16)
    act_cols = lax.dynamic_slice_in_dim(time_act, grid_at * shift_slice, shift_slice, 1)
    time_shift = total_tiles(plain_dot(act_cols, part_shift_w))

    patch_rows = latent.reshape(row_count, patch_width)
    skip_rows = skip_input.reshape(row_count, model_width)
    gain_skip = jnp.concatenate([norm_f[:, 8], norm_f[:, 10]])[None]
    bias_skip = jnp.concatenate([norm_f[:, 9], norm_f[:, 11]])[None]
    joined, joined_inv, skip_in = join_norm(patch_rows, skip_rows, f_patch, gain_skip, bias_skip)
    f_qkv = tiles_whole(widen(held_qkv, skip_in))
    f_three = tiles_whole(widen(held_three, skip_in, 3))
    f_out, f_query, f_cross = jnp.split(f_three, 3, axis=1)
    residual = plain_dot(skip_in, f_skip)
    first_z, first_inv = layer_norm(residual)
    first_pre = (first_z * norm_f[:, 0] + norm_f[:, 1]).reshape(
        images, tile_len, model_width
    ) + time_shift[:, None, :]
    first_in = first_pre.reshape(row_count, model_width).astype(BF16)
    part_text = widen(held_text, first_in)
    f_text = tiles_whole(part_text)
    first_rows = first_in.reshape(images, tile_len, model_width)
    own_qkv, qk_inv, tile_qkv, tile_att, tile_lse, att_rows = [], [], [], [], [], []
    for image in range(images):
        rows = first_rows[image]
        own, inverses = head_norm(
            rows,
            f_qkv,
            tables,
            valid[image : image + 1],
            grid_devices,
            head_dim,
            query_scale,
        )
        own_qkv.append(own)
        qk_inv.append(inverses)
        tile_qkv.append(swap_tiles(own))
    f_up = tiles_whole(widen(held_up, tile_qkv[0]))
    for image in range(images):
        att, lse = attend(tile_qkv[image], flags[image])
        tile_att.append(att)
        tile_lse.append(lse)
        own_att = swap_tiles(att).reshape(model_width, tile_len)
        att_rows.append(jnp.transpose(own_att))
    att_low = jnp.concatenate(att_rows, axis=0)
    residual_two = residual + plain_dot(att_low, f_out)
    f_down = tiles_whole(widen(held_down, residual_two))

    third_z, third_inv = layer_norm(residual_two)
    third_in = (third_z * norm_f[:, 2] + norm_f[:, 3]).astype(BF16)
    cross_pre = dot_over(f_query, third_in, 0, 1).reshape(head_count, head_dim, row_count)
    text_rows = jnp.pad(text_states, ((0, 0), (0, text_pad - text_len), (0, 0)))
    text_rows = text_rows.reshape(images * text_pad, -1)
    text_kv = dot_over(f_text, text_rows, 0, 1).reshape(2, head_count, head_dim, images * text_pad)
    crossed, cross_queries, cq_inv, cross_lse = cross_attend(
        cross_pre, text_kv, images, text_len, query_scale
    )
    cross_cols = crossed.reshape(model_width, row_count)
    residual_three = residual_two + left_dot(cross_cols, f_cross)
    second_z, second_inv = layer_norm(residual_three)
    second_in = (second_z * norm_f[:, 4] + norm_f[:, 5]).astype(BF16)
    up_pre = plain_dot(second_in, f_up)
    hidden_act, slope = lax.optimization_barrier(gelu_and_slope(up_pre))
    residual_four = residual_three + plain_dot(hidden_act, f_down)
    last_z, last_inv = layer_norm(residual_four)
    last_in = (last_z * norm_f[:, 6] + norm_f[:, 7]).astype(BF16)
    produced = plain_dot(last_in, f_final)
    prediction = (
        (produced * keep_rows).astype(BF16).reshape(images, rows_tile, cols_tile, out_width)
    )

    grad_out = (cotangent.reshape(row_count, out_width).astype(F32) * keep_rows).astype(BF16)
    d_final = left_dot(last_in, grad_out)
    grad_last = right_dot(grad_out, f_final)
    gain_final = jnp.sum(grad_last * last_z, axis=0)
    bias_final = jnp.sum(grad_last, axis=0)
    grad_four = norm_back(grad_last * norm_f[:, 6], last_z, last_inv)
    low_four = grad_four.astype(BF16)
    d_down = left_dot(hidden_act, low_four).astype(BF16)
    d_down, low_four = lax.optimization_barrier((d_down, low_four))
    t_down = over_tiles(d_down)
    grad_hidden = right_dot(low_four, f_down)
    grad_up = (grad_hidden * slope).astype(BF16)
    d_up = left_dot(second_in, grad_up).astype(BF16)
    d_up, grad_up = lax.optimization_barrier((d_up, grad_up))
    t_up = over_tiles(d_up)
    grad_second = right_dot(grad_up, f_up)
    gain_second = jnp.sum(grad_second * second_z, axis=0)
    bias_second = jnp.sum(grad_second, axis=0)
    grad_three = grad_four + norm_back(grad_second * norm_f[:, 4], second_z, second_inv)
    low_three = grad_three.astype(BF16)
    d_cross = plain_dot(cross_cols, low_three).astype(BF16)
    grad_crossed = dot_over(f_cross, low_three, 1, 1).astype(BF16)
    grad_cross_q, d_text_key, d_text_value = cross_back(
        cross_queries,
        text_kv,
        grad_crossed.reshape(head_count, head_dim, row_count),
        crossed,
        cq_inv,
        cross_lse,
        images,
        query_scale,
        score_scale,
    )
    t_down, grad_cross_q = lax.optimization_barrier((t_down, grad_cross_q))
    grad_cross_q = grad_cross_q.reshape(model_width, row_count)
    d_query = dot_over(third_in, grad_cross_q, 0, 1).astype(BF16)
    grad_third = dot_over(grad_cross_q, f_query, 0, 1)
    gain_third = jnp.sum(grad_third * third_z, axis=0)
    bias_third = jnp.sum(grad_third, axis=0)
    grad_two = grad_three + norm_back(grad_third * norm_f[:, 2], third_z, third_inv)
    low_two = grad_two.astype(BF16)
    low_two_rows = low_two.reshape(images, tile_len, model_width)
    tile_grads = []
    for image in range(images):
        grad_att = dot_over(f_out, low_two_rows[image], 1, 1).astype(BF16)
        tile_grads.append(swap_tiles(grad_att.reshape(tile_att[image].shape)))
    d_out = left_dot(att_low, low_two).astype(BF16)
    d_joint = jnp.concatenate(
        [
            d_out,
            d_query,
            d_cross,
            d_text_key.reshape(model_width, -1),
            d_text_value.reshape(model_width, -1),
        ],
        axis=1,
    )
    d_joint = with_layout_constraint(d_joint, Layout(major_to_minor=(0, 1)))
    d_joint, tile_grads[0] = lax.optimization_barrier((d_joint, tile_grads[0]))
    t_joint = over_tiles(d_joint)
    own_grads, grad_qkv, tile_back = [], None, None
    for image in range(images):
        if tile_back is not None:
            down_grad = narrow(t_down, tile_back)
            down_grad, tile_grads[image], tile_back = lax.optimization_barrier(
                (down_grad, tile_grads[image], tile_back)
            )
            own_grads.append(swap_tiles(tile_back))
        tile_back = attend_back(
            tile_qkv[image], tile_grads[image], tile_att[image], tile_lse[image], score_scale
        )
    own_grads.append(swap_tiles(tile_back))
    for image in range(images):
        if image == images - 1:
            up_grad = narrow(t_up, tile_back)
            up_grad, own_grads[-1], grad_qkv = lax.optimization_barrier(
                (up_grad, own_grads[-1], grad_qkv)
            )
        grad_qkv = head_back(
            own_grads[image],
            own_qkv[image],
            qk_inv[image],
            tables,
            valid[image : image + 1],
            query_scale,
            image,
            images,
            grad_qkv,
        )
    sum_text_kv = t_joint[:, 3 * model_width :].astype(F32)
    sum_text_kv = jnp.transpose(
        sum_text_kv.reshape(-1, head_dim, 2, images * text_pad), (2, 0, 1, 3)
    )
    group_heads = head_count // grid_devices
    own_key = lax.dynamic_slice_in_dim(text_kv[0], grid_at * group_heads, group_heads, 0)
    ck_z, ck_inv = layer_norm(jnp.swapaxes(own_key, 1, 2))
    grad_ckey = jnp.swapaxes(norm_back(jnp.swapaxes(sum_text_kv[0], 1, 2), ck_z, ck_inv), 1, 2)
    grad_kv = jnp.stack([grad_ckey, sum_text_kv[1]]).astype(BF16)
    grad_kv = grad_kv.reshape(-1, images * text_pad)
    t_joint, grad_qkv = lax.optimization_barrier((t_joint, grad_qkv))
    grad_qkv = grad_qkv.reshape(3 * model_width, row_count)
    d_qkv = dot_over(first_in, grad_qkv, 0, 1).astype(BF16)
    d_qkv, grad_qkv = lax.optimization_barrier((d_qkv, grad_qkv))
    t_qkv = over_tiles(d_qkv)
    text_slice = text_states.shape[2] // grid_devices
    own_cols = lax.dynamic_slice_in_dim(
        f_text.reshape(f_text.shape[0], 2, -1), grid_at * group_heads * head_dim, group_heads * head_dim, 2
    ).reshape(f_text.shape[0], -1)
    text_parts = jnp.concatenate(
        [dot_over(text_rows, grad_kv, 0, 1).astype(BF16), plain_dot(own_cols, grad_kv).astype(BF16)],
        axis=1,
    )
    text_parts, grad_qkv = lax.optimization_barrier((text_parts, grad_qkv))
    grad_first = dot_over(grad_qkv, f_qkv, 0, 1)
    joint_blocks = by_device(jnp.split(t_joint[:, : 3 * model_width], 3, axis=1), 1)
    joint_grad = narrow_blocks(joint_blocks, grad_first)
    gain_first = jnp.sum(grad_first * first_z, axis=0)
    bias_first = jnp.sum(grad_first, axis=0)
    part_shift = jnp.sum(grad_first.reshape(images, tile_len, model_width), axis=1)
    grad_one = grad_two + norm_back(grad_first * norm_f[:, 0], first_z, first_inv)

    text_parts = swap_tiles(text_parts.reshape(grid_devices, text_slice, -1))
    own_width = own_cols.shape[1]
    d_text = text_parts[:, :, :own_width].reshape(grid_devices, text_slice, 2, -1)
    d_text = jnp.transpose(d_text, (1, 2, 0, 3)).reshape(text_slice, -1)
    shift_low = total_tiles(part_shift).astype(BF16)
    d_shift = left_dot(act_cols, shift_low).astype(BF16)
    grad_time_act = total_tiles(
        lax.dynamic_update_slice_in_dim(
            jnp.zeros_like(time_pre), right_dot(shift_low, part_shift_w), grid_at * shift_slice, 1
        )
    )
    grad_time_pre = silu_pull(grad_time_act)[0].astype(BF16)
    d_time = left_dot(embed_cols, grad_time_pre).astype(BF16)
    low_one = grad_one.astype(BF16)
    d_skip_w = left_dot(skip_in, low_one).astype(BF16)
    d_skip_w, low_one = lax.optimization_barrier((d_skip_w, low_one))
    skip_grad, grad_patch, skip_sums = join_back(low_one, f_skip, joined, joined_inv, gain_skip)
    t_qkv, d_skip_w, joint_grad, d_text, d_time, d_shift = lax.optimization_barrier(
        (t_qkv, d_skip_w, joint_grad, d_text, d_time, d_shift)
    )
    out_grad, query_w_grad, cross_grad = jnp.split(joint_grad, 3, axis=1)
    t_skip = over_tiles(d_skip_w)

    text_grad = jnp.sum(text_parts[:, :, own_width:].astype(F32), axis=0)
    text_grad = jnp.transpose(text_grad).reshape(images, text_pad, text_slice)
    text_grad = text_grad[:, :text_len]

    late, width = [], w_shift.shape[1]
    for at in range(dp_devices):
        pair = d_text[:, 2 * at * width : 2 * (at + 1) * width]
        own = slice(at * width, (at + 1) * width)
        late.append(
            jnp.concatenate([pair[:, :width], pair[:, width:], d_time[:, own], d_shift[:, own]])
        )
    late, qkv_grad = narrow_blocks(late, skip_sums), narrow(t_qkv, skip_sums)
    late, qkv_grad, skip_sums, grad_patch, skip_grad = lax.optimization_barrier(
        (late, qkv_grad, skip_sums, grad_patch, skip_grad)
    )
    rows = d_text.shape[0]
    text_w_grad = jnp.concatenate([late[:rows], late[rows : 2 * rows]], axis=1)
    time_w_grad, shift_w_grad = jnp.split(late[2 * rows :], [d_time.shape[0]], axis=0)
    skip_grad = skip_grad.reshape(images, rows_tile, cols_tile, model_width)
    gain_skips, bias_skips = skip_sums[0], skip_sums[1]
    d_patch = left_dot(grad_patch, patch_rows)
    latent_grad = plain_dot(grad_patch, f_patch).reshape(images, rows_tile, cols_tile, patch_width)
    d_norms = jnp.stack(
        [
            gain_first,
            bias_first,
            gain_third,
            bias_third,
            gain_second,
            bias_second,
            gain_final,
            bias_final,
            gain_skips[:model_width],
            bias_skips[:model_width],
            gain_skips[model_width:],
            bias_skips[model_width:],
        ],
        axis=1,
    )
    small_grads = jnp.concatenate(
        [
            grad.reshape(model_width, dp_devices, -1)
            for grad in (d_patch, d_final, d_norms)
        ],
        axis=2,
    )
    small_grads = narrow(sum_tiles(small_grads.reshape(model_width, -1)))
    skip_w_grad = narrow(t_skip)
    patch_grad, final_grad, norms_grad = (
        small_grads[:, cuts[at] : cuts[at + 1]] for at in range(3)
    )
    return (
        prediction,
        latent_grad,
        skip_grad,
        text_grad,
        patch_grad,
        skip_w_grad,
        time_w_grad,
        shift_w_grad,
        qkv_grad,
        out_grad,
        query_w_grad,
        text_w_grad,
        cross_grad,
        up_grad,
        down_grad,
        final_grad,
        norms_grad,
    )


def local(sizes, latent, *others):
    grid_devices = sizes["row"] * sizes["col"]
    tile_len = latent.shape[1] * latent.shape[2]
    if HEADS % grid_devices == 0 and tile_len % 128 == 0:
        return local_heads(latent, *others)
    return local_gathered(latent, *others)


def solution(mesh):
    return jax.shard_map(
        functools.partial(local, mesh.shape),
        mesh=mesh,
        in_specs=(
            P("dp", "row", "col", None),
            P("dp", "row", "col", None),
            P("dp", None, None),
            P("dp"),
            P("dp"),
            P("dp", "row", "col", None),
            P(("row", "col"), "dp"),
            P(("row", "col"), "dp"),
            P(("row", "col"), "dp"),
            P(("row", "col"), "dp"),
            P(("row", "col"), "dp"),
            P(("row", "col"), "dp"),
            P(("row", "col"), "dp"),
            P(("row", "col"), "dp"),
            P(("row", "col"), "dp"),
            P(("row", "col"), "dp"),
            P(("row", "col"), "dp"),
            P(("row", "col"), "dp"),
            P(("row", "col"), "dp"),
        ),
        out_specs=(
            P("dp", "row", "col", None),
            P("dp", "row", "col", None),
            P("dp", "row", "col", None),
            P("dp", None, ("row", "col")),
            P(("row", "col"), "dp"),
            P(("row", "col"), "dp"),
            P(("row", "col"), "dp"),
            P(("row", "col"), "dp"),
            P(("row", "col"), "dp"),
            P(("row", "col"), "dp"),
            P(("row", "col"), "dp"),
            P(("row", "col"), "dp"),
            P(("row", "col"), "dp"),
            P(("row", "col"), "dp"),
            P(("row", "col"), "dp"),
            P(("row", "col"), "dp"),
            P(("row", "col"), "dp"),
        ),
        check_vma=False,
    )
```

```python
import functools
import math

import jax
import jax.numpy as jnp
from jax import lax
from jax.experimental import pallas as pl
from jax.experimental.layout import Layout, with_layout_constraint
from jax.experimental.pallas import tpu as pltpu
from jax.sharding import PartitionSpec as P

HEADS = 16
FREQ = 256


EPSILON = 1e-06


def layer_norm(values_in):
    centred = values_in - jnp.mean(values_in, axis=-1, keepdims=True)
    inverse = lax.rsqrt(jnp.mean(centred * centred, axis=-1, keepdims=True) + EPSILON)
    return (centred * inverse, inverse)


def norm_back(grad_normed, normed, inverse):
    mean_grad = jnp.mean(grad_normed, axis=-1, keepdims=True)
    mean_cross = jnp.mean(grad_normed * normed, axis=-1, keepdims=True)
    return inverse * (grad_normed - mean_grad - normed * mean_cross)


def turn_half(piece_half, cosine, sine_tab):
    quarter = cosine.shape[-1]
    lower = piece_half[..., :quarter]
    higher = piece_half[..., quarter:]
    return jnp.concatenate(
        [lower * cosine - higher * sine_tab, higher * cosine + lower * sine_tab], axis=-1
    )


def rotate(values_in, tables, signum):
    cos_row, sin_row, cos_col, sin_col = tables
    half_dim = values_in.shape[-1] // 2
    return jnp.concatenate(
        [
            turn_half(values_in[..., :half_dim], cos_row, signum * sin_row),
            turn_half(values_in[..., half_dim:], cos_col, signum * sin_col),
        ],
        axis=-1,
    )


def rope_tables(row_pos, col_pos, head_size):
    quarter = head_size // 4
    frequency = jnp.exp(jnp.arange(quarter, dtype=jnp.float32) * (-math.log(10000.0) / quarter))
    row_ang = row_pos.astype(jnp.float32)[:, None, None] * frequency
    col_ang = col_pos.astype(jnp.float32)[:, None, None] * frequency
    return (jnp.cos(row_ang), jnp.sin(row_ang), jnp.cos(col_ang), jnp.sin(col_ang))


def time_embed(step_values, freq_count):
    half_dim = freq_count // 2
    rate_list = jnp.exp(jnp.arange(half_dim, dtype=jnp.float32) * (-math.log(10000.0) / half_dim))
    angles = step_values.astype(jnp.float32)[..., None] * rate_list
    return jnp.concatenate([jnp.cos(angles), jnp.sin(angles)], axis=-1)


def gelu_tanh(inputs):
    return jax.nn.gelu(inputs, approximate=True)


def plain_dot(left_mat, right_mat):
    return jnp.dot(left_mat, right_mat, preferred_element_type=jnp.float32)


def left_dot(left_mat, right_mat):
    return lax.dot_general(
        left_mat, right_mat, (((0,), (0,)), ((), ())), preferred_element_type=jnp.float32
    )


def right_dot(left_mat, right_mat):
    return lax.dot_general(
        left_mat, right_mat, (((1,), (1,)), ((), ())), preferred_element_type=jnp.float32
    )


def block_size(key_count):
    block_len = key_count
    while block_len > 1024 and block_len % 2 == 0:
        block_len = block_len // 2
    return block_len


def local_gathered(
    latent,
    skip_input,
    text_states,
    timesteps,
    image_sides,
    cotangent,
    w_patch,
    w_skip,
    w_time,
    w_shift,
    w_qkv,
    w_out,
    w_query,
    w_text,
    w_cross,
    w_up,
    w_down,
    w_final,
    norm_params,
):
    widened = (
        lax.all_gather(w_patch, "dp", axis=1, tiled=True),
        lax.all_gather(w_skip, "dp", axis=1, tiled=True),
        lax.all_gather(w_time, "dp", axis=1, tiled=True),
        lax.all_gather(w_shift, "dp", axis=1, tiled=True),
        lax.all_gather(w_qkv, "dp", axis=1, tiled=True),
        lax.all_gather(w_out, "dp", axis=1, tiled=True),
        lax.all_gather(w_query, "dp", axis=1, tiled=True),
        lax.all_gather(w_text, "dp", axis=1, tiled=True),
        lax.all_gather(w_cross, "dp", axis=1, tiled=True),
        lax.all_gather(w_up, "dp", axis=1, tiled=True),
        lax.all_gather(w_down, "dp", axis=1, tiled=True),
        lax.all_gather(w_final, "dp", axis=1, tiled=True),
        lax.all_gather(norm_params, "dp", axis=1, tiled=True),
    )
    gathered = (
        lax.all_gather(widened[0], ("row", "col"), axis=0, tiled=True),
        lax.all_gather(widened[1], ("row", "col"), axis=0, tiled=True),
        lax.all_gather(widened[2], ("row", "col"), axis=0, tiled=True),
        lax.all_gather(widened[3], ("row", "col"), axis=0, tiled=True),
        lax.all_gather(widened[4], ("row", "col"), axis=0, tiled=True),
        lax.all_gather(widened[5], ("row", "col"), axis=0, tiled=True),
        lax.all_gather(widened[6], ("row", "col"), axis=0, tiled=True),
        lax.all_gather(widened[7], ("row", "col"), axis=0, tiled=True),
        lax.all_gather(widened[8], ("row", "col"), axis=0, tiled=True),
        lax.all_gather(widened[9], ("row", "col"), axis=0, tiled=True),
        lax.all_gather(widened[10], ("row", "col"), axis=0, tiled=True),
        lax.all_gather(widened[11], ("row", "col"), axis=0, tiled=True),
        lax.all_gather(widened[12], ("row", "col"), axis=0, tiled=True),
    )
    (
        f_patch,
        f_skip,
        f_time,
        f_shift,
        f_qkv,
        f_out,
        f_query,
        f_text,
        f_cross,
        f_up,
        f_down,
        f_final,
        f_norms,
    ) = gathered
    part_text = widened[7]
    images, rows_tile, cols_tile, patch_width = latent.shape
    tile_len = rows_tile * cols_tile
    row_count = images * tile_len
    model_width = f_qkv.shape[0]
    head_count = HEADS
    head_dim = model_width // head_count
    text_len = text_states.shape[1]
    grid_devices = lax.axis_size(("row", "col"))
    col_devices = lax.axis_size("col")
    grid_at = lax.axis_index(("row", "col"))
    row_at = lax.axis_index("row")
    col_at = lax.axis_index("col")
    score_scale = head_dim ** (-0.5)
    positions = jnp.arange(tile_len, dtype=jnp.int32)
    row_pos = row_at * rows_tile + positions // cols_tile
    col_pos = col_at * cols_tile + positions % cols_tile
    query_ok = (row_pos[None, :] < image_sides[:, None]) & (col_pos[None, :] < image_sides[:, None])
    keep_rows = query_ok.astype(jnp.float32).reshape(row_count, 1)
    tables = rope_tables(row_pos, col_pos, head_dim)
    norm_f = f_norms.astype(jnp.float32)

    def valid_keys(offset, block_len):
        index_list = offset + jnp.arange(block_len, dtype=jnp.int32)
        source = index_list // tile_len
        within = index_list % tile_len
        key_row = source // col_devices * rows_tile + within // cols_tile
        key_col = source % col_devices * cols_tile + within % cols_tile
        return (key_row[None, :] < image_sides[:, None]) & (key_col[None, :] < image_sides[:, None])

    patch_rows = latent.reshape(row_count, patch_width)
    patch_feat = right_dot(patch_rows, f_patch)
    skip_rows = skip_input.reshape(row_count, model_width).astype(jnp.float32)
    gain_skip = jnp.concatenate([norm_f[:, 8], norm_f[:, 10]])
    bias_skip = jnp.concatenate([norm_f[:, 9], norm_f[:, 11]])
    joined, joined_inv = layer_norm(jnp.concatenate([patch_feat, skip_rows], axis=-1))
    skip_in = (joined * gain_skip + bias_skip).astype(jnp.bfloat16)
    residual = plain_dot(skip_in, f_skip)
    embedding = time_embed(timesteps, FREQ).astype(jnp.bfloat16)
    time_pre = plain_dot(embedding, f_time)
    time_float, silu_pull = jax.vjp(jax.nn.silu, time_pre)
    time_act = time_float.astype(jnp.bfloat16)
    time_shift = plain_dot(time_act, f_shift)
    first_z, first_inv = layer_norm(residual)
    first_pre = (first_z * norm_f[:, 0] + norm_f[:, 1]).reshape(
        images, tile_len, model_width
    ) + time_shift[:, None, :]
    first_in = first_pre.reshape(row_count, model_width).astype(jnp.bfloat16)
    qkv = plain_dot(first_in, f_qkv)
    query_z, query_inv = layer_norm(
        qkv[:, :model_width].reshape(images, tile_len, head_count, head_dim)
    )
    key_z, key_inv = layer_norm(
        qkv[:, model_width : 2 * model_width].reshape(images, tile_len, head_count, head_dim)
    )
    queries = rotate(query_z, tables, 1.0).astype(jnp.bfloat16)
    queries_h = jnp.transpose(queries, (0, 2, 1, 3))
    keys = rotate(key_z, tables, 1.0).astype(jnp.bfloat16).reshape(images, tile_len, model_width)
    values = qkv[:, 2 * model_width :].astype(jnp.bfloat16).reshape(images, tile_len, model_width)
    start_carry = (
        jnp.full((images, head_count, tile_len), -1e30, jnp.float32),
        jnp.zeros((images, head_count, tile_len), jnp.float32),
        jnp.zeros((images, head_count, tile_len, head_dim), jnp.float32),
    )
    key_rows = lax.all_gather(keys, ("row", "col"), axis=1, tiled=True)
    value_rows = lax.all_gather(values, ("row", "col"), axis=1, tiled=True)
    key_count = key_rows.shape[1]
    block_len = block_size(key_count)

    def forward_block_step(block_index, running):
        running_max, weight_sum, accum_sum = running
        offset = block_index * block_len
        key_blk = lax.dynamic_slice_in_dim(key_rows, offset, block_len, 1).reshape(
            images, block_len, head_count, head_dim
        )
        value_blk = lax.dynamic_slice_in_dim(value_rows, offset, block_len, 1).reshape(
            images, block_len, head_count, head_dim
        )
        key_ok = valid_keys(offset, block_len)
        scores = (
            jnp.einsum("ihqe,ikhe->ihqk", queries_h, key_blk, preferred_element_type=jnp.float32)
            * score_scale
        )
        scores = jnp.where(key_ok[:, None, None, :], scores, -jnp.inf)
        new_max = jnp.maximum(running_max, jnp.max(scores, axis=-1))
        weight = jnp.exp(scores - new_max[..., None])
        rescale = jnp.exp(running_max - new_max)
        weight_sum = weight_sum * rescale + jnp.sum(weight, axis=-1)
        accum_sum = accum_sum * rescale[..., None] + jnp.einsum(
            "ihqk,ikhe->ihqe",
            weight.astype(jnp.bfloat16),
            value_blk,
            preferred_element_type=jnp.float32,
        )
        return (new_max, weight_sum, accum_sum)

    running_max, weight_sum, accum_sum = lax.fori_loop(
        0, key_count // block_len, forward_block_step, start_carry
    )
    attended = accum_sum / weight_sum[..., None]
    log_sum = running_max + jnp.log(weight_sum)
    att_low = (
        jnp.transpose(attended, (0, 2, 1, 3)).reshape(row_count, model_width).astype(jnp.bfloat16)
    )
    residual_two = residual + plain_dot(att_low, f_out)
    third_z, third_inv = layer_norm(residual_two)
    third_in = (third_z * norm_f[:, 2] + norm_f[:, 3]).astype(jnp.bfloat16)
    cross_pre = plain_dot(third_in, f_query)
    cq_z, cq_inv = layer_norm(cross_pre.reshape(images, tile_len, head_count, head_dim))
    cross_queries = cq_z.astype(jnp.bfloat16)
    text_kv = jnp.einsum("itc,cd->itd", text_states, f_text, preferred_element_type=jnp.float32)
    ck_z, ck_inv = layer_norm(
        text_kv[..., :model_width].reshape(images, text_len, head_count, head_dim)
    )
    cross_keys = ck_z.astype(jnp.bfloat16)
    cross_values = (
        text_kv[..., model_width:]
        .astype(jnp.bfloat16)
        .reshape(images, text_len, head_count, head_dim)
    )

    def cross_softmax():
        scores = (
            jnp.einsum(
                "iqhe,ikhe->ihqk", cross_queries, cross_keys, preferred_element_type=jnp.float32
            )
            * score_scale
        )
        return jax.nn.softmax(scores, axis=-1)

    crossed = jnp.einsum(
        "ihqk,ikhe->iqhe",
        cross_softmax().astype(jnp.bfloat16),
        cross_values,
        preferred_element_type=jnp.float32,
    )
    cross_low = crossed.reshape(row_count, model_width).astype(jnp.bfloat16)
    residual_three = residual_two + plain_dot(cross_low, f_cross)
    second_z, second_inv = layer_norm(residual_three)
    second_in = (second_z * norm_f[:, 4] + norm_f[:, 5]).astype(jnp.bfloat16)
    up_pre = plain_dot(second_in, f_up)
    hidden_float, gelu_pull = jax.vjp(gelu_tanh, up_pre)
    hidden_act = hidden_float.astype(jnp.bfloat16)
    residual_four = residual_three + plain_dot(hidden_act, f_down)
    last_z, last_inv = layer_norm(residual_four)
    last_in = (last_z * norm_f[:, 6] + norm_f[:, 7]).astype(jnp.bfloat16)
    produced = plain_dot(last_in, f_final)
    prediction = (
        (produced * keep_rows)
        .astype(jnp.bfloat16)
        .reshape(images, rows_tile, cols_tile, produced.shape[1])
    )
    grad_out = (
        cotangent.reshape(row_count, produced.shape[1]).astype(jnp.float32) * keep_rows
    ).astype(jnp.bfloat16)
    d_final = left_dot(last_in, grad_out)
    grad_last = right_dot(grad_out, f_final)
    gain_final = jnp.sum(grad_last * last_z, axis=0)
    bias_final = jnp.sum(grad_last, axis=0)
    grad_four = norm_back(grad_last * norm_f[:, 6], last_z, last_inv)
    low_four = grad_four.astype(jnp.bfloat16)
    d_down = left_dot(hidden_act, low_four)
    grad_hidden = right_dot(low_four, f_down)
    grad_up = gelu_pull(grad_hidden)[0].astype(jnp.bfloat16)
    d_up = left_dot(second_in, grad_up)
    grad_second = right_dot(grad_up, f_up)
    gain_second = jnp.sum(grad_second * second_z, axis=0)
    bias_second = jnp.sum(grad_second, axis=0)
    grad_three = grad_four + norm_back(grad_second * norm_f[:, 4], second_z, second_inv)
    low_three = grad_three.astype(jnp.bfloat16)
    d_cross = left_dot(cross_low, low_three)
    grad_crossed = (
        right_dot(low_three, f_cross)
        .astype(jnp.bfloat16)
        .reshape(images, tile_len, head_count, head_dim)
    )
    cross_probs = cross_softmax()
    cross_delta = jnp.transpose(
        jnp.sum(grad_crossed.astype(jnp.float32) * crossed, axis=-1), (0, 2, 1)
    )
    grad_probs = jnp.einsum(
        "iqhe,ikhe->ihqk", grad_crossed, cross_values, preferred_element_type=jnp.float32
    )
    grad_cscore = (cross_probs * (grad_probs - cross_delta[..., None])).astype(jnp.bfloat16)
    grad_cq = score_scale * jnp.einsum(
        "ihqk,ikhe->iqhe", grad_cscore, cross_keys, preferred_element_type=jnp.float32
    )
    part_ckey = score_scale * jnp.einsum(
        "ihqk,iqhe->ikhe", grad_cscore, cross_queries, preferred_element_type=jnp.float32
    )
    part_cvalue = jnp.einsum(
        "ihqk,iqhe->ikhe",
        cross_probs.astype(jnp.bfloat16),
        grad_crossed,
        preferred_element_type=jnp.float32,
    )
    grad_cross_q = (
        norm_back(grad_cq, cq_z, cq_inv).reshape(row_count, model_width).astype(jnp.bfloat16)
    )
    d_query = left_dot(third_in, grad_cross_q)
    grad_third = right_dot(grad_cross_q, f_query)
    gain_third = jnp.sum(grad_third * third_z, axis=0)
    bias_third = jnp.sum(grad_third, axis=0)
    grad_two = grad_three + norm_back(grad_third * norm_f[:, 2], third_z, third_inv)
    sum_ckey, sum_cvalue = lax.psum((part_ckey, part_cvalue), ("row", "col"))
    low_two = grad_two.astype(jnp.bfloat16)
    d_out = left_dot(att_low, low_two)
    grad_att = (
        right_dot(low_two, f_out)
        .astype(jnp.bfloat16)
        .reshape(images, tile_len, head_count, head_dim)
    )
    grad_att_h = jnp.transpose(grad_att, (0, 2, 1, 3))
    delta_rows = jnp.sum(grad_att_h.astype(jnp.float32) * attended, axis=-1)
    back_carry = (
        jnp.zeros((images, head_count, tile_len, head_dim), jnp.float32),
        jnp.zeros((images, tile_len * grid_devices, model_width), jnp.float32),
        jnp.zeros((images, tile_len * grid_devices, model_width), jnp.float32),
    )
    backward_key_rows = lax.all_gather(keys, ("row", "col"), axis=1, tiled=True)
    backward_value_rows = lax.all_gather(values, ("row", "col"), axis=1, tiled=True)
    key_count = backward_key_rows.shape[1]
    backward_block_len = block_size(key_count)

    def backward_block_step(block_index, running):
        grad_query, grad_key_all, grad_value_all = running
        offset = block_index * backward_block_len
        key_blk = lax.dynamic_slice_in_dim(
            backward_key_rows, offset, backward_block_len, 1
        ).reshape(images, backward_block_len, head_count, head_dim)
        value_blk = lax.dynamic_slice_in_dim(
            backward_value_rows, offset, backward_block_len, 1
        ).reshape(images, backward_block_len, head_count, head_dim)
        key_ok = valid_keys(offset, backward_block_len)
        scores = (
            jnp.einsum("ihqe,ikhe->ihqk", queries_h, key_blk, preferred_element_type=jnp.float32)
            * score_scale
        )
        scores = jnp.where(key_ok[:, None, None, :], scores, -jnp.inf)
        attn_probs = jnp.exp(scores - log_sum[..., None])
        grad_prob = jnp.einsum(
            "ihqe,ikhe->ihqk", grad_att_h, value_blk, preferred_element_type=jnp.float32
        )
        grad_score = (attn_probs * (grad_prob - delta_rows[..., None])).astype(jnp.bfloat16)
        grad_query = grad_query + score_scale * jnp.einsum(
            "ihqk,ikhe->ihqe", grad_score, key_blk, preferred_element_type=jnp.float32
        )
        key_part = score_scale * jnp.einsum(
            "ihqk,ihqe->ikhe", grad_score, queries_h, preferred_element_type=jnp.float32
        )
        value_part = jnp.einsum(
            "ihqk,ihqe->ikhe",
            attn_probs.astype(jnp.bfloat16),
            grad_att_h,
            preferred_element_type=jnp.float32,
        )
        grad_key_all = lax.dynamic_update_slice_in_dim(
            grad_key_all, key_part.reshape(images, backward_block_len, model_width), offset, 1
        )
        grad_value_all = lax.dynamic_update_slice_in_dim(
            grad_value_all, value_part.reshape(images, backward_block_len, model_width), offset, 1
        )
        return (grad_query, grad_key_all, grad_value_all)

    grad_query, grad_key_all, grad_value_all = lax.fori_loop(
        0, key_count // backward_block_len, backward_block_step, back_carry
    )
    grad_key_own, grad_value_own = (
        lax.psum_scatter(grad_key_all, ("row", "col"), scatter_dimension=1, tiled=True),
        lax.psum_scatter(grad_value_all, ("row", "col"), scatter_dimension=1, tiled=True),
    )
    grad_qn = rotate(jnp.transpose(grad_query, (0, 2, 1, 3)), tables, -1.0)
    grad_kn = rotate(grad_key_own.reshape(images, tile_len, head_count, head_dim), tables, -1.0)
    grad_qkv = jnp.concatenate(
        [
            norm_back(grad_qn, query_z, query_inv).reshape(row_count, model_width),
            norm_back(grad_kn, key_z, key_inv).reshape(row_count, model_width),
            grad_value_own.reshape(row_count, model_width),
        ],
        axis=-1,
    ).astype(jnp.bfloat16)
    d_qkv = left_dot(first_in, grad_qkv)
    grad_first = right_dot(grad_qkv, f_qkv)
    gain_first = jnp.sum(grad_first * first_z, axis=0)
    bias_first = jnp.sum(grad_first, axis=0)
    part_shift = jnp.sum(grad_first.reshape(images, tile_len, model_width), axis=1)
    grad_one = grad_two + norm_back(grad_first * norm_f[:, 0], first_z, first_inv)
    shift_grad = lax.psum(part_shift, ("row", "col"))
    grad_ckey = norm_back(sum_ckey, ck_z, ck_inv).reshape(images, text_len, model_width)
    grad_kv = jnp.concatenate(
        [grad_ckey, sum_cvalue.reshape(images, text_len, model_width)], axis=-1
    ).astype(jnp.bfloat16)
    text_slice = text_states.shape[2] // grid_devices
    text_cols = lax.dynamic_slice_in_dim(text_states, grid_at * text_slice, text_slice, 2)
    d_text_w = jnp.einsum("itc,itd->cd", text_cols, grad_kv, preferred_element_type=jnp.float32)
    text_grad = jnp.einsum("itd,cd->itc", grad_kv, part_text, preferred_element_type=jnp.float32)
    shift_low = shift_grad.astype(jnp.bfloat16)
    shift_slice = model_width // grid_devices
    act_cols = lax.dynamic_slice_in_dim(time_act, grid_at * shift_slice, shift_slice, 1)
    d_shift_w = jnp.einsum("ic,id->cd", act_cols, shift_low, preferred_element_type=jnp.float32)
    grad_time_act = right_dot(shift_low, f_shift)
    grad_time_pre = silu_pull(grad_time_act)[0].astype(jnp.bfloat16)
    freq_slice = embedding.shape[1] // grid_devices
    embed_cols = lax.dynamic_slice_in_dim(embedding, grid_at * freq_slice, freq_slice, 1)
    d_time_w = jnp.einsum(
        "ic,id->cd", embed_cols, grad_time_pre, preferred_element_type=jnp.float32
    )
    low_one = grad_one.astype(jnp.bfloat16)
    d_skip_w = left_dot(skip_in, low_one)
    grad_skip_in = right_dot(low_one, f_skip)
    gain_skips = jnp.sum(grad_skip_in * joined, axis=0)
    bias_skips = jnp.sum(grad_skip_in, axis=0)
    grad_joined = norm_back(grad_skip_in * gain_skip, joined, joined_inv)
    skip_grad = grad_joined[:, model_width:].reshape(images, rows_tile, cols_tile, model_width)
    grad_patch = grad_joined[:, :model_width].astype(jnp.bfloat16)
    d_patch = left_dot(grad_patch, patch_rows)
    latent_grad = plain_dot(grad_patch, f_patch).reshape(images, rows_tile, cols_tile, patch_width)
    d_norms = jnp.stack(
        [
            gain_first,
            bias_first,
            gain_third,
            bias_third,
            gain_second,
            bias_second,
            gain_final,
            bias_final,
            gain_skips[:model_width],
            bias_skips[:model_width],
            gain_skips[model_width:],
            bias_skips[model_width:],
        ],
        axis=1,
    )
    tile_done = (
        lax.psum_scatter(d_patch, ("row", "col"), scatter_dimension=0, tiled=True),
        lax.psum_scatter(d_skip_w, ("row", "col"), scatter_dimension=0, tiled=True),
        lax.psum_scatter(d_qkv, ("row", "col"), scatter_dimension=0, tiled=True),
        lax.psum_scatter(d_out, ("row", "col"), scatter_dimension=0, tiled=True),
        lax.psum_scatter(d_query, ("row", "col"), scatter_dimension=0, tiled=True),
        lax.psum_scatter(d_cross, ("row", "col"), scatter_dimension=0, tiled=True),
        lax.psum_scatter(d_up, ("row", "col"), scatter_dimension=0, tiled=True),
        lax.psum_scatter(d_down, ("row", "col"), scatter_dimension=0, tiled=True),
        lax.psum_scatter(d_final, ("row", "col"), scatter_dimension=0, tiled=True),
        lax.psum_scatter(d_norms, ("row", "col"), scatter_dimension=0, tiled=True),
    )
    reduced = (
        lax.psum_scatter(
            tile_done[0].astype(jnp.bfloat16), "dp", scatter_dimension=1, tiled=True
        ).astype(jnp.float32),
        lax.psum_scatter(
            tile_done[1].astype(jnp.bfloat16), "dp", scatter_dimension=1, tiled=True
        ).astype(jnp.float32),
        lax.psum_scatter(
            tile_done[2].astype(jnp.bfloat16), "dp", scatter_dimension=1, tiled=True
        ).astype(jnp.float32),
        lax.psum_scatter(
            tile_done[3].astype(jnp.bfloat16), "dp", scatter_dimension=1, tiled=True
        ).astype(jnp.float32),
        lax.psum_scatter(
            tile_done[4].astype(jnp.bfloat16), "dp", scatter_dimension=1, tiled=True
        ).astype(jnp.float32),
        lax.psum_scatter(
            tile_done[5].astype(jnp.bfloat16), "dp", scatter_dimension=1, tiled=True
        ).astype(jnp.float32),
        lax.psum_scatter(
            tile_done[6].astype(jnp.bfloat16), "dp", scatter_dimension=1, tiled=True
        ).astype(jnp.float32),
        lax.psum_scatter(
            tile_done[7].astype(jnp.bfloat16), "dp", scatter_dimension=1, tiled=True
        ).astype(jnp.float32),
        lax.psum_scatter(
            tile_done[8].astype(jnp.bfloat16), "dp", scatter_dimension=1, tiled=True
        ).astype(jnp.float32),
        lax.psum_scatter(
            tile_done[9].astype(jnp.bfloat16), "dp", scatter_dimension=1, tiled=True
        ).astype(jnp.float32),
        lax.psum_scatter(
            d_time_w.astype(jnp.bfloat16), "dp", scatter_dimension=1, tiled=True
        ).astype(jnp.float32),
        lax.psum_scatter(
            d_shift_w.astype(jnp.bfloat16), "dp", scatter_dimension=1, tiled=True
        ).astype(jnp.float32),
        lax.psum_scatter(
            d_text_w.astype(jnp.bfloat16), "dp", scatter_dimension=1, tiled=True
        ).astype(jnp.float32),
    )
    return (
        prediction,
        latent_grad,
        skip_grad,
        text_grad,
        reduced[0],
        reduced[1],
        reduced[10],
        reduced[11],
        reduced[2],
        reduced[3],
        reduced[4],
        reduced[12],
        reduced[5],
        reduced[6],
        reduced[7],
        reduced[8],
        reduced[9],
    )


TILE = ("row", "col")
EVERY = ("dp", "row", "col")
LOG2E = math.log2(math.e)
F32 = jnp.float32
BF16 = jnp.bfloat16
VMEM_BYTES = 56 * 2**20


def kernel_call(body, flops, moved, **options):
    return pl.pallas_call(
        body,
        compiler_params=pltpu.CompilerParams(vmem_limit_bytes=VMEM_BYTES),
        cost_estimate=pl.CostEstimate(flops=flops, bytes_accessed=moved, transcendentals=0),
        **options,
    )


def pair_swap(values_in):
    quarter = values_in.shape[0] // 4
    parts = [values_in[at * quarter : (at + 1) * quarter] for at in (1, 0, 3, 2)]
    return jnp.concatenate(parts, axis=0)


def column_norm(values_in):
    centred = values_in - jnp.mean(values_in, axis=0, keepdims=True)
    inverse = lax.rsqrt(jnp.mean(centred * centred, axis=0, keepdims=True) + EPSILON)
    return (centred * inverse, inverse)


def column_norm_back(grad_normed, normed, inverse):
    mean_grad = jnp.mean(grad_normed, axis=0, keepdims=True)
    mean_cross = jnp.mean(grad_normed * normed, axis=0, keepdims=True)
    return inverse * (grad_normed - mean_grad - normed * mean_cross)


def minus_pieces(row_values):
    high = row_values.astype(BF16).astype(F32)
    rest = row_values - high
    middle = rest.astype(BF16).astype(F32)
    lower = rest - middle
    at = lax.broadcasted_iota(jnp.int32, (8, row_values.shape[1]), 0)
    zero = jnp.zeros((8, row_values.shape[1]), F32)
    picked = jnp.where(at == 0, high, jnp.where(at == 1, middle, jnp.where(at == 2, lower, zero)))
    return -picked


def piece_flags(width):
    return (lax.broadcasted_iota(jnp.int32, (8, width), 0) < 3).astype(F32)


def head_norm_body(
    query_scale, rows_ref, weight_ref, cos_ref, sin_ref, ok_ref, out_ref, inv_ref
):
    groups, _, heads, head_dim, _ = out_ref.shape
    part = pl.program_id(0)
    made = jnp.dot(rows_ref[...], weight_ref[...], preferred_element_type=F32).T
    valid = ok_ref[...]

    @pl.when(part < 2)
    def _():
        factor = jnp.where(part == 0, query_scale, valid)
        cosine, sine = cos_ref[...] * factor, sin_ref[...] * factor
        for group in range(groups):
            for head in range(heads):
                at = (group * heads + head) * head_dim
                normed, inverse = column_norm(made[at : at + head_dim])
                turned = normed * cosine + pair_swap(normed) * sine
                out_ref[group, 0, head] = turned.astype(BF16)
                inv_ref[group, 0, head : head + 1] = inverse

    @pl.when(part == 2)
    def _():
        for group in range(groups):
            for head in range(heads):
                at = (group * heads + head) * head_dim
                out_ref[group, 0, head] = (made[at : at + head_dim] * valid).astype(BF16)
                inv_ref[group, 0, head : head + 1] = valid


def head_norm(rows, weight, tables, valid, groups, head_dim, query_scale):
    tile_len, depth = rows.shape
    width = weight.shape[1] // 3
    heads = width // groups // head_dim
    table = pl.BlockSpec((head_dim, tile_len), lambda p: (0, 0))
    return kernel_call(
        functools.partial(head_norm_body, query_scale),
        6 * tile_len * depth * width,
        6 * depth * width,
        grid=(3,),
        in_specs=[
            pl.BlockSpec((tile_len, depth), lambda p: (0, 0)),
            pl.BlockSpec((depth, width), lambda p: (0, p)),
            table,
            table,
            pl.BlockSpec((1, tile_len), lambda p: (0, 0)),
        ],
        out_specs=[
            pl.BlockSpec((groups, 1, heads, head_dim, tile_len), lambda p: (0, p, 0, 0, 0)),
            pl.BlockSpec((groups, 1, heads, tile_len), lambda p: (0, p, 0, 0)),
        ],
        out_shape=[
            jax.ShapeDtypeStruct((groups, 3, heads, head_dim, tile_len), BF16),
            jax.ShapeDtypeStruct((groups, 3, heads, tile_len), F32),
        ],
    )(rows, weight, *tables, valid)


def head_back_body(
    query_scale, grad_ref, own_ref, inv_ref, cos_ref, sin_ref, ok_ref, *others
):
    out_ref = others[-1]
    heads, head_dim = own_ref.shape[2], own_ref.shape[3]
    cosine, sine, valid = cos_ref[...], sin_ref[...], ok_ref[...]

    def unturn(values_in):
        return values_in * cosine - pair_swap(values_in) * sine

    for part in range(3):
        pieces = []
        for head in range(heads):
            grad = grad_ref[0, part, head].astype(F32)
            if part > 0:
                grad = grad * valid
            if part < 2:
                normed = unturn(own_ref[0, part, head].astype(F32))
                if part == 0:
                    normed = normed * (1.0 / query_scale)
                inverse = inv_ref[0, part, head : head + 1]
                grad = column_norm_back(unturn(grad), normed, inverse)
            pieces.append(grad)
        out_ref[part, 0] = jnp.concatenate(pieces, axis=0).astype(BF16)


def head_back(grads, own, inverses, tables, valid, query_scale, image, images, before):
    groups, _, heads, head_dim, tile_len = own.shape
    group_rows = heads * head_dim
    stacked = pl.BlockSpec((1, 3, heads, head_dim, tile_len), lambda g: (g, 0, 0, 0, 0))
    table = pl.BlockSpec((head_dim, tile_len), lambda g: (0, 0))
    earlier = () if before is None else (before,)
    return kernel_call(
        functools.partial(head_back_body, query_scale),
        0,
        6 * own.size,
        grid=(groups,),
        in_specs=[
            stacked,
            stacked,
            pl.BlockSpec((1, 3, heads, tile_len), lambda g: (g, 0, 0, 0)),
            table,
            table,
            pl.BlockSpec((1, tile_len), lambda g: (0, 0)),
        ]
        + [pl.BlockSpec(memory_space=pl.ANY)] * len(earlier),
        out_specs=pl.BlockSpec((3, 1, group_rows, tile_len), lambda g: (0, g, 0, image)),
        out_shape=jax.ShapeDtypeStruct((3, groups, group_rows, images * tile_len), BF16),
        input_output_aliases={6: 0} if earlier else {},
    )(grads, own, inverses, *tables, valid, *earlier)


def attend_body(query_ref, key_ref, value_ref, ok_ref, out_ref, lse_ref, key_nat, value_ext):
    tiles, tile_len, head_dim = key_ref.shape[0], key_ref.shape[-1], key_ref.shape[-2]

    @pl.when(pl.program_id(1) == 0)
    def _():
        for tile in range(tiles):
            key_nat[tile * tile_len : (tile + 1) * tile_len, :] = key_ref[tile, 0, 0].T
            value_ext[tile] = jnp.concatenate(
                [value_ref[tile, 0, 0].astype(F32), ok_ref[tile]], axis=0
            ).astype(BF16)

    query = query_ref[0, 0, 0]
    total = jnp.zeros((head_dim + 8, tile_len), F32)
    held = None
    for tile in range(tiles + 1):
        scores = None
        if tile < tiles:
            rows = slice(tile * tile_len, (tile + 1) * tile_len)
            scores = jnp.dot(key_nat[rows, :], query, preferred_element_type=F32)
        if held is not None:
            weight = jnp.exp2(held).astype(BF16)
            total = total + jnp.dot(value_ext[tile - 1], weight, preferred_element_type=F32)
        held = scores
    weight_sum = total[head_dim : head_dim + 1]
    out_ref[0, 0] = (total[:head_dim] / weight_sum).astype(BF16)
    lse_ref[0, 0] = jnp.log2(weight_sum)


def attend(qkv, flags):
    tiles, _, heads, head_dim, tile_len = qkv.shape
    return kernel_call(
        attend_body,
        1024 * heads * tiles**2 * tile_len**2,
        8 * qkv.size,
        grid=(heads, tiles),
        in_specs=[
            pl.BlockSpec((1, 1, 1, head_dim, tile_len), lambda h, t: (t, 0, h, 0, 0)),
            pl.BlockSpec((tiles, 1, 1, head_dim, tile_len), lambda h, t: (0, 1, h, 0, 0)),
            pl.BlockSpec((tiles, 1, 1, head_dim, tile_len), lambda h, t: (0, 2, h, 0, 0)),
            pl.BlockSpec((tiles, 8, tile_len), lambda h, t: (0, 0, 0)),
        ],
        out_specs=[
            pl.BlockSpec((1, 1, head_dim, tile_len), lambda h, t: (t, h, 0, 0)),
            pl.BlockSpec((1, 1, 1, tile_len), lambda h, t: (t, h, 0, 0)),
        ],
        out_shape=[
            jax.ShapeDtypeStruct((tiles, heads, head_dim, tile_len), BF16),
            jax.ShapeDtypeStruct((tiles, heads, 1, tile_len), F32),
        ],
        scratch_shapes=[
            pltpu.VMEM((tiles * tile_len, head_dim), BF16),
            pltpu.VMEM((tiles, head_dim + 8, tile_len), BF16),
        ],
    )(qkv, qkv, qkv, flags)


def attend_back_body(
    score_scale,
    query_ref,
    key_ref,
    value_ref,
    grad_ref,
    att_ref,
    lse_ref,
    out_ref,
    key_nat,
    value_nat,
    key_sum,
    value_sum,
):
    tiles, tile_len, head_dim = key_ref.shape[0], key_ref.shape[-1], key_ref.shape[-2]
    at = pl.program_id(1)

    @pl.when(at == 0)
    def _():
        ones = piece_flags(tile_len)
        for tile in range(tiles):
            rows = slice(tile * tile_len, (tile + 1) * tile_len)
            for source, kept in ((key_ref, key_nat), (value_ref, value_nat)):
                wide = jnp.concatenate([source[tile, 0, 0].astype(F32), ones], axis=0)
                kept[rows, :] = wide.T.astype(BF16)
        key_sum[...] = jnp.zeros_like(key_sum)
        value_sum[...] = jnp.zeros_like(value_sum)

    query = query_ref[0, 0, 0].astype(F32)
    grad = grad_ref[0, 0].astype(F32)
    delta = jnp.sum(grad * att_ref[0, 0].astype(F32), axis=0, keepdims=True)
    query_ext = jnp.concatenate([query, minus_pieces(lse_ref[0, 0])], axis=0)
    grad_ext = jnp.concatenate([grad, minus_pieces(delta)], axis=0)
    query_cols, grad_cols = query_ext.astype(BF16), grad_ext.astype(BF16)
    query_nat, grad_nat = query_ext.T.astype(BF16), grad_ext.T.astype(BF16)

    def step(tile, total):
        rows = pl.ds(pl.multiple_of(tile * tile_len, tile_len), tile_len)
        scores = jnp.dot(key_nat[rows, :], query_cols, preferred_element_type=F32)
        probs = jnp.exp2(scores)
        grad_probs = jnp.dot(value_nat[rows, :], grad_cols, preferred_element_type=F32)
        grad_scores = (probs * grad_probs).astype(BF16)
        value_sum[rows, :] += jnp.dot(probs.astype(BF16), grad_nat, preferred_element_type=F32)
        key_sum[rows, :] += jnp.dot(grad_scores, query_nat, preferred_element_type=F32)
        return total + jnp.dot(key_ref[tile, 0, 0], grad_scores, preferred_element_type=F32)

    start = jnp.zeros((head_dim, tile_len), F32)
    total = lax.fori_loop(0, tiles, step, start, unroll=8)
    out_ref[at, 0, 0] = (total * score_scale).astype(BF16)

    @pl.when(at == tiles - 1)
    def _():
        for tile in range(tiles):
            rows = slice(tile * tile_len, (tile + 1) * tile_len)
            key_grad = key_sum[rows, :].T[:head_dim] * (1.0 / LOG2E)
            out_ref[tile, 1, 0] = key_grad.astype(BF16)
            out_ref[tile, 2, 0] = value_sum[rows, :].T[:head_dim].astype(BF16)


def attend_back(qkv, grad_att, att, lse, score_scale):
    tiles, _, heads, head_dim, tile_len = qkv.shape
    one = pl.BlockSpec((1, 1, head_dim, tile_len), lambda h, t: (t, h, 0, 0))
    return kernel_call(
        functools.partial(attend_back_body, score_scale),
        2560 * heads * tiles**2 * tile_len**2,
        8 * qkv.size,
        grid=(heads, tiles),
        in_specs=[
            pl.BlockSpec((1, 1, 1, head_dim, tile_len), lambda h, t: (t, 0, h, 0, 0)),
            pl.BlockSpec((tiles, 1, 1, head_dim, tile_len), lambda h, t: (0, 1, h, 0, 0)),
            pl.BlockSpec((tiles, 1, 1, head_dim, tile_len), lambda h, t: (0, 2, h, 0, 0)),
            one,
            one,
            pl.BlockSpec((1, 1, 1, tile_len), lambda h, t: (t, h, 0, 0)),
        ],
        out_specs=pl.BlockSpec(
            (tiles, 3, 1, head_dim, tile_len), lambda h, t: (0, 0, h, 0, 0)
        ),
        out_shape=jax.ShapeDtypeStruct(qkv.shape, BF16),
        scratch_shapes=[
            pltpu.VMEM((tiles * tile_len, head_dim + 8), BF16),
            pltpu.VMEM((tiles * tile_len, head_dim + 8), BF16),
            pltpu.VMEM((tiles * tile_len, head_dim + 8), F32),
            pltpu.VMEM((tiles * tile_len, head_dim + 8), F32),
        ],
    )(qkv, qkv, qkv, grad_att, att, lse)


def cross_body(text_len, query_scale, pre_ref, kv_ref, att_ref, query_ref, inv_ref, lse_ref):
    head_dim, text_pad = kv_ref.shape[2], kv_ref.shape[3]
    at = lax.broadcasted_iota(jnp.int32, (8, text_pad), 0)
    text_at = lax.broadcasted_iota(jnp.int32, (8, text_pad), 1)
    flags = ((at == 0) & (text_at < text_len)).astype(F32)
    for head in range(pre_ref.shape[0]):
        normed, inverse = column_norm(pre_ref[head])
        query = (normed * query_scale).astype(BF16)
        query_ref[head] = query
        inv_ref[head] = inverse
        key = column_norm(kv_ref[0, head])[0].astype(BF16)
        value_ext = jnp.concatenate([kv_ref[1, head], flags], axis=0).astype(BF16)
        scores = jnp.dot(key.T, query, preferred_element_type=F32)
        weight = jnp.exp2(scores).astype(BF16)
        total = jnp.dot(value_ext, weight, preferred_element_type=F32)
        weight_sum = total[head_dim : head_dim + 1]
        att_ref[head] = (total[:head_dim] / weight_sum).astype(BF16)
        lse_ref[head] = jnp.log2(weight_sum)


def cross_attend(pre, text_kv, images, text_len, query_scale):
    heads, head_dim, tokens = pre.shape
    tile_len, text_pad = tokens // images, text_kv.shape[3] // images
    block = math.gcd(heads, 4)
    wide = pl.BlockSpec((block, head_dim, tile_len), lambda i, h: (h, 0, i))
    row = pl.BlockSpec((block, 1, tile_len), lambda i, h: (h, 0, i))
    return kernel_call(
        functools.partial(cross_body, text_len, query_scale),
        1024 * heads * tokens * text_pad,
        8 * pre.size,
        grid=(images, heads // block),
        in_specs=[wide, pl.BlockSpec((2, block, head_dim, text_pad), lambda i, h: (0, h, 0, i))],
        out_specs=[wide, wide, row, row],
        out_shape=[
            jax.ShapeDtypeStruct(pre.shape, BF16),
            jax.ShapeDtypeStruct(pre.shape, BF16),
            jax.ShapeDtypeStruct((heads, 1, tokens), F32),
            jax.ShapeDtypeStruct((heads, 1, tokens), F32),
        ],
    )(pre, text_kv)


def cross_back_body(
    query_scale,
    score_scale,
    query_ref,
    kv_ref,
    grad_ref,
    att_ref,
    inv_ref,
    lse_ref,
    out_ref,
    key_ref,
    value_ref,
):
    head_dim, text_pad = kv_ref.shape[2], kv_ref.shape[3]
    ones = piece_flags(text_pad)
    for head in range(query_ref.shape[0]):
        query = query_ref[head].astype(F32)
        grad = grad_ref[head].astype(F32)
        delta = jnp.sum(grad * att_ref[head].astype(F32), axis=0, keepdims=True)
        query_ext = jnp.concatenate([query, minus_pieces(lse_ref[head])], axis=0).astype(BF16)
        grad_ext = jnp.concatenate([grad, minus_pieces(delta)], axis=0).astype(BF16)
        key = column_norm(kv_ref[0, head])[0].astype(BF16)
        key_ext = jnp.concatenate([key.astype(F32), ones], axis=0).T.astype(BF16)
        value_ext = jnp.concatenate([kv_ref[1, head], ones], axis=0).T.astype(BF16)
        probs = jnp.exp2(jnp.dot(key_ext, query_ext, preferred_element_type=F32))
        grad_probs = jnp.dot(value_ext, grad_ext, preferred_element_type=F32)
        grad_scores = (probs * grad_probs).astype(BF16)
        value_grad = right_dot(grad_ext, probs.astype(BF16))[:head_dim]
        key_grad = right_dot(query_ext, grad_scores)[:head_dim]
        key_ref[head] = (key_grad * (1.0 / LOG2E)).astype(BF16)
        value_ref[head] = value_grad.astype(BF16)
        query_grad = jnp.dot(key, grad_scores, preferred_element_type=F32) * score_scale
        normed = query * (1.0 / query_scale)
        out_ref[head] = column_norm_back(query_grad, normed, inv_ref[head]).astype(BF16)


def cross_back(query, text_kv, grad, att, inverse, lse, images, query_scale, score_scale):
    heads, head_dim, tokens = query.shape
    tile_len, text_pad = tokens // images, text_kv.shape[3] // images
    block = math.gcd(heads, 4)
    wide = pl.BlockSpec((block, head_dim, tile_len), lambda i, h: (h, 0, i))
    row = pl.BlockSpec((block, 1, tile_len), lambda i, h: (h, 0, i))
    text = pl.BlockSpec((2, block, head_dim, text_pad), lambda i, h: (0, h, 0, i))
    text_out = pl.BlockSpec((block, head_dim, text_pad), lambda i, h: (h, 0, i))
    return kernel_call(
        functools.partial(cross_back_body, query_scale, score_scale),
        2560 * heads * tokens * text_pad,
        16 * query.size,
        grid=(images, heads // block),
        in_specs=[wide, text, wide, wide, row, row],
        out_specs=[
            wide,
            text_out,
            text_out,
        ],
        out_shape=[
            jax.ShapeDtypeStruct(query.shape, BF16),
            jax.ShapeDtypeStruct((heads, head_dim, images * text_pad), BF16),
            jax.ShapeDtypeStruct((heads, head_dim, images * text_pad), BF16),
        ],
    )(query, text_kv, grad, att, inverse, lse)


def join_norm_body(patch_ref, skip_ref, weight_ref, gain_ref, bias_ref, z_ref, inv_ref, in_ref):
    width = skip_ref.shape[1]
    patch_feat = right_dot(patch_ref[...], weight_ref[...])
    joined = jnp.concatenate([patch_feat, skip_ref[...].astype(F32)], axis=1)
    normed, inverse = layer_norm(joined)
    z_ref[...] = normed
    inv_ref[...] = inverse
    in_ref[...] = (normed * gain_ref[...] + bias_ref[...]).astype(BF16)


def join_norm(patch_rows, skip_rows, f_patch, gain, bias):
    tokens, width = skip_rows.shape
    block = math.gcd(tokens, 256)
    rows = lambda columns: pl.BlockSpec((block, columns), lambda t: (t, 0))
    fixed = lambda shape: pl.BlockSpec(shape, lambda t: (0, 0))
    return kernel_call(
        join_norm_body,
        64 * tokens * width,
        16 * tokens * width,
        grid=(tokens // block,),
        in_specs=[
            rows(patch_rows.shape[1]),
            rows(width),
            fixed(f_patch.shape),
            fixed(gain.shape),
            fixed(bias.shape),
        ],
        out_specs=[rows(2 * width), rows(1), rows(2 * width)],
        out_shape=[
            jax.ShapeDtypeStruct((tokens, 2 * width), F32),
            jax.ShapeDtypeStruct((tokens, 1), F32),
            jax.ShapeDtypeStruct((tokens, 2 * width), BF16),
        ],
    )(patch_rows, skip_rows, f_patch, gain, bias)


def join_back_body(low_ref, weight_ref, z_ref, inv_ref, gain_ref, skip_ref, patch_ref, sums_ref):
    width = skip_ref.shape[1]
    grad, normed = right_dot(low_ref[...], weight_ref[...]), z_ref[...]

    @pl.when(pl.program_id(0) == 0)
    def _():
        sums_ref[...] = jnp.zeros_like(sums_ref)

    sums_ref[0:1] += jnp.sum(grad * normed, axis=0, keepdims=True)
    sums_ref[1:2] += jnp.sum(grad, axis=0, keepdims=True)
    back = norm_back(grad * gain_ref[...], normed, inv_ref[...])
    patch_ref[...] = back[:, :width].astype(BF16)
    skip_ref[...] = back[:, width:]


def join_back(low_rows, f_skip, normed, inverse, gain):
    tokens, width = low_rows.shape
    block = math.gcd(tokens, 256)
    rows = lambda columns: pl.BlockSpec((block, columns), lambda t: (t, 0))
    fixed = lambda shape: pl.BlockSpec(shape, lambda t: (0, 0))
    return kernel_call(
        join_back_body,
        4 * tokens * width * width,
        18 * tokens * width,
        grid=(tokens // block,),
        in_specs=[rows(width), fixed(f_skip.shape), rows(2 * width), rows(1), fixed(gain.shape)],
        out_specs=[rows(width), rows(width), fixed((2, 2 * width))],
        out_shape=[
            jax.ShapeDtypeStruct((tokens, width), F32),
            jax.ShapeDtypeStruct((tokens, width), BF16),
            jax.ShapeDtypeStruct((2, 2 * width), F32),
        ],
    )(low_rows, f_skip, normed, inverse, gain)


def gelu_and_slope(inputs):
    scale, cubic = math.sqrt(2.0 / math.pi), 0.044715
    square = inputs * inputs
    curve = jnp.tanh(scale * inputs * (1.0 + cubic * square))
    half = 0.5 * (1.0 + curve)
    bend = 0.5 * inputs * (1.0 - curve * curve) * (scale * (1.0 + 3.0 * cubic * square))
    return ((inputs * half).astype(BF16), (half + bend).astype(BF16))


def swap_tiles(values_in):
    return lax.all_to_all(values_in, TILE, split_axis=0, concat_axis=0, tiled=True)


def shift_pairs(devices, step):
    return [(at, (at + step) % devices) for at in range(devices)]


def fetch(weight):
    devices = lax.axis_size("dp")
    return [weight] + [
        lax.ppermute(weight, "dp", shift_pairs(devices, step)) for step in range(1, devices)
    ]


def widen(pieces, first=None, joined=1):
    devices, me = lax.axis_size("dp"), lax.axis_index("dp")
    if first is not None:
        pieces = after(first, *pieces)
    slots = [lax.select_n((me - at) % devices, *pieces) for at in range(devices)]
    if joined > 1:
        split = [jnp.split(slot, joined, axis=1) for slot in slots]
        slots = [each for group in zip(*split) for each in group]
    return jnp.concatenate(slots, axis=1)


def narrow_blocks(blocks, first=None):
    devices, me = lax.axis_size("dp"), lax.axis_index("dp")
    received = []
    for step in range(1, devices):
        sent = lax.select_n((me + step) % devices, *blocks)
        received.append(lax.ppermute(sent, "dp", shift_pairs(devices, step)))
    if first is not None:
        received = after(first, *received)
    total = lax.select_n(me, *blocks).astype(F32)
    for piece in received:
        total = total + piece.astype(F32)
    return total


def narrow(weight_grad, first=None):
    return narrow_blocks(jnp.split(weight_grad, lax.axis_size("dp"), axis=1), first)


def by_device(weight_grads, parts):
    devices = lax.axis_size("dp")
    split = [jnp.split(weight_grad, devices, axis=1) for weight_grad in weight_grads]
    return [jnp.concatenate(blocks, axis=parts) for blocks in zip(*split)]


def sum_tiles(part_sums):
    devices, me = lax.axis_size(TILE), lax.axis_index(TILE)
    total, step = part_sums, devices // 2
    while step > 0:
        pairs = [(at, at ^ step) for at in range(devices)]
        lower, upper = jnp.split(total, 2, axis=0)
        high = (me // step) % 2 == 1
        sent = jnp.where(high, lower, upper)
        total = jnp.where(high, upper, lower) + lax.ppermute(sent, TILE, pairs)
        step //= 2
    return total


def total_tiles(part_sum):
    devices = lax.axis_size(TILE)
    total, step = part_sum, 1
    while step < devices:
        pairs = [(at, at ^ step) for at in range(devices)]
        total = total + lax.ppermute(total, TILE, pairs)
        step *= 2
    return total


def over_tiles(weight_grad):
    return lax.optimization_barrier(
        lax.psum_scatter(weight_grad, TILE, scatter_dimension=0, tiled=True)
    )


def tiles_whole(weight):
    return lax.all_gather(weight, TILE, axis=0, tiled=True)


def after(first, *values_in):
    return lax.optimization_barrier((first, *values_in))[1:]


def dot_over(left_mat, right_mat, left_axis, right_axis):
    return lax.dot_general(
        left_mat,
        right_mat,
        (((left_axis,), (right_axis,)), ((), ())),
        preferred_element_type=F32,
    )


def local_heads(
    latent,
    skip_input,
    text_states,
    timesteps,
    image_sides,
    cotangent,
    w_patch,
    w_skip,
    w_time,
    w_shift,
    w_qkv,
    w_out,
    w_query,
    w_text,
    w_cross,
    w_up,
    w_down,
    w_final,
    norm_params,
):
    dp_devices = lax.axis_size("dp")
    grid_devices = lax.axis_size(TILE)
    col_devices = lax.axis_size("col")
    grid_at = lax.axis_index(TILE)
    row_at = lax.axis_index("row")
    col_at = lax.axis_index("col")
    images, rows_tile, cols_tile, patch_width = latent.shape
    tile_len = rows_tile * cols_tile
    row_count = images * tile_len
    out_width = cotangent.shape[3]

    f_skip = tiles_whole(widen(fetch(w_skip)))
    small = jnp.concatenate([w_patch, w_final, norm_params], axis=1)
    small_widths = (w_patch.shape[1], w_final.shape[1], norm_params.shape[1])
    cuts = (0, small_widths[0], sum(small_widths[:2]), sum(small_widths))
    early = [jnp.pad(small, ((0, 0), (0, w_shift.shape[1] - small.shape[1]))), w_time, w_shift]
    ends = (small.shape[0], small.shape[0] + w_time.shape[0])
    part_small, part_time, part_shift_w = jnp.split(
        widen(fetch(jnp.concatenate(early, axis=0))), ends, axis=0
    )
    part_small = part_small.reshape(small.shape[0], dp_devices, -1)[:, :, : small.shape[1]]
    part_small = part_small.reshape(small.shape[0], -1)
    f_small = tiles_whole(part_small).reshape(-1, dp_devices, sum(small_widths))
    f_patch, f_final, f_norms = (
        f_small[:, :, cuts[at] : cuts[at + 1]].reshape(f_small.shape[0], -1) for at in range(3)
    )
    held_qkv = fetch(w_qkv)
    held_three = fetch(jnp.concatenate([w_out, w_query, w_cross], axis=1))
    held_text = fetch(w_text)
    held_up, held_down = fetch(w_up), fetch(w_down)
    model_width = skip_input.shape[3]
    head_count = HEADS
    head_dim = model_width // head_count
    text_len = text_states.shape[1]
    text_pad = -(-text_len // 128) * 128
    score_scale = head_dim ** (-0.5)
    query_scale = score_scale * LOG2E
    positions = jnp.arange(tile_len, dtype=jnp.int32)
    row_pos = row_at * rows_tile + positions // cols_tile
    col_pos = col_at * cols_tile + positions % cols_tile
    query_ok = (row_pos[None, :] < image_sides[:, None]) & (col_pos[None, :] < image_sides[:, None])
    valid = query_ok.astype(F32)
    keep_rows = query_ok.astype(F32).reshape(row_count, 1)
    tile_list = jnp.arange(grid_devices, dtype=jnp.int32)[:, None]
    key_row = tile_list // col_devices * rows_tile + (positions // cols_tile)[None, :]
    key_col = tile_list % col_devices * cols_tile + (positions % cols_tile)[None, :]
    sides = image_sides[:, None, None]
    key_ok = ((key_row[None] < sides) & (key_col[None] < sides)).astype(F32)
    flags = jnp.concatenate(
        [key_ok[:, :, None, :], jnp.zeros((images, grid_devices, 7, tile_len), F32)], axis=2
    )
    cos_row, sin_row, cos_col, sin_col = (
        jnp.transpose(table[:, 0, :]) for table in rope_tables(row_pos, col_pos, head_dim)
    )
    tables = (
        jnp.concatenate([cos_row, cos_row, cos_col, cos_col], axis=0),
        jnp.concatenate([-sin_row, sin_row, -sin_col, sin_col], axis=0),
    )
    norm_f = f_norms.astype(F32)

    embedding = time_embed(timesteps, FREQ).astype(BF16)
    freq_slice = part_time.shape[0]
    shift_slice = part_shift_w.shape[0]
    embed_cols = lax.dynamic_slice_in_dim(embedding, grid_at * freq_slice, freq_slice, 1)
    time_pre = total_tiles(plain_dot(embed_cols, part_time))
    time_float, silu_pull = jax.vjp(jax.nn.silu, time_pre)
    time_act = time_float.astype(BF16)
    act_cols = lax.dynamic_slice_in_dim(time_act, grid_at * shift_slice, shift_slice, 1)
    time_shift = total_tiles(plain_dot(act_cols, part_shift_w))

    patch_rows = latent.reshape(row_count, patch_width)
    skip_rows = skip_input.reshape(row_count, model_width)
    gain_skip = jnp.concatenate([norm_f[:, 8], norm_f[:, 10]])[None]
    bias_skip = jnp.concatenate([norm_f[:, 9], norm_f[:, 11]])[None]
    joined, joined_inv, skip_in = join_norm(patch_rows, skip_rows, f_patch, gain_skip, bias_skip)
    f_qkv = tiles_whole(widen(held_qkv, skip_in))
    part_three = widen(held_three, skip_in, 3)
    f_three = tiles_whole(part_three)
    f_out, f_query, f_cross = jnp.split(f_three, 3, axis=1)
    residual = plain_dot(skip_in, f_skip)
    first_z, first_inv = layer_norm(residual)
    first_pre = (first_z * norm_f[:, 0] + norm_f[:, 1]).reshape(
        images, tile_len, model_width
    ) + time_shift[:, None, :]
    first_in = first_pre.reshape(row_count, model_width).astype(BF16)
    part_text = widen(held_text, first_in)
    f_text = tiles_whole(part_text)
    first_rows = first_in.reshape(images, tile_len, model_width)
    own_qkv, qk_inv, tile_qkv, tile_att, tile_lse, att_rows = [], [], [], [], [], []
    for image in range(images):
        rows = first_rows[image]
        own, inverses = head_norm(
            rows,
            f_qkv,
            tables,
            valid[image : image + 1],
            grid_devices,
            head_dim,
            query_scale,
        )
        own_qkv.append(own)
        qk_inv.append(inverses)
        tile_qkv.append(swap_tiles(own))
    f_up = tiles_whole(widen(held_up, tile_qkv[0]))
    for image in range(images):
        att, lse = attend(tile_qkv[image], flags[image])
        tile_att.append(att)
        tile_lse.append(lse)
        own_att = swap_tiles(att).reshape(model_width, tile_len)
        att_rows.append(jnp.transpose(own_att))
    att_low = jnp.concatenate(att_rows, axis=0)
    residual_two = residual + plain_dot(att_low, f_out)
    f_down = tiles_whole(widen(held_down, residual_two))

    third_z, third_inv = layer_norm(residual_two)
    third_in = (third_z * norm_f[:, 2] + norm_f[:, 3]).astype(BF16)
    cross_pre = dot_over(f_query, third_in, 0, 1).reshape(head_count, head_dim, row_count)
    text_rows = jnp.pad(text_states, ((0, 0), (0, text_pad - text_len), (0, 0)))
    text_rows = text_rows.reshape(images * text_pad, -1)
    text_kv = dot_over(f_text, text_rows, 0, 1).reshape(2, head_count, head_dim, images * text_pad)
    crossed, cross_queries, cq_inv, cross_lse = cross_attend(
        cross_pre, text_kv, images, text_len, query_scale
    )
    cross_cols = crossed.reshape(model_width, row_count)
    residual_three = residual_two + left_dot(cross_cols, f_cross)
    second_z, second_inv = layer_norm(residual_three)
    second_in = (second_z * norm_f[:, 4] + norm_f[:, 5]).astype(BF16)
    up_pre = plain_dot(second_in, f_up)
    hidden_act, slope = lax.optimization_barrier(gelu_and_slope(up_pre))
    residual_four = residual_three + plain_dot(hidden_act, f_down)
    last_z, last_inv = layer_norm(residual_four)
    last_in = (last_z * norm_f[:, 6] + norm_f[:, 7]).astype(BF16)
    produced = plain_dot(last_in, f_final)
    prediction = (
        (produced * keep_rows).astype(BF16).reshape(images, rows_tile, cols_tile, out_width)
    )

    grad_out = (cotangent.reshape(row_count, out_width).astype(F32) * keep_rows).astype(BF16)
    d_final = left_dot(last_in, grad_out)
    grad_last = right_dot(grad_out, f_final)
    gain_final = jnp.sum(grad_last * last_z, axis=0)
    bias_final = jnp.sum(grad_last, axis=0)
    grad_four = norm_back(grad_last * norm_f[:, 6], last_z, last_inv)
    low_four = grad_four.astype(BF16)
    d_down = left_dot(hidden_act, low_four).astype(BF16)
    d_down, low_four = lax.optimization_barrier((d_down, low_four))
    t_down = over_tiles(d_down)
    grad_hidden = right_dot(low_four, f_down)
    grad_up = (grad_hidden * slope).astype(BF16)
    d_up = left_dot(second_in, grad_up).astype(BF16)
    d_up, grad_up = lax.optimization_barrier((d_up, grad_up))
    t_up = over_tiles(d_up)
    grad_second = right_dot(grad_up, f_up)
    gain_second = jnp.sum(grad_second * second_z, axis=0)
    bias_second = jnp.sum(grad_second, axis=0)
    grad_three = grad_four + norm_back(grad_second * norm_f[:, 4], second_z, second_inv)
    low_three = grad_three.astype(BF16)
    d_cross = plain_dot(cross_cols, low_three).astype(BF16)
    grad_crossed = dot_over(f_cross, low_three, 1, 1).astype(BF16)
    grad_cross_q, d_text_key, d_text_value = cross_back(
        cross_queries,
        text_kv,
        grad_crossed.reshape(head_count, head_dim, row_count),
        crossed,
        cq_inv,
        cross_lse,
        images,
        query_scale,
        score_scale,
    )
    t_down, grad_cross_q = lax.optimization_barrier((t_down, grad_cross_q))
    grad_cross_q = grad_cross_q.reshape(model_width, row_count)
    d_query = dot_over(third_in, grad_cross_q, 0, 1).astype(BF16)
    grad_third = dot_over(grad_cross_q, f_query, 0, 1)
    gain_third = jnp.sum(grad_third * third_z, axis=0)
    bias_third = jnp.sum(grad_third, axis=0)
    grad_two = grad_three + norm_back(grad_third * norm_f[:, 2], third_z, third_inv)
    low_two = grad_two.astype(BF16)
    low_two_rows = low_two.reshape(images, tile_len, model_width)
    tile_grads = []
    for image in range(images):
        grad_att = dot_over(f_out, low_two_rows[image], 1, 1).astype(BF16)
        tile_grads.append(swap_tiles(grad_att.reshape(tile_att[image].shape)))
    d_out = left_dot(att_low, low_two).astype(BF16)
    d_joint = jnp.concatenate(
        [
            d_out,
            d_query,
            d_cross,
            d_text_key.reshape(model_width, -1),
            d_text_value.reshape(model_width, -1),
        ],
        axis=1,
    )
    d_joint = with_layout_constraint(d_joint, Layout(major_to_minor=(0, 1)))
    d_joint, tile_grads[0] = lax.optimization_barrier((d_joint, tile_grads[0]))
    t_joint = over_tiles(d_joint)
    own_grads, grad_qkv, tile_back = [], None, None
    for image in range(images):
        if tile_back is not None:
            down_grad = narrow(t_down, tile_back)
            down_grad, tile_grads[image], tile_back = lax.optimization_barrier(
                (down_grad, tile_grads[image], tile_back)
            )
            own_grads.append(swap_tiles(tile_back))
        tile_back = attend_back(
            tile_qkv[image], tile_grads[image], tile_att[image], tile_lse[image], score_scale
        )
    own_grads.append(swap_tiles(tile_back))
    for image in range(images):
        if image == images - 1:
            up_grad = narrow(t_up, tile_back)
            up_grad, own_grads[-1], grad_qkv = lax.optimization_barrier(
                (up_grad, own_grads[-1], grad_qkv)
            )
        grad_qkv = head_back(
            own_grads[image],
            own_qkv[image],
            qk_inv[image],
            tables,
            valid[image : image + 1],
            query_scale,
            image,
            images,
            grad_qkv,
        )
    sum_text_kv = t_joint[:, 3 * model_width :].astype(F32)
    sum_text_kv = jnp.transpose(
        sum_text_kv.reshape(-1, head_dim, 2, images * text_pad), (2, 0, 1, 3)
    )
    group_heads = head_count // grid_devices
    own_key = lax.dynamic_slice_in_dim(text_kv[0], grid_at * group_heads, group_heads, 0)
    ck_z, ck_inv = layer_norm(jnp.swapaxes(own_key, 1, 2))
    grad_ckey = jnp.swapaxes(norm_back(jnp.swapaxes(sum_text_kv[0], 1, 2), ck_z, ck_inv), 1, 2)
    grad_kv = jnp.stack([grad_ckey, sum_text_kv[1]]).astype(BF16)
    grad_kv = tiles_whole(grad_kv.reshape(-1, images * text_pad))
    grad_qkv = grad_qkv.reshape(3 * model_width, row_count)
    d_qkv = dot_over(first_in, grad_qkv, 0, 1).astype(BF16)
    d_qkv, grad_qkv = lax.optimization_barrier((d_qkv, grad_qkv))
    t_qkv = over_tiles(d_qkv)
    grad_first = dot_over(grad_qkv, f_qkv, 0, 1)
    joint_blocks = by_device(jnp.split(t_joint[:, : 3 * model_width], 3, axis=1), 1)
    joint_grad = narrow_blocks(joint_blocks, grad_first)
    gain_first = jnp.sum(grad_first * first_z, axis=0)
    bias_first = jnp.sum(grad_first, axis=0)
    part_shift = jnp.sum(grad_first.reshape(images, tile_len, model_width), axis=1)
    grad_one = grad_two + norm_back(grad_first * norm_f[:, 0], first_z, first_inv)

    low_one = grad_one.astype(BF16)
    d_skip_w = left_dot(skip_in, low_one).astype(BF16)
    d_skip_w, low_one = lax.optimization_barrier((d_skip_w, low_one))
    skip_grad, grad_patch, skip_sums = join_back(low_one, f_skip, joined, joined_inv, gain_skip)
    t_qkv, d_skip_w, joint_grad, skip_sums = lax.optimization_barrier(
        (t_qkv, d_skip_w, joint_grad, skip_sums)
    )
    out_grad, query_w_grad, cross_grad = jnp.split(joint_grad, 3, axis=1)
    t_skip = over_tiles(d_skip_w)

    group_shape = (-1, 2, grid_devices, model_width // grid_devices)
    text_slice = text_states.shape[2] // grid_devices
    text_cols = lax.dynamic_slice_in_dim(text_rows, grid_at * text_slice, text_slice, 1)
    d_text = dot_over(text_cols, grad_kv, 0, 1).astype(BF16)
    d_text = jnp.swapaxes(d_text.reshape(text_slice, grid_devices, 2, -1), 1, 2)
    d_text = d_text.reshape(text_slice, -1)
    grouped_text = jnp.swapaxes(part_text.reshape(group_shape), 1, 2).reshape(part_text.shape)
    text_grad = dot_over(grad_kv, grouped_text, 0, 1).reshape(images, text_pad, text_slice)
    text_grad = text_grad[:, :text_len]

    shift_low = total_tiles(part_shift).astype(BF16)
    d_shift = left_dot(act_cols, shift_low).astype(BF16)
    grad_time_act = total_tiles(
        lax.dynamic_update_slice_in_dim(
            jnp.zeros_like(time_pre), right_dot(shift_low, part_shift_w), grid_at * shift_slice, 1
        )
    )
    grad_time_pre = silu_pull(grad_time_act)[0].astype(BF16)
    d_time = left_dot(embed_cols, grad_time_pre).astype(BF16)
    late, width = [], w_shift.shape[1]
    for at in range(dp_devices):
        pair = d_text[:, 2 * at * width : 2 * (at + 1) * width]
        own = slice(at * width, (at + 1) * width)
        late.append(
            jnp.concatenate([pair[:, :width], pair[:, width:], d_time[:, own], d_shift[:, own]])
        )
    qkv_grad = narrow(t_qkv, d_text)
    qkv_grad, *late = lax.optimization_barrier((qkv_grad, *late))
    late = narrow_blocks(late)
    rows = d_text.shape[0]
    text_w_grad = jnp.concatenate([late[:rows], late[rows : 2 * rows]], axis=1)
    time_w_grad, shift_w_grad = jnp.split(late[2 * rows :], [d_time.shape[0]], axis=0)

    skip_grad = skip_grad.reshape(images, rows_tile, cols_tile, model_width)
    gain_skips, bias_skips = skip_sums[0], skip_sums[1]
    d_patch = left_dot(grad_patch, patch_rows)
    latent_grad = plain_dot(grad_patch, f_patch).reshape(images, rows_tile, cols_tile, patch_width)
    d_norms = jnp.stack(
        [
            gain_first,
            bias_first,
            gain_third,
            bias_third,
            gain_second,
            bias_second,
            gain_final,
            bias_final,
            gain_skips[:model_width],
            bias_skips[:model_width],
            gain_skips[model_width:],
            bias_skips[model_width:],
        ],
        axis=1,
    )
    small_grads = jnp.concatenate(
        [
            grad.reshape(model_width, dp_devices, -1)
            for grad in (d_patch, d_final, d_norms)
        ],
        axis=2,
    )
    small_grads = sum_tiles(small_grads.reshape(model_width, -1))
    last, small_rows, small_width = [], small_grads.shape[0], sum(small_widths)
    for at in range(dp_devices):
        few = small_grads[:, at * small_width : (at + 1) * small_width].astype(BF16).reshape(-1)
        few = jnp.pad(few, (0, -few.shape[0] % width)).reshape(-1, width)
        last.append(jnp.concatenate([t_skip[:, at * width : (at + 1) * width], few]))
    last = narrow_blocks(last)
    skip_w_grad = last[: t_skip.shape[0]]
    small_grads = last[t_skip.shape[0] :].reshape(-1)[: small_rows * small_width]
    small_grads = small_grads.reshape(small_rows, small_width)
    patch_grad, final_grad, norms_grad = (
        small_grads[:, cuts[at] : cuts[at + 1]] for at in range(3)
    )
    return (
        prediction,
        latent_grad,
        skip_grad,
        text_grad,
        patch_grad,
        skip_w_grad,
        time_w_grad,
        shift_w_grad,
        qkv_grad,
        out_grad,
        query_w_grad,
        text_w_grad,
        cross_grad,
        up_grad,
        down_grad,
        final_grad,
        norms_grad,
    )


def local(sizes, latent, *others):
    grid_devices = sizes["row"] * sizes["col"]
    tile_len = latent.shape[1] * latent.shape[2]
    if HEADS % grid_devices == 0 and tile_len % 128 == 0:
        return local_heads(latent, *others)
    return local_gathered(latent, *others)


def solution(mesh):
    return jax.shard_map(
        functools.partial(local, mesh.shape),
        mesh=mesh,
        in_specs=(
            P("dp", "row", "col", None),
            P("dp", "row", "col", None),
            P("dp", None, None),
            P("dp"),
            P("dp"),
            P("dp", "row", "col", None),
            P(("row", "col"), "dp"),
            P(("row", "col"), "dp"),
            P(("row", "col"), "dp"),
            P(("row", "col"), "dp"),
            P(("row", "col"), "dp"),
            P(("row", "col"), "dp"),
            P(("row", "col"), "dp"),
            P(("row", "col"), "dp"),
            P(("row", "col"), "dp"),
            P(("row", "col"), "dp"),
            P(("row", "col"), "dp"),
            P(("row", "col"), "dp"),
            P(("row", "col"), "dp"),
        ),
        out_specs=(
            P("dp", "row", "col", None),
            P("dp", "row", "col", None),
            P("dp", "row", "col", None),
            P("dp", None, ("row", "col")),
            P(("row", "col"), "dp"),
            P(("row", "col"), "dp"),
            P(("row", "col"), "dp"),
            P(("row", "col"), "dp"),
            P(("row", "col"), "dp"),
            P(("row", "col"), "dp"),
            P(("row", "col"), "dp"),
            P(("row", "col"), "dp"),
            P(("row", "col"), "dp"),
            P(("row", "col"), "dp"),
            P(("row", "col"), "dp"),
            P(("row", "col"), "dp"),
            P(("row", "col"), "dp"),
        ),
        check_vma=False,
    )
```

```python
import functools
import math

import jax
import jax.numpy as jnp
from jax import lax
from jax.experimental import pallas as pl
from jax.experimental.layout import Layout, with_layout_constraint
from jax.experimental.pallas import tpu as pltpu
from jax.sharding import PartitionSpec as P

HEADS = 16
FREQ = 256


EPSILON = 1e-06


def layer_norm(values_in):
    centred = values_in - jnp.mean(values_in, axis=-1, keepdims=True)
    inverse = lax.rsqrt(jnp.mean(centred * centred, axis=-1, keepdims=True) + EPSILON)
    return (centred * inverse, inverse)


def norm_back(grad_normed, normed, inverse):
    mean_grad = jnp.mean(grad_normed, axis=-1, keepdims=True)
    mean_cross = jnp.mean(grad_normed * normed, axis=-1, keepdims=True)
    return inverse * (grad_normed - mean_grad - normed * mean_cross)


def turn_half(piece_half, cosine, sine_tab):
    quarter = cosine.shape[-1]
    lower = piece_half[..., :quarter]
    higher = piece_half[..., quarter:]
    return jnp.concatenate(
        [lower * cosine - higher * sine_tab, higher * cosine + lower * sine_tab], axis=-1
    )


def rotate(values_in, tables, signum):
    cos_row, sin_row, cos_col, sin_col = tables
    half_dim = values_in.shape[-1] // 2
    return jnp.concatenate(
        [
            turn_half(values_in[..., :half_dim], cos_row, signum * sin_row),
            turn_half(values_in[..., half_dim:], cos_col, signum * sin_col),
        ],
        axis=-1,
    )


def rope_tables(row_pos, col_pos, head_size):
    quarter = head_size // 4
    frequency = jnp.exp(jnp.arange(quarter, dtype=jnp.float32) * (-math.log(10000.0) / quarter))
    row_ang = row_pos.astype(jnp.float32)[:, None, None] * frequency
    col_ang = col_pos.astype(jnp.float32)[:, None, None] * frequency
    return (jnp.cos(row_ang), jnp.sin(row_ang), jnp.cos(col_ang), jnp.sin(col_ang))


def time_embed(step_values, freq_count):
    half_dim = freq_count // 2
    rate_list = jnp.exp(jnp.arange(half_dim, dtype=jnp.float32) * (-math.log(10000.0) / half_dim))
    angles = step_values.astype(jnp.float32)[..., None] * rate_list
    return jnp.concatenate([jnp.cos(angles), jnp.sin(angles)], axis=-1)


def gelu_tanh(inputs):
    return jax.nn.gelu(inputs, approximate=True)


def plain_dot(left_mat, right_mat):
    return jnp.dot(left_mat, right_mat, preferred_element_type=jnp.float32)


def left_dot(left_mat, right_mat):
    return lax.dot_general(
        left_mat, right_mat, (((0,), (0,)), ((), ())), preferred_element_type=jnp.float32
    )


def right_dot(left_mat, right_mat):
    return lax.dot_general(
        left_mat, right_mat, (((1,), (1,)), ((), ())), preferred_element_type=jnp.float32
    )


def block_size(key_count):
    block_len = key_count
    while block_len > 1024 and block_len % 2 == 0:
        block_len = block_len // 2
    return block_len


def local_gathered(
    latent,
    skip_input,
    text_states,
    timesteps,
    image_sides,
    cotangent,
    w_patch,
    w_skip,
    w_time,
    w_shift,
    w_qkv,
    w_out,
    w_query,
    w_text,
    w_cross,
    w_up,
    w_down,
    w_final,
    norm_params,
):
    widened = (
        lax.all_gather(w_patch, "dp", axis=1, tiled=True),
        lax.all_gather(w_skip, "dp", axis=1, tiled=True),
        lax.all_gather(w_time, "dp", axis=1, tiled=True),
        lax.all_gather(w_shift, "dp", axis=1, tiled=True),
        lax.all_gather(w_qkv, "dp", axis=1, tiled=True),
        lax.all_gather(w_out, "dp", axis=1, tiled=True),
        lax.all_gather(w_query, "dp", axis=1, tiled=True),
        lax.all_gather(w_text, "dp", axis=1, tiled=True),
        lax.all_gather(w_cross, "dp", axis=1, tiled=True),
        lax.all_gather(w_up, "dp", axis=1, tiled=True),
        lax.all_gather(w_down, "dp", axis=1, tiled=True),
        lax.all_gather(w_final, "dp", axis=1, tiled=True),
        lax.all_gather(norm_params, "dp", axis=1, tiled=True),
    )
    gathered = (
        lax.all_gather(widened[0], ("row", "col"), axis=0, tiled=True),
        lax.all_gather(widened[1], ("row", "col"), axis=0, tiled=True),
        lax.all_gather(widened[2], ("row", "col"), axis=0, tiled=True),
        lax.all_gather(widened[3], ("row", "col"), axis=0, tiled=True),
        lax.all_gather(widened[4], ("row", "col"), axis=0, tiled=True),
        lax.all_gather(widened[5], ("row", "col"), axis=0, tiled=True),
        lax.all_gather(widened[6], ("row", "col"), axis=0, tiled=True),
        lax.all_gather(widened[7], ("row", "col"), axis=0, tiled=True),
        lax.all_gather(widened[8], ("row", "col"), axis=0, tiled=True),
        lax.all_gather(widened[9], ("row", "col"), axis=0, tiled=True),
        lax.all_gather(widened[10], ("row", "col"), axis=0, tiled=True),
        lax.all_gather(widened[11], ("row", "col"), axis=0, tiled=True),
        lax.all_gather(widened[12], ("row", "col"), axis=0, tiled=True),
    )
    (
        f_patch,
        f_skip,
        f_time,
        f_shift,
        f_qkv,
        f_out,
        f_query,
        f_text,
        f_cross,
        f_up,
        f_down,
        f_final,
        f_norms,
    ) = gathered
    part_text = widened[7]
    images, rows_tile, cols_tile, patch_width = latent.shape
    tile_len = rows_tile * cols_tile
    row_count = images * tile_len
    model_width = f_qkv.shape[0]
    head_count = HEADS
    head_dim = model_width // head_count
    text_len = text_states.shape[1]
    grid_devices = lax.axis_size(("row", "col"))
    col_devices = lax.axis_size("col")
    grid_at = lax.axis_index(("row", "col"))
    row_at = lax.axis_index("row")
    col_at = lax.axis_index("col")
    score_scale = head_dim ** (-0.5)
    positions = jnp.arange(tile_len, dtype=jnp.int32)
    row_pos = row_at * rows_tile + positions // cols_tile
    col_pos = col_at * cols_tile + positions % cols_tile
    query_ok = (row_pos[None, :] < image_sides[:, None]) & (col_pos[None, :] < image_sides[:, None])
    keep_rows = query_ok.astype(jnp.float32).reshape(row_count, 1)
    tables = rope_tables(row_pos, col_pos, head_dim)
    norm_f = f_norms.astype(jnp.float32)

    def valid_keys(offset, block_len):
        index_list = offset + jnp.arange(block_len, dtype=jnp.int32)
        source = index_list // tile_len
        within = index_list % tile_len
        key_row = source // col_devices * rows_tile + within // cols_tile
        key_col = source % col_devices * cols_tile + within % cols_tile
        return (key_row[None, :] < image_sides[:, None]) & (key_col[None, :] < image_sides[:, None])

    patch_rows = latent.reshape(row_count, patch_width)
    patch_feat = right_dot(patch_rows, f_patch)
    skip_rows = skip_input.reshape(row_count, model_width).astype(jnp.float32)
    gain_skip = jnp.concatenate([norm_f[:, 8], norm_f[:, 10]])
    bias_skip = jnp.concatenate([norm_f[:, 9], norm_f[:, 11]])
    joined, joined_inv = layer_norm(jnp.concatenate([patch_feat, skip_rows], axis=-1))
    skip_in = (joined * gain_skip + bias_skip).astype(jnp.bfloat16)
    residual = plain_dot(skip_in, f_skip)
    embedding = time_embed(timesteps, FREQ).astype(jnp.bfloat16)
    time_pre = plain_dot(embedding, f_time)
    time_float, silu_pull = jax.vjp(jax.nn.silu, time_pre)
    time_act = time_float.astype(jnp.bfloat16)
    time_shift = plain_dot(time_act, f_shift)
    first_z, first_inv = layer_norm(residual)
    first_pre = (first_z * norm_f[:, 0] + norm_f[:, 1]).reshape(
        images, tile_len, model_width
    ) + time_shift[:, None, :]
    first_in = first_pre.reshape(row_count, model_width).astype(jnp.bfloat16)
    qkv = plain_dot(first_in, f_qkv)
    query_z, query_inv = layer_norm(
        qkv[:, :model_width].reshape(images, tile_len, head_count, head_dim)
    )
    key_z, key_inv = layer_norm(
        qkv[:, model_width : 2 * model_width].reshape(images, tile_len, head_count, head_dim)
    )
    queries = rotate(query_z, tables, 1.0).astype(jnp.bfloat16)
    queries_h = jnp.transpose(queries, (0, 2, 1, 3))
    keys = rotate(key_z, tables, 1.0).astype(jnp.bfloat16).reshape(images, tile_len, model_width)
    values = qkv[:, 2 * model_width :].astype(jnp.bfloat16).reshape(images, tile_len, model_width)
    start_carry = (
        jnp.full((images, head_count, tile_len), -1e30, jnp.float32),
        jnp.zeros((images, head_count, tile_len), jnp.float32),
        jnp.zeros((images, head_count, tile_len, head_dim), jnp.float32),
    )
    key_rows = lax.all_gather(keys, ("row", "col"), axis=1, tiled=True)
    value_rows = lax.all_gather(values, ("row", "col"), axis=1, tiled=True)
    key_count = key_rows.shape[1]
    block_len = block_size(key_count)

    def forward_block_step(block_index, running):
        running_max, weight_sum, accum_sum = running
        offset = block_index * block_len
        key_blk = lax.dynamic_slice_in_dim(key_rows, offset, block_len, 1).reshape(
            images, block_len, head_count, head_dim
        )
        value_blk = lax.dynamic_slice_in_dim(value_rows, offset, block_len, 1).reshape(
            images, block_len, head_count, head_dim
        )
        key_ok = valid_keys(offset, block_len)
        scores = (
            jnp.einsum("ihqe,ikhe->ihqk", queries_h, key_blk, preferred_element_type=jnp.float32)
            * score_scale
        )
        scores = jnp.where(key_ok[:, None, None, :], scores, -jnp.inf)
        new_max = jnp.maximum(running_max, jnp.max(scores, axis=-1))
        weight = jnp.exp(scores - new_max[..., None])
        rescale = jnp.exp(running_max - new_max)
        weight_sum = weight_sum * rescale + jnp.sum(weight, axis=-1)
        accum_sum = accum_sum * rescale[..., None] + jnp.einsum(
            "ihqk,ikhe->ihqe",
            weight.astype(jnp.bfloat16),
            value_blk,
            preferred_element_type=jnp.float32,
        )
        return (new_max, weight_sum, accum_sum)

    running_max, weight_sum, accum_sum = lax.fori_loop(
        0, key_count // block_len, forward_block_step, start_carry
    )
    attended = accum_sum / weight_sum[..., None]
    log_sum = running_max + jnp.log(weight_sum)
    att_low = (
        jnp.transpose(attended, (0, 2, 1, 3)).reshape(row_count, model_width).astype(jnp.bfloat16)
    )
    residual_two = residual + plain_dot(att_low, f_out)
    third_z, third_inv = layer_norm(residual_two)
    third_in = (third_z * norm_f[:, 2] + norm_f[:, 3]).astype(jnp.bfloat16)
    cross_pre = plain_dot(third_in, f_query)
    cq_z, cq_inv = layer_norm(cross_pre.reshape(images, tile_len, head_count, head_dim))
    cross_queries = cq_z.astype(jnp.bfloat16)
    text_kv = jnp.einsum("itc,cd->itd", text_states, f_text, preferred_element_type=jnp.float32)
    ck_z, ck_inv = layer_norm(
        text_kv[..., :model_width].reshape(images, text_len, head_count, head_dim)
    )
    cross_keys = ck_z.astype(jnp.bfloat16)
    cross_values = (
        text_kv[..., model_width:]
        .astype(jnp.bfloat16)
        .reshape(images, text_len, head_count, head_dim)
    )

    def cross_softmax():
        scores = (
            jnp.einsum(
                "iqhe,ikhe->ihqk", cross_queries, cross_keys, preferred_element_type=jnp.float32
            )
            * score_scale
        )
        return jax.nn.softmax(scores, axis=-1)

    crossed = jnp.einsum(
        "ihqk,ikhe->iqhe",
        cross_softmax().astype(jnp.bfloat16),
        cross_values,
        preferred_element_type=jnp.float32,
    )
    cross_low = crossed.reshape(row_count, model_width).astype(jnp.bfloat16)
    residual_three = residual_two + plain_dot(cross_low, f_cross)
    second_z, second_inv = layer_norm(residual_three)
    second_in = (second_z * norm_f[:, 4] + norm_f[:, 5]).astype(jnp.bfloat16)
    up_pre = plain_dot(second_in, f_up)
    hidden_float, gelu_pull = jax.vjp(gelu_tanh, up_pre)
    hidden_act = hidden_float.astype(jnp.bfloat16)
    residual_four = residual_three + plain_dot(hidden_act, f_down)
    last_z, last_inv = layer_norm(residual_four)
    last_in = (last_z * norm_f[:, 6] + norm_f[:, 7]).astype(jnp.bfloat16)
    produced = plain_dot(last_in, f_final)
    prediction = (
        (produced * keep_rows)
        .astype(jnp.bfloat16)
        .reshape(images, rows_tile, cols_tile, produced.shape[1])
    )
    grad_out = (
        cotangent.reshape(row_count, produced.shape[1]).astype(jnp.float32) * keep_rows
    ).astype(jnp.bfloat16)
    d_final = left_dot(last_in, grad_out)
    grad_last = right_dot(grad_out, f_final)
    gain_final = jnp.sum(grad_last * last_z, axis=0)
    bias_final = jnp.sum(grad_last, axis=0)
    grad_four = norm_back(grad_last * norm_f[:, 6], last_z, last_inv)
    low_four = grad_four.astype(jnp.bfloat16)
    d_down = left_dot(hidden_act, low_four)
    grad_hidden = right_dot(low_four, f_down)
    grad_up = gelu_pull(grad_hidden)[0].astype(jnp.bfloat16)
    d_up = left_dot(second_in, grad_up)
    grad_second = right_dot(grad_up, f_up)
    gain_second = jnp.sum(grad_second * second_z, axis=0)
    bias_second = jnp.sum(grad_second, axis=0)
    grad_three = grad_four + norm_back(grad_second * norm_f[:, 4], second_z, second_inv)
    low_three = grad_three.astype(jnp.bfloat16)
    d_cross = left_dot(cross_low, low_three)
    grad_crossed = (
        right_dot(low_three, f_cross)
        .astype(jnp.bfloat16)
        .reshape(images, tile_len, head_count, head_dim)
    )
    cross_probs = cross_softmax()
    cross_delta = jnp.transpose(
        jnp.sum(grad_crossed.astype(jnp.float32) * crossed, axis=-1), (0, 2, 1)
    )
    grad_probs = jnp.einsum(
        "iqhe,ikhe->ihqk", grad_crossed, cross_values, preferred_element_type=jnp.float32
    )
    grad_cscore = (cross_probs * (grad_probs - cross_delta[..., None])).astype(jnp.bfloat16)
    grad_cq = score_scale * jnp.einsum(
        "ihqk,ikhe->iqhe", grad_cscore, cross_keys, preferred_element_type=jnp.float32
    )
    part_ckey = score_scale * jnp.einsum(
        "ihqk,iqhe->ikhe", grad_cscore, cross_queries, preferred_element_type=jnp.float32
    )
    part_cvalue = jnp.einsum(
        "ihqk,iqhe->ikhe",
        cross_probs.astype(jnp.bfloat16),
        grad_crossed,
        preferred_element_type=jnp.float32,
    )
    grad_cross_q = (
        norm_back(grad_cq, cq_z, cq_inv).reshape(row_count, model_width).astype(jnp.bfloat16)
    )
    d_query = left_dot(third_in, grad_cross_q)
    grad_third = right_dot(grad_cross_q, f_query)
    gain_third = jnp.sum(grad_third * third_z, axis=0)
    bias_third = jnp.sum(grad_third, axis=0)
    grad_two = grad_three + norm_back(grad_third * norm_f[:, 2], third_z, third_inv)
    sum_ckey, sum_cvalue = lax.psum((part_ckey, part_cvalue), ("row", "col"))
    low_two = grad_two.astype(jnp.bfloat16)
    d_out = left_dot(att_low, low_two)
    grad_att = (
        right_dot(low_two, f_out)
        .astype(jnp.bfloat16)
        .reshape(images, tile_len, head_count, head_dim)
    )
    grad_att_h = jnp.transpose(grad_att, (0, 2, 1, 3))
    delta_rows = jnp.sum(grad_att_h.astype(jnp.float32) * attended, axis=-1)
    back_carry = (
        jnp.zeros((images, head_count, tile_len, head_dim), jnp.float32),
        jnp.zeros((images, tile_len * grid_devices, model_width), jnp.float32),
        jnp.zeros((images, tile_len * grid_devices, model_width), jnp.float32),
    )
    backward_key_rows = lax.all_gather(keys, ("row", "col"), axis=1, tiled=True)
    backward_value_rows = lax.all_gather(values, ("row", "col"), axis=1, tiled=True)
    key_count = backward_key_rows.shape[1]
    backward_block_len = block_size(key_count)

    def backward_block_step(block_index, running):
        grad_query, grad_key_all, grad_value_all = running
        offset = block_index * backward_block_len
        key_blk = lax.dynamic_slice_in_dim(
            backward_key_rows, offset, backward_block_len, 1
        ).reshape(images, backward_block_len, head_count, head_dim)
        value_blk = lax.dynamic_slice_in_dim(
            backward_value_rows, offset, backward_block_len, 1
        ).reshape(images, backward_block_len, head_count, head_dim)
        key_ok = valid_keys(offset, backward_block_len)
        scores = (
            jnp.einsum("ihqe,ikhe->ihqk", queries_h, key_blk, preferred_element_type=jnp.float32)
            * score_scale
        )
        scores = jnp.where(key_ok[:, None, None, :], scores, -jnp.inf)
        attn_probs = jnp.exp(scores - log_sum[..., None])
        grad_prob = jnp.einsum(
            "ihqe,ikhe->ihqk", grad_att_h, value_blk, preferred_element_type=jnp.float32
        )
        grad_score = (attn_probs * (grad_prob - delta_rows[..., None])).astype(jnp.bfloat16)
        grad_query = grad_query + score_scale * jnp.einsum(
            "ihqk,ikhe->ihqe", grad_score, key_blk, preferred_element_type=jnp.float32
        )
        key_part = score_scale * jnp.einsum(
            "ihqk,ihqe->ikhe", grad_score, queries_h, preferred_element_type=jnp.float32
        )
        value_part = jnp.einsum(
            "ihqk,ihqe->ikhe",
            attn_probs.astype(jnp.bfloat16),
            grad_att_h,
            preferred_element_type=jnp.float32,
        )
        grad_key_all = lax.dynamic_update_slice_in_dim(
            grad_key_all, key_part.reshape(images, backward_block_len, model_width), offset, 1
        )
        grad_value_all = lax.dynamic_update_slice_in_dim(
            grad_value_all, value_part.reshape(images, backward_block_len, model_width), offset, 1
        )
        return (grad_query, grad_key_all, grad_value_all)

    grad_query, grad_key_all, grad_value_all = lax.fori_loop(
        0, key_count // backward_block_len, backward_block_step, back_carry
    )
    grad_key_own, grad_value_own = (
        lax.psum_scatter(grad_key_all, ("row", "col"), scatter_dimension=1, tiled=True),
        lax.psum_scatter(grad_value_all, ("row", "col"), scatter_dimension=1, tiled=True),
    )
    grad_qn = rotate(jnp.transpose(grad_query, (0, 2, 1, 3)), tables, -1.0)
    grad_kn = rotate(grad_key_own.reshape(images, tile_len, head_count, head_dim), tables, -1.0)
    grad_qkv = jnp.concatenate(
        [
            norm_back(grad_qn, query_z, query_inv).reshape(row_count, model_width),
            norm_back(grad_kn, key_z, key_inv).reshape(row_count, model_width),
            grad_value_own.reshape(row_count, model_width),
        ],
        axis=-1,
    ).astype(jnp.bfloat16)
    d_qkv = left_dot(first_in, grad_qkv)
    grad_first = right_dot(grad_qkv, f_qkv)
    gain_first = jnp.sum(grad_first * first_z, axis=0)
    bias_first = jnp.sum(grad_first, axis=0)
    part_shift = jnp.sum(grad_first.reshape(images, tile_len, model_width), axis=1)
    grad_one = grad_two + norm_back(grad_first * norm_f[:, 0], first_z, first_inv)
    shift_grad = lax.psum(part_shift, ("row", "col"))
    grad_ckey = norm_back(sum_ckey, ck_z, ck_inv).reshape(images, text_len, model_width)
    grad_kv = jnp.concatenate(
        [grad_ckey, sum_cvalue.reshape(images, text_len, model_width)], axis=-1
    ).astype(jnp.bfloat16)
    text_slice = text_states.shape[2] // grid_devices
    text_cols = lax.dynamic_slice_in_dim(text_states, grid_at * text_slice, text_slice, 2)
    d_text_w = jnp.einsum("itc,itd->cd", text_cols, grad_kv, preferred_element_type=jnp.float32)
    text_grad = jnp.einsum("itd,cd->itc", grad_kv, part_text, preferred_element_type=jnp.float32)
    shift_low = shift_grad.astype(jnp.bfloat16)
    shift_slice = model_width // grid_devices
    act_cols = lax.dynamic_slice_in_dim(time_act, grid_at * shift_slice, shift_slice, 1)
    d_shift_w = jnp.einsum("ic,id->cd", act_cols, shift_low, preferred_element_type=jnp.float32)
    grad_time_act = right_dot(shift_low, f_shift)
    grad_time_pre = silu_pull(grad_time_act)[0].astype(jnp.bfloat16)
    freq_slice = embedding.shape[1] // grid_devices
    embed_cols = lax.dynamic_slice_in_dim(embedding, grid_at * freq_slice, freq_slice, 1)
    d_time_w = jnp.einsum(
        "ic,id->cd", embed_cols, grad_time_pre, preferred_element_type=jnp.float32
    )
    low_one = grad_one.astype(jnp.bfloat16)
    d_skip_w = left_dot(skip_in, low_one)
    grad_skip_in = right_dot(low_one, f_skip)
    gain_skips = jnp.sum(grad_skip_in * joined, axis=0)
    bias_skips = jnp.sum(grad_skip_in, axis=0)
    grad_joined = norm_back(grad_skip_in * gain_skip, joined, joined_inv)
    skip_grad = grad_joined[:, model_width:].reshape(images, rows_tile, cols_tile, model_width)
    grad_patch = grad_joined[:, :model_width].astype(jnp.bfloat16)
    d_patch = left_dot(grad_patch, patch_rows)
    latent_grad = plain_dot(grad_patch, f_patch).reshape(images, rows_tile, cols_tile, patch_width)
    d_norms = jnp.stack(
        [
            gain_first,
            bias_first,
            gain_third,
            bias_third,
            gain_second,
            bias_second,
            gain_final,
            bias_final,
            gain_skips[:model_width],
            bias_skips[:model_width],
            gain_skips[model_width:],
            bias_skips[model_width:],
        ],
        axis=1,
    )
    tile_done = (
        lax.psum_scatter(d_patch, ("row", "col"), scatter_dimension=0, tiled=True),
        lax.psum_scatter(d_skip_w, ("row", "col"), scatter_dimension=0, tiled=True),
        lax.psum_scatter(d_qkv, ("row", "col"), scatter_dimension=0, tiled=True),
        lax.psum_scatter(d_out, ("row", "col"), scatter_dimension=0, tiled=True),
        lax.psum_scatter(d_query, ("row", "col"), scatter_dimension=0, tiled=True),
        lax.psum_scatter(d_cross, ("row", "col"), scatter_dimension=0, tiled=True),
        lax.psum_scatter(d_up, ("row", "col"), scatter_dimension=0, tiled=True),
        lax.psum_scatter(d_down, ("row", "col"), scatter_dimension=0, tiled=True),
        lax.psum_scatter(d_final, ("row", "col"), scatter_dimension=0, tiled=True),
        lax.psum_scatter(d_norms, ("row", "col"), scatter_dimension=0, tiled=True),
    )
    reduced = (
        lax.psum_scatter(
            tile_done[0].astype(jnp.bfloat16), "dp", scatter_dimension=1, tiled=True
        ).astype(jnp.float32),
        lax.psum_scatter(
            tile_done[1].astype(jnp.bfloat16), "dp", scatter_dimension=1, tiled=True
        ).astype(jnp.float32),
        lax.psum_scatter(
            tile_done[2].astype(jnp.bfloat16), "dp", scatter_dimension=1, tiled=True
        ).astype(jnp.float32),
        lax.psum_scatter(
            tile_done[3].astype(jnp.bfloat16), "dp", scatter_dimension=1, tiled=True
        ).astype(jnp.float32),
        lax.psum_scatter(
            tile_done[4].astype(jnp.bfloat16), "dp", scatter_dimension=1, tiled=True
        ).astype(jnp.float32),
        lax.psum_scatter(
            tile_done[5].astype(jnp.bfloat16), "dp", scatter_dimension=1, tiled=True
        ).astype(jnp.float32),
        lax.psum_scatter(
            tile_done[6].astype(jnp.bfloat16), "dp", scatter_dimension=1, tiled=True
        ).astype(jnp.float32),
        lax.psum_scatter(
            tile_done[7].astype(jnp.bfloat16), "dp", scatter_dimension=1, tiled=True
        ).astype(jnp.float32),
        lax.psum_scatter(
            tile_done[8].astype(jnp.bfloat16), "dp", scatter_dimension=1, tiled=True
        ).astype(jnp.float32),
        lax.psum_scatter(
            tile_done[9].astype(jnp.bfloat16), "dp", scatter_dimension=1, tiled=True
        ).astype(jnp.float32),
        lax.psum_scatter(
            d_time_w.astype(jnp.bfloat16), "dp", scatter_dimension=1, tiled=True
        ).astype(jnp.float32),
        lax.psum_scatter(
            d_shift_w.astype(jnp.bfloat16), "dp", scatter_dimension=1, tiled=True
        ).astype(jnp.float32),
        lax.psum_scatter(
            d_text_w.astype(jnp.bfloat16), "dp", scatter_dimension=1, tiled=True
        ).astype(jnp.float32),
    )
    return (
        prediction,
        latent_grad,
        skip_grad,
        text_grad,
        reduced[0],
        reduced[1],
        reduced[10],
        reduced[11],
        reduced[2],
        reduced[3],
        reduced[4],
        reduced[12],
        reduced[5],
        reduced[6],
        reduced[7],
        reduced[8],
        reduced[9],
    )


TILE = ("row", "col")
EVERY = ("dp", "row", "col")
LOG2E = math.log2(math.e)
F32 = jnp.float32
BF16 = jnp.bfloat16
VMEM_BYTES = 56 * 2**20


def kernel_call(body, flops, moved, **options):
    return pl.pallas_call(
        body,
        compiler_params=pltpu.CompilerParams(vmem_limit_bytes=VMEM_BYTES),
        cost_estimate=pl.CostEstimate(flops=flops, bytes_accessed=moved, transcendentals=0),
        **options,
    )


def pair_swap(values_in):
    quarter = values_in.shape[0] // 4
    parts = [values_in[at * quarter : (at + 1) * quarter] for at in (1, 0, 3, 2)]
    return jnp.concatenate(parts, axis=0)


def column_norm(values_in):
    centred = values_in - jnp.mean(values_in, axis=0, keepdims=True)
    inverse = lax.rsqrt(jnp.mean(centred * centred, axis=0, keepdims=True) + EPSILON)
    return (centred * inverse, inverse)


def column_norm_back(grad_normed, normed, inverse):
    mean_grad = jnp.mean(grad_normed, axis=0, keepdims=True)
    mean_cross = jnp.mean(grad_normed * normed, axis=0, keepdims=True)
    return inverse * (grad_normed - mean_grad - normed * mean_cross)


def minus_pieces(row_values):
    high = row_values.astype(BF16).astype(F32)
    rest = row_values - high
    middle = rest.astype(BF16).astype(F32)
    lower = rest - middle
    at = lax.broadcasted_iota(jnp.int32, (8, row_values.shape[1]), 0)
    zero = jnp.zeros((8, row_values.shape[1]), F32)
    picked = jnp.where(at == 0, high, jnp.where(at == 1, middle, jnp.where(at == 2, lower, zero)))
    return -picked


def piece_flags(width):
    return (lax.broadcasted_iota(jnp.int32, (8, width), 0) < 3).astype(F32)


def head_norm_body(
    query_scale, rows_ref, weight_ref, cos_ref, sin_ref, ok_ref, out_ref, inv_ref
):
    groups, _, heads, head_dim, _ = out_ref.shape
    part = pl.program_id(0)
    made = jnp.dot(rows_ref[...], weight_ref[...], preferred_element_type=F32).T
    valid = ok_ref[...]

    @pl.when(part < 2)
    def _():
        factor = jnp.where(part == 0, query_scale, valid)
        cosine, sine = cos_ref[...] * factor, sin_ref[...] * factor
        for group in range(groups):
            for head in range(heads):
                at = (group * heads + head) * head_dim
                normed, inverse = column_norm(made[at : at + head_dim])
                turned = normed * cosine + pair_swap(normed) * sine
                out_ref[group, 0, head] = turned.astype(BF16)
                inv_ref[group, 0, head : head + 1] = inverse

    @pl.when(part == 2)
    def _():
        for group in range(groups):
            for head in range(heads):
                at = (group * heads + head) * head_dim
                out_ref[group, 0, head] = (made[at : at + head_dim] * valid).astype(BF16)
                inv_ref[group, 0, head : head + 1] = valid


def head_norm(rows, weight, tables, valid, groups, head_dim, query_scale):
    tile_len, depth = rows.shape
    width = weight.shape[1] // 3
    heads = width // groups // head_dim
    table = pl.BlockSpec((head_dim, tile_len), lambda p: (0, 0))
    return kernel_call(
        functools.partial(head_norm_body, query_scale),
        6 * tile_len * depth * width,
        6 * depth * width,
        grid=(3,),
        in_specs=[
            pl.BlockSpec((tile_len, depth), lambda p: (0, 0)),
            pl.BlockSpec((depth, width), lambda p: (0, p)),
            table,
            table,
            pl.BlockSpec((1, tile_len), lambda p: (0, 0)),
        ],
        out_specs=[
            pl.BlockSpec((groups, 1, heads, head_dim, tile_len), lambda p: (0, p, 0, 0, 0)),
            pl.BlockSpec((groups, 1, heads, tile_len), lambda p: (0, p, 0, 0)),
        ],
        out_shape=[
            jax.ShapeDtypeStruct((groups, 3, heads, head_dim, tile_len), BF16),
            jax.ShapeDtypeStruct((groups, 3, heads, tile_len), F32),
        ],
    )(rows, weight, *tables, valid)


def head_back_body(
    query_scale, grad_ref, own_ref, inv_ref, cos_ref, sin_ref, ok_ref, *others
):
    out_ref = others[-1]
    heads, head_dim = own_ref.shape[2], own_ref.shape[3]
    cosine, sine, valid = cos_ref[...], sin_ref[...], ok_ref[...]

    def unturn(values_in):
        return values_in * cosine - pair_swap(values_in) * sine

    for part in range(3):
        pieces = []
        for head in range(heads):
            grad = grad_ref[0, part, head].astype(F32)
            if part > 0:
                grad = grad * valid
            if part < 2:
                normed = unturn(own_ref[0, part, head].astype(F32))
                if part == 0:
                    normed = normed * (1.0 / query_scale)
                inverse = inv_ref[0, part, head : head + 1]
                grad = column_norm_back(unturn(grad), normed, inverse)
            pieces.append(grad)
        out_ref[part, 0] = jnp.concatenate(pieces, axis=0).astype(BF16)


def head_back(grads, own, inverses, tables, valid, query_scale, image, images, before):
    groups, _, heads, head_dim, tile_len = own.shape
    group_rows = heads * head_dim
    stacked = pl.BlockSpec((1, 3, heads, head_dim, tile_len), lambda g: (g, 0, 0, 0, 0))
    table = pl.BlockSpec((head_dim, tile_len), lambda g: (0, 0))
    earlier = () if before is None else (before,)
    return kernel_call(
        functools.partial(head_back_body, query_scale),
        0,
        6 * own.size,
        grid=(groups,),
        in_specs=[
            stacked,
            stacked,
            pl.BlockSpec((1, 3, heads, tile_len), lambda g: (g, 0, 0, 0)),
            table,
            table,
            pl.BlockSpec((1, tile_len), lambda g: (0, 0)),
        ]
        + [pl.BlockSpec(memory_space=pl.ANY)] * len(earlier),
        out_specs=pl.BlockSpec((3, 1, group_rows, tile_len), lambda g: (0, g, 0, image)),
        out_shape=jax.ShapeDtypeStruct((3, groups, group_rows, images * tile_len), BF16),
        input_output_aliases={6: 0} if earlier else {},
    )(grads, own, inverses, *tables, valid, *earlier)


def attend_body(query_ref, key_ref, value_ref, ok_ref, out_ref, lse_ref, key_nat, value_ext):
    tiles, tile_len, head_dim = key_ref.shape[0], key_ref.shape[-1], key_ref.shape[-2]

    @pl.when(pl.program_id(1) == 0)
    def _():
        for tile in range(tiles):
            key_nat[tile * tile_len : (tile + 1) * tile_len, :] = key_ref[tile, 0, 0].T
            value_ext[tile] = jnp.concatenate(
                [value_ref[tile, 0, 0].astype(F32), ok_ref[tile]], axis=0
            ).astype(BF16)

    query = query_ref[0, 0, 0]
    total = jnp.zeros((head_dim + 8, tile_len), F32)
    held = None
    for tile in range(tiles + 1):
        scores = None
        if tile < tiles:
            rows = slice(tile * tile_len, (tile + 1) * tile_len)
            scores = jnp.dot(key_nat[rows, :], query, preferred_element_type=F32)
        if held is not None:
            weight = jnp.exp2(held).astype(BF16)
            total = total + jnp.dot(value_ext[tile - 1], weight, preferred_element_type=F32)
        held = scores
    weight_sum = total[head_dim : head_dim + 1]
    out_ref[0, 0] = (total[:head_dim] / weight_sum).astype(BF16)
    lse_ref[0, 0] = jnp.log2(weight_sum)


def attend(qkv, flags):
    tiles, _, heads, head_dim, tile_len = qkv.shape
    return kernel_call(
        attend_body,
        1024 * heads * tiles**2 * tile_len**2,
        8 * qkv.size,
        grid=(heads, tiles),
        in_specs=[
            pl.BlockSpec((1, 1, 1, head_dim, tile_len), lambda h, t: (t, 0, h, 0, 0)),
            pl.BlockSpec((tiles, 1, 1, head_dim, tile_len), lambda h, t: (0, 1, h, 0, 0)),
            pl.BlockSpec((tiles, 1, 1, head_dim, tile_len), lambda h, t: (0, 2, h, 0, 0)),
            pl.BlockSpec((tiles, 8, tile_len), lambda h, t: (0, 0, 0)),
        ],
        out_specs=[
            pl.BlockSpec((1, 1, head_dim, tile_len), lambda h, t: (t, h, 0, 0)),
            pl.BlockSpec((1, 1, 1, tile_len), lambda h, t: (t, h, 0, 0)),
        ],
        out_shape=[
            jax.ShapeDtypeStruct((tiles, heads, head_dim, tile_len), BF16),
            jax.ShapeDtypeStruct((tiles, heads, 1, tile_len), F32),
        ],
        scratch_shapes=[
            pltpu.VMEM((tiles * tile_len, head_dim), BF16),
            pltpu.VMEM((tiles, head_dim + 8, tile_len), BF16),
        ],
    )(qkv, qkv, qkv, flags)


def attend_back_body(
    score_scale,
    query_ref,
    key_ref,
    value_ref,
    grad_ref,
    att_ref,
    lse_ref,
    out_ref,
    key_nat,
    value_nat,
    key_sum,
    value_sum,
):
    tiles, tile_len, head_dim = key_ref.shape[0], key_ref.shape[-1], key_ref.shape[-2]
    at = pl.program_id(1)

    @pl.when(at == 0)
    def _():
        ones = piece_flags(tile_len)
        for tile in range(tiles):
            rows = slice(tile * tile_len, (tile + 1) * tile_len)
            for source, kept in ((key_ref, key_nat), (value_ref, value_nat)):
                wide = jnp.concatenate([source[tile, 0, 0].astype(F32), ones], axis=0)
                kept[rows, :] = wide.T.astype(BF16)
        key_sum[...] = jnp.zeros_like(key_sum)
        value_sum[...] = jnp.zeros_like(value_sum)

    query = query_ref[0, 0, 0].astype(F32)
    grad = grad_ref[0, 0].astype(F32)
    delta = jnp.sum(grad * att_ref[0, 0].astype(F32), axis=0, keepdims=True)
    query_ext = jnp.concatenate([query, minus_pieces(lse_ref[0, 0])], axis=0)
    grad_ext = jnp.concatenate([grad, minus_pieces(delta)], axis=0)
    query_cols, grad_cols = query_ext.astype(BF16), grad_ext.astype(BF16)
    query_nat, grad_nat = query_ext.T.astype(BF16), grad_ext.T.astype(BF16)

    def step(tile, total):
        rows = pl.ds(pl.multiple_of(tile * tile_len, tile_len), tile_len)
        scores = jnp.dot(key_nat[rows, :], query_cols, preferred_element_type=F32)
        probs = jnp.exp2(scores)
        grad_probs = jnp.dot(value_nat[rows, :], grad_cols, preferred_element_type=F32)
        grad_scores = (probs * grad_probs).astype(BF16)
        value_sum[rows, :] += jnp.dot(probs.astype(BF16), grad_nat, preferred_element_type=F32)
        key_sum[rows, :] += jnp.dot(grad_scores, query_nat, preferred_element_type=F32)
        return total + jnp.dot(key_ref[tile, 0, 0], grad_scores, preferred_element_type=F32)

    start = jnp.zeros((head_dim, tile_len), F32)
    total = lax.fori_loop(0, tiles, step, start, unroll=8)
    out_ref[at, 0, 0] = (total * score_scale).astype(BF16)

    @pl.when(at == tiles - 1)
    def _():
        for tile in range(tiles):
            rows = slice(tile * tile_len, (tile + 1) * tile_len)
            key_grad = key_sum[rows, :].T[:head_dim] * (1.0 / LOG2E)
            out_ref[tile, 1, 0] = key_grad.astype(BF16)
            out_ref[tile, 2, 0] = value_sum[rows, :].T[:head_dim].astype(BF16)


def attend_back(qkv, grad_att, att, lse, score_scale):
    tiles, _, heads, head_dim, tile_len = qkv.shape
    one = pl.BlockSpec((1, 1, head_dim, tile_len), lambda h, t: (t, h, 0, 0))
    return kernel_call(
        functools.partial(attend_back_body, score_scale),
        2560 * heads * tiles**2 * tile_len**2,
        8 * qkv.size,
        grid=(heads, tiles),
        in_specs=[
            pl.BlockSpec((1, 1, 1, head_dim, tile_len), lambda h, t: (t, 0, h, 0, 0)),
            pl.BlockSpec((tiles, 1, 1, head_dim, tile_len), lambda h, t: (0, 1, h, 0, 0)),
            pl.BlockSpec((tiles, 1, 1, head_dim, tile_len), lambda h, t: (0, 2, h, 0, 0)),
            one,
            one,
            pl.BlockSpec((1, 1, 1, tile_len), lambda h, t: (t, h, 0, 0)),
        ],
        out_specs=pl.BlockSpec(
            (tiles, 3, 1, head_dim, tile_len), lambda h, t: (0, 0, h, 0, 0)
        ),
        out_shape=jax.ShapeDtypeStruct(qkv.shape, BF16),
        scratch_shapes=[
            pltpu.VMEM((tiles * tile_len, head_dim + 8), BF16),
            pltpu.VMEM((tiles * tile_len, head_dim + 8), BF16),
            pltpu.VMEM((tiles * tile_len, head_dim + 8), F32),
            pltpu.VMEM((tiles * tile_len, head_dim + 8), F32),
        ],
    )(qkv, qkv, qkv, grad_att, att, lse)


def cross_body(text_len, query_scale, pre_ref, kv_ref, att_ref, query_ref, inv_ref, lse_ref):
    head_dim, text_pad = kv_ref.shape[2], kv_ref.shape[3]
    at = lax.broadcasted_iota(jnp.int32, (8, text_pad), 0)
    text_at = lax.broadcasted_iota(jnp.int32, (8, text_pad), 1)
    flags = ((at == 0) & (text_at < text_len)).astype(F32)
    for head in range(pre_ref.shape[0]):
        normed, inverse = column_norm(pre_ref[head])
        query = (normed * query_scale).astype(BF16)
        query_ref[head] = query
        inv_ref[head] = inverse
        key = column_norm(kv_ref[0, head])[0].astype(BF16)
        value_ext = jnp.concatenate([kv_ref[1, head], flags], axis=0).astype(BF16)
        scores = jnp.dot(key.T, query, preferred_element_type=F32)
        weight = jnp.exp2(scores).astype(BF16)
        total = jnp.dot(value_ext, weight, preferred_element_type=F32)
        weight_sum = total[head_dim : head_dim + 1]
        att_ref[head] = (total[:head_dim] / weight_sum).astype(BF16)
        lse_ref[head] = jnp.log2(weight_sum)


def cross_attend(pre, text_kv, images, text_len, query_scale):
    heads, head_dim, tokens = pre.shape
    tile_len, text_pad = tokens // images, text_kv.shape[3] // images
    block = math.gcd(heads, 4)
    wide = pl.BlockSpec((block, head_dim, tile_len), lambda i, h: (h, 0, i))
    row = pl.BlockSpec((block, 1, tile_len), lambda i, h: (h, 0, i))
    return kernel_call(
        functools.partial(cross_body, text_len, query_scale),
        1024 * heads * tokens * text_pad,
        8 * pre.size,
        grid=(images, heads // block),
        in_specs=[wide, pl.BlockSpec((2, block, head_dim, text_pad), lambda i, h: (0, h, 0, i))],
        out_specs=[wide, wide, row, row],
        out_shape=[
            jax.ShapeDtypeStruct(pre.shape, BF16),
            jax.ShapeDtypeStruct(pre.shape, BF16),
            jax.ShapeDtypeStruct((heads, 1, tokens), F32),
            jax.ShapeDtypeStruct((heads, 1, tokens), F32),
        ],
    )(pre, text_kv)


def cross_back_body(
    query_scale,
    score_scale,
    query_ref,
    kv_ref,
    grad_ref,
    att_ref,
    inv_ref,
    lse_ref,
    out_ref,
    key_ref,
    value_ref,
):
    head_dim, text_pad = kv_ref.shape[2], kv_ref.shape[3]
    ones = piece_flags(text_pad)
    for head in range(query_ref.shape[0]):
        query = query_ref[head].astype(F32)
        grad = grad_ref[head].astype(F32)
        delta = jnp.sum(grad * att_ref[head].astype(F32), axis=0, keepdims=True)
        query_ext = jnp.concatenate([query, minus_pieces(lse_ref[head])], axis=0).astype(BF16)
        grad_ext = jnp.concatenate([grad, minus_pieces(delta)], axis=0).astype(BF16)
        key = column_norm(kv_ref[0, head])[0].astype(BF16)
        key_ext = jnp.concatenate([key.astype(F32), ones], axis=0).T.astype(BF16)
        value_ext = jnp.concatenate([kv_ref[1, head], ones], axis=0).T.astype(BF16)
        probs = jnp.exp2(jnp.dot(key_ext, query_ext, preferred_element_type=F32))
        grad_probs = jnp.dot(value_ext, grad_ext, preferred_element_type=F32)
        grad_scores = (probs * grad_probs).astype(BF16)
        value_grad = right_dot(grad_ext, probs.astype(BF16))[:head_dim]
        key_grad = right_dot(query_ext, grad_scores)[:head_dim]
        key_ref[head] = (key_grad * (1.0 / LOG2E)).astype(BF16)
        value_ref[head] = value_grad.astype(BF16)
        query_grad = jnp.dot(key, grad_scores, preferred_element_type=F32) * score_scale
        normed = query * (1.0 / query_scale)
        out_ref[head] = column_norm_back(query_grad, normed, inv_ref[head]).astype(BF16)


def cross_back(query, text_kv, grad, att, inverse, lse, images, query_scale, score_scale):
    heads, head_dim, tokens = query.shape
    tile_len, text_pad = tokens // images, text_kv.shape[3] // images
    block = math.gcd(heads, 4)
    wide = pl.BlockSpec((block, head_dim, tile_len), lambda i, h: (h, 0, i))
    row = pl.BlockSpec((block, 1, tile_len), lambda i, h: (h, 0, i))
    text = pl.BlockSpec((2, block, head_dim, text_pad), lambda i, h: (0, h, 0, i))
    text_out = pl.BlockSpec((block, head_dim, text_pad), lambda i, h: (h, 0, i))
    return kernel_call(
        functools.partial(cross_back_body, query_scale, score_scale),
        2560 * heads * tokens * text_pad,
        16 * query.size,
        grid=(images, heads // block),
        in_specs=[wide, text, wide, wide, row, row],
        out_specs=[
            wide,
            text_out,
            text_out,
        ],
        out_shape=[
            jax.ShapeDtypeStruct(query.shape, BF16),
            jax.ShapeDtypeStruct((heads, head_dim, images * text_pad), BF16),
            jax.ShapeDtypeStruct((heads, head_dim, images * text_pad), BF16),
        ],
    )(query, text_kv, grad, att, inverse, lse)


def join_norm_body(patch_ref, skip_ref, weight_ref, gain_ref, bias_ref, z_ref, inv_ref, in_ref):
    width = skip_ref.shape[1]
    patch_feat = right_dot(patch_ref[...], weight_ref[...])
    joined = jnp.concatenate([patch_feat, skip_ref[...].astype(F32)], axis=1)
    normed, inverse = layer_norm(joined)
    z_ref[...] = normed
    inv_ref[...] = inverse
    in_ref[...] = (normed * gain_ref[...] + bias_ref[...]).astype(BF16)


def join_norm(patch_rows, skip_rows, f_patch, gain, bias):
    tokens, width = skip_rows.shape
    block = math.gcd(tokens, 256)
    rows = lambda columns: pl.BlockSpec((block, columns), lambda t: (t, 0))
    fixed = lambda shape: pl.BlockSpec(shape, lambda t: (0, 0))
    return kernel_call(
        join_norm_body,
        64 * tokens * width,
        16 * tokens * width,
        grid=(tokens // block,),
        in_specs=[
            rows(patch_rows.shape[1]),
            rows(width),
            fixed(f_patch.shape),
            fixed(gain.shape),
            fixed(bias.shape),
        ],
        out_specs=[rows(2 * width), rows(1), rows(2 * width)],
        out_shape=[
            jax.ShapeDtypeStruct((tokens, 2 * width), F32),
            jax.ShapeDtypeStruct((tokens, 1), F32),
            jax.ShapeDtypeStruct((tokens, 2 * width), BF16),
        ],
    )(patch_rows, skip_rows, f_patch, gain, bias)


def join_back_body(low_ref, weight_ref, z_ref, inv_ref, gain_ref, skip_ref, patch_ref, sums_ref):
    width = skip_ref.shape[1]
    grad, normed = right_dot(low_ref[...], weight_ref[...]), z_ref[...]

    @pl.when(pl.program_id(0) == 0)
    def _():
        sums_ref[...] = jnp.zeros_like(sums_ref)

    sums_ref[0:1] += jnp.sum(grad * normed, axis=0, keepdims=True)
    sums_ref[1:2] += jnp.sum(grad, axis=0, keepdims=True)
    back = norm_back(grad * gain_ref[...], normed, inv_ref[...])
    patch_ref[...] = back[:, :width].astype(BF16)
    skip_ref[...] = back[:, width:]


def join_back(low_rows, f_skip, normed, inverse, gain):
    tokens, width = low_rows.shape
    block = math.gcd(tokens, 256)
    rows = lambda columns: pl.BlockSpec((block, columns), lambda t: (t, 0))
    fixed = lambda shape: pl.BlockSpec(shape, lambda t: (0, 0))
    return kernel_call(
        join_back_body,
        4 * tokens * width * width,
        18 * tokens * width,
        grid=(tokens // block,),
        in_specs=[rows(width), fixed(f_skip.shape), rows(2 * width), rows(1), fixed(gain.shape)],
        out_specs=[rows(width), rows(width), fixed((2, 2 * width))],
        out_shape=[
            jax.ShapeDtypeStruct((tokens, width), F32),
            jax.ShapeDtypeStruct((tokens, width), BF16),
            jax.ShapeDtypeStruct((2, 2 * width), F32),
        ],
    )(low_rows, f_skip, normed, inverse, gain)


def gelu_and_slope(inputs):
    scale, cubic = math.sqrt(2.0 / math.pi), 0.044715
    square = inputs * inputs
    curve = jnp.tanh(scale * inputs * (1.0 + cubic * square))
    half = 0.5 * (1.0 + curve)
    bend = 0.5 * inputs * (1.0 - curve * curve) * (scale * (1.0 + 3.0 * cubic * square))
    return ((inputs * half).astype(BF16), (half + bend).astype(BF16))


def swap_tiles(values_in):
    return lax.all_to_all(values_in, TILE, split_axis=0, concat_axis=0, tiled=True)


def shift_pairs(devices, step):
    return [(at, (at + step) % devices) for at in range(devices)]


def fetch(weight):
    devices = lax.axis_size("dp")
    return [weight] + [
        lax.ppermute(weight, "dp", shift_pairs(devices, step)) for step in range(1, devices)
    ]


def widen(pieces, first=None, joined=1):
    devices, me = lax.axis_size("dp"), lax.axis_index("dp")
    if first is not None:
        pieces = after(first, *pieces)
    slots = [lax.select_n((me - at) % devices, *pieces) for at in range(devices)]
    if joined > 1:
        split = [jnp.split(slot, joined, axis=1) for slot in slots]
        slots = [each for group in zip(*split) for each in group]
    return jnp.concatenate(slots, axis=1)


def narrow_blocks(blocks, first=None):
    devices, me = lax.axis_size("dp"), lax.axis_index("dp")
    received = []
    for step in range(1, devices):
        sent = lax.select_n((me + step) % devices, *blocks)
        received.append(lax.ppermute(sent, "dp", shift_pairs(devices, step)))
    if first is not None:
        received = after(first, *received)
    total = lax.select_n(me, *blocks).astype(F32)
    for piece in received:
        total = total + piece.astype(F32)
    return total


def narrow(weight_grad, first=None):
    return narrow_blocks(jnp.split(weight_grad, lax.axis_size("dp"), axis=1), first)


def by_device(weight_grads, parts):
    devices = lax.axis_size("dp")
    split = [jnp.split(weight_grad, devices, axis=1) for weight_grad in weight_grads]
    return [jnp.concatenate(blocks, axis=parts) for blocks in zip(*split)]


def sum_tiles(part_sums):
    devices, me = lax.axis_size(TILE), lax.axis_index(TILE)
    total, step = part_sums, devices // 2
    while step > 0:
        pairs = [(at, at ^ step) for at in range(devices)]
        lower, upper = jnp.split(total, 2, axis=0)
        high = (me // step) % 2 == 1
        sent = jnp.where(high, lower, upper)
        total = jnp.where(high, upper, lower) + lax.ppermute(sent, TILE, pairs)
        step //= 2
    return total


def total_tiles(part_sum):
    devices = lax.axis_size(TILE)
    total, step = part_sum, 1
    while step < devices:
        pairs = [(at, at ^ step) for at in range(devices)]
        total = total + lax.ppermute(total, TILE, pairs)
        step *= 2
    return total


def over_tiles(weight_grad):
    return lax.optimization_barrier(
        lax.psum_scatter(weight_grad, TILE, scatter_dimension=0, tiled=True)
    )


def tiles_whole(weight):
    return lax.all_gather(weight, TILE, axis=0, tiled=True)


def after(first, *values_in):
    return lax.optimization_barrier((first, *values_in))[1:]


def dot_over(left_mat, right_mat, left_axis, right_axis):
    return lax.dot_general(
        left_mat,
        right_mat,
        (((left_axis,), (right_axis,)), ((), ())),
        preferred_element_type=F32,
    )


def local_heads(
    latent,
    skip_input,
    text_states,
    timesteps,
    image_sides,
    cotangent,
    w_patch,
    w_skip,
    w_time,
    w_shift,
    w_qkv,
    w_out,
    w_query,
    w_text,
    w_cross,
    w_up,
    w_down,
    w_final,
    norm_params,
):
    dp_devices = lax.axis_size("dp")
    grid_devices = lax.axis_size(TILE)
    col_devices = lax.axis_size("col")
    grid_at = lax.axis_index(TILE)
    row_at = lax.axis_index("row")
    col_at = lax.axis_index("col")
    images, rows_tile, cols_tile, patch_width = latent.shape
    tile_len = rows_tile * cols_tile
    row_count = images * tile_len
    out_width = cotangent.shape[3]

    f_skip = tiles_whole(widen(fetch(w_skip)))
    small = jnp.concatenate([w_patch, w_final, norm_params], axis=1)
    small_widths = (w_patch.shape[1], w_final.shape[1], norm_params.shape[1])
    cuts = (0, small_widths[0], sum(small_widths[:2]), sum(small_widths))
    early = [jnp.pad(small, ((0, 0), (0, w_shift.shape[1] - small.shape[1]))), w_time, w_shift]
    ends = (small.shape[0], small.shape[0] + w_time.shape[0])
    part_small, part_time, part_shift_w = jnp.split(
        widen(fetch(jnp.concatenate(early, axis=0))), ends, axis=0
    )
    part_small = part_small.reshape(small.shape[0], dp_devices, -1)[:, :, : small.shape[1]]
    part_small = part_small.reshape(small.shape[0], -1)
    f_small = tiles_whole(part_small).reshape(-1, dp_devices, sum(small_widths))
    f_patch, f_final, f_norms = (
        f_small[:, :, cuts[at] : cuts[at + 1]].reshape(f_small.shape[0], -1) for at in range(3)
    )
    held_qkv = fetch(w_qkv)
    held_three = fetch(jnp.concatenate([w_out, w_query, w_cross], axis=1))
    held_text = fetch(w_text)
    held_up, held_down = fetch(w_up), fetch(w_down)
    model_width = skip_input.shape[3]
    head_count = HEADS
    head_dim = model_width // head_count
    text_len = text_states.shape[1]
    text_pad = -(-text_len // 128) * 128
    score_scale = head_dim ** (-0.5)
    query_scale = score_scale * LOG2E
    positions = jnp.arange(tile_len, dtype=jnp.int32)
    row_pos = row_at * rows_tile + positions // cols_tile
    col_pos = col_at * cols_tile + positions % cols_tile
    query_ok = (row_pos[None, :] < image_sides[:, None]) & (col_pos[None, :] < image_sides[:, None])
    valid = query_ok.astype(F32)
    keep_rows = query_ok.astype(F32).reshape(row_count, 1)
    tile_list = jnp.arange(grid_devices, dtype=jnp.int32)[:, None]
    key_row = tile_list // col_devices * rows_tile + (positions // cols_tile)[None, :]
    key_col = tile_list % col_devices * cols_tile + (positions % cols_tile)[None, :]
    sides = image_sides[:, None, None]
    key_ok = ((key_row[None] < sides) & (key_col[None] < sides)).astype(F32)
    flags = jnp.concatenate(
        [key_ok[:, :, None, :], jnp.zeros((images, grid_devices, 7, tile_len), F32)], axis=2
    )
    cos_row, sin_row, cos_col, sin_col = (
        jnp.transpose(table[:, 0, :]) for table in rope_tables(row_pos, col_pos, head_dim)
    )
    tables = (
        jnp.concatenate([cos_row, cos_row, cos_col, cos_col], axis=0),
        jnp.concatenate([-sin_row, sin_row, -sin_col, sin_col], axis=0),
    )
    norm_f = f_norms.astype(F32)

    embedding = time_embed(timesteps, FREQ).astype(BF16)
    freq_slice = part_time.shape[0]
    shift_slice = part_shift_w.shape[0]
    embed_cols = lax.dynamic_slice_in_dim(embedding, grid_at * freq_slice, freq_slice, 1)
    time_pre = total_tiles(plain_dot(embed_cols, part_time))
    time_float, silu_pull = jax.vjp(jax.nn.silu, time_pre)
    time_act = time_float.astype(BF16)
    act_cols = lax.dynamic_slice_in_dim(time_act, grid_at * shift_slice, shift_slice, 1)
    time_shift = total_tiles(plain_dot(act_cols, part_shift_w))

    patch_rows = latent.reshape(row_count, patch_width)
    skip_rows = skip_input.reshape(row_count, model_width)
    gain_skip = jnp.concatenate([norm_f[:, 8], norm_f[:, 10]])[None]
    bias_skip = jnp.concatenate([norm_f[:, 9], norm_f[:, 11]])[None]
    joined, joined_inv, skip_in = join_norm(patch_rows, skip_rows, f_patch, gain_skip, bias_skip)
    f_qkv = tiles_whole(widen(held_qkv, skip_in))
    part_three = widen(held_three, skip_in, 3)
    f_three = tiles_whole(part_three)
    f_out, f_query, f_cross = jnp.split(f_three, 3, axis=1)
    residual = plain_dot(skip_in, f_skip)
    first_z, first_inv = layer_norm(residual)
    first_pre = (first_z * norm_f[:, 0] + norm_f[:, 1]).reshape(
        images, tile_len, model_width
    ) + time_shift[:, None, :]
    first_in = first_pre.reshape(row_count, model_width).astype(BF16)
    part_text = widen(held_text, first_in)
    f_text = tiles_whole(part_text)
    first_rows = first_in.reshape(images, tile_len, model_width)
    own_qkv, qk_inv, tile_qkv, tile_att, tile_lse, att_rows = [], [], [], [], [], []
    for image in range(images):
        rows = first_rows[image]
        own, inverses = head_norm(
            rows,
            f_qkv,
            tables,
            valid[image : image + 1],
            grid_devices,
            head_dim,
            query_scale,
        )
        own_qkv.append(own)
        qk_inv.append(inverses)
        tile_qkv.append(swap_tiles(own))
    f_up = tiles_whole(widen(held_up, tile_qkv[0]))
    for image in range(images):
        att, lse = attend(tile_qkv[image], flags[image])
        tile_att.append(att)
        tile_lse.append(lse)
        own_att = swap_tiles(att).reshape(model_width, tile_len)
        att_rows.append(jnp.transpose(own_att))
    att_low = jnp.concatenate(att_rows, axis=0)
    residual_two = residual + plain_dot(att_low, f_out)
    f_down = tiles_whole(widen(held_down, residual_two))

    third_z, third_inv = layer_norm(residual_two)
    third_in = (third_z * norm_f[:, 2] + norm_f[:, 3]).astype(BF16)
    cross_pre = dot_over(f_query, third_in, 0, 1).reshape(head_count, head_dim, row_count)
    text_rows = jnp.pad(text_states, ((0, 0), (0, text_pad - text_len), (0, 0)))
    text_rows = text_rows.reshape(images * text_pad, -1)
    text_kv = dot_over(f_text, text_rows, 0, 1).reshape(2, head_count, head_dim, images * text_pad)
    crossed, cross_queries, cq_inv, cross_lse = cross_attend(
        cross_pre, text_kv, images, text_len, query_scale
    )
    cross_cols = crossed.reshape(model_width, row_count)
    residual_three = residual_two + left_dot(cross_cols, f_cross)
    second_z, second_inv = layer_norm(residual_three)
    second_in = (second_z * norm_f[:, 4] + norm_f[:, 5]).astype(BF16)
    up_pre = plain_dot(second_in, f_up)
    hidden_act, slope = lax.optimization_barrier(gelu_and_slope(up_pre))
    residual_four = residual_three + plain_dot(hidden_act, f_down)
    last_z, last_inv = layer_norm(residual_four)
    last_in = (last_z * norm_f[:, 6] + norm_f[:, 7]).astype(BF16)
    produced = plain_dot(last_in, f_final)
    prediction = (
        (produced * keep_rows).astype(BF16).reshape(images, rows_tile, cols_tile, out_width)
    )

    grad_out = (cotangent.reshape(row_count, out_width).astype(F32) * keep_rows).astype(BF16)
    d_final = left_dot(last_in, grad_out)
    grad_last = right_dot(grad_out, f_final)
    gain_final = jnp.sum(grad_last * last_z, axis=0)
    bias_final = jnp.sum(grad_last, axis=0)
    grad_four = norm_back(grad_last * norm_f[:, 6], last_z, last_inv)
    low_four = grad_four.astype(BF16)
    d_down = left_dot(hidden_act, low_four).astype(BF16)
    d_down, low_four = lax.optimization_barrier((d_down, low_four))
    t_down = over_tiles(d_down)
    grad_hidden = right_dot(low_four, f_down)
    grad_up = (grad_hidden * slope).astype(BF16)
    d_up = left_dot(second_in, grad_up).astype(BF16)
    d_up, grad_up = lax.optimization_barrier((d_up, grad_up))
    t_up = over_tiles(d_up)
    grad_second = right_dot(grad_up, f_up)
    gain_second = jnp.sum(grad_second * second_z, axis=0)
    bias_second = jnp.sum(grad_second, axis=0)
    grad_three = grad_four + norm_back(grad_second * norm_f[:, 4], second_z, second_inv)
    low_three = grad_three.astype(BF16)
    d_cross = plain_dot(cross_cols, low_three).astype(BF16)
    grad_crossed = dot_over(f_cross, low_three, 1, 1).astype(BF16)
    grad_cross_q, d_text_key, d_text_value = cross_back(
        cross_queries,
        text_kv,
        grad_crossed.reshape(head_count, head_dim, row_count),
        crossed,
        cq_inv,
        cross_lse,
        images,
        query_scale,
        score_scale,
    )
    t_down, grad_cross_q = lax.optimization_barrier((t_down, grad_cross_q))
    grad_cross_q = grad_cross_q.reshape(model_width, row_count)
    d_query = dot_over(third_in, grad_cross_q, 0, 1).astype(BF16)
    grad_third = dot_over(grad_cross_q, f_query, 0, 1)
    gain_third = jnp.sum(grad_third * third_z, axis=0)
    bias_third = jnp.sum(grad_third, axis=0)
    grad_two = grad_three + norm_back(grad_third * norm_f[:, 2], third_z, third_inv)
    low_two = grad_two.astype(BF16)
    low_two_rows = low_two.reshape(images, tile_len, model_width)
    tile_grads = []
    for image in range(images):
        grad_att = dot_over(f_out, low_two_rows[image], 1, 1).astype(BF16)
        tile_grads.append(swap_tiles(grad_att.reshape(tile_att[image].shape)))
    d_out = left_dot(att_low, low_two).astype(BF16)
    d_joint = jnp.concatenate(
        [
            d_out,
            d_query,
            d_cross,
            d_text_key.reshape(model_width, -1),
            d_text_value.reshape(model_width, -1),
        ],
        axis=1,
    )
    d_joint = with_layout_constraint(d_joint, Layout(major_to_minor=(0, 1)))
    d_joint, tile_grads[0] = lax.optimization_barrier((d_joint, tile_grads[0]))
    t_joint = over_tiles(d_joint)
    own_grads, grad_qkv, tile_back = [], None, None
    for image in range(images):
        if tile_back is not None:
            down_grad = narrow(t_down, tile_back)
            down_grad, tile_grads[image], tile_back = lax.optimization_barrier(
                (down_grad, tile_grads[image], tile_back)
            )
            own_grads.append(swap_tiles(tile_back))
        tile_back = attend_back(
            tile_qkv[image], tile_grads[image], tile_att[image], tile_lse[image], score_scale
        )
    own_grads.append(swap_tiles(tile_back))
    for image in range(images):
        if image == images - 1:
            up_grad = narrow(t_up, tile_back)
            up_grad, own_grads[-1], grad_qkv = lax.optimization_barrier(
                (up_grad, own_grads[-1], grad_qkv)
            )
        grad_qkv = head_back(
            own_grads[image],
            own_qkv[image],
            qk_inv[image],
            tables,
            valid[image : image + 1],
            query_scale,
            image,
            images,
            grad_qkv,
        )
    sum_text_kv = t_joint[:, 3 * model_width :].astype(F32)
    sum_text_kv = jnp.transpose(
        sum_text_kv.reshape(-1, head_dim, 2, images * text_pad), (2, 0, 1, 3)
    )
    group_heads = head_count // grid_devices
    own_key = lax.dynamic_slice_in_dim(text_kv[0], grid_at * group_heads, group_heads, 0)
    ck_z, ck_inv = layer_norm(jnp.swapaxes(own_key, 1, 2))
    grad_ckey = jnp.swapaxes(norm_back(jnp.swapaxes(sum_text_kv[0], 1, 2), ck_z, ck_inv), 1, 2)
    grad_kv = jnp.stack([grad_ckey, sum_text_kv[1]]).astype(BF16)
    grad_kv = tiles_whole(grad_kv.reshape(-1, images * text_pad))
    grad_qkv = grad_qkv.reshape(3 * model_width, row_count)
    d_qkv = dot_over(first_in, grad_qkv, 0, 1).astype(BF16)
    d_qkv, grad_qkv = lax.optimization_barrier((d_qkv, grad_qkv))
    t_qkv = over_tiles(d_qkv)
    grad_first = dot_over(grad_qkv, f_qkv, 0, 1)
    joint_blocks = by_device(jnp.split(t_joint[:, : 3 * model_width], 3, axis=1), 1)
    joint_grad = narrow_blocks(joint_blocks, grad_first)
    gain_first = jnp.sum(grad_first * first_z, axis=0)
    bias_first = jnp.sum(grad_first, axis=0)
    part_shift = jnp.sum(grad_first.reshape(images, tile_len, model_width), axis=1)
    grad_one = grad_two + norm_back(grad_first * norm_f[:, 0], first_z, first_inv)

    shift_low = total_tiles(part_shift).astype(BF16)
    d_shift = left_dot(act_cols, shift_low).astype(BF16)
    grad_time_act = total_tiles(
        lax.dynamic_update_slice_in_dim(
            jnp.zeros_like(time_pre), right_dot(shift_low, part_shift_w), grid_at * shift_slice, 1
        )
    )
    grad_time_pre = silu_pull(grad_time_act)[0].astype(BF16)
    d_time = left_dot(embed_cols, grad_time_pre).astype(BF16)
    low_one = grad_one.astype(BF16)
    d_skip_w = left_dot(skip_in, low_one).astype(BF16)
    d_skip_w, low_one = lax.optimization_barrier((d_skip_w, low_one))
    t_qkv, d_skip_w, joint_grad, low_join, d_time, d_shift = lax.optimization_barrier(
        (t_qkv, d_skip_w, joint_grad, low_one, d_time, d_shift)
    )
    skip_grad, grad_patch, skip_sums = join_back(low_join, f_skip, joined, joined_inv, gain_skip)
    qkv_grad = narrow(t_qkv, skip_sums)
    qkv_grad, grad_kv, grad_patch, skip_grad, skip_sums = lax.optimization_barrier(
        (qkv_grad, grad_kv, grad_patch, skip_grad, skip_sums)
    )
    out_grad, query_w_grad, cross_grad = jnp.split(joint_grad, 3, axis=1)
    t_skip = over_tiles(d_skip_w)

    group_shape = (-1, 2, grid_devices, model_width // grid_devices)
    text_slice = text_states.shape[2] // grid_devices
    text_cols = lax.dynamic_slice_in_dim(text_rows, grid_at * text_slice, text_slice, 1)
    d_text = dot_over(text_cols, grad_kv, 0, 1).astype(BF16)
    d_text = jnp.swapaxes(d_text.reshape(text_slice, grid_devices, 2, -1), 1, 2)
    d_text = d_text.reshape(text_slice, -1)
    grouped_text = jnp.swapaxes(part_text.reshape(group_shape), 1, 2).reshape(part_text.shape)
    text_grad = dot_over(grad_kv, grouped_text, 0, 1).reshape(images, text_pad, text_slice)
    text_grad = text_grad[:, :text_len]

    late, width = [], w_shift.shape[1]
    for at in range(dp_devices):
        pair = d_text[:, 2 * at * width : 2 * (at + 1) * width]
        own = slice(at * width, (at + 1) * width)
        late.append(
            jnp.concatenate([pair[:, :width], pair[:, width:], d_time[:, own], d_shift[:, own]])
        )
    late_blocks = late
    skip_grad = skip_grad.reshape(images, rows_tile, cols_tile, model_width)
    gain_skips, bias_skips = skip_sums[0], skip_sums[1]
    d_patch = left_dot(grad_patch, patch_rows)
    latent_grad = plain_dot(grad_patch, f_patch).reshape(images, rows_tile, cols_tile, patch_width)
    d_norms = jnp.stack(
        [
            gain_first,
            bias_first,
            gain_third,
            bias_third,
            gain_second,
            bias_second,
            gain_final,
            bias_final,
            gain_skips[:model_width],
            bias_skips[:model_width],
            gain_skips[model_width:],
            bias_skips[model_width:],
        ],
        axis=1,
    )
    small_grads = jnp.concatenate(
        [
            grad.reshape(model_width, dp_devices, -1)
            for grad in (d_patch, d_final, d_norms)
        ],
        axis=2,
    )
    small_grads = sum_tiles(small_grads.reshape(model_width, -1))
    late = narrow_blocks(late_blocks, small_grads)
    rows = d_text.shape[0]
    text_w_grad = jnp.concatenate([late[:rows], late[rows : 2 * rows]], axis=1)
    time_w_grad, shift_w_grad = jnp.split(late[2 * rows :], [d_time.shape[0]], axis=0)
    last, small_rows, small_width = [], small_grads.shape[0], sum(small_widths)
    for at in range(dp_devices):
        few = small_grads[:, at * small_width : (at + 1) * small_width].astype(BF16).reshape(-1)
        few = jnp.pad(few, (0, -few.shape[0] % width)).reshape(-1, width)
        last.append(jnp.concatenate([t_skip[:, at * width : (at + 1) * width], few]))
    last = narrow_blocks(last)
    skip_w_grad = last[: t_skip.shape[0]]
    small_grads = last[t_skip.shape[0] :].reshape(-1)[: small_rows * small_width]
    small_grads = small_grads.reshape(small_rows, small_width)
    patch_grad, final_grad, norms_grad = (
        small_grads[:, cuts[at] : cuts[at + 1]] for at in range(3)
    )
    return (
        prediction,
        latent_grad,
        skip_grad,
        text_grad,
        patch_grad,
        skip_w_grad,
        time_w_grad,
        shift_w_grad,
        qkv_grad,
        out_grad,
        query_w_grad,
        text_w_grad,
        cross_grad,
        up_grad,
        down_grad,
        final_grad,
        norms_grad,
    )


def local(sizes, latent, *others):
    grid_devices = sizes["row"] * sizes["col"]
    tile_len = latent.shape[1] * latent.shape[2]
    if HEADS % grid_devices == 0 and tile_len % 128 == 0:
        return local_heads(latent, *others)
    return local_gathered(latent, *others)


def solution(mesh):
    return jax.shard_map(
        functools.partial(local, mesh.shape),
        mesh=mesh,
        in_specs=(
            P("dp", "row", "col", None),
            P("dp", "row", "col", None),
            P("dp", None, None),
            P("dp"),
            P("dp"),
            P("dp", "row", "col", None),
            P(("row", "col"), "dp"),
            P(("row", "col"), "dp"),
            P(("row", "col"), "dp"),
            P(("row", "col"), "dp"),
            P(("row", "col"), "dp"),
            P(("row", "col"), "dp"),
            P(("row", "col"), "dp"),
            P(("row", "col"), "dp"),
            P(("row", "col"), "dp"),
            P(("row", "col"), "dp"),
            P(("row", "col"), "dp"),
            P(("row", "col"), "dp"),
            P(("row", "col"), "dp"),
        ),
        out_specs=(
            P("dp", "row", "col", None),
            P("dp", "row", "col", None),
            P("dp", "row", "col", None),
            P("dp", None, ("row", "col")),
            P(("row", "col"), "dp"),
            P(("row", "col"), "dp"),
            P(("row", "col"), "dp"),
            P(("row", "col"), "dp"),
            P(("row", "col"), "dp"),
            P(("row", "col"), "dp"),
            P(("row", "col"), "dp"),
            P(("row", "col"), "dp"),
            P(("row", "col"), "dp"),
            P(("row", "col"), "dp"),
            P(("row", "col"), "dp"),
            P(("row", "col"), "dp"),
            P(("row", "col"), "dp"),
        ),
        check_vma=False,
    )
```

```python
import functools
import math

import jax
import jax.numpy as jnp
from jax import lax
from jax.experimental import pallas as pl
from jax.experimental.layout import Layout, with_layout_constraint
from jax.experimental.pallas import tpu as pltpu
from jax.sharding import PartitionSpec as P

HEADS = 16
FREQ = 256


EPSILON = 1e-06


def layer_norm(values_in):
    centred = values_in - jnp.mean(values_in, axis=-1, keepdims=True)
    inverse = lax.rsqrt(jnp.mean(centred * centred, axis=-1, keepdims=True) + EPSILON)
    return (centred * inverse, inverse)


def norm_back(grad_normed, normed, inverse):
    mean_grad = jnp.mean(grad_normed, axis=-1, keepdims=True)
    mean_cross = jnp.mean(grad_normed * normed, axis=-1, keepdims=True)
    return inverse * (grad_normed - mean_grad - normed * mean_cross)


def turn_half(piece_half, cosine, sine_tab):
    quarter = cosine.shape[-1]
    lower = piece_half[..., :quarter]
    higher = piece_half[..., quarter:]
    return jnp.concatenate(
        [lower * cosine - higher * sine_tab, higher * cosine + lower * sine_tab], axis=-1
    )


def rotate(values_in, tables, signum):
    cos_row, sin_row, cos_col, sin_col = tables
    half_dim = values_in.shape[-1] // 2
    return jnp.concatenate(
        [
            turn_half(values_in[..., :half_dim], cos_row, signum * sin_row),
            turn_half(values_in[..., half_dim:], cos_col, signum * sin_col),
        ],
        axis=-1,
    )


def rope_tables(row_pos, col_pos, head_size):
    quarter = head_size // 4
    frequency = jnp.exp(jnp.arange(quarter, dtype=jnp.float32) * (-math.log(10000.0) / quarter))
    row_ang = row_pos.astype(jnp.float32)[:, None, None] * frequency
    col_ang = col_pos.astype(jnp.float32)[:, None, None] * frequency
    return (jnp.cos(row_ang), jnp.sin(row_ang), jnp.cos(col_ang), jnp.sin(col_ang))


def time_embed(step_values, freq_count):
    half_dim = freq_count // 2
    rate_list = jnp.exp(jnp.arange(half_dim, dtype=jnp.float32) * (-math.log(10000.0) / half_dim))
    angles = step_values.astype(jnp.float32)[..., None] * rate_list
    return jnp.concatenate([jnp.cos(angles), jnp.sin(angles)], axis=-1)


def gelu_tanh(inputs):
    return jax.nn.gelu(inputs, approximate=True)


def plain_dot(left_mat, right_mat):
    return jnp.dot(left_mat, right_mat, preferred_element_type=jnp.float32)


def left_dot(left_mat, right_mat):
    return lax.dot_general(
        left_mat, right_mat, (((0,), (0,)), ((), ())), preferred_element_type=jnp.float32
    )


def right_dot(left_mat, right_mat):
    return lax.dot_general(
        left_mat, right_mat, (((1,), (1,)), ((), ())), preferred_element_type=jnp.float32
    )


def block_size(key_count):
    block_len = key_count
    while block_len > 1024 and block_len % 2 == 0:
        block_len = block_len // 2
    return block_len


def local_gathered(
    latent,
    skip_input,
    text_states,
    timesteps,
    image_sides,
    cotangent,
    w_patch,
    w_skip,
    w_time,
    w_shift,
    w_qkv,
    w_out,
    w_query,
    w_text,
    w_cross,
    w_up,
    w_down,
    w_final,
    norm_params,
):
    widened = (
        lax.all_gather(w_patch, "dp", axis=1, tiled=True),
        lax.all_gather(w_skip, "dp", axis=1, tiled=True),
        lax.all_gather(w_time, "dp", axis=1, tiled=True),
        lax.all_gather(w_shift, "dp", axis=1, tiled=True),
        lax.all_gather(w_qkv, "dp", axis=1, tiled=True),
        lax.all_gather(w_out, "dp", axis=1, tiled=True),
        lax.all_gather(w_query, "dp", axis=1, tiled=True),
        lax.all_gather(w_text, "dp", axis=1, tiled=True),
        lax.all_gather(w_cross, "dp", axis=1, tiled=True),
        lax.all_gather(w_up, "dp", axis=1, tiled=True),
        lax.all_gather(w_down, "dp", axis=1, tiled=True),
        lax.all_gather(w_final, "dp", axis=1, tiled=True),
        lax.all_gather(norm_params, "dp", axis=1, tiled=True),
    )
    gathered = (
        lax.all_gather(widened[0], ("row", "col"), axis=0, tiled=True),
        lax.all_gather(widened[1], ("row", "col"), axis=0, tiled=True),
        lax.all_gather(widened[2], ("row", "col"), axis=0, tiled=True),
        lax.all_gather(widened[3], ("row", "col"), axis=0, tiled=True),
        lax.all_gather(widened[4], ("row", "col"), axis=0, tiled=True),
        lax.all_gather(widened[5], ("row", "col"), axis=0, tiled=True),
        lax.all_gather(widened[6], ("row", "col"), axis=0, tiled=True),
        lax.all_gather(widened[7], ("row", "col"), axis=0, tiled=True),
        lax.all_gather(widened[8], ("row", "col"), axis=0, tiled=True),
        lax.all_gather(widened[9], ("row", "col"), axis=0, tiled=True),
        lax.all_gather(widened[10], ("row", "col"), axis=0, tiled=True),
        lax.all_gather(widened[11], ("row", "col"), axis=0, tiled=True),
        lax.all_gather(widened[12], ("row", "col"), axis=0, tiled=True),
    )
    (
        f_patch,
        f_skip,
        f_time,
        f_shift,
        f_qkv,
        f_out,
        f_query,
        f_text,
        f_cross,
        f_up,
        f_down,
        f_final,
        f_norms,
    ) = gathered
    part_text = widened[7]
    images, rows_tile, cols_tile, patch_width = latent.shape
    tile_len = rows_tile * cols_tile
    row_count = images * tile_len
    model_width = f_qkv.shape[0]
    head_count = HEADS
    head_dim = model_width // head_count
    text_len = text_states.shape[1]
    grid_devices = lax.axis_size(("row", "col"))
    col_devices = lax.axis_size("col")
    grid_at = lax.axis_index(("row", "col"))
    row_at = lax.axis_index("row")
    col_at = lax.axis_index("col")
    score_scale = head_dim ** (-0.5)
    positions = jnp.arange(tile_len, dtype=jnp.int32)
    row_pos = row_at * rows_tile + positions // cols_tile
    col_pos = col_at * cols_tile + positions % cols_tile
    query_ok = (row_pos[None, :] < image_sides[:, None]) & (col_pos[None, :] < image_sides[:, None])
    keep_rows = query_ok.astype(jnp.float32).reshape(row_count, 1)
    tables = rope_tables(row_pos, col_pos, head_dim)
    norm_f = f_norms.astype(jnp.float32)

    def valid_keys(offset, block_len):
        index_list = offset + jnp.arange(block_len, dtype=jnp.int32)
        source = index_list // tile_len
        within = index_list % tile_len
        key_row = source // col_devices * rows_tile + within // cols_tile
        key_col = source % col_devices * cols_tile + within % cols_tile
        return (key_row[None, :] < image_sides[:, None]) & (key_col[None, :] < image_sides[:, None])

    patch_rows = latent.reshape(row_count, patch_width)
    patch_feat = right_dot(patch_rows, f_patch)
    skip_rows = skip_input.reshape(row_count, model_width).astype(jnp.float32)
    gain_skip = jnp.concatenate([norm_f[:, 8], norm_f[:, 10]])
    bias_skip = jnp.concatenate([norm_f[:, 9], norm_f[:, 11]])
    joined, joined_inv = layer_norm(jnp.concatenate([patch_feat, skip_rows], axis=-1))
    skip_in = (joined * gain_skip + bias_skip).astype(jnp.bfloat16)
    residual = plain_dot(skip_in, f_skip)
    embedding = time_embed(timesteps, FREQ).astype(jnp.bfloat16)
    time_pre = plain_dot(embedding, f_time)
    time_float, silu_pull = jax.vjp(jax.nn.silu, time_pre)
    time_act = time_float.astype(jnp.bfloat16)
    time_shift = plain_dot(time_act, f_shift)
    first_z, first_inv = layer_norm(residual)
    first_pre = (first_z * norm_f[:, 0] + norm_f[:, 1]).reshape(
        images, tile_len, model_width
    ) + time_shift[:, None, :]
    first_in = first_pre.reshape(row_count, model_width).astype(jnp.bfloat16)
    qkv = plain_dot(first_in, f_qkv)
    query_z, query_inv = layer_norm(
        qkv[:, :model_width].reshape(images, tile_len, head_count, head_dim)
    )
    key_z, key_inv = layer_norm(
        qkv[:, model_width : 2 * model_width].reshape(images, tile_len, head_count, head_dim)
    )
    queries = rotate(query_z, tables, 1.0).astype(jnp.bfloat16)
    queries_h = jnp.transpose(queries, (0, 2, 1, 3))
    keys = rotate(key_z, tables, 1.0).astype(jnp.bfloat16).reshape(images, tile_len, model_width)
    values = qkv[:, 2 * model_width :].astype(jnp.bfloat16).reshape(images, tile_len, model_width)
    start_carry = (
        jnp.full((images, head_count, tile_len), -1e30, jnp.float32),
        jnp.zeros((images, head_count, tile_len), jnp.float32),
        jnp.zeros((images, head_count, tile_len, head_dim), jnp.float32),
    )
    key_rows = lax.all_gather(keys, ("row", "col"), axis=1, tiled=True)
    value_rows = lax.all_gather(values, ("row", "col"), axis=1, tiled=True)
    key_count = key_rows.shape[1]
    block_len = block_size(key_count)

    def forward_block_step(block_index, running):
        running_max, weight_sum, accum_sum = running
        offset = block_index * block_len
        key_blk = lax.dynamic_slice_in_dim(key_rows, offset, block_len, 1).reshape(
            images, block_len, head_count, head_dim
        )
        value_blk = lax.dynamic_slice_in_dim(value_rows, offset, block_len, 1).reshape(
            images, block_len, head_count, head_dim
        )
        key_ok = valid_keys(offset, block_len)
        scores = (
            jnp.einsum("ihqe,ikhe->ihqk", queries_h, key_blk, preferred_element_type=jnp.float32)
            * score_scale
        )
        scores = jnp.where(key_ok[:, None, None, :], scores, -jnp.inf)
        new_max = jnp.maximum(running_max, jnp.max(scores, axis=-1))
        weight = jnp.exp(scores - new_max[..., None])
        rescale = jnp.exp(running_max - new_max)
        weight_sum = weight_sum * rescale + jnp.sum(weight, axis=-1)
        accum_sum = accum_sum * rescale[..., None] + jnp.einsum(
            "ihqk,ikhe->ihqe",
            weight.astype(jnp.bfloat16),
            value_blk,
            preferred_element_type=jnp.float32,
        )
        return (new_max, weight_sum, accum_sum)

    running_max, weight_sum, accum_sum = lax.fori_loop(
        0, key_count // block_len, forward_block_step, start_carry
    )
    attended = accum_sum / weight_sum[..., None]
    log_sum = running_max + jnp.log(weight_sum)
    att_low = (
        jnp.transpose(attended, (0, 2, 1, 3)).reshape(row_count, model_width).astype(jnp.bfloat16)
    )
    residual_two = residual + plain_dot(att_low, f_out)
    third_z, third_inv = layer_norm(residual_two)
    third_in = (third_z * norm_f[:, 2] + norm_f[:, 3]).astype(jnp.bfloat16)
    cross_pre = plain_dot(third_in, f_query)
    cq_z, cq_inv = layer_norm(cross_pre.reshape(images, tile_len, head_count, head_dim))
    cross_queries = cq_z.astype(jnp.bfloat16)
    text_kv = jnp.einsum("itc,cd->itd", text_states, f_text, preferred_element_type=jnp.float32)
    ck_z, ck_inv = layer_norm(
        text_kv[..., :model_width].reshape(images, text_len, head_count, head_dim)
    )
    cross_keys = ck_z.astype(jnp.bfloat16)
    cross_values = (
        text_kv[..., model_width:]
        .astype(jnp.bfloat16)
        .reshape(images, text_len, head_count, head_dim)
    )

    def cross_softmax():
        scores = (
            jnp.einsum(
                "iqhe,ikhe->ihqk", cross_queries, cross_keys, preferred_element_type=jnp.float32
            )
            * score_scale
        )
        return jax.nn.softmax(scores, axis=-1)

    crossed = jnp.einsum(
        "ihqk,ikhe->iqhe",
        cross_softmax().astype(jnp.bfloat16),
        cross_values,
        preferred_element_type=jnp.float32,
    )
    cross_low = crossed.reshape(row_count, model_width).astype(jnp.bfloat16)
    residual_three = residual_two + plain_dot(cross_low, f_cross)
    second_z, second_inv = layer_norm(residual_three)
    second_in = (second_z * norm_f[:, 4] + norm_f[:, 5]).astype(jnp.bfloat16)
    up_pre = plain_dot(second_in, f_up)
    hidden_float, gelu_pull = jax.vjp(gelu_tanh, up_pre)
    hidden_act = hidden_float.astype(jnp.bfloat16)
    residual_four = residual_three + plain_dot(hidden_act, f_down)
    last_z, last_inv = layer_norm(residual_four)
    last_in = (last_z * norm_f[:, 6] + norm_f[:, 7]).astype(jnp.bfloat16)
    produced = plain_dot(last_in, f_final)
    prediction = (
        (produced * keep_rows)
        .astype(jnp.bfloat16)
        .reshape(images, rows_tile, cols_tile, produced.shape[1])
    )
    grad_out = (
        cotangent.reshape(row_count, produced.shape[1]).astype(jnp.float32) * keep_rows
    ).astype(jnp.bfloat16)
    d_final = left_dot(last_in, grad_out)
    grad_last = right_dot(grad_out, f_final)
    gain_final = jnp.sum(grad_last * last_z, axis=0)
    bias_final = jnp.sum(grad_last, axis=0)
    grad_four = norm_back(grad_last * norm_f[:, 6], last_z, last_inv)
    low_four = grad_four.astype(jnp.bfloat16)
    d_down = left_dot(hidden_act, low_four)
    grad_hidden = right_dot(low_four, f_down)
    grad_up = gelu_pull(grad_hidden)[0].astype(jnp.bfloat16)
    d_up = left_dot(second_in, grad_up)
    grad_second = right_dot(grad_up, f_up)
    gain_second = jnp.sum(grad_second * second_z, axis=0)
    bias_second = jnp.sum(grad_second, axis=0)
    grad_three = grad_four + norm_back(grad_second * norm_f[:, 4], second_z, second_inv)
    low_three = grad_three.astype(jnp.bfloat16)
    d_cross = left_dot(cross_low, low_three)
    grad_crossed = (
        right_dot(low_three, f_cross)
        .astype(jnp.bfloat16)
        .reshape(images, tile_len, head_count, head_dim)
    )
    cross_probs = cross_softmax()
    cross_delta = jnp.transpose(
        jnp.sum(grad_crossed.astype(jnp.float32) * crossed, axis=-1), (0, 2, 1)
    )
    grad_probs = jnp.einsum(
        "iqhe,ikhe->ihqk", grad_crossed, cross_values, preferred_element_type=jnp.float32
    )
    grad_cscore = (cross_probs * (grad_probs - cross_delta[..., None])).astype(jnp.bfloat16)
    grad_cq = score_scale * jnp.einsum(
        "ihqk,ikhe->iqhe", grad_cscore, cross_keys, preferred_element_type=jnp.float32
    )
    part_ckey = score_scale * jnp.einsum(
        "ihqk,iqhe->ikhe", grad_cscore, cross_queries, preferred_element_type=jnp.float32
    )
    part_cvalue = jnp.einsum(
        "ihqk,iqhe->ikhe",
        cross_probs.astype(jnp.bfloat16),
        grad_crossed,
        preferred_element_type=jnp.float32,
    )
    grad_cross_q = (
        norm_back(grad_cq, cq_z, cq_inv).reshape(row_count, model_width).astype(jnp.bfloat16)
    )
    d_query = left_dot(third_in, grad_cross_q)
    grad_third = right_dot(grad_cross_q, f_query)
    gain_third = jnp.sum(grad_third * third_z, axis=0)
    bias_third = jnp.sum(grad_third, axis=0)
    grad_two = grad_three + norm_back(grad_third * norm_f[:, 2], third_z, third_inv)
    sum_ckey, sum_cvalue = lax.psum((part_ckey, part_cvalue), ("row", "col"))
    low_two = grad_two.astype(jnp.bfloat16)
    d_out = left_dot(att_low, low_two)
    grad_att = (
        right_dot(low_two, f_out)
        .astype(jnp.bfloat16)
        .reshape(images, tile_len, head_count, head_dim)
    )
    grad_att_h = jnp.transpose(grad_att, (0, 2, 1, 3))
    delta_rows = jnp.sum(grad_att_h.astype(jnp.float32) * attended, axis=-1)
    back_carry = (
        jnp.zeros((images, head_count, tile_len, head_dim), jnp.float32),
        jnp.zeros((images, tile_len * grid_devices, model_width), jnp.float32),
        jnp.zeros((images, tile_len * grid_devices, model_width), jnp.float32),
    )
    backward_key_rows = lax.all_gather(keys, ("row", "col"), axis=1, tiled=True)
    backward_value_rows = lax.all_gather(values, ("row", "col"), axis=1, tiled=True)
    key_count = backward_key_rows.shape[1]
    backward_block_len = block_size(key_count)

    def backward_block_step(block_index, running):
        grad_query, grad_key_all, grad_value_all = running
        offset = block_index * backward_block_len
        key_blk = lax.dynamic_slice_in_dim(
            backward_key_rows, offset, backward_block_len, 1
        ).reshape(images, backward_block_len, head_count, head_dim)
        value_blk = lax.dynamic_slice_in_dim(
            backward_value_rows, offset, backward_block_len, 1
        ).reshape(images, backward_block_len, head_count, head_dim)
        key_ok = valid_keys(offset, backward_block_len)
        scores = (
            jnp.einsum("ihqe,ikhe->ihqk", queries_h, key_blk, preferred_element_type=jnp.float32)
            * score_scale
        )
        scores = jnp.where(key_ok[:, None, None, :], scores, -jnp.inf)
        attn_probs = jnp.exp(scores - log_sum[..., None])
        grad_prob = jnp.einsum(
            "ihqe,ikhe->ihqk", grad_att_h, value_blk, preferred_element_type=jnp.float32
        )
        grad_score = (attn_probs * (grad_prob - delta_rows[..., None])).astype(jnp.bfloat16)
        grad_query = grad_query + score_scale * jnp.einsum(
            "ihqk,ikhe->ihqe", grad_score, key_blk, preferred_element_type=jnp.float32
        )
        key_part = score_scale * jnp.einsum(
            "ihqk,ihqe->ikhe", grad_score, queries_h, preferred_element_type=jnp.float32
        )
        value_part = jnp.einsum(
            "ihqk,ihqe->ikhe",
            attn_probs.astype(jnp.bfloat16),
            grad_att_h,
            preferred_element_type=jnp.float32,
        )
        grad_key_all = lax.dynamic_update_slice_in_dim(
            grad_key_all, key_part.reshape(images, backward_block_len, model_width), offset, 1
        )
        grad_value_all = lax.dynamic_update_slice_in_dim(
            grad_value_all, value_part.reshape(images, backward_block_len, model_width), offset, 1
        )
        return (grad_query, grad_key_all, grad_value_all)

    grad_query, grad_key_all, grad_value_all = lax.fori_loop(
        0, key_count // backward_block_len, backward_block_step, back_carry
    )
    grad_key_own, grad_value_own = (
        lax.psum_scatter(grad_key_all, ("row", "col"), scatter_dimension=1, tiled=True),
        lax.psum_scatter(grad_value_all, ("row", "col"), scatter_dimension=1, tiled=True),
    )
    grad_qn = rotate(jnp.transpose(grad_query, (0, 2, 1, 3)), tables, -1.0)
    grad_kn = rotate(grad_key_own.reshape(images, tile_len, head_count, head_dim), tables, -1.0)
    grad_qkv = jnp.concatenate(
        [
            norm_back(grad_qn, query_z, query_inv).reshape(row_count, model_width),
            norm_back(grad_kn, key_z, key_inv).reshape(row_count, model_width),
            grad_value_own.reshape(row_count, model_width),
        ],
        axis=-1,
    ).astype(jnp.bfloat16)
    d_qkv = left_dot(first_in, grad_qkv)
    grad_first = right_dot(grad_qkv, f_qkv)
    gain_first = jnp.sum(grad_first * first_z, axis=0)
    bias_first = jnp.sum(grad_first, axis=0)
    part_shift = jnp.sum(grad_first.reshape(images, tile_len, model_width), axis=1)
    grad_one = grad_two + norm_back(grad_first * norm_f[:, 0], first_z, first_inv)
    shift_grad = lax.psum(part_shift, ("row", "col"))
    grad_ckey = norm_back(sum_ckey, ck_z, ck_inv).reshape(images, text_len, model_width)
    grad_kv = jnp.concatenate(
        [grad_ckey, sum_cvalue.reshape(images, text_len, model_width)], axis=-1
    ).astype(jnp.bfloat16)
    text_slice = text_states.shape[2] // grid_devices
    text_cols = lax.dynamic_slice_in_dim(text_states, grid_at * text_slice, text_slice, 2)
    d_text_w = jnp.einsum("itc,itd->cd", text_cols, grad_kv, preferred_element_type=jnp.float32)
    text_grad = jnp.einsum("itd,cd->itc", grad_kv, part_text, preferred_element_type=jnp.float32)
    shift_low = shift_grad.astype(jnp.bfloat16)
    shift_slice = model_width // grid_devices
    act_cols = lax.dynamic_slice_in_dim(time_act, grid_at * shift_slice, shift_slice, 1)
    d_shift_w = jnp.einsum("ic,id->cd", act_cols, shift_low, preferred_element_type=jnp.float32)
    grad_time_act = right_dot(shift_low, f_shift)
    grad_time_pre = silu_pull(grad_time_act)[0].astype(jnp.bfloat16)
    freq_slice = embedding.shape[1] // grid_devices
    embed_cols = lax.dynamic_slice_in_dim(embedding, grid_at * freq_slice, freq_slice, 1)
    d_time_w = jnp.einsum(
        "ic,id->cd", embed_cols, grad_time_pre, preferred_element_type=jnp.float32
    )
    low_one = grad_one.astype(jnp.bfloat16)
    d_skip_w = left_dot(skip_in, low_one)
    grad_skip_in = right_dot(low_one, f_skip)
    gain_skips = jnp.sum(grad_skip_in * joined, axis=0)
    bias_skips = jnp.sum(grad_skip_in, axis=0)
    grad_joined = norm_back(grad_skip_in * gain_skip, joined, joined_inv)
    skip_grad = grad_joined[:, model_width:].reshape(images, rows_tile, cols_tile, model_width)
    grad_patch = grad_joined[:, :model_width].astype(jnp.bfloat16)
    d_patch = left_dot(grad_patch, patch_rows)
    latent_grad = plain_dot(grad_patch, f_patch).reshape(images, rows_tile, cols_tile, patch_width)
    d_norms = jnp.stack(
        [
            gain_first,
            bias_first,
            gain_third,
            bias_third,
            gain_second,
            bias_second,
            gain_final,
            bias_final,
            gain_skips[:model_width],
            bias_skips[:model_width],
            gain_skips[model_width:],
            bias_skips[model_width:],
        ],
        axis=1,
    )
    tile_done = (
        lax.psum_scatter(d_patch, ("row", "col"), scatter_dimension=0, tiled=True),
        lax.psum_scatter(d_skip_w, ("row", "col"), scatter_dimension=0, tiled=True),
        lax.psum_scatter(d_qkv, ("row", "col"), scatter_dimension=0, tiled=True),
        lax.psum_scatter(d_out, ("row", "col"), scatter_dimension=0, tiled=True),
        lax.psum_scatter(d_query, ("row", "col"), scatter_dimension=0, tiled=True),
        lax.psum_scatter(d_cross, ("row", "col"), scatter_dimension=0, tiled=True),
        lax.psum_scatter(d_up, ("row", "col"), scatter_dimension=0, tiled=True),
        lax.psum_scatter(d_down, ("row", "col"), scatter_dimension=0, tiled=True),
        lax.psum_scatter(d_final, ("row", "col"), scatter_dimension=0, tiled=True),
        lax.psum_scatter(d_norms, ("row", "col"), scatter_dimension=0, tiled=True),
    )
    reduced = (
        lax.psum_scatter(
            tile_done[0].astype(jnp.bfloat16), "dp", scatter_dimension=1, tiled=True
        ).astype(jnp.float32),
        lax.psum_scatter(
            tile_done[1].astype(jnp.bfloat16), "dp", scatter_dimension=1, tiled=True
        ).astype(jnp.float32),
        lax.psum_scatter(
            tile_done[2].astype(jnp.bfloat16), "dp", scatter_dimension=1, tiled=True
        ).astype(jnp.float32),
        lax.psum_scatter(
            tile_done[3].astype(jnp.bfloat16), "dp", scatter_dimension=1, tiled=True
        ).astype(jnp.float32),
        lax.psum_scatter(
            tile_done[4].astype(jnp.bfloat16), "dp", scatter_dimension=1, tiled=True
        ).astype(jnp.float32),
        lax.psum_scatter(
            tile_done[5].astype(jnp.bfloat16), "dp", scatter_dimension=1, tiled=True
        ).astype(jnp.float32),
        lax.psum_scatter(
            tile_done[6].astype(jnp.bfloat16), "dp", scatter_dimension=1, tiled=True
        ).astype(jnp.float32),
        lax.psum_scatter(
            tile_done[7].astype(jnp.bfloat16), "dp", scatter_dimension=1, tiled=True
        ).astype(jnp.float32),
        lax.psum_scatter(
            tile_done[8].astype(jnp.bfloat16), "dp", scatter_dimension=1, tiled=True
        ).astype(jnp.float32),
        lax.psum_scatter(
            tile_done[9].astype(jnp.bfloat16), "dp", scatter_dimension=1, tiled=True
        ).astype(jnp.float32),
        lax.psum_scatter(
            d_time_w.astype(jnp.bfloat16), "dp", scatter_dimension=1, tiled=True
        ).astype(jnp.float32),
        lax.psum_scatter(
            d_shift_w.astype(jnp.bfloat16), "dp", scatter_dimension=1, tiled=True
        ).astype(jnp.float32),
        lax.psum_scatter(
            d_text_w.astype(jnp.bfloat16), "dp", scatter_dimension=1, tiled=True
        ).astype(jnp.float32),
    )
    return (
        prediction,
        latent_grad,
        skip_grad,
        text_grad,
        reduced[0],
        reduced[1],
        reduced[10],
        reduced[11],
        reduced[2],
        reduced[3],
        reduced[4],
        reduced[12],
        reduced[5],
        reduced[6],
        reduced[7],
        reduced[8],
        reduced[9],
    )


TILE = ("row", "col")
EVERY = ("dp", "row", "col")
LOG2E = math.log2(math.e)
F32 = jnp.float32
BF16 = jnp.bfloat16
VMEM_BYTES = 56 * 2**20


def kernel_call(body, flops, moved, **options):
    return pl.pallas_call(
        body,
        compiler_params=pltpu.CompilerParams(vmem_limit_bytes=VMEM_BYTES),
        cost_estimate=pl.CostEstimate(flops=flops, bytes_accessed=moved, transcendentals=0),
        **options,
    )


def pair_swap(values_in):
    quarter = values_in.shape[0] // 4
    parts = [values_in[at * quarter : (at + 1) * quarter] for at in (1, 0, 3, 2)]
    return jnp.concatenate(parts, axis=0)


def column_norm(values_in):
    centred = values_in - jnp.mean(values_in, axis=0, keepdims=True)
    inverse = lax.rsqrt(jnp.mean(centred * centred, axis=0, keepdims=True) + EPSILON)
    return (centred * inverse, inverse)


def column_norm_back(grad_normed, normed, inverse):
    mean_grad = jnp.mean(grad_normed, axis=0, keepdims=True)
    mean_cross = jnp.mean(grad_normed * normed, axis=0, keepdims=True)
    return inverse * (grad_normed - mean_grad - normed * mean_cross)


def minus_pieces(row_values):
    high = row_values.astype(BF16).astype(F32)
    rest = row_values - high
    middle = rest.astype(BF16).astype(F32)
    lower = rest - middle
    at = lax.broadcasted_iota(jnp.int32, (8, row_values.shape[1]), 0)
    zero = jnp.zeros((8, row_values.shape[1]), F32)
    picked = jnp.where(at == 0, high, jnp.where(at == 1, middle, jnp.where(at == 2, lower, zero)))
    return -picked


def piece_flags(width):
    return (lax.broadcasted_iota(jnp.int32, (8, width), 0) < 3).astype(F32)


def head_norm_body(
    query_scale, rows_ref, weight_ref, cos_ref, sin_ref, ok_ref, out_ref, inv_ref
):
    groups, _, heads, head_dim, _ = out_ref.shape
    part = pl.program_id(0)
    made = jnp.dot(rows_ref[...], weight_ref[...], preferred_element_type=F32).T
    valid = ok_ref[...]

    @pl.when(part < 2)
    def _():
        factor = jnp.where(part == 0, query_scale, valid)
        cosine, sine = cos_ref[...] * factor, sin_ref[...] * factor
        for group in range(groups):
            for head in range(heads):
                at = (group * heads + head) * head_dim
                normed, inverse = column_norm(made[at : at + head_dim])
                turned = normed * cosine + pair_swap(normed) * sine
                out_ref[group, 0, head] = turned.astype(BF16)
                inv_ref[group, 0, head : head + 1] = inverse

    @pl.when(part == 2)
    def _():
        for group in range(groups):
            for head in range(heads):
                at = (group * heads + head) * head_dim
                out_ref[group, 0, head] = (made[at : at + head_dim] * valid).astype(BF16)
                inv_ref[group, 0, head : head + 1] = valid


def head_norm(rows, weight, tables, valid, groups, head_dim, query_scale):
    tile_len, depth = rows.shape
    width = weight.shape[1] // 3
    heads = width // groups // head_dim
    table = pl.BlockSpec((head_dim, tile_len), lambda p: (0, 0))
    return kernel_call(
        functools.partial(head_norm_body, query_scale),
        6 * tile_len * depth * width,
        6 * depth * width,
        grid=(3,),
        in_specs=[
            pl.BlockSpec((tile_len, depth), lambda p: (0, 0)),
            pl.BlockSpec((depth, width), lambda p: (0, p)),
            table,
            table,
            pl.BlockSpec((1, tile_len), lambda p: (0, 0)),
        ],
        out_specs=[
            pl.BlockSpec((groups, 1, heads, head_dim, tile_len), lambda p: (0, p, 0, 0, 0)),
            pl.BlockSpec((groups, 1, heads, tile_len), lambda p: (0, p, 0, 0)),
        ],
        out_shape=[
            jax.ShapeDtypeStruct((groups, 3, heads, head_dim, tile_len), BF16),
            jax.ShapeDtypeStruct((groups, 3, heads, tile_len), F32),
        ],
    )(rows, weight, *tables, valid)


def head_back_body(
    query_scale, grad_ref, own_ref, inv_ref, cos_ref, sin_ref, ok_ref, *others
):
    out_ref = others[-1]
    heads, head_dim = own_ref.shape[2], own_ref.shape[3]
    cosine, sine, valid = cos_ref[...], sin_ref[...], ok_ref[...]

    def unturn(values_in):
        return values_in * cosine - pair_swap(values_in) * sine

    for part in range(3):
        pieces = []
        for head in range(heads):
            grad = grad_ref[0, part, head].astype(F32)
            if part > 0:
                grad = grad * valid
            if part < 2:
                normed = unturn(own_ref[0, part, head].astype(F32))
                if part == 0:
                    normed = normed * (1.0 / query_scale)
                inverse = inv_ref[0, part, head : head + 1]
                grad = column_norm_back(unturn(grad), normed, inverse)
            pieces.append(grad)
        out_ref[part, 0] = jnp.concatenate(pieces, axis=0).astype(BF16)


def head_back(grads, own, inverses, tables, valid, query_scale, image, images, before):
    groups, _, heads, head_dim, tile_len = own.shape
    group_rows = heads * head_dim
    stacked = pl.BlockSpec((1, 3, heads, head_dim, tile_len), lambda g: (g, 0, 0, 0, 0))
    table = pl.BlockSpec((head_dim, tile_len), lambda g: (0, 0))
    earlier = () if before is None else (before,)
    return kernel_call(
        functools.partial(head_back_body, query_scale),
        0,
        6 * own.size,
        grid=(groups,),
        in_specs=[
            stacked,
            stacked,
            pl.BlockSpec((1, 3, heads, tile_len), lambda g: (g, 0, 0, 0)),
            table,
            table,
            pl.BlockSpec((1, tile_len), lambda g: (0, 0)),
        ]
        + [pl.BlockSpec(memory_space=pl.ANY)] * len(earlier),
        out_specs=pl.BlockSpec((3, 1, group_rows, tile_len), lambda g: (0, g, 0, image)),
        out_shape=jax.ShapeDtypeStruct((3, groups, group_rows, images * tile_len), BF16),
        input_output_aliases={6: 0} if earlier else {},
    )(grads, own, inverses, *tables, valid, *earlier)


def attend_body(query_ref, key_ref, value_ref, ok_ref, out_ref, lse_ref, key_nat, value_ext):
    tiles, tile_len, head_dim = key_ref.shape[0], key_ref.shape[-1], key_ref.shape[-2]

    @pl.when(pl.program_id(1) == 0)
    def _():
        for tile in range(tiles):
            key_nat[tile * tile_len : (tile + 1) * tile_len, :] = key_ref[tile, 0, 0].T
            value_ext[tile] = jnp.concatenate(
                [value_ref[tile, 0, 0].astype(F32), ok_ref[tile]], axis=0
            ).astype(BF16)

    query = query_ref[0, 0, 0]
    total = jnp.zeros((head_dim + 8, tile_len), F32)
    held = None
    for tile in range(tiles + 1):
        scores = None
        if tile < tiles:
            rows = slice(tile * tile_len, (tile + 1) * tile_len)
            scores = jnp.dot(key_nat[rows, :], query, preferred_element_type=F32)
        if held is not None:
            weight = jnp.exp2(held).astype(BF16)
            total = total + jnp.dot(value_ext[tile - 1], weight, preferred_element_type=F32)
        held = scores
    weight_sum = total[head_dim : head_dim + 1]
    out_ref[0, 0] = (total[:head_dim] / weight_sum).astype(BF16)
    lse_ref[0, 0] = jnp.log2(weight_sum)


def attend(qkv, flags):
    tiles, _, heads, head_dim, tile_len = qkv.shape
    return kernel_call(
        attend_body,
        1024 * heads * tiles**2 * tile_len**2,
        8 * qkv.size,
        grid=(heads, tiles),
        in_specs=[
            pl.BlockSpec((1, 1, 1, head_dim, tile_len), lambda h, t: (t, 0, h, 0, 0)),
            pl.BlockSpec((tiles, 1, 1, head_dim, tile_len), lambda h, t: (0, 1, h, 0, 0)),
            pl.BlockSpec((tiles, 1, 1, head_dim, tile_len), lambda h, t: (0, 2, h, 0, 0)),
            pl.BlockSpec((tiles, 8, tile_len), lambda h, t: (0, 0, 0)),
        ],
        out_specs=[
            pl.BlockSpec((1, 1, head_dim, tile_len), lambda h, t: (t, h, 0, 0)),
            pl.BlockSpec((1, 1, 1, tile_len), lambda h, t: (t, h, 0, 0)),
        ],
        out_shape=[
            jax.ShapeDtypeStruct((tiles, heads, head_dim, tile_len), BF16),
            jax.ShapeDtypeStruct((tiles, heads, 1, tile_len), F32),
        ],
        scratch_shapes=[
            pltpu.VMEM((tiles * tile_len, head_dim), BF16),
            pltpu.VMEM((tiles, head_dim + 8, tile_len), BF16),
        ],
    )(qkv, qkv, qkv, flags)


def attend_back_body(
    score_scale,
    query_ref,
    key_ref,
    value_ref,
    grad_ref,
    att_ref,
    lse_ref,
    out_ref,
    key_nat,
    value_nat,
    key_sum,
    value_sum,
):
    tiles, tile_len, head_dim = key_ref.shape[0], key_ref.shape[-1], key_ref.shape[-2]
    at = pl.program_id(1)

    @pl.when(at == 0)
    def _():
        ones = piece_flags(tile_len)
        for tile in range(tiles):
            rows = slice(tile * tile_len, (tile + 1) * tile_len)
            for source, kept in ((key_ref, key_nat), (value_ref, value_nat)):
                wide = jnp.concatenate([source[tile, 0, 0].astype(F32), ones], axis=0)
                kept[rows, :] = wide.T.astype(BF16)
        key_sum[...] = jnp.zeros_like(key_sum)
        value_sum[...] = jnp.zeros_like(value_sum)

    query = query_ref[0, 0, 0].astype(F32)
    grad = grad_ref[0, 0].astype(F32)
    delta = jnp.sum(grad * att_ref[0, 0].astype(F32), axis=0, keepdims=True)
    query_ext = jnp.concatenate([query, minus_pieces(lse_ref[0, 0])], axis=0)
    grad_ext = jnp.concatenate([grad, minus_pieces(delta)], axis=0)
    query_cols, grad_cols = query_ext.astype(BF16), grad_ext.astype(BF16)
    query_nat, grad_nat = query_ext.T.astype(BF16), grad_ext.T.astype(BF16)

    def step(tile, total):
        rows = pl.ds(pl.multiple_of(tile * tile_len, tile_len), tile_len)
        scores = jnp.dot(key_nat[rows, :], query_cols, preferred_element_type=F32)
        probs = jnp.exp2(scores)
        grad_probs = jnp.dot(value_nat[rows, :], grad_cols, preferred_element_type=F32)
        grad_scores = (probs * grad_probs).astype(BF16)
        value_sum[rows, :] += jnp.dot(probs.astype(BF16), grad_nat, preferred_element_type=F32)
        key_sum[rows, :] += jnp.dot(grad_scores, query_nat, preferred_element_type=F32)
        return total + jnp.dot(key_ref[tile, 0, 0], grad_scores, preferred_element_type=F32)

    start = jnp.zeros((head_dim, tile_len), F32)
    total = lax.fori_loop(0, tiles, step, start, unroll=8)
    out_ref[at, 0, 0] = (total * score_scale).astype(BF16)

    @pl.when(at == tiles - 1)
    def _():
        for tile in range(tiles):
            rows = slice(tile * tile_len, (tile + 1) * tile_len)
            key_grad = key_sum[rows, :].T[:head_dim] * (1.0 / LOG2E)
            out_ref[tile, 1, 0] = key_grad.astype(BF16)
            out_ref[tile, 2, 0] = value_sum[rows, :].T[:head_dim].astype(BF16)


def attend_back(qkv, grad_att, att, lse, score_scale):
    tiles, _, heads, head_dim, tile_len = qkv.shape
    one = pl.BlockSpec((1, 1, head_dim, tile_len), lambda h, t: (t, h, 0, 0))
    return kernel_call(
        functools.partial(attend_back_body, score_scale),
        2560 * heads * tiles**2 * tile_len**2,
        8 * qkv.size,
        grid=(heads, tiles),
        in_specs=[
            pl.BlockSpec((1, 1, 1, head_dim, tile_len), lambda h, t: (t, 0, h, 0, 0)),
            pl.BlockSpec((tiles, 1, 1, head_dim, tile_len), lambda h, t: (0, 1, h, 0, 0)),
            pl.BlockSpec((tiles, 1, 1, head_dim, tile_len), lambda h, t: (0, 2, h, 0, 0)),
            one,
            one,
            pl.BlockSpec((1, 1, 1, tile_len), lambda h, t: (t, h, 0, 0)),
        ],
        out_specs=pl.BlockSpec(
            (tiles, 3, 1, head_dim, tile_len), lambda h, t: (0, 0, h, 0, 0)
        ),
        out_shape=jax.ShapeDtypeStruct(qkv.shape, BF16),
        scratch_shapes=[
            pltpu.VMEM((tiles * tile_len, head_dim + 8), BF16),
            pltpu.VMEM((tiles * tile_len, head_dim + 8), BF16),
            pltpu.VMEM((tiles * tile_len, head_dim + 8), F32),
            pltpu.VMEM((tiles * tile_len, head_dim + 8), F32),
        ],
    )(qkv, qkv, qkv, grad_att, att, lse)


def cross_body(text_len, query_scale, pre_ref, kv_ref, att_ref, query_ref, inv_ref, lse_ref):
    head_dim, text_pad = kv_ref.shape[2], kv_ref.shape[3]
    at = lax.broadcasted_iota(jnp.int32, (8, text_pad), 0)
    text_at = lax.broadcasted_iota(jnp.int32, (8, text_pad), 1)
    flags = ((at == 0) & (text_at < text_len)).astype(F32)
    for head in range(pre_ref.shape[0]):
        normed, inverse = column_norm(pre_ref[head])
        query = (normed * query_scale).astype(BF16)
        query_ref[head] = query
        inv_ref[head] = inverse
        key = column_norm(kv_ref[0, head])[0].astype(BF16)
        value_ext = jnp.concatenate([kv_ref[1, head], flags], axis=0).astype(BF16)
        scores = jnp.dot(key.T, query, preferred_element_type=F32)
        weight = jnp.exp2(scores).astype(BF16)
        total = jnp.dot(value_ext, weight, preferred_element_type=F32)
        weight_sum = total[head_dim : head_dim + 1]
        att_ref[head] = (total[:head_dim] / weight_sum).astype(BF16)
        lse_ref[head] = jnp.log2(weight_sum)


def cross_attend(pre, text_kv, images, text_len, query_scale):
    heads, head_dim, tokens = pre.shape
    tile_len, text_pad = tokens // images, text_kv.shape[3] // images
    block = math.gcd(heads, 4)
    wide = pl.BlockSpec((block, head_dim, tile_len), lambda i, h: (h, 0, i))
    row = pl.BlockSpec((block, 1, tile_len), lambda i, h: (h, 0, i))
    return kernel_call(
        functools.partial(cross_body, text_len, query_scale),
        1024 * heads * tokens * text_pad,
        8 * pre.size,
        grid=(images, heads // block),
        in_specs=[wide, pl.BlockSpec((2, block, head_dim, text_pad), lambda i, h: (0, h, 0, i))],
        out_specs=[wide, wide, row, row],
        out_shape=[
            jax.ShapeDtypeStruct(pre.shape, BF16),
            jax.ShapeDtypeStruct(pre.shape, BF16),
            jax.ShapeDtypeStruct((heads, 1, tokens), F32),
            jax.ShapeDtypeStruct((heads, 1, tokens), F32),
        ],
    )(pre, text_kv)


def cross_back_body(
    query_scale,
    score_scale,
    query_ref,
    kv_ref,
    grad_ref,
    att_ref,
    inv_ref,
    lse_ref,
    out_ref,
    key_ref,
    value_ref,
):
    head_dim, text_pad = kv_ref.shape[2], kv_ref.shape[3]
    ones = piece_flags(text_pad)
    for head in range(query_ref.shape[0]):
        query = query_ref[head].astype(F32)
        grad = grad_ref[head].astype(F32)
        delta = jnp.sum(grad * att_ref[head].astype(F32), axis=0, keepdims=True)
        query_ext = jnp.concatenate([query, minus_pieces(lse_ref[head])], axis=0).astype(BF16)
        grad_ext = jnp.concatenate([grad, minus_pieces(delta)], axis=0).astype(BF16)
        key = column_norm(kv_ref[0, head])[0].astype(BF16)
        key_ext = jnp.concatenate([key.astype(F32), ones], axis=0).T.astype(BF16)
        value_ext = jnp.concatenate([kv_ref[1, head], ones], axis=0).T.astype(BF16)
        probs = jnp.exp2(jnp.dot(key_ext, query_ext, preferred_element_type=F32))
        grad_probs = jnp.dot(value_ext, grad_ext, preferred_element_type=F32)
        grad_scores = (probs * grad_probs).astype(BF16)
        value_grad = right_dot(grad_ext, probs.astype(BF16))[:head_dim]
        key_grad = right_dot(query_ext, grad_scores)[:head_dim]
        key_ref[head] = (key_grad * (1.0 / LOG2E)).astype(BF16)
        value_ref[head] = value_grad.astype(BF16)
        query_grad = jnp.dot(key, grad_scores, preferred_element_type=F32) * score_scale
        normed = query * (1.0 / query_scale)
        out_ref[head] = column_norm_back(query_grad, normed, inv_ref[head]).astype(BF16)


def cross_back(query, text_kv, grad, att, inverse, lse, images, query_scale, score_scale):
    heads, head_dim, tokens = query.shape
    tile_len, text_pad = tokens // images, text_kv.shape[3] // images
    block = math.gcd(heads, 4)
    wide = pl.BlockSpec((block, head_dim, tile_len), lambda i, h: (h, 0, i))
    row = pl.BlockSpec((block, 1, tile_len), lambda i, h: (h, 0, i))
    text = pl.BlockSpec((2, block, head_dim, text_pad), lambda i, h: (0, h, 0, i))
    text_out = pl.BlockSpec((block, head_dim, text_pad), lambda i, h: (h, 0, i))
    return kernel_call(
        functools.partial(cross_back_body, query_scale, score_scale),
        2560 * heads * tokens * text_pad,
        16 * query.size,
        grid=(images, heads // block),
        in_specs=[wide, text, wide, wide, row, row],
        out_specs=[
            wide,
            text_out,
            text_out,
        ],
        out_shape=[
            jax.ShapeDtypeStruct(query.shape, BF16),
            jax.ShapeDtypeStruct((heads, head_dim, images * text_pad), BF16),
            jax.ShapeDtypeStruct((heads, head_dim, images * text_pad), BF16),
        ],
    )(query, text_kv, grad, att, inverse, lse)


def join_norm_body(patch_ref, skip_ref, weight_ref, gain_ref, bias_ref, z_ref, inv_ref, in_ref):
    width = skip_ref.shape[1]
    patch_feat = right_dot(patch_ref[...], weight_ref[...])
    joined = jnp.concatenate([patch_feat, skip_ref[...].astype(F32)], axis=1)
    normed, inverse = layer_norm(joined)
    z_ref[...] = normed
    inv_ref[...] = inverse
    in_ref[...] = (normed * gain_ref[...] + bias_ref[...]).astype(BF16)


def join_norm(patch_rows, skip_rows, f_patch, gain, bias):
    tokens, width = skip_rows.shape
    block = math.gcd(tokens, 256)
    rows = lambda columns: pl.BlockSpec((block, columns), lambda t: (t, 0))
    fixed = lambda shape: pl.BlockSpec(shape, lambda t: (0, 0))
    return kernel_call(
        join_norm_body,
        64 * tokens * width,
        16 * tokens * width,
        grid=(tokens // block,),
        in_specs=[
            rows(patch_rows.shape[1]),
            rows(width),
            fixed(f_patch.shape),
            fixed(gain.shape),
            fixed(bias.shape),
        ],
        out_specs=[rows(2 * width), rows(1), rows(2 * width)],
        out_shape=[
            jax.ShapeDtypeStruct((tokens, 2 * width), F32),
            jax.ShapeDtypeStruct((tokens, 1), F32),
            jax.ShapeDtypeStruct((tokens, 2 * width), BF16),
        ],
    )(patch_rows, skip_rows, f_patch, gain, bias)


def join_back_body(low_ref, weight_ref, z_ref, inv_ref, gain_ref, skip_ref, patch_ref, sums_ref):
    width = skip_ref.shape[1]
    grad, normed = right_dot(low_ref[...], weight_ref[...]), z_ref[...]

    @pl.when(pl.program_id(0) == 0)
    def _():
        sums_ref[...] = jnp.zeros_like(sums_ref)

    sums_ref[0:1] += jnp.sum(grad * normed, axis=0, keepdims=True)
    sums_ref[1:2] += jnp.sum(grad, axis=0, keepdims=True)
    back = norm_back(grad * gain_ref[...], normed, inv_ref[...])
    patch_ref[...] = back[:, :width].astype(BF16)
    skip_ref[...] = back[:, width:]


def join_back(low_rows, f_skip, normed, inverse, gain):
    tokens, width = low_rows.shape
    block = math.gcd(tokens, 256)
    rows = lambda columns: pl.BlockSpec((block, columns), lambda t: (t, 0))
    fixed = lambda shape: pl.BlockSpec(shape, lambda t: (0, 0))
    return kernel_call(
        join_back_body,
        4 * tokens * width * width,
        18 * tokens * width,
        grid=(tokens // block,),
        in_specs=[rows(width), fixed(f_skip.shape), rows(2 * width), rows(1), fixed(gain.shape)],
        out_specs=[rows(width), rows(width), fixed((2, 2 * width))],
        out_shape=[
            jax.ShapeDtypeStruct((tokens, width), F32),
            jax.ShapeDtypeStruct((tokens, width), BF16),
            jax.ShapeDtypeStruct((2, 2 * width), F32),
        ],
    )(low_rows, f_skip, normed, inverse, gain)


def gelu_and_slope(inputs):
    scale, cubic = math.sqrt(2.0 / math.pi), 0.044715
    square = inputs * inputs
    curve = jnp.tanh(scale * inputs * (1.0 + cubic * square))
    half = 0.5 * (1.0 + curve)
    bend = 0.5 * inputs * (1.0 - curve * curve) * (scale * (1.0 + 3.0 * cubic * square))
    return ((inputs * half).astype(BF16), (half + bend).astype(BF16))


def swap_tiles(values_in):
    return lax.all_to_all(values_in, TILE, split_axis=0, concat_axis=0, tiled=True)


def shift_pairs(devices, step):
    return [(at, (at + step) % devices) for at in range(devices)]


def fetch(weight):
    devices = lax.axis_size("dp")
    return [weight] + [
        lax.ppermute(weight, "dp", shift_pairs(devices, step)) for step in range(1, devices)
    ]


def widen(pieces, first=None, joined=1):
    devices, me = lax.axis_size("dp"), lax.axis_index("dp")
    if first is not None:
        pieces = after(first, *pieces)
    slots = [lax.select_n((me - at) % devices, *pieces) for at in range(devices)]
    if joined > 1:
        split = [jnp.split(slot, joined, axis=1) for slot in slots]
        slots = [each for group in zip(*split) for each in group]
    return jnp.concatenate(slots, axis=1)


def narrow_blocks(blocks, first=None):
    devices, me = lax.axis_size("dp"), lax.axis_index("dp")
    received = []
    for step in range(1, devices):
        sent = lax.select_n((me + step) % devices, *blocks)
        received.append(lax.ppermute(sent, "dp", shift_pairs(devices, step)))
    if first is not None:
        received = after(first, *received)
    total = lax.select_n(me, *blocks).astype(F32)
    for piece in received:
        total = total + piece.astype(F32)
    return total


def narrow(weight_grad, first=None):
    return narrow_blocks(jnp.split(weight_grad, lax.axis_size("dp"), axis=1), first)


def by_device(weight_grads, parts):
    devices = lax.axis_size("dp")
    split = [jnp.split(weight_grad, devices, axis=1) for weight_grad in weight_grads]
    return [jnp.concatenate(blocks, axis=parts) for blocks in zip(*split)]


def sum_tiles(part_sums):
    devices, me = lax.axis_size(TILE), lax.axis_index(TILE)
    total, step = part_sums, devices // 2
    while step > 0:
        pairs = [(at, at ^ step) for at in range(devices)]
        lower, upper = jnp.split(total, 2, axis=0)
        high = (me // step) % 2 == 1
        sent = jnp.where(high, lower, upper)
        total = jnp.where(high, upper, lower) + lax.ppermute(sent, TILE, pairs)
        step //= 2
    return total


def total_tiles(part_sum):
    devices = lax.axis_size(TILE)
    total, step = part_sum, 1
    while step < devices:
        pairs = [(at, at ^ step) for at in range(devices)]
        total = total + lax.ppermute(total, TILE, pairs)
        step *= 2
    return total


def over_tiles(weight_grad):
    return lax.optimization_barrier(
        lax.psum_scatter(weight_grad, TILE, scatter_dimension=0, tiled=True)
    )


def tiles_whole(weight):
    return lax.all_gather(weight, TILE, axis=0, tiled=True)


def after(first, *values_in):
    return lax.optimization_barrier((first, *values_in))[1:]


def dot_over(left_mat, right_mat, left_axis, right_axis):
    return lax.dot_general(
        left_mat,
        right_mat,
        (((left_axis,), (right_axis,)), ((), ())),
        preferred_element_type=F32,
    )


def local_heads(
    latent,
    skip_input,
    text_states,
    timesteps,
    image_sides,
    cotangent,
    w_patch,
    w_skip,
    w_time,
    w_shift,
    w_qkv,
    w_out,
    w_query,
    w_text,
    w_cross,
    w_up,
    w_down,
    w_final,
    norm_params,
):
    dp_devices = lax.axis_size("dp")
    grid_devices = lax.axis_size(TILE)
    col_devices = lax.axis_size("col")
    grid_at = lax.axis_index(TILE)
    row_at = lax.axis_index("row")
    col_at = lax.axis_index("col")
    images, rows_tile, cols_tile, patch_width = latent.shape
    tile_len = rows_tile * cols_tile
    row_count = images * tile_len
    out_width = cotangent.shape[3]

    f_skip = tiles_whole(widen(fetch(w_skip)))
    small = jnp.concatenate([w_patch, w_final, norm_params], axis=1)
    small_widths = (w_patch.shape[1], w_final.shape[1], norm_params.shape[1])
    cuts = (0, small_widths[0], sum(small_widths[:2]), sum(small_widths))
    early = [jnp.pad(small, ((0, 0), (0, w_shift.shape[1] - small.shape[1]))), w_time, w_shift]
    ends = (small.shape[0], small.shape[0] + w_time.shape[0])
    part_small, part_time, part_shift_w = jnp.split(
        widen(fetch(jnp.concatenate(early, axis=0))), ends, axis=0
    )
    part_small = part_small.reshape(small.shape[0], dp_devices, -1)[:, :, : small.shape[1]]
    part_small = part_small.reshape(small.shape[0], -1)
    f_small = tiles_whole(part_small).reshape(-1, dp_devices, sum(small_widths))
    f_patch, f_final, f_norms = (
        f_small[:, :, cuts[at] : cuts[at + 1]].reshape(f_small.shape[0], -1) for at in range(3)
    )
    held_qkv = fetch(w_qkv)
    held_three = fetch(jnp.concatenate([w_out, w_query, w_cross], axis=1))
    held_text = fetch(w_text)
    held_up, held_down = fetch(w_up), fetch(w_down)
    model_width = skip_input.shape[3]
    head_count = HEADS
    head_dim = model_width // head_count
    text_len = text_states.shape[1]
    text_pad = -(-text_len // 128) * 128
    score_scale = head_dim ** (-0.5)
    query_scale = score_scale * LOG2E
    positions = jnp.arange(tile_len, dtype=jnp.int32)
    row_pos = row_at * rows_tile + positions // cols_tile
    col_pos = col_at * cols_tile + positions % cols_tile
    query_ok = (row_pos[None, :] < image_sides[:, None]) & (col_pos[None, :] < image_sides[:, None])
    valid = query_ok.astype(F32)
    keep_rows = query_ok.astype(F32).reshape(row_count, 1)
    tile_list = jnp.arange(grid_devices, dtype=jnp.int32)[:, None]
    key_row = tile_list // col_devices * rows_tile + (positions // cols_tile)[None, :]
    key_col = tile_list % col_devices * cols_tile + (positions % cols_tile)[None, :]
    sides = image_sides[:, None, None]
    key_ok = ((key_row[None] < sides) & (key_col[None] < sides)).astype(F32)
    flags = jnp.concatenate(
        [key_ok[:, :, None, :], jnp.zeros((images, grid_devices, 7, tile_len), F32)], axis=2
    )
    cos_row, sin_row, cos_col, sin_col = (
        jnp.transpose(table[:, 0, :]) for table in rope_tables(row_pos, col_pos, head_dim)
    )
    tables = (
        jnp.concatenate([cos_row, cos_row, cos_col, cos_col], axis=0),
        jnp.concatenate([-sin_row, sin_row, -sin_col, sin_col], axis=0),
    )
    norm_f = f_norms.astype(F32)

    embedding = time_embed(timesteps, FREQ).astype(BF16)
    freq_slice = part_time.shape[0]
    shift_slice = part_shift_w.shape[0]
    embed_cols = lax.dynamic_slice_in_dim(embedding, grid_at * freq_slice, freq_slice, 1)
    time_pre = total_tiles(plain_dot(embed_cols, part_time))
    time_float, silu_pull = jax.vjp(jax.nn.silu, time_pre)
    time_act = time_float.astype(BF16)
    act_cols = lax.dynamic_slice_in_dim(time_act, grid_at * shift_slice, shift_slice, 1)
    time_shift = total_tiles(plain_dot(act_cols, part_shift_w))

    patch_rows = latent.reshape(row_count, patch_width)
    skip_rows = skip_input.reshape(row_count, model_width)
    gain_skip = jnp.concatenate([norm_f[:, 8], norm_f[:, 10]])[None]
    bias_skip = jnp.concatenate([norm_f[:, 9], norm_f[:, 11]])[None]
    joined, joined_inv, skip_in = join_norm(patch_rows, skip_rows, f_patch, gain_skip, bias_skip)
    f_qkv = tiles_whole(widen(held_qkv, skip_in))
    part_three = widen(held_three, skip_in, 3)
    f_three = tiles_whole(part_three)
    f_out, f_query, f_cross = jnp.split(f_three, 3, axis=1)
    residual = plain_dot(skip_in, f_skip)
    first_z, first_inv = layer_norm(residual)
    first_pre = (first_z * norm_f[:, 0] + norm_f[:, 1]).reshape(
        images, tile_len, model_width
    ) + time_shift[:, None, :]
    first_in = first_pre.reshape(row_count, model_width).astype(BF16)
    part_text = widen(held_text, first_in)
    f_text = tiles_whole(part_text)
    first_rows = first_in.reshape(images, tile_len, model_width)
    own_qkv, qk_inv, tile_qkv, tile_att, tile_lse, att_rows = [], [], [], [], [], []
    for image in range(images):
        rows = first_rows[image]
        own, inverses = head_norm(
            rows,
            f_qkv,
            tables,
            valid[image : image + 1],
            grid_devices,
            head_dim,
            query_scale,
        )
        own_qkv.append(own)
        qk_inv.append(inverses)
        tile_qkv.append(swap_tiles(own))
    f_up = tiles_whole(widen(held_up, tile_qkv[0]))
    for image in range(images):
        att, lse = attend(tile_qkv[image], flags[image])
        tile_att.append(att)
        tile_lse.append(lse)
        own_att = swap_tiles(att).reshape(model_width, tile_len)
        att_rows.append(jnp.transpose(own_att))
    att_low = jnp.concatenate(att_rows, axis=0)
    residual_two = residual + plain_dot(att_low, f_out)
    f_down = tiles_whole(widen(held_down, residual_two))

    third_z, third_inv = layer_norm(residual_two)
    third_in = (third_z * norm_f[:, 2] + norm_f[:, 3]).astype(BF16)
    cross_pre = dot_over(f_query, third_in, 0, 1).reshape(head_count, head_dim, row_count)
    text_rows = jnp.pad(text_states, ((0, 0), (0, text_pad - text_len), (0, 0)))
    text_rows = text_rows.reshape(images * text_pad, -1)
    text_kv = dot_over(f_text, text_rows, 0, 1).reshape(2, head_count, head_dim, images * text_pad)
    crossed, cross_queries, cq_inv, cross_lse = cross_attend(
        cross_pre, text_kv, images, text_len, query_scale
    )
    cross_cols = crossed.reshape(model_width, row_count)
    residual_three = residual_two + left_dot(cross_cols, f_cross)
    second_z, second_inv = layer_norm(residual_three)
    second_in = (second_z * norm_f[:, 4] + norm_f[:, 5]).astype(BF16)
    up_pre = plain_dot(second_in, f_up)
    hidden_act, slope = lax.optimization_barrier(gelu_and_slope(up_pre))
    residual_four = residual_three + plain_dot(hidden_act, f_down)
    last_z, last_inv = layer_norm(residual_four)
    last_in = (last_z * norm_f[:, 6] + norm_f[:, 7]).astype(BF16)
    produced = plain_dot(last_in, f_final)
    prediction = (
        (produced * keep_rows).astype(BF16).reshape(images, rows_tile, cols_tile, out_width)
    )

    grad_out = (cotangent.reshape(row_count, out_width).astype(F32) * keep_rows).astype(BF16)
    d_final = left_dot(last_in, grad_out)
    grad_last = right_dot(grad_out, f_final)
    gain_final = jnp.sum(grad_last * last_z, axis=0)
    bias_final = jnp.sum(grad_last, axis=0)
    grad_four = norm_back(grad_last * norm_f[:, 6], last_z, last_inv)
    low_four = grad_four.astype(BF16)
    d_down = left_dot(hidden_act, low_four).astype(BF16)
    d_down, low_four = lax.optimization_barrier((d_down, low_four))
    t_down = over_tiles(d_down)
    grad_hidden = right_dot(low_four, f_down)
    grad_up = (grad_hidden * slope).astype(BF16)
    d_up = left_dot(second_in, grad_up).astype(BF16)
    d_up, grad_up = lax.optimization_barrier((d_up, grad_up))
    t_up = over_tiles(d_up)
    grad_second = right_dot(grad_up, f_up)
    gain_second = jnp.sum(grad_second * second_z, axis=0)
    bias_second = jnp.sum(grad_second, axis=0)
    grad_three = grad_four + norm_back(grad_second * norm_f[:, 4], second_z, second_inv)
    low_three = grad_three.astype(BF16)
    d_cross = plain_dot(cross_cols, low_three).astype(BF16)
    grad_crossed = dot_over(f_cross, low_three, 1, 1).astype(BF16)
    grad_cross_q, d_text_key, d_text_value = cross_back(
        cross_queries,
        text_kv,
        grad_crossed.reshape(head_count, head_dim, row_count),
        crossed,
        cq_inv,
        cross_lse,
        images,
        query_scale,
        score_scale,
    )
    t_down, grad_cross_q = lax.optimization_barrier((t_down, grad_cross_q))
    grad_cross_q = grad_cross_q.reshape(model_width, row_count)
    d_query = dot_over(third_in, grad_cross_q, 0, 1).astype(BF16)
    grad_third = dot_over(grad_cross_q, f_query, 0, 1)
    gain_third = jnp.sum(grad_third * third_z, axis=0)
    bias_third = jnp.sum(grad_third, axis=0)
    grad_two = grad_three + norm_back(grad_third * norm_f[:, 2], third_z, third_inv)
    low_two = grad_two.astype(BF16)
    low_two_rows = low_two.reshape(images, tile_len, model_width)
    tile_grads = []
    for image in range(images):
        grad_att = dot_over(f_out, low_two_rows[image], 1, 1).astype(BF16)
        tile_grads.append(swap_tiles(grad_att.reshape(tile_att[image].shape)))
    d_out = left_dot(att_low, low_two).astype(BF16)
    d_joint = jnp.concatenate(
        [
            d_out,
            d_query,
            d_cross,
            d_text_key.reshape(model_width, -1),
            d_text_value.reshape(model_width, -1),
        ],
        axis=1,
    )
    d_joint = with_layout_constraint(d_joint, Layout(major_to_minor=(0, 1)))
    d_joint, tile_grads[0] = lax.optimization_barrier((d_joint, tile_grads[0]))
    t_joint = over_tiles(d_joint)
    own_grads, grad_qkv, tile_back = [], None, None
    for image in range(images):
        if tile_back is not None:
            down_grad = narrow(t_down, tile_back)
            down_grad, tile_grads[image], tile_back = lax.optimization_barrier(
                (down_grad, tile_grads[image], tile_back)
            )
            own_grads.append(swap_tiles(tile_back))
        tile_back = attend_back(
            tile_qkv[image], tile_grads[image], tile_att[image], tile_lse[image], score_scale
        )
    own_grads.append(swap_tiles(tile_back))
    for image in range(images):
        if image == images - 1:
            up_grad = narrow(t_up, tile_back)
            up_grad, own_grads[-1], grad_qkv = lax.optimization_barrier(
                (up_grad, own_grads[-1], grad_qkv)
            )
        grad_qkv = head_back(
            own_grads[image],
            own_qkv[image],
            qk_inv[image],
            tables,
            valid[image : image + 1],
            query_scale,
            image,
            images,
            grad_qkv,
        )
    sum_text_kv = t_joint[:, 3 * model_width :].astype(F32)
    sum_text_kv = jnp.transpose(
        sum_text_kv.reshape(-1, head_dim, 2, images * text_pad), (2, 0, 1, 3)
    )
    group_heads = head_count // grid_devices
    own_key = lax.dynamic_slice_in_dim(text_kv[0], grid_at * group_heads, group_heads, 0)
    ck_z, ck_inv = layer_norm(jnp.swapaxes(own_key, 1, 2))
    grad_ckey = jnp.swapaxes(norm_back(jnp.swapaxes(sum_text_kv[0], 1, 2), ck_z, ck_inv), 1, 2)
    grad_kv = jnp.stack([grad_ckey, sum_text_kv[1]]).astype(BF16)
    grad_kv = tiles_whole(grad_kv.reshape(-1, images * text_pad))
    grad_qkv = grad_qkv.reshape(3 * model_width, row_count)
    d_qkv = dot_over(first_in, grad_qkv, 0, 1).astype(BF16)
    d_qkv, grad_qkv = lax.optimization_barrier((d_qkv, grad_qkv))
    t_qkv = over_tiles(d_qkv)
    grad_first = dot_over(grad_qkv, f_qkv, 0, 1)
    joint_blocks = by_device(jnp.split(t_joint[:, : 3 * model_width], 3, axis=1), 1)
    joint_grad = narrow_blocks(joint_blocks, grad_first)
    gain_first = jnp.sum(grad_first * first_z, axis=0)
    bias_first = jnp.sum(grad_first, axis=0)
    part_shift = jnp.sum(grad_first.reshape(images, tile_len, model_width), axis=1)
    grad_one = grad_two + norm_back(grad_first * norm_f[:, 0], first_z, first_inv)

    joint_grad, part_shift = lax.optimization_barrier((joint_grad, part_shift))
    shift_low = total_tiles(part_shift).astype(BF16)
    d_shift = left_dot(act_cols, shift_low).astype(BF16)
    grad_time_act = total_tiles(
        lax.dynamic_update_slice_in_dim(
            jnp.zeros_like(time_pre), right_dot(shift_low, part_shift_w), grid_at * shift_slice, 1
        )
    )
    grad_time_pre = silu_pull(grad_time_act)[0].astype(BF16)
    d_time = left_dot(embed_cols, grad_time_pre).astype(BF16)
    low_one = grad_one.astype(BF16)
    d_skip_w = left_dot(skip_in, low_one).astype(BF16)
    d_skip_w, low_one = lax.optimization_barrier((d_skip_w, low_one))
    t_qkv, d_skip_w, low_join, d_time, d_shift = lax.optimization_barrier(
        (t_qkv, d_skip_w, low_one, d_time, d_shift)
    )
    skip_grad, grad_patch, skip_sums = join_back(low_join, f_skip, joined, joined_inv, gain_skip)
    qkv_grad = narrow(t_qkv, skip_sums)
    qkv_grad, grad_kv, grad_patch, skip_grad, skip_sums = lax.optimization_barrier(
        (qkv_grad, grad_kv, grad_patch, skip_grad, skip_sums)
    )
    out_grad, query_w_grad, cross_grad = jnp.split(joint_grad, 3, axis=1)
    t_skip = over_tiles(d_skip_w)

    group_shape = (-1, 2, grid_devices, model_width // grid_devices)
    text_slice = text_states.shape[2] // grid_devices
    text_cols = lax.dynamic_slice_in_dim(text_rows, grid_at * text_slice, text_slice, 1)
    d_text = dot_over(text_cols, grad_kv, 0, 1).astype(BF16)
    d_text = jnp.swapaxes(d_text.reshape(text_slice, grid_devices, 2, -1), 1, 2)
    d_text = d_text.reshape(text_slice, -1)
    grouped_text = jnp.swapaxes(part_text.reshape(group_shape), 1, 2).reshape(part_text.shape)
    text_grad = dot_over(grad_kv, grouped_text, 0, 1).reshape(images, text_pad, text_slice)
    text_grad = text_grad[:, :text_len]

    late, width = [], w_shift.shape[1]
    for at in range(dp_devices):
        pair = d_text[:, 2 * at * width : 2 * (at + 1) * width]
        own = slice(at * width, (at + 1) * width)
        late.append(
            jnp.concatenate([pair[:, :width], pair[:, width:], d_time[:, own], d_shift[:, own]])
        )
    late_blocks = late
    skip_grad = skip_grad.reshape(images, rows_tile, cols_tile, model_width)
    gain_skips, bias_skips = skip_sums[0], skip_sums[1]
    d_patch = left_dot(grad_patch, patch_rows)
    latent_grad = plain_dot(grad_patch, f_patch).reshape(images, rows_tile, cols_tile, patch_width)
    d_norms = jnp.stack(
        [
            gain_first,
            bias_first,
            gain_third,
            bias_third,
            gain_second,
            bias_second,
            gain_final,
            bias_final,
            gain_skips[:model_width],
            bias_skips[:model_width],
            gain_skips[model_width:],
            bias_skips[model_width:],
        ],
        axis=1,
    )
    small_grads = jnp.concatenate(
        [
            grad.reshape(model_width, dp_devices, -1)
            for grad in (d_patch, d_final, d_norms)
        ],
        axis=2,
    )
    small_grads = sum_tiles(small_grads.reshape(model_width, -1))
    late = narrow_blocks(late_blocks, small_grads)
    rows = d_text.shape[0]
    text_w_grad = jnp.concatenate([late[:rows], late[rows : 2 * rows]], axis=1)
    time_w_grad, shift_w_grad = jnp.split(late[2 * rows :], [d_time.shape[0]], axis=0)
    last, small_rows, small_width = [], small_grads.shape[0], sum(small_widths)
    for at in range(dp_devices):
        few = small_grads[:, at * small_width : (at + 1) * small_width].astype(BF16).reshape(-1)
        few = jnp.pad(few, (0, -few.shape[0] % width)).reshape(-1, width)
        last.append(jnp.concatenate([t_skip[:, at * width : (at + 1) * width], few]))
    last = narrow_blocks(last)
    skip_w_grad = last[: t_skip.shape[0]]
    small_grads = last[t_skip.shape[0] :].reshape(-1)[: small_rows * small_width]
    small_grads = small_grads.reshape(small_rows, small_width)
    patch_grad, final_grad, norms_grad = (
        small_grads[:, cuts[at] : cuts[at + 1]] for at in range(3)
    )
    return (
        prediction,
        latent_grad,
        skip_grad,
        text_grad,
        patch_grad,
        skip_w_grad,
        time_w_grad,
        shift_w_grad,
        qkv_grad,
        out_grad,
        query_w_grad,
        text_w_grad,
        cross_grad,
        up_grad,
        down_grad,
        final_grad,
        norms_grad,
    )


def local(sizes, latent, *others):
    grid_devices = sizes["row"] * sizes["col"]
    tile_len = latent.shape[1] * latent.shape[2]
    if HEADS % grid_devices == 0 and tile_len % 128 == 0:
        return local_heads(latent, *others)
    return local_gathered(latent, *others)


def solution(mesh):
    return jax.shard_map(
        functools.partial(local, mesh.shape),
        mesh=mesh,
        in_specs=(
            P("dp", "row", "col", None),
            P("dp", "row", "col", None),
            P("dp", None, None),
            P("dp"),
            P("dp"),
            P("dp", "row", "col", None),
            P(("row", "col"), "dp"),
            P(("row", "col"), "dp"),
            P(("row", "col"), "dp"),
            P(("row", "col"), "dp"),
            P(("row", "col"), "dp"),
            P(("row", "col"), "dp"),
            P(("row", "col"), "dp"),
            P(("row", "col"), "dp"),
            P(("row", "col"), "dp"),
            P(("row", "col"), "dp"),
            P(("row", "col"), "dp"),
            P(("row", "col"), "dp"),
            P(("row", "col"), "dp"),
        ),
        out_specs=(
            P("dp", "row", "col", None),
            P("dp", "row", "col", None),
            P("dp", "row", "col", None),
            P("dp", None, ("row", "col")),
            P(("row", "col"), "dp"),
            P(("row", "col"), "dp"),
            P(("row", "col"), "dp"),
            P(("row", "col"), "dp"),
            P(("row", "col"), "dp"),
            P(("row", "col"), "dp"),
            P(("row", "col"), "dp"),
            P(("row", "col"), "dp"),
            P(("row", "col"), "dp"),
            P(("row", "col"), "dp"),
            P(("row", "col"), "dp"),
            P(("row", "col"), "dp"),
            P(("row", "col"), "dp"),
        ),
        check_vma=False,
    )
```
